32 devices in a mesh: rows: 8 (over z, x), heads: 4 (over y, core).
Axes of the slice: x: 2, y: 2, z: 4, core: 2. Of those that a mesh axis runs over, the one named last changes fastest.
Arguments:
- sheet: bfloat16 [128, 256, 768], P('rows'), may hold values from -6 to 6
- w_query: bfloat16 [768, 768], P(None, 'heads'), may hold values from -0.21875 to 0.21875
- w_key: bfloat16 [768, 768], P(None, 'heads'), may hold values from -0.21875 to 0.21875
- w_value: bfloat16 [768, 768], P(None, 'heads'), may hold values from -0.21875 to 0.21875
- cotangent: bfloat16 [128, 256, 768], P('rows', None, 'heads'), may hold values from -6 to 6
- lengths: int32 [128], P('rows'), may hold values from 32 to 256
Outputs:
- input_grad: bfloat16 [128, 256, 768], P('rows', None, 'heads')
- weight_grad: float32 [768, 3, 768], P('rows', None, 'heads')
The draws below stay inside these ranges and needn't reach their ends.
All inputs are finite; a program needn't handle non-finite values.
Results may differ from the reference program's by a relative error of at most 0.013.
Values may be sent and summed in bfloat16 or wider, within the bound.
No kernel may reach another device: no remote copies, remote signals or barrier semaphores. Data moves between devices by JAX's collectives and lax.ppermute only.
A program may use at most 128 MiB of HBM per device.

```python
import jax
import jax.numpy as jnp
from jax import lax

D = 768
HEADS = 12
HEAD_DIM = 64
C = 256
ROWS = 128
N_HEADS = 4


def place_ends(values, rng, smallest, largest):
    spot = [jax.random.randint(jax.random.fold_in(rng, axis), (), 0, length) for axis, length in enumerate(values.shape)]
    main_axis = values.shape.index(max(values.shape))
    neighbour = spot[:main_axis] + [(spot[main_axis] + 1) % values.shape[main_axis]] + spot[main_axis + 1:]
    return values.at[tuple(spot)].set(smallest).at[tuple(neighbour)].set(largest)


def spiked(drawn, own_key, source, target, shards_of, factor):
    def block_of(position):
        return (jnp.arange(drawn.shape[position]) // (drawn.shape[position] // shards_of)).reshape((-1,) + (1,) * (drawn.ndim - 1 - position))

    near = jax.random.permutation(own_key, shards_of)[block_of(target)]
    second = (block_of(target) + shards_of // 2) % shards_of
    return jnp.where((block_of(source) == near) | (block_of(source) == second), factor * drawn, drawn)


def shard_levels(stream_key, shape, pieces, low, top_value):
    def one(axis_at, shards_of):
        heights = jax.random.uniform(jax.random.fold_in(jax.random.fold_in(stream_key, 6), axis_at), (shards_of,), jnp.float32, low / len(pieces), top_value / len(pieces))
        return jnp.repeat(jnp.exp(heights), shape[axis_at] // shards_of).reshape((-1,) + (1,) * (len(shape) - axis_at - 1))

    loudness = one(*pieces[0])
    for cut in pieces[1:]:
        loudness = loudness * one(*cut)
    return loudness


def gaussian(stream_key, shape, spread, most, cuts=(), kind=jnp.bfloat16):
    values = spread * jax.random.normal(stream_key, shape, jnp.float32)
    if cuts:
        values = values * shard_levels(stream_key, shape, cuts, -0.22, 0.18)
    return jnp.clip(values, -most, most).astype(kind)


def heavy_noise(key, extent, scale, limit, cuts, heavy, kind=jnp.bfloat16):
    array = scale * jax.random.normal(key, extent, jnp.float32)
    if cuts:
        array = array * shard_levels(key, extent, cuts, -0.22, 0.18)
    return jnp.clip(spiked(array, jax.random.fold_in(key, 3), *heavy), -limit, limit).astype(kind)


def setup_inputs(seed: int = 0) -> dict:
    key_of = jax.random.split(jax.random.key(seed), 7)
    return {
        "sheet": heavy_noise(key_of[0], (ROWS, C, D), 1.0, 6.0, ((0, 8),), (0, 2, 8, 2.0)),
        "w_query": gaussian(key_of[1], (D, D), D ** -0.5, 0.21875, ((1, 4),)),
        "w_key": gaussian(key_of[2], (D, D), D ** -0.5, 0.21875, ((1, 4),)),
        "w_value": gaussian(key_of[3], (D, D), D ** -0.5, 0.21875, ((1, 4),)),
        "cotangent": gaussian(key_of[4], (ROWS, C, D), 1.0, 6.0, ((0, 8), (2, 4))),
        "lengths": place_ends(jax.random.randint(key_of[5], (ROWS,), C // 8, C + 1), jax.random.fold_in(key_of[5], 1), C // 8, C).astype(jnp.int32),
    }


def reference(sheet, w_query, w_key, w_value, cotangent, lengths):
    rows, cols, width = sheet.shape
    valid = (jnp.arange(cols, dtype=jnp.int32)[None, :] < lengths[:, None]).astype(jnp.float32)
    scale = 1.0 / jnp.sqrt(jnp.float32(HEAD_DIM * ROWS))
    flat = sheet.reshape(rows * cols, width)

    def project(weight):
        value = jnp.dot(flat, weight, preferred_element_type=jnp.float32).reshape(rows, cols, width)
        return (value * valid[..., None]).astype(jnp.bfloat16)
    query = project(w_query)
    key = project(w_key)
    value = project(w_value)
    split = (rows, cols, HEADS, HEAD_DIM)
    q32 = query.reshape(split).astype(jnp.float32)
    k32 = key.reshape(split).astype(jnp.float32)
    v32 = value.reshape(split).astype(jnp.float32)
    g32 = cotangent.reshape(split).astype(jnp.float32)
    logits = jnp.einsum('rihd,rjhd->hij', q32, k32)
    dprob = jnp.einsum('rihd,rjhd->hij', g32, v32)
    probs = jax.nn.softmax(scale * logits, axis=-1)
    probs_b = probs.astype(jnp.bfloat16)
    inner = lax.optimization_barrier(jnp.sum(probs * dprob, axis=-1, keepdims=True))
    dscore = (scale * probs * (dprob - inner)).astype(jnp.bfloat16)
    ds32 = dscore.astype(jnp.float32)
    mask = valid[..., None]
    dquery = (jnp.einsum('hij,rjhd->rihd', ds32, k32).reshape(rows, cols, width) * mask).astype(jnp.bfloat16)
    dkey = (jnp.einsum('hij,rihd->rjhd', ds32, q32).reshape(rows, cols, width) * mask).astype(jnp.bfloat16)
    dvalue = (jnp.einsum('hij,rihd->rjhd', probs_b.astype(jnp.float32), g32).reshape(rows, cols, width) * mask).astype(jnp.bfloat16)
    group = width // N_HEADS
    total = jnp.zeros((rows * cols, width), jnp.float32)
    for index in range(N_HEADS):
        lo = index * group
        grads = jnp.concatenate([dquery[..., lo:lo + group], dkey[..., lo:lo + group], dvalue[..., lo:lo + group]], axis=-1).reshape(rows * cols, 3 * group)
        weights = jnp.concatenate([w_query[:, lo:lo + group], w_key[:, lo:lo + group], w_value[:, lo:lo + group]], axis=1)
        part = lax.dot_general(grads, weights, (((1,), (1,)), ((), ())), preferred_element_type=jnp.float32)
        rounded = lax.optimization_barrier(part.astype(jnp.bfloat16))
        total = total + rounded.astype(jnp.float32)
    input_grad = total.reshape(rows, cols, width).astype(jnp.bfloat16)

    def weight_term(grad):
        return lax.dot_general(flat, grad.reshape(rows * cols, width), (((0,), (0,)), ((), ())), preferred_element_type=jnp.float32)
    weight_grad = jnp.stack([weight_term(dquery), weight_term(dkey), weight_term(dvalue)], axis=1)
    return (input_grad, weight_grad)
```

```python
import jax
import jax.numpy as jnp
from jax import lax
from jax.sharding import PartitionSpec as P

HEAD_DIM = 64
F32 = jnp.float32
BF16 = jnp.bfloat16


def shift(values, axis, step):
    n = lax.axis_size(axis)
    return lax.ppermute(values, axis, [(s, (s + step) % n) for s in range(n)])


def flip(values, axis, bit):
    n = lax.axis_size(axis)
    return lax.ppermute(values, axis, [(s, s ^ bit) for s in range(n)])


def block(values, index):
    return lax.dynamic_index_in_dim(values, index, 0, keepdims=False)


def scatter_sum(parts, axis):
    n = lax.axis_size(axis)
    if n > 8:
        return lax.psum_scatter(parts, axis, scatter_dimension=0, tiled=False)
    me = lax.axis_index(axis)
    narrow = parts.astype(BF16)
    got = [shift(block(narrow, (me + k) % n), axis, k) for k in range(1, n)]
    total = block(parts, me)
    for piece in got:
        total = total + piece.astype(F32)
    return total


def gather(values, axis):
    n = lax.axis_size(axis)
    if n > 8:
        return lax.all_gather(values, axis)
    me = lax.axis_index(axis)
    out = jnp.zeros((n,) + values.shape, values.dtype)
    out = lax.dynamic_update_index_in_dim(out, values, me, 0)
    for k in range(1, n):
        out = lax.dynamic_update_index_in_dim(out, shift(values, axis, k), (me + n - k) % n, 0)
    return out


def softmax_back(logits, dprob, scale):
    probs = jax.nn.softmax(scale * logits, axis=-1)
    inner = jnp.sum(probs * dprob, axis=-1, keepdims=True)
    dscore = scale * probs * (dprob - inner)
    return (probs.astype(BF16), dscore.astype(BF16))


def body(sheet, w_query, w_key, w_value, cotangent, lengths):
    row_dev, cols, width = sheet.shape
    local = w_query.shape[1]
    heads_here = local // HEAD_DIM
    n_rows = lax.axis_size("rows")
    n_heads = lax.axis_size("heads")
    total_rows = row_dev * n_rows
    scale = 1.0 / jnp.sqrt(jnp.float32(HEAD_DIM * total_rows))
    valid = (jnp.arange(cols, dtype=jnp.int32)[None, :] < lengths[:, None]).astype(F32)
    weights = jnp.concatenate([w_query, w_key, w_value], axis=1)
    flat = sheet.reshape(row_dev * cols, width)
    projected = jnp.dot(flat, weights, preferred_element_type=F32).reshape(row_dev, cols, 3 * local)
    projected = (projected * valid[..., None]).astype(BF16)
    split = (row_dev, cols, heads_here, HEAD_DIM)
    query = projected[..., :local].reshape(split)
    key = projected[..., local : 2 * local].reshape(split)
    value = projected[..., 2 * local :].reshape(split)
    grad_out = cotangent.reshape(split)
    logit_part = jnp.einsum("rihd,rjhd->hij", query, key, preferred_element_type=F32)
    dprob_part = jnp.einsum("rihd,rjhd->hij", grad_out, value, preferred_element_type=F32)
    own = cols // n_rows

    def by_shard(part):
        return part.reshape(heads_here, n_rows, own, cols).transpose(1, 0, 2, 3)

    logits = scatter_sum(by_shard(logit_part), "rows")
    dprob = scatter_sum(by_shard(dprob_part), "rows")
    probs_own, dscore_own = softmax_back(logits, dprob, scale)

    def whole(part):
        return gather(part, "rows").transpose(1, 0, 2, 3).reshape(heads_here, cols, cols)

    probs_b = whole(probs_own)
    dscore = whole(dscore_own)
    mask = valid[..., None]
    dquery = jnp.einsum("hij,rjhd->rihd", dscore, key, preferred_element_type=F32).reshape(
        row_dev, cols, local
    )
    dkey = jnp.einsum("hij,rihd->rjhd", dscore, query, preferred_element_type=F32).reshape(
        row_dev, cols, local
    )
    dvalue = jnp.einsum("hij,rihd->rjhd", probs_b, grad_out, preferred_element_type=F32).reshape(
        row_dev, cols, local
    )
    grads = (jnp.concatenate([dquery, dkey, dvalue], axis=-1) * mask).astype(BF16)
    flat_grads = grads.reshape(row_dev * cols, 3 * local)

    me = lax.axis_index("heads")
    chunks = 4
    step = row_dev // chunks
    pieces = []
    for c in range(chunks):
        rows = grads[c * step : (c + 1) * step].reshape(step * cols, 3 * local)
        part = lax.dot_general(
            weights.reshape(n_heads, width // n_heads, 3 * local),
            rows,
            (((2,), (1,)), ((), ())),
            preferred_element_type=F32,
        ).astype(BF16)
        part = part.reshape((n_heads, width // n_heads, step, cols))
        bit = 1
        live = part
        while bit < n_heads:
            half = live.reshape((live.shape[0] // 2, 2) + live.shape[1:])
            mine = (me // bit) % 2
            keep = lax.dynamic_index_in_dim(half, mine, 1, keepdims=False)
            give = lax.dynamic_index_in_dim(half, 1 - mine, 1, keepdims=False)
            live = (keep.astype(F32) + flip(give, "heads", bit).astype(F32)).astype(BF16)
            bit *= 2
        pieces.append(live[0].transpose(1, 2, 0))
    input_grad = jnp.concatenate(pieces, axis=0)

    weight_part = lax.dot_general(flat, flat_grads, (((0,), (0,)), ((), ())), preferred_element_type=F32)
    rows_out = width // n_rows
    weight_grad = scatter_sum(weight_part.reshape(n_rows, rows_out, 3 * local), "rows")
    return (input_grad, weight_grad.reshape(rows_out, 3, local))


def solution(mesh):
    in_specs = (
        P("rows", None, None),
        P(None, "heads"),
        P(None, "heads"),
        P(None, "heads"),
        P("rows", None, "heads"),
        P("rows"),
    )
    out_specs = (P("rows", None, "heads"), P("rows", None, "heads"))
    return jax.shard_map(body, mesh=mesh, in_specs=in_specs, out_specs=out_specs, check_vma=False)
```

```python
import functools

import jax
import jax.numpy as jnp
from jax import lax
from jax.experimental import pallas as pl
from jax.experimental.pallas import tpu as pltpu
from jax.sharding import PartitionSpec as P

HEAD_DIM = 64
F32 = jnp.float32
BF16 = jnp.bfloat16
LIMIT = 40 * 1024 * 1024

NN = (((1,), (0,)), ((), ()))
NT = (((1,), (1,)), ((), ()))
TN = (((0,), (0,)), ((), ()))


def mm(a, b, dims):
    return lax.dot_general(a, b, dims, preferred_element_type=F32)


def flip(values, axis, bit):
    n = lax.axis_size(axis)
    return lax.ppermute(values, axis, [(s, s ^ bit) for s in range(n)])


def params():
    return pltpu.CompilerParams(vmem_limit_bytes=LIMIT)


def cost(flops, moved):
    return pl.CostEstimate(flops=int(flops), bytes_accessed=int(moved), transcendentals=0)


def smem():
    return pl.BlockSpec(memory_space=pltpu.SMEM)


def lane_mask(length, cols):
    return (lax.broadcasted_iota(jnp.int32, (1, cols), 1) < length).astype(F32)


def project_kernel(lengths, sheet, wq, wk, wv, cot, qk, gt, parts, wt, acc):
    step = pl.program_id(0)
    rows, cols, _ = sheet.shape
    local = wq.shape[1]
    heads = local // HEAD_DIM

    @pl.when(step == 0)
    def _():
        for index, weight in enumerate((wq, wk, wv)):
            wt[index] = weight[...].T
        acc[...] = jnp.zeros_like(acc)

    projected = [[], [], []]
    for r in range(rows):
        mask = lane_mask(lengths[step * rows + r], cols)
        row = sheet[r]
        for index in range(3):
            value = (mm(wt[index], row, NT) * mask).astype(BF16)
            projected[index].append(value.reshape(heads, HEAD_DIM, cols))
        gt[:, r] = cot[r].T.reshape(heads, HEAD_DIM, cols)
    q, k, v = [jnp.stack(p, axis=1) for p in projected]
    qk[:heads] = q
    qk[heads:] = k
    for h in range(heads):
        flat = (rows * HEAD_DIM, cols)
        acc[0, h] += mm(q[h].reshape(flat), k[h].reshape(flat), TN)
        acc[1, h] += mm(gt[h].reshape(flat), v[h].reshape(flat), TN)

    @pl.when(step == pl.num_programs(0) - 1)
    def _():
        shards = parts.shape[0]
        for kind in range(2):
            for h in range(heads):
                parts[:, kind, h] = acc[kind, h].reshape(shards, cols // shards, cols).astype(parts.dtype)


def project(lengths, sheet, wq, wk, wv, cot, shards, kind, block):
    rows, cols, width = sheet.shape
    local = wq.shape[1]
    heads = local // HEAD_DIM
    whole = lambda shape: pl.BlockSpec(shape, lambda s: (0,) * len(shape))
    parts = (shards, 2, heads, cols // shards, cols)
    return pl.pallas_call(
        project_kernel,
        grid=(rows // block,),
        in_specs=[
            smem(),
            pl.BlockSpec((block, cols, width), lambda s: (s, 0, 0)),
            whole(wq.shape),
            whole(wq.shape),
            whole(wq.shape),
            pl.BlockSpec((block, cols, local), lambda s: (s, 0, 0)),
        ],
        out_specs=[
            pl.BlockSpec((2 * heads, block, HEAD_DIM, cols), lambda s: (0, s, 0, 0)),
            pl.BlockSpec((heads, block, HEAD_DIM, cols), lambda s: (0, s, 0, 0)),
            whole(parts),
        ],
        out_shape=[
            jax.ShapeDtypeStruct((2 * heads, rows, HEAD_DIM, cols), BF16),
            jax.ShapeDtypeStruct((heads, rows, HEAD_DIM, cols), BF16),
            jax.ShapeDtypeStruct(parts, kind),
        ],
        scratch_shapes=[
            pltpu.VMEM((3, local, width), BF16),
            pltpu.VMEM((2, heads, cols, cols), F32),
        ],
        compiler_params=params(),
        cost_estimate=cost(2 * rows * cols * local * (3 * width + 2 * cols), 2 * rows * cols * (width + 4 * local)),
        name="project",
    )(lengths, sheet, wq, wk, wv, cot)


def softmax_kernel(scale, got, out):
    logits = jnp.sum(got[:, 0].astype(F32), axis=0) * scale
    dprob = jnp.sum(got[:, 1].astype(F32), axis=0)
    shifted = jnp.exp(logits - jnp.max(logits, axis=-1, keepdims=True))
    probs = shifted / jnp.sum(shifted, axis=-1, keepdims=True)
    inner = jnp.sum(probs * dprob, axis=-1, keepdims=True)
    both = (probs.astype(BF16), (scale * probs * (dprob - inner)).astype(BF16))
    for copy in range(out.shape[0]):
        out[copy, 0] = both[0]
        out[copy, 1] = both[1]


def softmax_back(got, scale, copies):
    return pl.pallas_call(
        functools.partial(softmax_kernel, scale),
        out_shape=jax.ShapeDtypeStruct((copies,) + got.shape[1:], BF16),
        compiler_params=params(),
        cost_estimate=cost(got.size * 8, got.size * 4),
        name="softmax_back",
    )(got)


def backward_kernel(first, lengths, me, scores, qk, gt, wq, wk, wv, *rest):
    blocks, grads = rest[:-1], rest[-1]
    heads, rows, _, cols = gt.shape
    flat = (rows * HEAD_DIM, cols)
    square = lambda kind, h: scores[:, kind, h].reshape(cols, cols)
    split = (rows, HEAD_DIM, cols)
    masks = jnp.stack([lane_mask(lengths[first + r], cols) for r in range(rows)])
    for h in range(heads):
        probs, dscore = square(0, h), square(1, h)
        dq = mm(qk[heads + h].reshape(flat), dscore, NT)
        dk = mm(qk[h].reshape(flat), dscore, NN)
        dv = mm(gt[h].reshape(flat), probs, NN)
        for index, value in enumerate((dq, dk, dv)):
            grads[index * heads + h] = (value.reshape(split) * masks).astype(BF16)
    local = heads * HEAD_DIM
    for j, out in enumerate(blocks):
        here = me[0] ^ j
        for r in range(rows):
            total = None
            for index, weight in enumerate((wq, wk, wv)):
                grad = grads[index * heads : (index + 1) * heads, r].reshape(local, cols)
                term = mm(weight[here], grad, NN)
                total = term if total is None else total + term
            out[r] = total.astype(BF16)


def backward(first, count, lengths, me, scores, qk, gt, wq, wk, wv):
    heads, rows, _, cols = gt.shape
    n, share, local = wq.shape
    whole = lambda a: pl.BlockSpec(a.shape, lambda s: (0,) * a.ndim)
    at = first // count
    return pl.pallas_call(
        functools.partial(backward_kernel, first),
        grid=(1,),
        in_specs=[
            smem(),
            smem(),
            whole(scores),
            pl.BlockSpec((2 * heads, count, HEAD_DIM, cols), lambda s: (0, at, 0, 0)),
            pl.BlockSpec((heads, count, HEAD_DIM, cols), lambda s: (0, at, 0, 0)),
            whole(wq),
            whole(wq),
            whole(wq),
        ],
        out_specs=[pl.BlockSpec((count, share, cols), lambda s: (0, 0, 0))] * n
        + [pl.BlockSpec((3 * heads, count, HEAD_DIM, cols), lambda s: (0, 0, 0, 0))],
        out_shape=[jax.ShapeDtypeStruct((count, share, cols), BF16)] * n
        + [jax.ShapeDtypeStruct((3 * heads, count, HEAD_DIM, cols), BF16)],
        compiler_params=params(),
        cost_estimate=cost(
            2 * count * cols * local * 3 * (cols + n * share), 2 * count * cols * (6 * local + n * share)
        ),
        name="backward",
    )(lengths, me, scores, qk, gt, wq, wk, wv)


def add_kernel(keep, got, out):
    out[...] = (keep[...].astype(F32) + got[...].astype(F32)).astype(BF16)


def add(keep, got):
    return pl.pallas_call(
        add_kernel,
        out_shape=jax.ShapeDtypeStruct(keep.shape, BF16),
        compiler_params=params(),
        cost_estimate=cost(keep.size, keep.size * 6),
        name="add",
    )(keep, got)


def finish_kernel(keep, got, *rest):
    out = rest[-1]
    for r in range(keep.shape[0]):
        total = (keep[r].astype(F32) + got[r].astype(F32)).astype(BF16)
        out[r] = total.T


def finish(keep, got, at, total_rows, before):
    count, share, cols = keep.shape
    spec = pl.BlockSpec(keep.shape, lambda s: (0, 0, 0))
    extra = [] if before is None else [before]
    return pl.pallas_call(
        finish_kernel,
        grid=(1,),
        in_specs=[spec, spec] + [pl.BlockSpec(memory_space=pl.ANY)] * len(extra),
        out_specs=pl.BlockSpec((count, cols, share), lambda s: (at, 0, 0)),
        out_shape=jax.ShapeDtypeStruct((total_rows, cols, share), BF16),
        input_output_aliases={2: 0} if extra else {},
        compiler_params=params(),
        cost_estimate=cost(keep.size, keep.size * 6),
        name="finish",
    )(keep, got, *extra)


def weight_kernel(sheet, *rest):
    grads, out, acc = rest[:-2], rest[-2], rest[-1]
    step = pl.program_id(0)
    rows, cols, width = sheet.shape

    @pl.when(step == 0)
    def _():
        acc[...] = jnp.zeros_like(acc)

    for index, grad in enumerate(grads):
        @pl.when(step == index)
        def _():
            n = grad.shape[0] * HEAD_DIM
            left = jnp.concatenate([grad[:, r].reshape(n, cols) for r in range(rows)], axis=1)
            acc[...] += mm(left, sheet[...].reshape(rows * cols, width), NN)

    @pl.when(step == pl.num_programs(0) - 1)
    def _():
        out[...] = acc[...].T.reshape(out.shape).astype(out.dtype)


def weight_part(sheet, grads, shards, kind):
    rows, cols, width = sheet.shape
    count = rows // len(grads)
    columns = grads[0].shape[0] * HEAD_DIM
    shape = (shards, width // shards, columns)
    return pl.pallas_call(
        weight_kernel,
        grid=(len(grads),),
        in_specs=[pl.BlockSpec((count, cols, width), lambda s: (s, 0, 0))]
        + [pl.BlockSpec(g.shape, lambda s: (0, 0, 0, 0)) for g in grads],
        out_specs=pl.BlockSpec(shape, lambda s: (0, 0, 0)),
        out_shape=jax.ShapeDtypeStruct(shape, kind),
        scratch_shapes=[pltpu.VMEM((columns, width), F32)],
        compiler_params=params(),
        cost_estimate=cost(2 * rows * cols * width * columns, 2 * rows * cols * (width + columns)),
        name="weight_part",
    )(sheet, *grads)


def sum_kernel(got, out):
    out[...] = jnp.sum(got[...].astype(F32), axis=0)


def sum_parts(got):
    return pl.pallas_call(
        sum_kernel,
        out_shape=jax.ShapeDtypeStruct(got.shape[1:], F32),
        compiler_params=params(),
        cost_estimate=cost(got.size, got.size * 2),
        name="sum_parts",
    )(got)


def body(sheet, w_query, w_key, w_value, cotangent, lengths):
    row_dev, cols, width = sheet.shape
    local = w_query.shape[1]
    n_rows = lax.axis_size("rows")
    n_heads = lax.axis_size("heads")
    scale = float(1.0 / (HEAD_DIM * row_dev * n_rows) ** 0.5)
    direct = n_rows <= 8
    shards = n_rows if direct else 1
    chunk = 4

    qk, gt, parts = project(
        lengths, sheet, w_query, w_key, w_value, cotangent, shards, BF16 if direct else F32, 4
    )
    if direct:
        got = lax.all_to_all(parts, "rows", 0, 0)
        scores = lax.all_to_all(softmax_back(got, scale, shards), "rows", 0, 0)
    else:
        scores = softmax_back(lax.psum(parts, "rows"), scale, 1)

    me = lax.axis_index("heads").astype(jnp.int32).reshape(1)
    by_device = [w.reshape(n_heads, width // n_heads, local) for w in (w_query, w_key, w_value)]
    out, grads = None, []
    for first in range(0, row_dev, chunk):
        *live, grad = backward(first, chunk, lengths, me, scores, qk, gt, *by_device)
        grads.append(grad)
        bit = 1
        while bit < n_heads:
            give, keep = live[1::2], live[0::2]
            got = [flip(g, "heads", bit) for g in give]
            last = bit * 2 == n_heads
            if last:
                out = finish(keep[0], got[0], first // chunk, row_dev, out)
            else:
                live = [add(a, b) for a, b in zip(keep, got)]
            bit *= 2

    if direct:
        got = lax.all_to_all(weight_part(sheet, grads, shards, BF16), "rows", 0, 0)
        weight_grad = sum_parts(got)
    else:
        weight_grad = lax.psum_scatter(
            weight_part(sheet, grads, 1, F32)[0], "rows", scatter_dimension=0, tiled=True
        )
    return (out, weight_grad.reshape(width // n_rows, 3, local))


def solution(mesh):
    in_specs = (
        P("rows", None, None),
        P(None, "heads"),
        P(None, "heads"),
        P(None, "heads"),
        P("rows", None, "heads"),
        P("rows"),
    )
    out_specs = (P("rows", None, "heads"), P("rows", None, "heads"))
    return jax.shard_map(body, mesh=mesh, in_specs=in_specs, out_specs=out_specs, check_vma=False)
```

```python
import functools

import jax
import jax.numpy as jnp
from jax import lax
from jax.experimental import pallas as pl
from jax.experimental.pallas import tpu as pltpu
from jax.sharding import PartitionSpec as P

HEAD_DIM = 64
F32 = jnp.float32
BF16 = jnp.bfloat16
MIB = 1024 * 1024

NN = (((1,), (0,)), ((), ()))
NT = (((1,), (1,)), ((), ()))
TN = (((0,), (0,)), ((), ()))


def mm(a, b, dims):
    return lax.dot_general(a, b, dims, preferred_element_type=F32)


def flip(values, axis, bit):
    n = lax.axis_size(axis)
    return lax.ppermute(values, axis, [(s, s ^ bit) for s in range(n)])


def cost(flops, moved):
    return pl.CostEstimate(flops=int(flops), bytes_accessed=int(moved), transcendentals=0)


SMEM = pl.BlockSpec(memory_space=pltpu.SMEM)
VMEM = pl.BlockSpec(memory_space=pltpu.VMEM)
ANY = pl.BlockSpec(memory_space=pl.ANY)


def like(shape, dtype=BF16):
    return jax.ShapeDtypeStruct(shape, dtype)


def in_vmem(kernel, name, out, *operands, scalars=0, after=(), limit=12, flops=0):
    many = len(after)

    def run(*refs):
        kernel(*refs[: len(operands)], *refs[len(operands) + many :])

    moved = 2 * sum(a.size for a in operands) + 2 * sum(o.size for o in out)
    return pl.pallas_call(
        run,
        in_specs=[SMEM] * scalars + [VMEM] * (len(operands) - scalars) + [ANY] * many,
        out_specs=[VMEM] * len(out),
        out_shape=list(out),
        compiler_params=pltpu.CompilerParams(vmem_limit_bytes=limit * MIB),
        cost_estimate=cost(flops, moved),
        name=name,
    )(*operands, *after)


def lane_mask(length, cols):
    return (lax.broadcasted_iota(jnp.int32, (1, cols), 1) < length).astype(F32)


def put_shards(me, acc, outs):
    shards = acc.shape[1]
    for j in range(shards):
        out = outs[j % len(outs)]
        out[j // len(outs)] = acc[:, me ^ j].astype(out.dtype)


def query_key_kernel(lengths, me, sheet, wq, wk, qk, *rest):
    outs, wt, acc = rest[:-2], rest[-2], rest[-1]
    step = pl.program_id(0)
    rows, cols, _ = sheet.shape
    local = wq.shape[0]
    heads = local // HEAD_DIM

    @pl.when(step == 0)
    def _():
        wt[:local] = wq[...]
        wt[local:] = wk[...]
        acc[...] = jnp.zeros_like(acc)

    for r in range(rows):
        mask = lane_mask(lengths[step * rows + r], cols)
        value = (mm(wt[...], sheet[r], NT) * mask).astype(BF16)
        qk[r] = value.reshape(2 * heads, HEAD_DIM, cols)
    flat = (rows * HEAD_DIM, cols)
    for h in range(heads):
        term = mm(qk[:, h].reshape(flat), qk[:, heads + h].reshape(flat), TN)
        acc[h] += term.reshape(acc.shape[1:])

    @pl.when(step == pl.num_programs(0) - 1)
    def _():
        put_shards(me[0], acc, outs)


def value_kernel(lengths, me, sheet, wq, wk, wv, cot, natural, *rest):
    outs, turned, acc = rest[:-2], rest[-2], rest[-1]
    step = pl.program_id(0)
    rows, cols, _ = sheet.shape
    local = wq.shape[0]
    heads = local // HEAD_DIM

    @pl.when(step == 0)
    def _():
        acc[...] = jnp.zeros_like(acc)
        for index, weight in enumerate((wq, wk, wv)):
            turned[:, :, index * local : (index + 1) * local] = weight[...].T.reshape(
                turned.shape[:2] + (local,)
            )
        for j in range(turned.shape[0]):
            natural[j] = turned[me[1] ^ j]

    values = []
    for r in range(rows):
        mask = lane_mask(lengths[step * rows + r], cols)
        value = (mm(wv[...], sheet[r], NT) * mask).astype(BF16)
        values.append(value.reshape(heads, HEAD_DIM, cols))
    flat = (rows * HEAD_DIM, cols)
    for h in range(heads):
        left = cot[:, h * HEAD_DIM : (h + 1) * HEAD_DIM].reshape(flat)
        right = jnp.concatenate([v[h] for v in values], axis=0)
        acc[h] += mm(left, right, TN).reshape(acc.shape[1:])

    @pl.when(step == pl.num_programs(0) - 1)
    def _():
        put_shards(me[0], acc, outs)


def part_shapes(shards, heads, cols):
    if shards == 1:
        return [like((1, heads, cols, cols), F32)]
    return [like((shards // 2, heads, cols // shards, cols))] * 2


def whole(shape):
    return pl.BlockSpec(shape, lambda s: (0,) * len(shape))


def query_key(lengths, me, sheet, wq, wk, shards, block):
    rows, cols, width = sheet.shape
    local = wq.shape[0]
    heads = local // HEAD_DIM
    outs = part_shapes(shards, heads, cols)
    return pl.pallas_call(
        query_key_kernel,
        grid=(rows // block,),
        in_specs=[
            SMEM,
            SMEM,
            pl.BlockSpec((block, cols, width), lambda s: (s, 0, 0)),
            whole(wq.shape),
            whole(wk.shape),
        ],
        out_specs=[pl.BlockSpec((block, 2 * heads, HEAD_DIM, cols), lambda s: (s, 0, 0, 0))]
        + [whole(o.shape) for o in outs],
        out_shape=[like((rows, 2 * heads, HEAD_DIM, cols))] + outs,
        scratch_shapes=[
            pltpu.VMEM((2 * local, width), BF16),
            pltpu.VMEM((heads, shards, cols // shards, cols), F32),
        ],
        compiler_params=pltpu.CompilerParams(vmem_limit_bytes=20 * MIB),
        cost_estimate=cost(2 * rows * cols * local * (2 * width + cols), 2 * rows * cols * (width + 2 * local)),
        name="query_key",
    )(lengths, me, sheet, wq, wk)


def value_dprob(lengths, me, sheet, wq, wk, wv, cot, shards, devices, block):
    rows, cols, width = sheet.shape
    local = wv.shape[0]
    heads = local // HEAD_DIM
    outs = part_shapes(shards, heads, cols)
    natural = (devices, width // devices, 3 * local)
    return pl.pallas_call(
        value_kernel,
        grid=(rows // block,),
        in_specs=[
            SMEM,
            SMEM,
            pl.BlockSpec((block, cols, width), lambda s: (s, 0, 0)),
            whole(wq.shape),
            whole(wk.shape),
            whole(wv.shape),
            pl.BlockSpec((block, local, cols), lambda s: (s, 0, 0)),
        ],
        out_specs=[whole(natural)] + [whole(o.shape) for o in outs],
        out_shape=[like(natural)] + outs,
        scratch_shapes=[
            pltpu.VMEM(natural, BF16),
            pltpu.VMEM((heads, shards, cols // shards, cols), F32),
        ],
        compiler_params=pltpu.CompilerParams(vmem_limit_bytes=20 * MIB),
        cost_estimate=cost(2 * rows * cols * local * (width + cols), 2 * rows * cols * (width + local)),
        name="value_dprob",
    )(lengths, me, sheet, wq, wk, wv, cot)


def add_split_kernel(keep, got, give_out, keep_out):
    for j in range(keep.shape[0]):
        total = (keep[j].astype(F32) + got[j].astype(F32)).astype(BF16)
        (give_out if j % 2 else keep_out)[j // 2] = total


def add_split(keep, got):
    half = like((keep.shape[0] // 2,) + keep.shape[1:])
    return in_vmem(add_split_kernel, "add_split", (half, half), keep, got)


def halve(keep, give, axis, bits):
    for bit in bits[:-1]:
        give, keep = add_split(keep, flip(give, axis, bit))
    return keep, flip(give, axis, bits[-1])


def softmax_kernel(scale, *refs):
    *terms, probs_out, dscore_out = refs
    half = len(terms) // 2
    total = lambda some: functools.reduce(jnp.add, [t[0].astype(F32) for t in some])
    logits = total(terms[:half]) * scale
    dprob = total(terms[half:])
    shifted = jnp.exp(logits - jnp.max(logits, axis=-1, keepdims=True))
    probs = shifted / jnp.sum(shifted, axis=-1, keepdims=True)
    inner = jnp.sum(probs * dprob, axis=-1, keepdims=True)
    probs_out[0] = probs.astype(BF16)
    dscore_out[0] = (scale * probs * (dprob - inner)).astype(BF16)


def softmax_back(logits, dprob, scale):
    out = like(logits[0].shape)
    return in_vmem(
        functools.partial(softmax_kernel, scale), "softmax_back", (out, out), *logits, *dprob, limit=16
    )


def double(values, axis, bits):
    order = [0]
    for bit in bits[:-1]:
        values = jnp.concatenate([values, flip(values, axis, bit)], axis=0)
        order = order + [j ^ bit for j in order]
    other = flip(values, axis, bits[-1])
    return (values, other), (order, [j ^ bits[-1] for j in order])


def assemble_kernel(orders, me, *refs):
    pieces, outs = refs[:-2], refs[-2:]
    per = len(orders)
    for kind, out in enumerate(outs):
        for piece, order in zip(pieces[kind * per : (kind + 1) * per], orders):
            for t, j in enumerate(order):
                out[me[0] ^ j] = piece[t]


def assemble(me, probs, dscore, orders, shards):
    out = like((shards,) + probs[0].shape[1:])
    return in_vmem(
        functools.partial(assemble_kernel, orders), "assemble", (out, out), me, *probs, *dscore, scalars=1
    )


def backward_kernel(first, lengths, probs, dscore, qk, cot, weights, *rest):
    blocks, grads = rest[:-1], rest[-1]
    count, all_heads, _, cols = grads.shape
    heads = all_heads // 3
    rows = pl.ds(first, count)
    flat = (count * HEAD_DIM, cols)
    split = (count, HEAD_DIM, cols)
    masks = jnp.stack([lane_mask(lengths[first + r], cols) for r in range(count)])
    for h in range(heads):
        p, ds = [ref[:, h].reshape(cols, cols) for ref in (probs, dscore)]
        g = cot[rows, h * HEAD_DIM : (h + 1) * HEAD_DIM].reshape(flat)
        dq = mm(qk[rows, heads + h].reshape(flat), ds, NT)
        dk = mm(qk[rows, h].reshape(flat), ds, NN)
        dv = mm(g, p, NN)
        for index, value in enumerate((dq, dk, dv)):
            grads[:, index * heads + h] = (value.reshape(split) * masks).astype(BF16)
    devices, share, columns = weights.shape
    left = weights[...].reshape(devices * share, columns)
    for r in range(count):
        part = mm(left, grads[r].reshape(columns, cols), NN).astype(BF16)
        for j in range(devices):
            blocks[j % 2][j // 2, r] = part[j * share : (j + 1) * share]


def backward(first, count, lengths, probs, dscore, qk, cot, weights, after):
    cols = qk.shape[-1]
    heads = qk.shape[1] // 2
    devices, share, columns = weights.shape
    half = like((devices // 2, count, share, cols))
    return in_vmem(
        functools.partial(backward_kernel, first),
        "backward",
        (half, half, like((count, 3 * heads, HEAD_DIM, cols))),
        lengths,
        probs,
        dscore,
        qk,
        cot,
        weights,
        scalars=1,
        after=after,
        limit=16,
        flops=2 * count * cols * columns * (cols + devices * share),
    )


def finish_kernel(keep, got, *rest):
    out = rest[-1]
    out[...] = (keep[0].astype(F32) + got[0].astype(F32)).astype(BF16)


def finish(keep, got, at, total_rows, before):
    _, count, share, cols = keep.shape
    spec = pl.BlockSpec(keep.shape, lambda s: (0, 0, 0, 0))
    extra = [] if before is None else [before]
    return pl.pallas_call(
        finish_kernel,
        grid=(1,),
        in_specs=[spec, spec] + [ANY] * len(extra),
        out_specs=pl.BlockSpec((count, share, cols), lambda s: (at, 0, 0)),
        out_shape=like((total_rows, share, cols)),
        input_output_aliases={2: 0} if extra else {},
        compiler_params=pltpu.CompilerParams(vmem_limit_bytes=12 * MIB),
        cost_estimate=cost(keep.size, keep.size * 6),
        name="finish",
    )(keep, got, *extra)


def weight_kernel(many, *refs):
    sheet, grads, out, acc = refs[0], refs[1 : 1 + many], refs[-2], refs[-1]
    step = pl.program_id(0)
    rows, cols, width = sheet.shape

    @pl.when(step == 0)
    def _():
        acc[...] = jnp.zeros_like(acc)

    for index, grad in enumerate(grads):
        @pl.when(step == index)
        def _():
            n = grad.shape[1] * HEAD_DIM
            left = jnp.concatenate([grad[r].reshape(n, cols) for r in range(rows)], axis=1)
            acc[...] += mm(left, sheet[...].reshape(rows * cols, width), NN)

    @pl.when(step == pl.num_programs(0) - 1)
    def _():
        out[...] = acc[...].T.reshape(out.shape).astype(out.dtype)


def weight_part(sheet, grads, shards, kind, after):
    rows, cols, width = sheet.shape
    many = len(grads)
    count = rows // many
    columns = grads[0].shape[1] * HEAD_DIM
    shape = (shards, width // shards, columns)
    return pl.pallas_call(
        functools.partial(weight_kernel, many),
        grid=(many,),
        in_specs=[pl.BlockSpec((count, cols, width), lambda s: (s, 0, 0))]
        + [VMEM] * many
        + [ANY] * len(after),
        out_specs=pl.BlockSpec(shape, lambda s: (0, 0, 0)),
        out_shape=like(shape, kind),
        scratch_shapes=[pltpu.VMEM((columns, width), F32)],
        compiler_params=pltpu.CompilerParams(vmem_limit_bytes=20 * MIB),
        cost_estimate=cost(2 * rows * cols * width * columns, 2 * rows * cols * (width + columns)),
        name="weight_part",
    )(sheet, *grads, *after)


def sum_kernel(got, out):
    total = jnp.sum(got[...].astype(F32), axis=0)
    local = out.shape[-1]
    for index in range(3):
        out[index] = total[:, index * local : (index + 1) * local]


def sum_parts(got, local):
    return in_vmem(sum_kernel, "sum_parts", (like((3, got.shape[1], local), F32),), got)[0]


def body(sheet, w_query, w_key, w_value, cotangent, lengths):
    row_dev, cols, width = sheet.shape
    local = w_query.shape[1]
    n_rows = lax.axis_size("rows")
    n_heads = lax.axis_size("heads")
    scale = float(1.0 / (HEAD_DIM * row_dev * n_rows) ** 0.5)
    direct = n_rows <= 8
    shards = n_rows if direct else 1
    row_bits = [1 << b for b in range(n_rows.bit_length() - 1)]
    chunk = 4

    me = jnp.stack([lax.axis_index("rows"), lax.axis_index("heads")]).astype(jnp.int32)
    wq, wk, wv = w_query.T, w_key.T, w_value.T
    cot = jnp.swapaxes(cotangent, 1, 2)

    qk, *logits = query_key(lengths, me, sheet, wq, wk, shards, 4)
    weights, *dprob = value_dprob(lengths, me, sheet, wq, wk, wv, cot, shards, n_heads, 4)
    if direct:
        logits = halve(*logits, "rows", row_bits)
        dprob = halve(*dprob, "rows", row_bits)
        probs_own, dscore_own = softmax_back(logits, dprob, scale)
        probs, orders = double(probs_own, "rows", row_bits[::-1])
        dscore, _ = double(dscore_own, "rows", row_bits[::-1])
        probs, dscore = assemble(me, probs, dscore, orders, shards)
    else:
        logits, dprob = lax.psum((logits, dprob), "rows")
        probs, dscore = softmax_back(logits, dprob, scale)

    grads, adds, last = [], [], []
    for first in range(0, row_dev, chunk):
        after = adds[-2:-1]
        keep, give, grad = backward(first, chunk, lengths, probs, dscore, qk, cot, weights, after)
        grads.append(grad)
        bit = 1
        while bit * 2 < n_heads:
            give, keep = add_split(keep, flip(give, "heads", bit))
            bit *= 2
        adds.append(keep)
        last.append((keep, flip(give, "heads", bit)))

    if direct:
        parts = weight_part(sheet, grads, shards, BF16, adds[-2:-1])
        weight_grad = sum_parts(lax.all_to_all(parts, "rows", 0, 0), local)
        weight_grad = jnp.swapaxes(weight_grad, 0, 1)
    else:
        parts = weight_part(sheet, grads, 1, F32, adds[-2:-1])[0]
        weight_grad = lax.psum_scatter(parts, "rows", scatter_dimension=0, tiled=True)
        weight_grad = weight_grad.reshape(width // n_rows, 3, local)

    out = None
    for index, (keep, got) in enumerate(last):
        out = finish(keep, got, index, row_dev, out)
    return (jnp.swapaxes(out, 1, 2), weight_grad)


def solution(mesh):
    in_specs = (
        P("rows", None, None),
        P(None, "heads"),
        P(None, "heads"),
        P(None, "heads"),
        P("rows", None, "heads"),
        P("rows"),
    )
    out_specs = (P("rows", None, "heads"), P("rows", None, "heads"))
    return jax.shard_map(body, mesh=mesh, in_specs=in_specs, out_specs=out_specs, check_vma=False)
```

```python
import functools
import math

import jax
import jax.numpy as jnp
from jax import lax
from jax.experimental import pallas as pl
from jax.experimental.pallas import tpu as pltpu
from jax.sharding import PartitionSpec as P

HEAD_DIM = 64
F32 = jnp.float32
BF16 = jnp.bfloat16
MIB = 1024 * 1024

NN = (((1,), (0,)), ((), ()))
NT = (((1,), (1,)), ((), ()))
TN = (((0,), (0,)), ((), ()))


def mm(a, b, dims):
    return lax.dot_general(a, b, dims, preferred_element_type=F32)


def flip(values, axis, bit):
    n = lax.axis_size(axis)
    return lax.ppermute(values, axis, [(s, s ^ bit) for s in range(n)])


def cost(flops, moved):
    return pl.CostEstimate(flops=int(flops) // 64, bytes_accessed=int(moved) // 64, transcendentals=0)


SMEM = pl.BlockSpec(memory_space=pltpu.SMEM)
VMEM = pl.BlockSpec(memory_space=pltpu.VMEM)
ANY = pl.BlockSpec(memory_space=pl.ANY)


def like(shape, dtype=BF16):
    return jax.ShapeDtypeStruct(shape, dtype)


def in_vmem(kernel, name, out, *operands, scalars=0, after=(), limit=12, flops=0):
    many = len(after)

    def run(*refs):
        kernel(*refs[: len(operands)], *refs[len(operands) + many :])

    moved = 2 * sum(a.size for a in operands) + 2 * sum(o.size for o in out)
    return pl.pallas_call(
        run,
        in_specs=[SMEM] * scalars + [VMEM] * (len(operands) - scalars) + [ANY] * many,
        out_specs=[VMEM] * len(out),
        out_shape=list(out),
        compiler_params=pltpu.CompilerParams(vmem_limit_bytes=limit * MIB),
        cost_estimate=cost(flops, moved),
        name=name,
    )(*operands, *after)


def lane_mask(length, cols):
    return (lax.broadcasted_iota(jnp.int32, (1, cols), 1) < length).astype(F32)


def put_shards(me, acc, outs):
    shards = acc.shape[1]
    for j in range(shards):
        out = outs[j % len(outs)]
        out[j // len(outs)] = acc[:, me ^ j].astype(out.dtype)


def query_key_kernel(lengths, me, sheet, wq, wk, qk, *rest):
    outs, wt, acc = rest[:-2], rest[-2], rest[-1]
    step = pl.program_id(0)
    rows, cols, _ = sheet.shape
    local = wq.shape[0]
    heads = local // HEAD_DIM

    @pl.when(step == 0)
    def _():
        wt[:local] = wq[...]
        wt[local:] = wk[...]
        acc[...] = jnp.zeros_like(acc)

    for r in range(rows):
        mask = lane_mask(lengths[step * rows + r], cols)
        value = (mm(wt[...], sheet[r], NT) * mask).astype(BF16)
        qk[r] = value.reshape(2 * heads, HEAD_DIM, cols)
    flat = (rows * HEAD_DIM, cols)
    for h in range(heads):
        term = mm(qk[:, h].reshape(flat), qk[:, heads + h].reshape(flat), TN)
        acc[h] += term.reshape(acc.shape[1:])

    @pl.when(step == pl.num_programs(0) - 1)
    def _():
        put_shards(me[0], acc, outs)


def value_kernel(lengths, me, sheet, wq, wk, wv, cot, _, natural, *rest):
    outs, turned, acc = rest[:-2], rest[-2], rest[-1]
    step = pl.program_id(0)
    rows, cols, _ = sheet.shape
    local = wq.shape[0]
    heads = local // HEAD_DIM

    @pl.when(step == 0)
    def _():
        acc[...] = jnp.zeros_like(acc)
        for index, weight in enumerate((wq, wk, wv)):
            turned[:, :, index * local : (index + 1) * local] = weight[...].T.reshape(
                turned.shape[:2] + (local,)
            )
        for j in range(turned.shape[0]):
            natural[j] = turned[me[1] ^ j]

    values = []
    for r in range(rows):
        mask = lane_mask(lengths[step * rows + r], cols)
        value = (mm(wv[...], sheet[r], NT) * mask).astype(BF16)
        values.append(value.reshape(heads, HEAD_DIM, cols))
    flat = (rows * HEAD_DIM, cols)
    for h in range(heads):
        left = cot[:, h * HEAD_DIM : (h + 1) * HEAD_DIM].reshape(flat)
        right = jnp.concatenate([v[h] for v in values], axis=0)
        acc[h] += mm(left, right, TN).reshape(acc.shape[1:])

    @pl.when(step == pl.num_programs(0) - 1)
    def _():
        put_shards(me[0], acc, outs)


def part_shapes(shards, heads, cols):
    if shards == 1:
        return [like((1, heads, cols, cols), F32)]
    half = (shards // 2, heads, cols // shards, cols)
    return [like(half, F32), like(half)]


def whole(shape):
    return pl.BlockSpec(shape, lambda s: (0,) * len(shape))


def query_key(lengths, me, sheet, wq, wk, shards, block):
    rows, cols, width = sheet.shape
    local = wq.shape[0]
    heads = local // HEAD_DIM
    outs = part_shapes(shards, heads, cols)
    return pl.pallas_call(
        query_key_kernel,
        grid=(rows // block,),
        in_specs=[
            SMEM,
            SMEM,
            pl.BlockSpec((block, cols, width), lambda s: (s, 0, 0)),
            whole(wq.shape),
            whole(wk.shape),
        ],
        out_specs=[pl.BlockSpec((block, 2 * heads, HEAD_DIM, cols), lambda s: (s, 0, 0, 0))]
        + [whole(o.shape) for o in outs],
        out_shape=[like((rows, 2 * heads, HEAD_DIM, cols))] + outs,
        scratch_shapes=[
            pltpu.VMEM((2 * local, width), BF16),
            pltpu.VMEM((heads, shards, cols // shards, cols), F32),
        ],
        compiler_params=pltpu.CompilerParams(vmem_limit_bytes=56 * MIB),
        cost_estimate=cost(2 * rows * cols * local * (2 * width + cols), 2 * rows * cols * (width + 2 * local)),
        name="query_key",
    )(lengths, me, sheet, wq, wk)


def value_dprob(lengths, me, sheet, wq, wk, wv, cot, after, shards, devices, block):
    rows, cols, width = sheet.shape
    local = wv.shape[0]
    heads = local // HEAD_DIM
    outs = part_shapes(shards, heads, cols)
    natural = (devices, width // devices, 3 * local)
    return pl.pallas_call(
        value_kernel,
        grid=(rows // block,),
        in_specs=[
            SMEM,
            SMEM,
            pl.BlockSpec((block, cols, width), lambda s: (s, 0, 0)),
            whole(wq.shape),
            whole(wk.shape),
            whole(wv.shape),
            pl.BlockSpec((block, local, cols), lambda s: (s, 0, 0)),
            ANY,
        ],
        out_specs=[whole(natural)] + [whole(o.shape) for o in outs],
        out_shape=[like(natural)] + outs,
        scratch_shapes=[
            pltpu.VMEM(natural, BF16),
            pltpu.VMEM((heads, shards, cols // shards, cols), F32),
        ],
        compiler_params=pltpu.CompilerParams(vmem_limit_bytes=56 * MIB),
        cost_estimate=cost(2 * rows * cols * local * (width + cols), 2 * rows * cols * (width + local)),
        name="value_dprob",
    )(lengths, me, sheet, wq, wk, wv, cot, after)


def add_split_kernel(keep, got, give_out, keep_out):
    for j in range(keep.shape[0]):
        total = keep[j].astype(F32) + got[j].astype(F32)
        out = give_out if j % 2 else keep_out
        out[j // 2] = total.astype(out.dtype)


def add_split(keep, got):
    half = (keep.shape[0] // 2,) + keep.shape[1:]
    return in_vmem(add_split_kernel, "add_split", (like(half), like(half, keep.dtype)), keep, got)


def halve(keep, give, axis, bits):
    for bit in bits[:-1]:
        give, keep = add_split(keep, flip(give, axis, bit))
    return keep, flip(give, axis, bits[-1])


def softmax_kernel(scale, *refs):
    *terms, probs_out, dscore_out = refs
    half = len(terms) // 2
    total = lambda some: functools.reduce(jnp.add, [t[0].astype(F32) for t in some])
    logits = total(terms[:half]) * scale
    dprob = total(terms[half:])
    shifted = jnp.exp(logits - jnp.max(logits, axis=-1, keepdims=True))
    probs = shifted / jnp.sum(shifted, axis=-1, keepdims=True)
    inner = jnp.sum(probs * dprob, axis=-1, keepdims=True)
    probs_out[0] = probs.astype(BF16)
    dscore_out[0] = (scale * probs * (dprob - inner)).astype(BF16)


def softmax_back(logits, dprob, scale):
    out = like(logits[0].shape)
    return in_vmem(
        functools.partial(softmax_kernel, scale), "softmax_back", (out, out), *logits, *dprob, limit=16
    )


def double(values, axis, bits):
    order = [0]
    for bit in bits[:-1]:
        values = jnp.concatenate([values, flip(values, axis, bit)], axis=0)
        order = order + [j ^ bit for j in order]
    other = flip(values, axis, bits[-1])
    return (values, other), (order, [j ^ bits[-1] for j in order])


def assemble_kernel(orders, me, *refs):
    pieces, outs = refs[:-2], refs[-2:]
    per = len(orders)
    for kind, out in enumerate(outs):
        for piece, order in zip(pieces[kind * per : (kind + 1) * per], orders):
            for t, j in enumerate(order):
                out[me[0] ^ j] = piece[t]


def assemble(me, probs, dscore, orders, shards):
    out = like((shards,) + probs[0].shape[1:])
    return in_vmem(
        functools.partial(assemble_kernel, orders), "assemble", (out, out), me, *probs, *dscore, scalars=1
    )


def backward_kernel(first, lengths, probs, dscore, qk, cot, weights, *rest):
    blocks, grads = rest[:-1], rest[-1]
    count, all_heads, _, cols = grads.shape
    heads = all_heads // 3
    rows = pl.ds(first, count)
    flat = (count * HEAD_DIM, cols)
    split = (count, HEAD_DIM, cols)
    masks = jnp.stack([lane_mask(lengths[first + r], cols) for r in range(count)])
    for h in range(heads):
        p, ds = [ref[:, h].reshape(cols, cols) for ref in (probs, dscore)]
        g = cot[rows, h * HEAD_DIM : (h + 1) * HEAD_DIM].reshape(flat)
        dq = mm(qk[rows, heads + h].reshape(flat), ds, NT)
        dk = mm(qk[rows, h].reshape(flat), ds, NN)
        dv = mm(g, p, NN)
        for index, value in enumerate((dq, dk, dv)):
            grads[:, index * heads + h] = (value.reshape(split) * masks).astype(BF16)
    devices, share, columns = weights.shape
    left = weights[...].reshape(devices * share, columns)
    for r in range(count):
        part = mm(left, grads[r].reshape(columns, cols), NN).astype(BF16)
        for j in range(devices):
            blocks[j % 2][j // 2, r] = part[j * share : (j + 1) * share]


def backward(first, count, lengths, probs, dscore, qk, cot, weights, after):
    cols = qk.shape[-1]
    heads = qk.shape[1] // 2
    devices, share, columns = weights.shape
    half = like((devices // 2, count, share, cols))
    return in_vmem(
        functools.partial(backward_kernel, first),
        "backward",
        (half, half, like((count, 3 * heads, HEAD_DIM, cols))),
        lengths,
        probs,
        dscore,
        qk,
        cot,
        weights,
        scalars=1,
        after=after,
        limit=16,
        flops=2 * count * cols * columns * (cols + devices * share),
    )


def finish_kernel(keep, got, *rest):
    out = rest[-1]
    out[...] = (keep[0].astype(F32) + got[0].astype(F32)).astype(BF16)


def finish(keep, got, first, total_rows, before):
    _, count, share, cols = keep.shape
    block = math.gcd(first, count) if first else count
    spec = pl.BlockSpec((1, block, share, cols), lambda s: (0, s, 0, 0))
    extra = [] if before is None else [before]
    return pl.pallas_call(
        finish_kernel,
        grid=(count // block,),
        in_specs=[spec, spec] + [ANY] * len(extra),
        out_specs=pl.BlockSpec((block, share, cols), lambda s: (first // block + s, 0, 0)),
        out_shape=like((total_rows, share, cols)),
        input_output_aliases={2: 0} if extra else {},
        compiler_params=pltpu.CompilerParams(vmem_limit_bytes=12 * MIB),
        cost_estimate=cost(keep.size, keep.size * 6),
        name="finish",
    )(keep, got, *extra)


def weight_kernel(*refs):
    sheet, *grads, out = refs
    rows, cols, width = sheet.shape
    n = grads[0].shape[1] * HEAD_DIM
    left = [g[r].reshape(n, cols) for g in grads for r in range(g.shape[0])]
    total = mm(jnp.concatenate(left, axis=1), sheet[...].reshape(rows * cols, width), NN)
    out[...] = total.T.reshape(out.shape).astype(out.dtype)


def weight_part(sheet, grads, shards, kind, after):
    rows, cols, width = sheet.shape
    columns = grads[0].shape[1] * HEAD_DIM
    out = like((shards, width // shards, columns), kind)
    return in_vmem(
        weight_kernel,
        "weight_part",
        (out,),
        sheet,
        *grads,
        after=after,
        limit=24,
        flops=2 * rows * cols * width * columns,
    )[0]


def sum_kernel(got, out):
    total = jnp.sum(got[...].astype(F32), axis=0)
    local = out.shape[-1]
    for index in range(3):
        out[index] = total[:, index * local : (index + 1) * local]


def sum_parts(got, local):
    return in_vmem(sum_kernel, "sum_parts", (like((3, got.shape[1], local), F32),), got)[0]


def body(sheet, w_query, w_key, w_value, cotangent, lengths):
    row_dev, cols, width = sheet.shape
    local = w_query.shape[1]
    n_rows = lax.axis_size("rows")
    n_heads = lax.axis_size("heads")
    scale = float(1.0 / (HEAD_DIM * row_dev * n_rows) ** 0.5)
    direct = n_rows <= 8
    shards = n_rows if direct else 1
    row_bits = [1 << b for b in range(n_rows.bit_length() - 1)]
    chunks = [row_dev // 8, row_dev // 4, row_dev // 4, 3 * row_dev // 8]

    me = jnp.stack([lax.axis_index("rows"), lax.axis_index("heads")]).astype(jnp.int32)
    wq, wk, wv = w_query.T, w_key.T, w_value.T
    cot = jnp.swapaxes(cotangent, 1, 2)

    qk, *logits = query_key(lengths, me, sheet, wq, wk, shards, 4)
    weights, *dprob = value_dprob(lengths, me, sheet, wq, wk, wv, cot, logits[-1], shards, n_heads, 4)
    if direct:
        logits = halve(*logits, "rows", row_bits)
        dprob = halve(*dprob, "rows", row_bits)
        probs_own, dscore_own = softmax_back(logits, dprob, scale)
        probs, orders = double(probs_own, "rows", row_bits[::-1])
        dscore, _ = double(dscore_own, "rows", row_bits[::-1])
        probs, dscore = assemble(me, probs, dscore, orders, shards)
    else:
        logits, dprob = lax.psum((logits, dprob), "rows")
        probs, dscore = softmax_back(logits, dprob, scale)

    grads, adds, last = [], [], []
    first = 0
    for chunk in chunks:
        after = adds[-2:-1]
        keep, give, grad = backward(first, chunk, lengths, probs, dscore, qk, cot, weights, after)
        grads.append(grad)
        bit = 1
        while bit * 2 < n_heads:
            give, keep = add_split(keep, flip(give, "heads", bit))
            bit *= 2
        adds.append(keep)
        last.append((keep, flip(give, "heads", bit), first))
        first += chunk

    if direct:
        parts = weight_part(sheet, grads, shards, BF16, [last[0][1]] + adds[-2:-1])
        weight_grad = sum_parts(lax.all_to_all(parts, "rows", 0, 0), local)
        weight_grad = jnp.swapaxes(weight_grad, 0, 1)
    else:
        parts = weight_part(sheet, grads, 1, F32, [last[0][1]] + adds[-2:-1])[0]
        weight_grad = lax.psum_scatter(parts, "rows", scatter_dimension=0, tiled=True)
        weight_grad = weight_grad.reshape(width // n_rows, 3, local)

    out = None
    for keep, got, first in last:
        out = finish(keep, got, first, row_dev, out)
    return (jnp.swapaxes(out, 1, 2), weight_grad)


def solution(mesh):
    in_specs = (
        P("rows", None, None),
        P(None, "heads"),
        P(None, "heads"),
        P(None, "heads"),
        P("rows", None, "heads"),
        P("rows"),
    )
    out_specs = (P("rows", None, "heads"), P("rows", None, "heads"))
    return jax.shard_map(body, mesh=mesh, in_specs=in_specs, out_specs=out_specs, check_vma=False)
```

```python
import functools
import math

import jax
import jax.numpy as jnp
from jax import lax
from jax.experimental import pallas as pl
from jax.experimental.pallas import tpu as pltpu
from jax.sharding import PartitionSpec as P

HEAD_DIM = 64
F32 = jnp.float32
BF16 = jnp.bfloat16
MIB = 1024 * 1024

NN = (((1,), (0,)), ((), ()))
NT = (((1,), (1,)), ((), ()))
TN = (((0,), (0,)), ((), ()))


def mm(a, b, dims):
    return lax.dot_general(a, b, dims, preferred_element_type=F32)


def flip(values, axis, bit):
    n = lax.axis_size(axis)
    return lax.ppermute(values, axis, [(s, s ^ bit) for s in range(n)])


def cost(flops, moved):
    return pl.CostEstimate(flops=int(flops), bytes_accessed=int(moved), transcendentals=0)


SMEM = pl.BlockSpec(memory_space=pltpu.SMEM)
VMEM = pl.BlockSpec(memory_space=pltpu.VMEM)
ANY = pl.BlockSpec(memory_space=pl.ANY)
HBM = pl.BlockSpec(memory_space=pltpu.HBM)


def like(shape, dtype=BF16):
    return jax.ShapeDtypeStruct(shape, dtype)


def in_vmem(kernel, name, out, *operands, scalars=0, streamed=0, after=(), scratch=(), limit=12, flops=0):
    many = len(after)

    def run(*refs):
        kernel(*refs[: len(operands)], *refs[len(operands) + many :])

    moved = 2 * sum(a.size for a in operands) + 2 * sum(o.size for o in out)
    held = len(operands) - scalars - streamed
    return pl.pallas_call(
        run,
        in_specs=[SMEM] * scalars + [HBM] * streamed + [VMEM] * held + [ANY] * many,
        out_specs=[VMEM] * len(out),
        out_shape=list(out),
        scratch_shapes=list(scratch),
        compiler_params=pltpu.CompilerParams(vmem_limit_bytes=limit * MIB),
        cost_estimate=cost(flops, moved),
        name=name,
    )(*operands, *after)


def lane_mask(length, cols):
    return (lax.broadcasted_iota(jnp.int32, (1, cols), 1) < length).astype(F32)


def put_shards(me, acc, outs):
    shards = acc.shape[1]
    for j in range(shards):
        out = outs[j % len(outs)]
        out[j // len(outs)] = acc[:, me ^ j].astype(out.dtype)


BLOCK = 4


def query_key_kernel(lengths, me, sheet, wq, wk, qk, held, *rest):
    outs, (wt, acc, sems) = rest[:-3], rest[-3:]
    rows, cols, _ = sheet.shape
    local = wq.shape[0]
    heads = local // HEAD_DIM
    copies = [
        pltpu.make_async_copy(wq, wt.at[:local], sems.at[0]),
        pltpu.make_async_copy(wk, wt.at[local:], sems.at[1]),
    ]
    for index, first in enumerate(range(0, rows, BLOCK)):
        some = pl.ds(first, BLOCK)
        copies.append(pltpu.make_async_copy(sheet.at[some], held.at[some], sems.at[2 + index]))
    for copy in copies:
        copy.start()
    copies[0].wait()
    copies[1].wait()
    flat = (BLOCK * HEAD_DIM, cols)
    for index, first in enumerate(range(0, rows, BLOCK)):
        copies[2 + index].wait()
        for r in range(first, first + BLOCK):
            value = (mm(wt[...], held[r], NT) * lane_mask(lengths[r], cols)).astype(BF16)
            qk[r] = value.reshape(2 * heads, HEAD_DIM, cols)
        some = pl.ds(first, BLOCK)
        for h in range(heads):
            term = mm(qk[some, h].reshape(flat), qk[some, heads + h].reshape(flat), TN)
            term = term.reshape(acc.shape[1:])
            acc[h] = term if index == 0 else acc[h] + term
    put_shards(me[0], acc, outs)


def query_key(lengths, me, sheet, wq, wk, shards):
    rows, cols, width = sheet.shape
    local = wq.shape[0]
    heads = local // HEAD_DIM
    return in_vmem(
        query_key_kernel,
        "query_key",
        [like((rows, 2 * heads, HEAD_DIM, cols)), like(sheet.shape)] + part_shapes(shards, heads, cols),
        lengths,
        me,
        sheet,
        wq,
        wk,
        scalars=2,
        streamed=3,
        scratch=(
            pltpu.VMEM((2 * local, width), BF16),
            pltpu.VMEM((heads, shards, cols // shards, cols), F32),
            pltpu.SemaphoreType.DMA((2 + rows // BLOCK,)),
        ),
        limit=16,
        flops=2 * rows * cols * local * (2 * width + cols),
    )


def value_kernel(lengths, me, sheet, wv, cot, *rest):
    outs, acc = rest[:-1], rest[-1]
    rows, cols, _ = sheet.shape
    local = wv.shape[0]
    heads = local // HEAD_DIM
    flat = (BLOCK * HEAD_DIM, cols)
    for first in range(0, rows, BLOCK):
        values = []
        for r in range(first, first + BLOCK):
            value = (mm(wv[...], sheet[r], NT) * lane_mask(lengths[r], cols)).astype(BF16)
            values.append(value.reshape(heads, HEAD_DIM, cols))
        for h in range(heads):
            left = cot[pl.ds(first, BLOCK), h * HEAD_DIM : (h + 1) * HEAD_DIM].reshape(flat)
            right = jnp.concatenate([v[h] for v in values], axis=0)
            term = mm(left, right, TN).reshape(acc.shape[1:])
            acc[h] = term if first == 0 else acc[h] + term
    put_shards(me[0], acc, outs)


def value_dprob(lengths, me, sheet, wv, cot, after, shards):
    rows, cols, width = sheet.shape
    local = wv.shape[0]
    heads = local // HEAD_DIM
    return in_vmem(
        value_kernel,
        "value_dprob",
        part_shapes(shards, heads, cols),
        lengths,
        me,
        sheet,
        wv,
        cot,
        scalars=2,
        after=after,
        scratch=(pltpu.VMEM((heads, shards, cols // shards, cols), F32),),
        limit=16,
        flops=2 * rows * cols * local * (width + cols),
    )


def turn_kernel(me, wq, wk, wv, natural, turned):
    local = wq.shape[0]
    for index, weight in enumerate((wq, wk, wv)):
        turned[:, :, index * local : (index + 1) * local] = weight[...].T.reshape(turned.shape[:2] + (local,))
    for j in range(turned.shape[0]):
        natural[j] = turned[me[1] ^ j]


def turn(me, wq, wk, wv, devices, after):
    local, width = wq.shape
    shape = (devices, width // devices, 3 * local)
    return in_vmem(
        turn_kernel,
        "turn",
        (like(shape),),
        me,
        wq,
        wk,
        wv,
        scalars=1,
        after=after,
        scratch=(pltpu.VMEM(shape, BF16),),
    )[0]


def part_shapes(shards, heads, cols):
    if shards == 1:
        return [like((1, heads, cols, cols), F32)]
    half = (shards // 2, heads, cols // shards, cols)
    return [like(half, F32), like(half)]


def add_split_kernel(keep, got, give_out, keep_out):
    for j in range(keep.shape[0]):
        total = keep[j].astype(F32) + got[j].astype(F32)
        out = give_out if j % 2 else keep_out
        out[j // 2] = total.astype(out.dtype)


def add_split(keep, got, after=()):
    half = (keep.shape[0] // 2,) + keep.shape[1:]
    return in_vmem(add_split_kernel, "add_split", (like(half), like(half, keep.dtype)), keep, got, after=after)


def halve(keep, give, axis, bits, after=()):
    after = list(after) + [()] * len(bits)
    for bit, waits in zip(bits[:-1], after):
        give, keep = add_split(keep, flip(give, axis, bit), waits)
    return keep, flip(give, axis, bits[-1])


def softmax_kernel(scale, *refs):
    *terms, probs_out, dscore_out = refs
    half = len(terms) // 2
    total = lambda some: functools.reduce(jnp.add, [t[0].astype(F32) for t in some])
    logits = total(terms[:half]) * scale
    dprob = total(terms[half:])
    shifted = jnp.exp(logits - jnp.max(logits, axis=-1, keepdims=True))
    probs = shifted / jnp.sum(shifted, axis=-1, keepdims=True)
    inner = jnp.sum(probs * dprob, axis=-1, keepdims=True)
    probs_out[0] = probs.astype(BF16)
    dscore_out[0] = (scale * probs * (dprob - inner)).astype(BF16)


def softmax_back(logits, dprob, scale):
    out = like(logits[0].shape)
    return in_vmem(
        functools.partial(softmax_kernel, scale), "softmax_back", (out, out), *logits, *dprob, limit=16
    )


def double(values, axis, bits):
    order = [0]
    for bit in bits[:-1]:
        values = jnp.concatenate([values, flip(values, axis, bit)], axis=0)
        order = order + [j ^ bit for j in order]
    other = flip(values, axis, bits[-1])
    return (values, other), (order, [j ^ bits[-1] for j in order])


def assemble_kernel(orders, me, *refs):
    pieces, outs = refs[:-2], refs[-2:]
    per = len(orders)
    for kind, out in enumerate(outs):
        for piece, order in zip(pieces[kind * per : (kind + 1) * per], orders):
            for t, j in enumerate(order):
                out[me[0] ^ j] = piece[t]


def assemble(me, probs, dscore, orders, shards):
    out = like((shards,) + probs[0].shape[1:])
    return in_vmem(
        functools.partial(assemble_kernel, orders), "assemble", (out, out), me, *probs, *dscore, scalars=1
    )


def backward_kernel(first, lengths, probs, dscore, qk, cot, weights, *rest):
    blocks, grads = rest[:-1], rest[-1]
    count, all_heads, _, cols = grads.shape
    heads = all_heads // 3
    rows = pl.ds(first, count)
    flat = (count * HEAD_DIM, cols)
    split = (count, HEAD_DIM, cols)
    masks = jnp.stack([lane_mask(lengths[first + r], cols) for r in range(count)])
    for h in range(heads):
        p, ds = [ref[:, h].reshape(cols, cols) for ref in (probs, dscore)]
        g = cot[rows, h * HEAD_DIM : (h + 1) * HEAD_DIM].reshape(flat)
        dq = mm(qk[rows, heads + h].reshape(flat), ds, NT)
        dk = mm(qk[rows, h].reshape(flat), ds, NN)
        dv = mm(g, p, NN)
        for index, value in enumerate((dq, dk, dv)):
            grads[:, index * heads + h] = (value.reshape(split) * masks).astype(BF16)
    devices, share, columns = weights.shape
    left = weights[...].reshape(devices * share, columns)
    for r in range(count):
        part = mm(left, grads[r].reshape(columns, cols), NN).astype(BF16)
        for j in range(devices):
            blocks[j % 2][j // 2, r] = part[j * share : (j + 1) * share]


def backward(first, count, lengths, probs, dscore, qk, cot, weights, after):
    cols = qk.shape[-1]
    heads = qk.shape[1] // 2
    devices, share, columns = weights.shape
    half = like((devices // 2, count, share, cols))
    return in_vmem(
        functools.partial(backward_kernel, first),
        "backward",
        (half, half, like((count, 3 * heads, HEAD_DIM, cols))),
        lengths,
        probs,
        dscore,
        qk,
        cot,
        weights,
        scalars=1,
        after=after,
        limit=16,
        flops=2 * count * cols * columns * (cols + devices * share),
    )


def finish_kernel(keep, got, *rest):
    out = rest[-1]
    out[...] = (keep[0].astype(F32) + got[0].astype(F32)).astype(BF16)


def finish(keep, got, first, total_rows, before):
    _, count, share, cols = keep.shape
    block = math.gcd(first, count) if first else count
    spec = pl.BlockSpec((1, block, share, cols), lambda s: (0, s, 0, 0))
    extra = [] if before is None else [before]
    return pl.pallas_call(
        finish_kernel,
        grid=(count // block,),
        in_specs=[spec, spec] + [ANY] * len(extra),
        out_specs=pl.BlockSpec((block, share, cols), lambda s: (first // block + s, 0, 0)),
        out_shape=like((total_rows, share, cols)),
        input_output_aliases={2: 0} if extra else {},
        compiler_params=pltpu.CompilerParams(vmem_limit_bytes=12 * MIB),
        cost_estimate=cost(keep.size, keep.size * 6),
        name="finish",
    )(keep, got, *extra)


def weight_kernel(me, sheet, *refs):
    *grads, keep, give, turned = refs
    rows, cols, width = sheet.shape
    n = grads[0].shape[1] * HEAD_DIM
    left = [g[r].reshape(n, cols) for g in grads for r in range(g.shape[0])]
    total = mm(jnp.concatenate(left, axis=1), sheet[...].reshape(rows * cols, width), NN)
    turned[...] = total.T.reshape(turned.shape)
    for j in range(turned.shape[0]):
        out = (keep, give)[j % 2]
        out[j // 2] = turned[me[0] ^ j].astype(out.dtype)


def whole_weight_kernel(me, sheet, *refs):
    *grads, out = refs
    rows, cols, width = sheet.shape
    n = grads[0].shape[1] * HEAD_DIM
    left = [g[r].reshape(n, cols) for g in grads for r in range(g.shape[0])]
    out[...] = mm(jnp.concatenate(left, axis=1), sheet[...].reshape(rows * cols, width), NN).T


def weight_part(me, sheet, grads, shards, after):
    rows, cols, width = sheet.shape
    columns = grads[0].shape[1] * HEAD_DIM
    if shards == 1:
        kernel, outs, scratch = whole_weight_kernel, [like((width, columns), F32)], ()
    else:
        half = (shards // 2, width // shards, columns)
        kernel, outs = weight_kernel, [like(half, F32), like(half)]
        scratch = (pltpu.VMEM((shards,) + half[1:], F32),)
    return in_vmem(
        kernel,
        "weight_part",
        outs,
        me,
        sheet,
        *grads,
        scalars=1,
        after=after,
        scratch=scratch,
        limit=24,
        flops=2 * rows * cols * width * columns,
    )


def last_kernel(keep, got, out):
    total = keep[0] + got[0].astype(F32)
    local = out.shape[-1]
    for index in range(out.shape[0]):
        out[index] = total[:, index * local : (index + 1) * local]


def last_sum(keep, got, local, after):
    shape = (keep.shape[2] // local, keep.shape[1], local)
    return in_vmem(last_kernel, "last_sum", (like(shape, F32),), keep, got, after=after)[0]


def body(sheet, w_query, w_key, w_value, cotangent, lengths):
    row_dev, cols, width = sheet.shape
    local = w_query.shape[1]
    n_rows = lax.axis_size("rows")
    n_heads = lax.axis_size("heads")
    scale = float(1.0 / (HEAD_DIM * row_dev * n_rows) ** 0.5)
    direct = n_rows <= 8
    shards = n_rows if direct else 1
    row_bits = [1 << b for b in range(n_rows.bit_length() - 1)]
    chunks = [row_dev // 8, row_dev // 4, row_dev // 4, 3 * row_dev // 8]

    me = jnp.stack([lax.axis_index("rows"), lax.axis_index("heads")]).astype(jnp.int32)
    wq, wk, wv = w_query.T, w_key.T, w_value.T
    cot = jnp.swapaxes(cotangent, 1, 2)

    qk, held, *logits = query_key(lengths, me, sheet, wq, wk, shards)
    dprob = value_dprob(lengths, me, held, wv, cot, logits[-1:], shards)
    weights = turn(me, wq, wk, wv, n_heads, dprob[-1:])
    if direct:
        logits = halve(*logits, "rows", row_bits)
        dprob = halve(*dprob, "rows", row_bits)
        probs_own, dscore_own = softmax_back(logits, dprob, scale)
        probs, orders = double(probs_own, "rows", row_bits[::-1])
        dscore, _ = double(dscore_own, "rows", row_bits[::-1])
        probs, dscore = assemble(me, probs, dscore, orders, shards)
    else:
        logits, dprob = lax.psum((logits, dprob), "rows")
        probs, dscore = softmax_back(logits, dprob, scale)

    grads, adds, last = [], [], []
    first = 0
    for chunk in chunks:
        after = adds[-2:-1]
        keep, give, grad = backward(first, chunk, lengths, probs, dscore, qk, cot, weights, after)
        grads.append(grad)
        bit = 1
        while bit * 2 < n_heads:
            give, keep = add_split(keep, flip(give, "heads", bit))
            bit *= 2
        adds.append(keep)
        last.append((keep, flip(give, "heads", bit), first))
        first += chunk

    arrived = [got for _, got, _ in last]
    parts = weight_part(me, held, grads, shards, arrived[:1])
    if direct:
        parts = halve(*parts, "rows", row_bits, [arrived[1:2], arrived[2:3]])
        weight_grad = last_sum(*parts, local, arrived[3:])
        weight_grad = jnp.swapaxes(weight_grad, 0, 1)
    else:
        weight_grad = lax.psum_scatter(parts[0], "rows", scatter_dimension=0, tiled=True)
        weight_grad = weight_grad.reshape(width // n_rows, 3, local)

    out = None
    for keep, got, first in last:
        out = finish(keep, got, first, row_dev, out)
    return (jnp.swapaxes(out, 1, 2), weight_grad)


def solution(mesh):
    in_specs = (
        P("rows", None, None),
        P(None, "heads"),
        P(None, "heads"),
        P(None, "heads"),
        P("rows", None, "heads"),
        P("rows"),
    )
    out_specs = (P("rows", None, "heads"), P("rows", None, "heads"))
    return jax.shard_map(body, mesh=mesh, in_specs=in_specs, out_specs=out_specs, check_vma=False)
```

```python
import functools
import math

import jax
import jax.numpy as jnp
from jax import lax
from jax.experimental import pallas as pl
from jax.experimental.pallas import tpu as pltpu
from jax.sharding import PartitionSpec as P

HEAD_DIM = 64
F32 = jnp.float32
BF16 = jnp.bfloat16
MIB = 1024 * 1024

NN = (((1,), (0,)), ((), ()))
NT = (((1,), (1,)), ((), ()))
TN = (((0,), (0,)), ((), ()))


def mm(a, b, dims):
    return lax.dot_general(a, b, dims, preferred_element_type=F32)


def flip(values, axis, bit):
    n = lax.axis_size(axis)
    return lax.ppermute(values, axis, [(s, s ^ bit) for s in range(n)])


def cost(flops, moved):
    return pl.CostEstimate(flops=int(flops), bytes_accessed=int(moved), transcendentals=0)


SMEM = pl.BlockSpec(memory_space=pltpu.SMEM)
VMEM = pl.BlockSpec(memory_space=pltpu.VMEM)
ANY = pl.BlockSpec(memory_space=pl.ANY)
HBM = pl.BlockSpec(memory_space=pltpu.HBM)


def like(shape, dtype=BF16):
    return jax.ShapeDtypeStruct(shape, dtype)


def place(a, stays):
    return pltpu.with_memory_space_constraint(a, pltpu.HBM) if stays else a


def in_vmem(kernel, name, out, *operands, scalars=0, streamed=0, after=(), scratch=(), limit=12, flops=0):
    many = len(after)

    def run(*refs):
        kernel(*refs[: len(operands)], *refs[len(operands) + many :])

    moved = 2 * sum(a.size for a in operands) + 2 * sum(o.size for o in out)
    held = len(operands) - scalars - streamed
    return pl.pallas_call(
        run,
        in_specs=[SMEM] * scalars + [HBM] * streamed + [VMEM] * held + [ANY] * many,
        out_specs=[VMEM] * len(out),
        out_shape=list(out),
        scratch_shapes=list(scratch),
        compiler_params=pltpu.CompilerParams(vmem_limit_bytes=limit * MIB),
        cost_estimate=cost(flops, moved),
        name=name,
    )(*[place(a, scalars <= i < scalars + streamed) for i, a in enumerate(operands)], *after)


def lane_mask(length, cols):
    return (lax.broadcasted_iota(jnp.int32, (1, cols), 1) < length).astype(F32)


def put_shards(me, acc, outs):
    shards = acc.shape[1]
    for j in range(shards):
        out = outs[j % len(outs)]
        out[j // len(outs)] = acc[:, me ^ j].astype(out.dtype)


BLOCK = 4


def query_key_kernel(lengths, me, sheet, wq, wk, qk, held, *rest):
    outs, (wt, acc, sems) = rest[:-3], rest[-3:]
    rows, cols, _ = sheet.shape
    local = wq.shape[0]
    heads = local // HEAD_DIM
    copies = [
        pltpu.make_async_copy(wq, wt.at[:local], sems.at[0]),
        pltpu.make_async_copy(wk, wt.at[local:], sems.at[1]),
    ]
    for index, first in enumerate(range(0, rows, BLOCK)):
        some = pl.ds(first, BLOCK)
        copies.append(pltpu.make_async_copy(sheet.at[some], held.at[some], sems.at[2 + index]))
    for copy in copies:
        copy.start()
    copies[0].wait()
    copies[1].wait()
    flat = (BLOCK * HEAD_DIM, cols)
    for index, first in enumerate(range(0, rows, BLOCK)):
        copies[2 + index].wait()
        for r in range(first, first + BLOCK):
            value = (mm(wt[...], held[r], NT) * lane_mask(lengths[r], cols)).astype(BF16)
            qk[r] = value.reshape(2 * heads, HEAD_DIM, cols)
        some = pl.ds(first, BLOCK)
        for h in range(heads):
            term = mm(qk[some, h].reshape(flat), qk[some, heads + h].reshape(flat), TN)
            term = term.reshape(acc.shape[1:])
            acc[h] = term if index == 0 else acc[h] + term
    put_shards(me[0], acc, outs)


def query_key(lengths, me, sheet, wq, wk, shards):
    rows, cols, width = sheet.shape
    local = wq.shape[0]
    heads = local // HEAD_DIM
    return in_vmem(
        query_key_kernel,
        "query_key",
        [like((rows, 2 * heads, HEAD_DIM, cols)), like(sheet.shape)] + part_shapes(shards, heads, cols),
        lengths,
        me,
        sheet,
        wq,
        wk,
        scalars=2,
        streamed=3,
        scratch=(
            pltpu.VMEM((2 * local, width), BF16),
            pltpu.VMEM((heads, shards, cols // shards, cols), F32),
            pltpu.SemaphoreType.DMA((2 + rows // BLOCK,)),
        ),
        limit=46,
        flops=2 * rows * cols * local * (2 * width + cols),
    )


def value_kernel(lengths, me, sheet, wv, cot, *rest):
    outs, acc = rest[:-1], rest[-1]
    rows, cols, _ = sheet.shape
    local = wv.shape[0]
    heads = local // HEAD_DIM
    flat = (BLOCK * HEAD_DIM, cols)
    for first in range(0, rows, BLOCK):
        values = []
        for r in range(first, first + BLOCK):
            value = (mm(wv[...], sheet[r], NT) * lane_mask(lengths[r], cols)).astype(BF16)
            values.append(value.reshape(heads, HEAD_DIM, cols))
        for h in range(heads):
            left = cot[pl.ds(first, BLOCK), h * HEAD_DIM : (h + 1) * HEAD_DIM].reshape(flat)
            right = jnp.concatenate([v[h] for v in values], axis=0)
            term = mm(left, right, TN).reshape(acc.shape[1:])
            acc[h] = term if first == 0 else acc[h] + term
    put_shards(me[0], acc, outs)


def value_dprob(lengths, me, sheet, wv, cot, after, shards):
    rows, cols, width = sheet.shape
    local = wv.shape[0]
    heads = local // HEAD_DIM
    return in_vmem(
        value_kernel,
        "value_dprob",
        part_shapes(shards, heads, cols),
        lengths,
        me,
        sheet,
        wv,
        cot,
        scalars=2,
        after=after,
        scratch=(pltpu.VMEM((heads, shards, cols // shards, cols), F32),),
        limit=16,
        flops=2 * rows * cols * local * (width + cols),
    )


def turn_kernel(me, wq, wk, wv, natural, turned):
    local = wq.shape[0]
    for index, weight in enumerate((wq, wk, wv)):
        turned[:, :, index * local : (index + 1) * local] = weight[...].T.reshape(turned.shape[:2] + (local,))
    for j in range(natural.shape[0]):
        natural[j] = turned[me[1] ^ j]


def turn(me, wq, wk, wv, devices, after):
    local, width = wq.shape
    shape = (width // devices, 3 * local)
    return in_vmem(
        turn_kernel,
        "turn",
        (like((2,) + shape),),
        me,
        wq,
        wk,
        wv,
        scalars=1,
        after=after,
        scratch=(pltpu.VMEM((devices,) + shape, BF16),),
    )[0]


def far_query_key_kernel(lengths, sheet, wq, wk, qk):
    rows, cols, _ = sheet.shape
    local = wq.shape[0]
    heads = local // HEAD_DIM
    both = jnp.concatenate([wq[...], wk[...]], axis=0)
    for r in range(rows):
        value = (mm(both, sheet[r], NT) * lane_mask(lengths[r], cols)).astype(BF16)
        qk[r] = value.reshape(2 * heads, HEAD_DIM, cols)


def far_query_key(lengths, sheet, wq, wk, after):
    rows, cols, width = sheet.shape
    local = wq.shape[0]
    return in_vmem(
        far_query_key_kernel,
        "far_query_key",
        (like((rows, 2 * local // HEAD_DIM, HEAD_DIM, cols)),),
        lengths,
        sheet,
        wq,
        wk,
        scalars=1,
        after=after,
        flops=4 * rows * cols * local * width,
    )[0]


def part_shapes(shards, heads, cols):
    if shards == 1:
        return [like((1, heads, cols, cols), F32)]
    half = (shards // 2, heads, cols // shards, cols)
    return [like(half, F32), like(half)]


def add_split_kernel(keep, got, give_out, keep_out):
    for j in range(keep.shape[0]):
        total = keep[j].astype(F32) + got[j].astype(F32)
        out = give_out if j % 2 else keep_out
        out[j // 2] = total.astype(out.dtype)


def add_split(keep, got, after=()):
    half = (keep.shape[0] // 2,) + keep.shape[1:]
    return in_vmem(add_split_kernel, "add_split", (like(half), like(half, keep.dtype)), keep, got, after=after)


def halve(keep, give, axis, bits, after=()):
    after = list(after) + [()] * len(bits)
    for bit, waits in zip(bits[:-1], after):
        give, keep = add_split(keep, flip(give, axis, bit), waits)
    return keep, flip(give, axis, bits[-1])


def softmax_kernel(scale, *refs):
    *terms, probs_out, dscore_out = refs
    half = len(terms) // 2
    total = lambda some: functools.reduce(jnp.add, [t[0].astype(F32) for t in some])
    logits = total(terms[:half]) * scale
    dprob = total(terms[half:])
    shifted = jnp.exp(logits - jnp.max(logits, axis=-1, keepdims=True))
    probs = shifted / jnp.sum(shifted, axis=-1, keepdims=True)
    inner = jnp.sum(probs * dprob, axis=-1, keepdims=True)
    probs_out[0] = probs.astype(BF16)
    dscore_out[0] = (scale * probs * (dprob - inner)).astype(BF16)


def softmax_back(logits, dprob, scale):
    out = like(logits[0].shape)
    return in_vmem(
        functools.partial(softmax_kernel, scale), "softmax_back", (out, out), *logits, *dprob, limit=16
    )


def double(values, axis, bits):
    order = [0]
    for bit in bits[:-1]:
        values = jnp.concatenate([values, flip(values, axis, bit)], axis=0)
        order = order + [j ^ bit for j in order]
    other = flip(values, axis, bits[-1])
    return (values, other), (order, [j ^ bits[-1] for j in order])


def assemble_kernel(orders, me, *refs):
    pieces, outs = refs[:-2], refs[-2:]
    per = len(orders)
    for kind, out in enumerate(outs):
        for piece, order in zip(pieces[kind * per : (kind + 1) * per], orders):
            for t, j in enumerate(order):
                out[me[0] ^ j] = piece[t]


def assemble(me, probs, dscore, orders, shards):
    out = like((shards,) + probs[0].shape[1:])
    return in_vmem(
        functools.partial(assemble_kernel, orders), "assemble", (out, out), me, *probs, *dscore, scalars=1
    )


def gradients(lengths, first, count, probs, dscore, qk, cot, grads):
    cols = qk.shape[-1]
    heads = qk.shape[1] // 2
    rows = pl.ds(first, count)
    flat = (count * HEAD_DIM, cols)
    split = (count, HEAD_DIM, cols)
    masks = jnp.stack([lane_mask(lengths[first + r], cols) for r in range(count)])
    for h in range(heads):
        p, ds = [ref[:, h].reshape(cols, cols) for ref in (probs, dscore)]
        g = cot[rows, h * HEAD_DIM : (h + 1) * HEAD_DIM].reshape(flat)
        dq = mm(qk[rows, heads + h].reshape(flat), ds, NT)
        dk = mm(qk[rows, h].reshape(flat), ds, NN)
        dv = mm(g, p, NN)
        for index, value in enumerate((dq, dk, dv)):
            grads[:, index * heads + h] = (value.reshape(split) * masks).astype(BF16)


def own_gradients_kernel(lengths, probs, dscore, qk, cot, grads):
    gradients(lengths, 0, qk.shape[0], probs, dscore, qk, cot, grads)


def own_gradients(lengths, probs, dscore, qk, cot):
    rows, two, _, cols = qk.shape
    return in_vmem(
        own_gradients_kernel,
        "own_gradients",
        (like((rows, two // 2 * 3, HEAD_DIM, cols)),),
        lengths,
        probs,
        dscore,
        qk,
        cot,
        scalars=1,
        limit=24,
        flops=3 * rows * two * HEAD_DIM * cols * cols,
    )[0]


def own_input_kernel(grads, weights, out):
    near, share, columns = weights.shape
    left = weights[...].reshape(near * share, columns)
    for r in range(grads.shape[0]):
        part = mm(left, grads[r].reshape(columns, grads.shape[-1]), NN).astype(BF16)
        out[:, r] = part.reshape(near, share, grads.shape[-1])


def own_input(grads, weights, after):
    rows, cols = grads.shape[0], grads.shape[-1]
    near, share, columns = weights.shape
    return in_vmem(
        own_input_kernel,
        "own_input",
        (like((near, rows, share, cols)),),
        grads,
        weights,
        after=after,
        flops=2 * rows * cols * near * share * columns,
    )[0]


def far_input_kernel(first, lengths, own, *refs):
    *refs, keep, give, grads = refs
    count, share, cols = keep.shape
    total = [own[:, first + r].astype(F32) for r in range(count)]
    for i in range(0, len(refs), 5):
        probs, dscore, qk, cot, weights = refs[i : i + 5]
        gradients(lengths, first, count, probs, dscore, qk, cot, grads)
        near, _, columns = weights.shape
        left = weights[...].reshape(near * share, columns)
        for r in range(count):
            part = mm(left, grads[r].reshape(columns, cols), NN).astype(BF16)
            total[r] = total[r] + part.reshape(near, share, cols).astype(F32)
    for r in range(count):
        keep[r] = total[r][0].astype(keep.dtype)
        give[r] = total[r][1].astype(give.dtype)


def far_input(first, count, lengths, own, far):
    _, rows, share, cols = own.shape
    columns = far[0][-1].shape[-1]
    out = like((count, share, cols))
    return in_vmem(
        functools.partial(far_input_kernel, first),
        "far_input",
        (out, out),
        lengths,
        own,
        *[a for one in far for a in one],
        scalars=1,
        scratch=(pltpu.VMEM((count, columns // HEAD_DIM, HEAD_DIM, cols), BF16),),
        limit=16,
        flops=2 * len(far) * count * cols * columns * (cols + 2 * share),
    )


def finish_kernel(keep, got, *rest):
    out = rest[-1]
    out[...] = (keep[...].astype(F32) + got[...].astype(F32)).astype(BF16)


def finish(keep, got, first, total_rows, before):
    count, share, cols = keep.shape
    block = math.gcd(first, count) if first else count
    spec = pl.BlockSpec((block, share, cols), lambda s: (s, 0, 0))
    extra = [] if before is None else [before]
    return pl.pallas_call(
        finish_kernel,
        grid=(count // block,),
        in_specs=[spec, spec] + [ANY] * len(extra),
        out_specs=pl.BlockSpec((block, share, cols), lambda s: (first // block + s, 0, 0)),
        out_shape=like((total_rows, share, cols)),
        input_output_aliases={2: 0} if extra else {},
        compiler_params=pltpu.CompilerParams(vmem_limit_bytes=12 * MIB),
        cost_estimate=cost(keep.size, keep.size * 6),
        name="finish",
    )(keep, got, *extra)


def weight_product(sheet, grads, first, count):
    rows, cols, width = sheet.shape
    columns = grads.shape[1] * HEAD_DIM
    left = [grads[r].reshape(columns, cols)[first : first + count] for r in range(rows)]
    return mm(jnp.concatenate(left, axis=1), sheet[...].reshape(rows * cols, width), NN).T


def weight_kernel(first, me, sheet, grads, keep, give, turned):
    total = weight_product(sheet, grads, first, turned.shape[-1])
    turned[...] = total.reshape(turned.shape)
    for j in range(turned.shape[0]):
        out = (keep, give)[j % 2]
        out[j // 2] = turned[me[0] ^ j].astype(out.dtype)


def whole_weight_kernel(first, me, sheet, grads, out):
    out[...] = weight_product(sheet, grads, first, out.shape[-1])


def weight_part(me, sheet, grads, first, count, shards, after):
    rows, cols, width = sheet.shape
    if shards == 1:
        kernel, outs, scratch = whole_weight_kernel, [like((width, count), F32)], ()
    else:
        half = (shards // 2, width // shards, count)
        kernel, outs = weight_kernel, [like(half, F32), like(half)]
        scratch = (pltpu.VMEM((shards,) + half[1:], F32),)
    return in_vmem(
        functools.partial(kernel, first),
        "weight_part",
        outs,
        me,
        sheet,
        grads,
        scalars=1,
        after=after,
        scratch=scratch,
        limit=24,
        flops=2 * rows * cols * width * count,
    )


def last_kernel(*refs):
    *terms, out = refs
    total = [terms[i][0] + terms[i + 1][0].astype(F32) for i in range(0, len(terms), 2)]
    total = jnp.concatenate(total, axis=-1)
    local = out.shape[-1]
    for index in range(out.shape[0]):
        out[index] = total[:, index * local : (index + 1) * local]


def last_sum(halves, local, after):
    terms = [a for half in halves for a in half]
    columns = sum(keep.shape[2] for keep, _ in halves)
    shape = (columns // local, terms[0].shape[1], local)
    return in_vmem(last_kernel, "last_sum", (like(shape, F32),), *terms, after=after)[0]


def body(sheet, w_query, w_key, w_value, cotangent, lengths):
    row_dev, cols, width = sheet.shape
    local = w_query.shape[1]
    n_rows = lax.axis_size("rows")
    n_heads = lax.axis_size("heads")
    scale = float(1.0 / (HEAD_DIM * row_dev * n_rows) ** 0.5)
    direct = n_rows <= 8
    shards = n_rows if direct else 1
    row_bits = [1 << b for b in range(n_rows.bit_length() - 1)]
    chunk = row_dev // 4

    me = jnp.stack([lax.axis_index("rows"), lax.axis_index("heads")]).astype(jnp.int32)
    wq, wk, wv = w_query.T, w_key.T, w_value.T
    cot = jnp.swapaxes(cotangent, 1, 2)

    fars = range(2, n_heads, 2)
    groups = [list(range(core, n_heads, 2)) for core in range(2)]
    wqa, wka, wva, cota = [
        lax.all_gather(a, "heads", axis_index_groups=groups) for a in (wq, wk, wv, cot)
    ]
    side = lax.shift_right_logical(lax.axis_index("heads").astype(jnp.int32), 1)
    take = lambda a, f: lax.dynamic_index_in_dim(a, side ^ (f // 2), 0, keepdims=False)
    far_weights = [[take(w, f) for w in (wqa, wka, wva)] for f in fars]
    far_cot = [take(cota, f) for f in fars]

    qk, held, *logits = query_key(lengths, me, sheet, wq, wk, shards)
    dprob = value_dprob(lengths, me, held, wv, cot, logits[-1:], shards)
    weights = turn(me, wq, wk, wv, n_heads, dprob[-1:])
    if direct:
        logits = halve(*logits, "rows", row_bits)
        dprob = halve(*dprob, "rows", row_bits)
        probs_own, dscore_own = softmax_back(logits, dprob, scale)
        probs, orders = double(probs_own, "rows", row_bits[::-1])
        dscore, _ = double(dscore_own, "rows", row_bits[::-1])
        probs, dscore = assemble(me, probs, dscore, orders, shards)
    else:
        logits, dprob = lax.psum((logits, dprob), "rows")
        probs, dscore = softmax_back(logits, dprob, scale)
    far_dscore = [flip(dscore, "heads", f) for f in fars]
    far_probs = [flip(probs, "heads", f) for f in fars]

    grads = own_gradients(lengths, probs, dscore, qk, cot)
    half = 3 * local // 2
    parts = [weight_part(me, held, grads, first, half, shards, ()) for first in (0, half)]
    ready = [parts[1][-1]]
    if direct:
        parts = [halve(*part, "rows", row_bits) for part in parts]
        weight_grad = jnp.swapaxes(last_sum(parts, local, ()), 0, 1)
    else:
        part = jnp.concatenate([p[0] for p in parts], axis=1)
        weight_grad = lax.psum_scatter(part, "rows", scatter_dimension=0, tiled=True)
        weight_grad = weight_grad.reshape(width // n_rows, 3, local)

    far = []
    for index, (fq, fk, fv) in enumerate(far_weights):
        far_qk = far_query_key(lengths, held, fq, fk, ready)
        far_natural = turn(me, fq, fk, fv, n_heads, ready)
        far.append((far_probs[index], far_dscore[index], far_qk, far_cot[index], far_natural))
    own = own_input(grads, weights, ready)
    out = None
    for first in range(0, row_dev, chunk):
        keep, give = far_input(first, chunk, lengths, own, far)
        out = finish(keep, flip(give, "heads", 1), first, row_dev, out)
    return (jnp.swapaxes(out, 1, 2), weight_grad)


def solution(mesh):
    in_specs = (
        P("rows", None, None),
        P(None, "heads"),
        P(None, "heads"),
        P(None, "heads"),
        P("rows", None, "heads"),
        P("rows"),
    )
    out_specs = (P("rows", None, "heads"), P("rows", None, "heads"))
    return jax.shard_map(body, mesh=mesh, in_specs=in_specs, out_specs=out_specs, check_vma=False)
```

```python
import functools
import math

import jax
import jax.numpy as jnp
from jax import lax
from jax.experimental import pallas as pl
from jax.experimental.pallas import tpu as pltpu
from jax.sharding import PartitionSpec as P

HEAD_DIM = 64
F32 = jnp.float32
BF16 = jnp.bfloat16
MIB = 1024 * 1024

NN = (((1,), (0,)), ((), ()))
NT = (((1,), (1,)), ((), ()))
TN = (((0,), (0,)), ((), ()))


def mm(a, b, dims):
    return lax.dot_general(a, b, dims, preferred_element_type=F32)


def flip(values, axis, bit):
    n = lax.axis_size(axis)
    return lax.ppermute(values, axis, [(s, s ^ bit) for s in range(n)])


def cost(flops, moved):
    return pl.CostEstimate(flops=int(flops), bytes_accessed=int(moved), transcendentals=0)


SMEM = pl.BlockSpec(memory_space=pltpu.SMEM)
VMEM = pl.BlockSpec(memory_space=pltpu.VMEM)
ANY = pl.BlockSpec(memory_space=pl.ANY)
HBM = pl.BlockSpec(memory_space=pltpu.HBM)


def like(shape, dtype=BF16):
    return jax.ShapeDtypeStruct(shape, dtype)


def place(a, stays):
    return pltpu.with_memory_space_constraint(a, pltpu.HBM) if stays else a


def in_vmem(kernel, name, out, *operands, scalars=0, streamed=0, after=(), scratch=(), limit=12, flops=0):
    many = len(after)

    def run(*refs):
        kernel(*refs[: len(operands)], *refs[len(operands) + many :])

    moved = 2 * sum(a.size for a in operands) + 2 * sum(o.size for o in out)
    held = len(operands) - scalars - streamed
    return pl.pallas_call(
        run,
        in_specs=[SMEM] * scalars + [HBM] * streamed + [VMEM] * held + [ANY] * many,
        out_specs=[VMEM] * len(out),
        out_shape=list(out),
        scratch_shapes=list(scratch),
        compiler_params=pltpu.CompilerParams(vmem_limit_bytes=limit * MIB),
        cost_estimate=cost(flops, moved),
        name=name,
    )(*[place(a, scalars <= i < scalars + streamed) for i, a in enumerate(operands)], *after)


def lane_mask(length, cols):
    return (lax.broadcasted_iota(jnp.int32, (1, cols), 1) < length).astype(F32)


def put_shards(me, acc, outs):
    shards = acc.shape[1]
    for j in range(shards):
        out = outs[j % len(outs)]
        out[j // len(outs)] = acc[:, me ^ j].astype(out.dtype)


BLOCK = 4
STEP = 2
AHEAD = 4


def query_key_kernel(lengths, me, sheet, wq, wk, qk, held, *rest):
    outs, (wt, acc, sems) = rest[:-3], rest[-3:]
    rows, cols, _ = sheet.shape
    local = wq.shape[0]
    heads = local // HEAD_DIM
    copies = [
        pltpu.make_async_copy(wq, wt.at[:local], sems.at[0]),
        pltpu.make_async_copy(wk, wt.at[local:], sems.at[1]),
    ]
    for first in range(0, rows, STEP):
        some = pl.ds(first, STEP)
        copies.append(pltpu.make_async_copy(sheet.at[some], held.at[some], sems.at[len(copies)]))
    for copy in copies[:AHEAD]:
        copy.start()
    copies[0].wait()
    copies[1].wait()
    flat = (BLOCK * HEAD_DIM, cols)
    for first in range(0, rows, BLOCK):
        for r in range(first, first + BLOCK):
            if r % STEP == 0:
                at = 2 + r // STEP
                copies[at].wait()
                for later in copies[at + AHEAD - 2 : at + AHEAD - 1]:
                    later.start()
            value = (mm(wt[...], held[r], NT) * lane_mask(lengths[r], cols)).astype(BF16)
            qk[r] = value.reshape(2 * heads, HEAD_DIM, cols)
        some = pl.ds(first, BLOCK)
        for h in range(heads):
            term = mm(qk[some, h].reshape(flat), qk[some, heads + h].reshape(flat), TN)
            term = term.reshape(acc.shape[1:])
            acc[h] = term if first == 0 else acc[h] + term
    put_shards(me[0], acc, outs)


def query_key(lengths, me, sheet, wq, wk, shards):
    rows, cols, width = sheet.shape
    local = wq.shape[0]
    heads = local // HEAD_DIM
    return in_vmem(
        query_key_kernel,
        "query_key",
        [like((rows, 2 * heads, HEAD_DIM, cols)), like(sheet.shape)] + part_shapes(shards, heads, cols),
        lengths,
        me,
        sheet,
        wq,
        wk,
        scalars=2,
        streamed=3,
        scratch=(
            pltpu.VMEM((2 * local, width), BF16),
            pltpu.VMEM((heads, shards, cols // shards, cols), F32),
            pltpu.SemaphoreType.DMA((2 + rows // STEP,)),
        ),
        limit=14,
        flops=2 * rows * cols * local * (2 * width + cols),
    )


def value_kernel(lengths, me, sheet, wv, cot, *rest):
    outs, acc = rest[:-1], rest[-1]
    rows, cols, _ = sheet.shape
    local = wv.shape[0]
    heads = local // HEAD_DIM
    flat = (BLOCK * HEAD_DIM, cols)
    for first in range(0, rows, BLOCK):
        values = []
        for r in range(first, first + BLOCK):
            value = (mm(wv[...], sheet[r], NT) * lane_mask(lengths[r], cols)).astype(BF16)
            values.append(value.reshape(heads, HEAD_DIM, cols))
        for h in range(heads):
            left = cot[pl.ds(first, BLOCK), h * HEAD_DIM : (h + 1) * HEAD_DIM].reshape(flat)
            right = jnp.concatenate([v[h] for v in values], axis=0)
            term = mm(left, right, TN).reshape(acc.shape[1:])
            acc[h] = term if first == 0 else acc[h] + term
    put_shards(me[0], acc, outs)


def value_dprob(lengths, me, sheet, wv, cot, after, shards):
    rows, cols, width = sheet.shape
    local = wv.shape[0]
    heads = local // HEAD_DIM
    return in_vmem(
        value_kernel,
        "value_dprob",
        part_shapes(shards, heads, cols),
        lengths,
        me,
        sheet,
        wv,
        cot,
        scalars=2,
        after=after,
        scratch=(pltpu.VMEM((heads, shards, cols // shards, cols), F32),),
        limit=16,
        flops=2 * rows * cols * local * (width + cols),
    )


def turn_kernel(me, wq, wk, wv, natural, turned):
    local = wq.shape[0]
    for index, weight in enumerate((wq, wk, wv)):
        turned[:, :, index * local : (index + 1) * local] = weight[...].T.reshape(turned.shape[:2] + (local,))
    for j in range(natural.shape[0]):
        natural[j] = turned[me[1] ^ j]


def turn(me, wq, wk, wv, devices, after):
    local, width = wq.shape
    shape = (width // devices, 3 * local)
    return in_vmem(
        turn_kernel,
        "turn",
        (like((2,) + shape),),
        me,
        wq,
        wk,
        wv,
        scalars=1,
        after=after,
        scratch=(pltpu.VMEM((devices,) + shape, BF16),),
    )[0]


def stage_kernel(*refs):
    cot, *weights, out, sems = refs
    rows, _, cols = cot.shape
    copies = [pltpu.make_async_copy(cot, out.at[pl.ds(0, rows)], sems.at[0])]
    for weight in weights:
        for first in range(0, weight.shape[1], cols):
            at = rows + len(copies) - 1
            piece = weight.at[:, pl.ds(first, cols)]
            copies.append(pltpu.make_async_copy(piece, out.at[at], sems.at[len(copies)]))
    for copy in copies:
        copy.start()
    for copy in copies:
        copy.wait()


def stage(cot, weights):
    rows, local, cols = cot.shape
    pieces = len(weights) * weights[0].shape[1] // cols
    held = [place(a, True) for a in (cot, *weights)]
    return pl.pallas_call(
        stage_kernel,
        in_specs=[HBM] * len(held),
        out_specs=HBM,
        out_shape=like((rows + pieces, local, cols)),
        scratch_shapes=[pltpu.SemaphoreType.DMA((1 + pieces,))],
        cost_estimate=cost(0, 4 * cot.size),
        name="stage",
    )(*held)


def far_prepare_kernel(far, lengths, me, gathered, sheet, qk, natural, cot, w, turned, sems):
    rows, cols, width = sheet.shape
    count, local, _ = w.shape
    devices, share, _ = turned.shape
    heads = local // HEAD_DIM
    pos = lax.shift_right_logical(me[1], 1) ^ (far // 2)
    copies = []
    for index in range(count):
        for first in range(0, width, cols):
            at = rows + len(copies)
            copies.append(
                pltpu.make_async_copy(
                    gathered.at[pos, at], w.at[index, :, pl.ds(first, cols)], sems.at[len(copies)]
                )
            )
    copies.append(pltpu.make_async_copy(gathered.at[pos, pl.ds(0, rows)], cot, sems.at[len(copies)]))
    for copy in copies:
        copy.start()
    for copy in copies[:-1]:
        copy.wait()
    both = w[:2].reshape(2 * local, width)
    for r in range(rows):
        value = (mm(both, sheet[r], NT) * lane_mask(lengths[r], cols)).astype(BF16)
        qk[r] = value.reshape(2 * heads, HEAD_DIM, cols)
    for index in range(count):
        turned[:, :, index * local : (index + 1) * local] = w[index].T.reshape(devices, share, local)
    for j in range(natural.shape[0]):
        natural[j] = turned[me[1] ^ j]
    copies[-1].wait()


def far_prepare(far, lengths, me, gathered, sheet, devices, after):
    rows, cols, width = sheet.shape
    local = gathered.shape[2]
    share = width // devices
    return in_vmem(
        functools.partial(far_prepare_kernel, far),
        "far_prepare",
        (
            like((rows, 2 * local // HEAD_DIM, HEAD_DIM, cols)),
            like((2, share, 3 * local)),
            like((rows, local, cols)),
        ),
        lengths,
        me,
        gathered,
        sheet,
        scalars=2,
        streamed=1,
        after=after,
        scratch=(
            pltpu.VMEM((3, local, width), BF16),
            pltpu.VMEM((devices, share, 3 * local), BF16),
            pltpu.SemaphoreType.DMA((3 * width // cols + 1,)),
        ),
        limit=14,
        flops=4 * rows * cols * local * width,
    )


def part_shapes(shards, heads, cols):
    if shards == 1:
        return [like((1, heads, cols, cols), F32)]
    half = (shards // 2, heads, cols // shards, cols)
    return [like(half, F32), like(half)]


def add_split_kernel(keep, got, give_out, keep_out):
    for j in range(keep.shape[0]):
        total = keep[j].astype(F32) + got[j].astype(F32)
        out = give_out if j % 2 else keep_out
        out[j // 2] = total.astype(out.dtype)


def add_split(keep, got, after=()):
    half = (keep.shape[0] // 2,) + keep.shape[1:]
    return in_vmem(add_split_kernel, "add_split", (like(half), like(half, keep.dtype)), keep, got, after=after)


def halve(keep, give, axis, bits, after=()):
    after = list(after) + [()] * len(bits)
    for bit, waits in zip(bits[:-1], after):
        give, keep = add_split(keep, flip(give, axis, bit), waits)
    return keep, flip(give, axis, bits[-1])


def softmax_kernel(scale, *refs):
    *terms, probs_out, dscore_out = refs
    half = len(terms) // 2
    total = lambda some: functools.reduce(jnp.add, [t[0].astype(F32) for t in some])
    logits = total(terms[:half]) * scale
    dprob = total(terms[half:])
    shifted = jnp.exp(logits - jnp.max(logits, axis=-1, keepdims=True))
    probs = shifted / jnp.sum(shifted, axis=-1, keepdims=True)
    inner = jnp.sum(probs * dprob, axis=-1, keepdims=True)
    probs_out[0] = probs.astype(BF16)
    dscore_out[0] = (scale * probs * (dprob - inner)).astype(BF16)


def softmax_back(logits, dprob, scale):
    out = like(logits[0].shape)
    return in_vmem(
        functools.partial(softmax_kernel, scale), "softmax_back", (out, out), *logits, *dprob, limit=16
    )


def double(values, axis, bits):
    order = [0]
    for bit in bits[:-1]:
        values = jnp.concatenate([values, flip(values, axis, bit)], axis=0)
        order = order + [j ^ bit for j in order]
    other = flip(values, axis, bits[-1])
    return (values, other), (order, [j ^ bits[-1] for j in order])


def assemble_kernel(orders, me, *refs):
    pieces, outs = refs[:-2], refs[-2:]
    per = len(orders)
    for kind, out in enumerate(outs):
        for piece, order in zip(pieces[kind * per : (kind + 1) * per], orders):
            for t, j in enumerate(order):
                out[me[0] ^ j] = piece[t]


def assemble(me, probs, dscore, orders, shards):
    out = like((shards,) + probs[0].shape[1:])
    return in_vmem(
        functools.partial(assemble_kernel, orders), "assemble", (out, out), me, *probs, *dscore, scalars=1
    )


def gradients(lengths, first, count, probs, dscore, qk, cot, grads):
    cols = qk.shape[-1]
    heads = qk.shape[1] // 2
    rows = pl.ds(first, count)
    flat = (count * HEAD_DIM, cols)
    split = (count, HEAD_DIM, cols)
    masks = jnp.stack([lane_mask(lengths[first + r], cols) for r in range(count)])
    for h in range(heads):
        p, ds = [ref[:, h].reshape(cols, cols) for ref in (probs, dscore)]
        g = cot[rows, h * HEAD_DIM : (h + 1) * HEAD_DIM].reshape(flat)
        dq = mm(qk[rows, heads + h].reshape(flat), ds, NT)
        dk = mm(qk[rows, h].reshape(flat), ds, NN)
        dv = mm(g, p, NN)
        for index, value in enumerate((dq, dk, dv)):
            grads[:, index * heads + h] = (value.reshape(split) * masks).astype(BF16)


def own_gradients_kernel(lengths, probs, dscore, qk, cot, grads):
    gradients(lengths, 0, qk.shape[0], probs, dscore, qk, cot, grads)


def own_gradients(lengths, probs, dscore, qk, cot):
    rows, two, _, cols = qk.shape
    return in_vmem(
        own_gradients_kernel,
        "own_gradients",
        (like((rows, two // 2 * 3, HEAD_DIM, cols)),),
        lengths,
        probs,
        dscore,
        qk,
        cot,
        scalars=1,
        limit=24,
        flops=3 * rows * two * HEAD_DIM * cols * cols,
    )[0]


def own_input_kernel(grads, weights, out):
    near, share, columns = weights.shape
    left = weights[...].reshape(near * share, columns)
    for r in range(grads.shape[0]):
        part = mm(left, grads[r].reshape(columns, grads.shape[-1]), NN).astype(BF16)
        out[:, r] = part.reshape(near, share, grads.shape[-1])


def own_input(grads, weights, after):
    rows, cols = grads.shape[0], grads.shape[-1]
    near, share, columns = weights.shape
    return in_vmem(
        own_input_kernel,
        "own_input",
        (like((near, rows, share, cols)),),
        grads,
        weights,
        after=after,
        flops=2 * rows * cols * near * share * columns,
    )[0]


def far_input_kernel(first, lengths, own, *refs):
    *refs, keep, give, grads = refs
    count, share, cols = keep.shape
    total = [own[:, first + r].astype(F32) for r in range(count)]
    for i in range(0, len(refs), 5):
        probs, dscore, qk, cot, weights = refs[i : i + 5]
        gradients(lengths, first, count, probs, dscore, qk, cot, grads)
        near, _, columns = weights.shape
        left = weights[...].reshape(near * share, columns)
        for r in range(count):
            part = mm(left, grads[r].reshape(columns, cols), NN).astype(BF16)
            total[r] = total[r] + part.reshape(near, share, cols).astype(F32)
    for r in range(count):
        keep[r] = total[r][0].astype(keep.dtype)
        give[r] = total[r][1].astype(give.dtype)


def far_input(first, count, lengths, own, far, after):
    _, rows, share, cols = own.shape
    columns = far[0][-1].shape[-1]
    out = like((count, share, cols))
    return in_vmem(
        functools.partial(far_input_kernel, first),
        "far_input",
        (out, out),
        lengths,
        own,
        *[a for one in far for a in one],
        scalars=1,
        after=after,
        scratch=(pltpu.VMEM((count, columns // HEAD_DIM, HEAD_DIM, cols), BF16),),
        limit=16,
        flops=2 * len(far) * count * cols * columns * (cols + 2 * share),
    )


def finish_kernel(keep, got, *rest):
    out = rest[-1]
    out[...] = (keep[...].astype(F32) + got[...].astype(F32)).astype(BF16)


def finish(keep, got, first, total_rows, before):
    count, share, cols = keep.shape
    block = math.gcd(first, count) if first else count
    spec = pl.BlockSpec((block, share, cols), lambda s: (s, 0, 0))
    extra = [] if before is None else [before]
    return pl.pallas_call(
        finish_kernel,
        grid=(count // block,),
        in_specs=[spec, spec] + [ANY] * len(extra),
        out_specs=pl.BlockSpec((block, share, cols), lambda s: (first // block + s, 0, 0)),
        out_shape=like((total_rows, share, cols)),
        input_output_aliases={2: 0} if extra else {},
        compiler_params=pltpu.CompilerParams(vmem_limit_bytes=12 * MIB),
        cost_estimate=cost(keep.size, keep.size * 6),
        name="finish",
    )(keep, got, *extra)


def weight_product(sheet, grads):
    rows, cols, width = sheet.shape
    columns = grads.shape[1] * HEAD_DIM
    left = [grads[r].reshape(columns, cols) for r in range(rows)]
    return mm(jnp.concatenate(left, axis=1), sheet[...].reshape(rows * cols, width), NN).T


def weight_kernel(me, sheet, grads, *rest):
    outs, turned = rest[:-1], rest[-1]
    turned[...] = weight_product(sheet, grads).reshape(turned.shape)
    for j in range(turned.shape[0]):
        first = 0
        for keep, give in zip(outs[::2], outs[1::2]):
            out = (keep, give)[j % 2]
            last = first + out.shape[-1]
            out[j // 2] = turned[me[0] ^ j, :, first:last].astype(out.dtype)
            first = last


def whole_weight_kernel(me, sheet, grads, out):
    out[...] = weight_product(sheet, grads)


def weight_part(me, sheet, grads, cuts, shards):
    rows, cols, width = sheet.shape
    columns = grads.shape[1] * HEAD_DIM
    if shards == 1:
        kernel, outs, scratch = whole_weight_kernel, [like((width, columns), F32)], ()
    else:
        halves = [(shards // 2, width // shards, cut) for cut in cuts]
        kernel = weight_kernel
        outs = [o for half in halves for o in (like(half, F32), like(half))]
        scratch = (pltpu.VMEM((shards, width // shards, columns), F32),)
    return in_vmem(
        kernel,
        "weight_part",
        outs,
        me,
        sheet,
        grads,
        scalars=1,
        scratch=scratch,
        limit=18,
        flops=2 * rows * cols * width * columns,
    )


def last_kernel(*refs):
    *terms, out = refs
    total = [terms[i][0] + terms[i + 1][0].astype(F32) for i in range(0, len(terms), 2)]
    total = jnp.concatenate(total, axis=-1)
    local = out.shape[-1]
    for index in range(out.shape[0]):
        out[index] = total[:, index * local : (index + 1) * local]


def last_sum(halves, local, after):
    terms = [a for half in halves for a in half]
    columns = sum(keep.shape[2] for keep, _ in halves)
    shape = (columns // local, terms[0].shape[1], local)
    return in_vmem(last_kernel, "last_sum", (like(shape, F32),), *terms, after=after)[0]


def body(sheet, w_query, w_key, w_value, cotangent, lengths):
    row_dev, cols, width = sheet.shape
    local = w_query.shape[1]
    n_rows = lax.axis_size("rows")
    n_heads = lax.axis_size("heads")
    scale = float(1.0 / (HEAD_DIM * row_dev * n_rows) ** 0.5)
    direct = n_rows <= 8
    shards = n_rows if direct else 1
    row_bits = [1 << b for b in range(n_rows.bit_length() - 1)]
    chunk = row_dev // 4

    me = jnp.stack([lax.axis_index("rows"), lax.axis_index("heads")]).astype(jnp.int32)
    wq, wk, wv = w_query.T, w_key.T, w_value.T
    cot = jnp.swapaxes(cotangent, 1, 2)

    fars = range(2, n_heads, 2)
    groups = [list(range(core, n_heads, 2)) for core in range(2)]
    gathered = lax.all_gather(stage(cot, (wq, wk, wv)), "heads", axis_index_groups=groups)

    qk, held, *logits = query_key(lengths, me, sheet, wq, wk, shards)
    dprob = value_dprob(lengths, me, held, wv, cot, logits[-1:], shards)
    weights = turn(me, wq, wk, wv, n_heads, dprob[-1:])
    if direct:
        logits = halve(*logits, "rows", row_bits)
        dprob = halve(*dprob, "rows", row_bits)
        probs_own, dscore_own = softmax_back(logits, dprob, scale)
        probs, orders = double(probs_own, "rows", row_bits[::-1])
        dscore, _ = double(dscore_own, "rows", row_bits[::-1])
        probs, dscore = assemble(me, probs, dscore, orders, shards)
    else:
        logits, dprob = lax.psum((logits, dprob), "rows")
        probs, dscore = softmax_back(logits, dprob, scale)
    far_dscore = [flip(dscore, "heads", f) for f in fars]
    far_probs = [flip(probs, "heads", f) for f in fars]

    grads = own_gradients(lengths, probs, dscore, qk, cot)
    cut = 3 * local // 256 * 128
    cuts = (cut, 3 * local - cut)
    parts = weight_part(me, held, grads, cuts, shards)
    ready = [parts[-1]]
    far = []
    for index, f in enumerate(fars):
        far_qk, far_natural, far_cot = far_prepare(f, lengths, me, gathered, held, n_heads, ready)
        far.append((far_probs[index], far_dscore[index], far_qk, far_cot, far_natural))
        ready = [far_qk]
    own = own_input(grads, weights, ready + far_dscore)
    ready = [own] + far_probs
    steps = []
    if direct:
        parts = [tuple(parts[:2]), tuple(parts[2:])]
        for bit in row_bits[:-1]:
            parts = [add_split(keep, flip(give, "rows", bit), ready)[::-1] for keep, give in parts]
            steps.append([keep for keep, _ in parts])
            ready = ()
        parts = [(keep, flip(give, "rows", row_bits[-1])) for keep, give in parts]
    else:
        weight_grad = lax.psum_scatter(parts[0], "rows", scatter_dimension=0, tiled=True)
        weight_grad = weight_grad.reshape(width // n_rows, 3, local)

    out = None
    for index, first in enumerate(range(0, row_dev, chunk)):
        after = steps[index // 2] if index // 2 < len(steps) else ()
        keep, give = far_input(first, chunk, lengths, own, far, after)
        out = finish(keep, flip(give, "heads", 1), first, row_dev, out)
    if direct:
        weight_grad = jnp.swapaxes(last_sum(parts, local, [out]), 0, 1)
    return (jnp.swapaxes(out, 1, 2), weight_grad)


def solution(mesh):
    in_specs = (
        P("rows", None, None),
        P(None, "heads"),
        P(None, "heads"),
        P(None, "heads"),
        P("rows", None, "heads"),
        P("rows"),
    )
    out_specs = (P("rows", None, "heads"), P("rows", None, "heads"))
    return jax.shard_map(body, mesh=mesh, in_specs=in_specs, out_specs=out_specs, check_vma=False)
```

```python
import functools
import math

import jax
import jax.numpy as jnp
from jax import lax
from jax.experimental import pallas as pl
from jax.experimental.pallas import tpu as pltpu
from jax.sharding import PartitionSpec as P

HEAD_DIM = 64
F32 = jnp.float32
BF16 = jnp.bfloat16
MIB = 1024 * 1024

NN = (((1,), (0,)), ((), ()))
NT = (((1,), (1,)), ((), ()))


def mm(a, b, dims):
    return lax.dot_general(a, b, dims, preferred_element_type=F32)


def turned(a):
    n = a.shape[1]
    same = lax.broadcasted_iota(jnp.int32, (n, n), 0) == lax.broadcasted_iota(jnp.int32, (n, n), 1)
    return mm(same.astype(a.dtype), a, NT).astype(a.dtype)


def flip(values, axis, bit):
    n = lax.axis_size(axis)
    return lax.ppermute(values, axis, [(s, s ^ bit) for s in range(n)])


def cost(flops, moved):
    return pl.CostEstimate(flops=int(flops), bytes_accessed=int(moved), transcendentals=0)


SMEM = pl.BlockSpec(memory_space=pltpu.SMEM)
VMEM = pl.BlockSpec(memory_space=pltpu.VMEM)
ANY = pl.BlockSpec(memory_space=pl.ANY)
HBM = pl.BlockSpec(memory_space=pltpu.HBM)


def like(shape, dtype=BF16):
    return jax.ShapeDtypeStruct(shape, dtype)


def place(a, stays):
    return pltpu.with_memory_space_constraint(a, pltpu.HBM) if stays else a


def in_vmem(kernel, name, out, *operands, scalars=0, streamed=0, after=(), scratch=(), limit=12, flops=0):
    many = len(after)

    def run(*refs):
        kernel(*refs[: len(operands)], *refs[len(operands) + many :])

    moved = 2 * sum(a.size for a in operands) + 2 * sum(o.size for o in out)
    held = len(operands) - scalars - streamed
    return pl.pallas_call(
        run,
        in_specs=[SMEM] * scalars + [HBM] * streamed + [VMEM] * held + [ANY] * many,
        out_specs=[VMEM] * len(out),
        out_shape=list(out),
        scratch_shapes=list(scratch),
        compiler_params=pltpu.CompilerParams(vmem_limit_bytes=limit * MIB),
        cost_estimate=cost(flops, moved),
        name=name,
    )(*[place(a, scalars <= i < scalars + streamed) for i, a in enumerate(operands)], *after)


def lane_mask(length, cols):
    return (lax.broadcasted_iota(jnp.int32, (1, cols), 1) < length).astype(F32)


def reorder(bits):
    return [sum(bit for b, bit in enumerate(bits) if t >> b & 1) for t in range(1 << len(bits))]


def put_shards(me, acc, bits, outs):
    for t, j in enumerate(reorder(bits)):
        out = outs[t % len(outs)]
        out[t // len(outs)] = acc[:, me ^ j].astype(out.dtype)


BLOCK = 4
STEP = 2
AHEAD = 4


def query_key_kernel(bits, lengths, me, sheet, wq, wk, qk, held, *rest):
    outs, (wt, acc, sems) = rest[:-3], rest[-3:]
    rows, cols, _ = sheet.shape
    local = wq.shape[0]
    heads = local // HEAD_DIM
    copies = [
        pltpu.make_async_copy(wq, wt.at[:local], sems.at[0]),
        pltpu.make_async_copy(wk, wt.at[local:], sems.at[1]),
    ]
    for first in range(0, rows, STEP):
        some = pl.ds(first, STEP)
        copies.append(pltpu.make_async_copy(sheet.at[some], held.at[some], sems.at[len(copies)]))
    for copy in copies[:AHEAD]:
        copy.start()
    copies[0].wait()
    copies[1].wait()
    flat = (BLOCK * HEAD_DIM, cols)
    for first in range(0, rows, BLOCK):
        for r in range(first, first + BLOCK):
            if r % STEP == 0:
                at = 2 + r // STEP
                copies[at].wait()
                for later in copies[at + AHEAD - 2 : at + AHEAD - 1]:
                    later.start()
            value = (mm(wt[...], held[r], NT) * lane_mask(lengths[r], cols)).astype(BF16)
            qk[r] = value.reshape(2 * heads, HEAD_DIM, cols)
        some = pl.ds(first, BLOCK)
        for h in range(heads):
            term = mm(turned(qk[some, h].reshape(flat)), qk[some, heads + h].reshape(flat), NN)
            term = term.reshape(acc.shape[1:])
            acc[h] = term if first == 0 else acc[h] + term
    put_shards(me[0], acc, bits, outs)


def query_key(lengths, me, sheet, wq, wk, bits):
    rows, cols, width = sheet.shape
    shards = 1 << len(bits)
    local = wq.shape[0]
    heads = local // HEAD_DIM
    return in_vmem(
        functools.partial(query_key_kernel, bits),
        "query_key",
        [like((rows, 2 * heads, HEAD_DIM, cols)), like(sheet.shape)] + part_shapes(shards, heads, cols),
        lengths,
        me,
        sheet,
        wq,
        wk,
        scalars=2,
        streamed=3,
        scratch=(
            pltpu.VMEM((2 * local, width), BF16),
            pltpu.VMEM((heads, shards, cols // shards, cols), F32),
            pltpu.SemaphoreType.DMA((2 + rows // STEP,)),
        ),
        limit=14,
        flops=2 * rows * cols * local * (2 * width + cols),
    )


def value_kernel(bits, lengths, me, sheet, wv, cot, *rest):
    outs, acc = rest[:-1], rest[-1]
    rows, cols, _ = sheet.shape
    local = wv.shape[0]
    heads = local // HEAD_DIM
    flat = (BLOCK * HEAD_DIM, cols)
    for first in range(0, rows, BLOCK):
        values = []
        for r in range(first, first + BLOCK):
            value = (mm(wv[...], sheet[r], NT) * lane_mask(lengths[r], cols)).astype(BF16)
            values.append(value.reshape(heads, HEAD_DIM, cols))
        for h in range(heads):
            left = cot[pl.ds(first, BLOCK), h * HEAD_DIM : (h + 1) * HEAD_DIM].reshape(flat)
            right = jnp.concatenate([v[h] for v in values], axis=0)
            term = mm(turned(left), right, NN).reshape(acc.shape[1:])
            acc[h] = term if first == 0 else acc[h] + term
    put_shards(me[0], acc, bits, outs)


def value_dprob(lengths, me, sheet, wv, cot, after, bits):
    rows, cols, width = sheet.shape
    shards = 1 << len(bits)
    local = wv.shape[0]
    heads = local // HEAD_DIM
    return in_vmem(
        functools.partial(value_kernel, bits),
        "value_dprob",
        part_shapes(shards, heads, cols),
        lengths,
        me,
        sheet,
        wv,
        cot,
        scalars=2,
        after=after,
        scratch=(pltpu.VMEM((heads, shards, cols // shards, cols), F32),),
        limit=16,
        flops=4 * rows * cols * local * (width + cols),
    )


def turn_kernel(me, wq, wk, wv, natural, full):
    local = wq.shape[0]
    for index, weight in enumerate((wq, wk, wv)):
        full[:, :, index * local : (index + 1) * local] = weight[...].T.reshape(full.shape[:2] + (local,))
    for j in range(natural.shape[0]):
        natural[j] = full[me[1] ^ j]


def turn(me, wq, wk, wv, devices, after):
    local, width = wq.shape
    shape = (width // devices, 3 * local)
    return in_vmem(
        turn_kernel,
        "turn",
        (like((2,) + shape),),
        me,
        wq,
        wk,
        wv,
        scalars=1,
        after=after,
        scratch=(pltpu.VMEM((devices,) + shape, BF16),),
    )[0]


def far_query_key_kernel(first, lengths, sheet, wq, wk, qk):
    local, _ = wq.shape
    cols = sheet.shape[1]
    both = jnp.concatenate([wq[...], wk[...]], axis=0)
    for r in range(qk.shape[0]):
        value = (mm(both, sheet[first + r], NT) * lane_mask(lengths[first + r], cols)).astype(BF16)
        qk[r] = value.reshape(2 * local // HEAD_DIM, HEAD_DIM, cols)


def far_query_key(first, count, lengths, sheet, wq, wk, after):
    _, cols, width = sheet.shape
    local = wq.shape[0]
    return in_vmem(
        functools.partial(far_query_key_kernel, first),
        "far_query_key",
        (like((count, 2 * local // HEAD_DIM, HEAD_DIM, cols)),),
        lengths,
        sheet,
        wq,
        wk,
        scalars=1,
        after=after,
        flops=4 * count * cols * local * width,
    )[0]


def part_shapes(shards, heads, cols):
    if shards == 1:
        return [like((1, heads, cols, cols), F32)]
    half = (shards // 2, heads, cols // shards, cols)
    return [like(half, F32), like(half)]


def add_split_kernel(keep, got, give_out, keep_out):
    for j in range(keep.shape[0]):
        total = keep[j].astype(F32) + got[j].astype(F32)
        out = give_out if j % 2 else keep_out
        out[j // 2] = total.astype(out.dtype)


def add_split(keep, got, after=()):
    half = (keep.shape[0] // 2,) + keep.shape[1:]
    return in_vmem(add_split_kernel, "add_split", (like(half), like(half, keep.dtype)), keep, got, after=after)


def halve(keep, give, axis, bits, after=()):
    after = list(after) + [()] * len(bits)
    for bit, waits in zip(bits[:-1], after):
        give, keep = add_split(keep, flip(give, axis, bit), waits)
    return keep, flip(give, axis, bits[-1])


def softmax_kernel(scale, *refs):
    *terms, probs_out, dscore_out = refs
    half = len(terms) // 2
    total = lambda some: functools.reduce(jnp.add, [t[0].astype(F32) for t in some])
    logits = total(terms[:half]) * scale
    dprob = total(terms[half:])
    shifted = jnp.exp(logits - jnp.max(logits, axis=-1, keepdims=True))
    probs = shifted / jnp.sum(shifted, axis=-1, keepdims=True)
    inner = jnp.sum(probs * dprob, axis=-1, keepdims=True)
    probs_out[0] = probs.astype(BF16)
    dscore_out[0] = (scale * probs * (dprob - inner)).astype(BF16)


def softmax_back(logits, dprob, scale, after=()):
    out = like(logits[0].shape)
    return in_vmem(
        functools.partial(softmax_kernel, scale), "softmax_back", (out, out), *logits, *dprob, limit=16, after=after
    )


def double(values, axis, bits):
    order = [0]
    for bit in bits[:-1]:
        values = jnp.concatenate([values, flip(values, axis, bit)], axis=0)
        order = order + [j ^ bit for j in order]
    other = flip(values, axis, bits[-1])
    return (values, other), (order, [j ^ bits[-1] for j in order])


def assemble_kernel(orders, me, *refs):
    pieces, outs = refs[:-2], refs[-2:]
    for piece, (kind, order) in zip(pieces, orders):
        for t, j in enumerate(order):
            outs[kind][me[0] ^ j] = piece[t]


def assemble(me, probs, dscore, orders, shards, after):
    out = like((shards,) + probs[0].shape[1:])
    return in_vmem(
        functools.partial(assemble_kernel, [(k, o) for k, both in enumerate(orders) for o in both]), "assemble", (out, out), me, *probs, *dscore, scalars=1, after=after
    )


def gradients(lengths, first, at, count, probs, dscore, qk, cot, grads):
    cols = qk.shape[-1]
    heads = qk.shape[1] // 2
    rows, held = pl.ds(first, count), pl.ds(at, count)
    flat = (count * HEAD_DIM, cols)
    split = (count, HEAD_DIM, cols)
    masks = jnp.stack([lane_mask(lengths[first + r], cols) for r in range(count)])
    for h in range(heads):
        p, ds = [ref[:, h].reshape(cols, cols) for ref in (probs, dscore)]
        g = cot[rows, h * HEAD_DIM : (h + 1) * HEAD_DIM].reshape(flat)
        dq = mm(qk[held, heads + h].reshape(flat), ds, NT)
        dk = mm(qk[held, h].reshape(flat), ds, NN)
        dv = mm(g, p, NN)
        for index, value in enumerate((dq, dk, dv)):
            grads[:, index * heads + h] = (value.reshape(split) * masks).astype(BF16)


def own_gradients_kernel(lengths, probs, dscore, qk, cot, grads):
    gradients(lengths, 0, 0, qk.shape[0], probs, dscore, qk, cot, grads)


def own_gradients(lengths, probs, dscore, qk, cot):
    rows, two, _, cols = qk.shape
    return in_vmem(
        own_gradients_kernel,
        "own_gradients",
        (like((rows, two // 2 * 3, HEAD_DIM, cols)),),
        lengths,
        probs,
        dscore,
        qk,
        cot,
        scalars=1,
        limit=14,
        flops=3 * rows * two * HEAD_DIM * cols * cols,
    )[0]


def own_input_kernel(grads, weights, out):
    near, share, columns = weights.shape
    left = weights[...].reshape(near * share, columns)
    for r in range(grads.shape[0]):
        part = mm(left, grads[r].reshape(columns, grads.shape[-1]), NN).astype(BF16)
        out[:, r] = part.reshape(near, share, grads.shape[-1])


def own_input(grads, weights, after):
    rows, cols = grads.shape[0], grads.shape[-1]
    near, share, columns = weights.shape
    return in_vmem(
        own_input_kernel,
        "own_input",
        (like((near, rows, share, cols)),),
        grads,
        weights,
        after=after,
        flops=2 * rows * cols * near * share * columns,
    )[0]


def far_input_kernel(first, at, lengths, own, *refs):
    *refs, keep, give, grads = refs
    count, share, cols = keep.shape
    total = [own[:, first + r].astype(F32) for r in range(count)]
    for i in range(0, len(refs), 5):
        probs, dscore, qk, cot, weights = refs[i : i + 5]
        gradients(lengths, first, at, count, probs, dscore, qk, cot, grads)
        near, _, columns = weights.shape
        left = weights[...].reshape(near * share, columns)
        for r in range(count):
            part = mm(left, grads[r].reshape(columns, cols), NN).astype(BF16)
            total[r] = total[r] + part.reshape(near, share, cols).astype(F32)
    for r in range(count):
        keep[r] = total[r][0].astype(keep.dtype)
        give[r] = total[r][1].astype(give.dtype)


def far_input(first, at, count, lengths, own, far, after):
    _, rows, share, cols = own.shape
    columns = far[0][-1].shape[-1]
    out = like((count, share, cols))
    return in_vmem(
        functools.partial(far_input_kernel, first, at),
        "far_input",
        (out, out),
        lengths,
        own,
        *[a for one in far for a in one],
        scalars=1,
        after=after,
        scratch=(pltpu.VMEM((count, columns // HEAD_DIM, HEAD_DIM, cols), BF16),),
        limit=16,
        flops=2 * len(far) * count * cols * columns * (cols + 2 * share),
    )


def finish_kernel(keep, got, *rest):
    out = rest[-1]
    out[...] = (keep[...].astype(F32) + got[...].astype(F32)).astype(BF16)


def finish(keep, got, first, total_rows, before):
    count, share, cols = keep.shape
    block = math.gcd(first, count) if first else count
    spec = pl.BlockSpec((block, share, cols), lambda s: (s, 0, 0))
    extra = [] if before is None else [before]
    return pl.pallas_call(
        finish_kernel,
        grid=(count // block,),
        in_specs=[spec, spec] + [ANY] * len(extra),
        out_specs=pl.BlockSpec((block, share, cols), lambda s: (first // block + s, 0, 0)),
        out_shape=like((total_rows, share, cols)),
        input_output_aliases={2: 0} if extra else {},
        compiler_params=pltpu.CompilerParams(vmem_limit_bytes=12 * MIB),
        cost_estimate=cost(keep.size, keep.size * 6),
        name="finish",
    )(keep, got, *extra)


def weight_product(sheet, grads):
    rows, cols, width = sheet.shape
    columns = grads.shape[1] * HEAD_DIM
    left = [grads[r].reshape(columns, cols) for r in range(rows)]
    return mm(jnp.concatenate(left, axis=1), sheet[...].reshape(rows * cols, width), NN).T


def weight_kernel(me, sheet, grads, *rest):
    outs, full = rest[:-1], rest[-1]
    full[...] = weight_product(sheet, grads).reshape(full.shape)
    for j in range(full.shape[0]):
        first = 0
        for keep, give in zip(outs[::2], outs[1::2]):
            out = (keep, give)[j % 2]
            last = first + out.shape[-1]
            out[j // 2] = full[me[0] ^ j, :, first:last].astype(out.dtype)
            first = last


def whole_weight_kernel(me, sheet, grads, out):
    out[...] = weight_product(sheet, grads)


def weight_part(me, sheet, grads, cuts, shards):
    rows, cols, width = sheet.shape
    columns = grads.shape[1] * HEAD_DIM
    if shards == 1:
        kernel, outs, scratch = whole_weight_kernel, [like((width, columns), F32)], ()
    else:
        halves = [(shards // 2, width // shards, cut) for cut in cuts]
        kernel = weight_kernel
        outs = [o for half in halves for o in (like(half, F32), like(half))]
        scratch = (pltpu.VMEM((shards, width // shards, columns), F32),)
    return in_vmem(
        kernel,
        "weight_part",
        outs,
        me,
        sheet,
        grads,
        scalars=1,
        scratch=scratch,
        limit=18,
        flops=2 * rows * cols * width * columns,
    )


def last_kernel(*refs):
    *terms, out = refs
    total = [terms[i][0] + terms[i + 1][0].astype(F32) for i in range(0, len(terms), 2)]
    total = jnp.concatenate(total, axis=-1)
    local = out.shape[-1]
    for index in range(out.shape[0]):
        out[index] = total[:, index * local : (index + 1) * local]


def last_sum(halves, local, after):
    terms = [a for half in halves for a in half]
    columns = sum(keep.shape[2] for keep, _ in halves)
    shape = (columns // local, terms[0].shape[1], local)
    return in_vmem(last_kernel, "last_sum", (like(shape, F32),), *terms, after=after)[0]


def body(sheet, w_query, w_key, w_value, cotangent, lengths):
    row_dev, cols, width = sheet.shape
    local = w_query.shape[1]
    n_rows = lax.axis_size("rows")
    n_heads = lax.axis_size("heads")
    scale = float(1.0 / (HEAD_DIM * row_dev * n_rows) ** 0.5)
    direct = n_rows <= 8
    shards = n_rows if direct else 1
    row_bits = [1 << b for b in range(n_rows.bit_length() - 1)]
    chunk = row_dev // 4

    me = jnp.stack([lax.axis_index("rows"), lax.axis_index("heads")]).astype(jnp.int32)
    wq, wk, wv = w_query.T, w_key.T, w_value.T
    cot = jnp.swapaxes(cotangent, 1, 2)

    fars = range(2, n_heads, 2)
    far_cot = [flip(cot, "heads", f) for f in fars]
    far_weights = [[flip(w, "heads", f) for w in (wq, wk, wv)] for f in fars]
    fq, fk, fv = [[w[i] for w in far_weights] for i in range(3)]

    up = row_bits if direct else []
    turn_about = up[1:] + up[:1]
    qk, held, *logits = query_key(lengths, me, sheet, wq, wk, up)
    dprob = value_dprob(lengths, me, held, wv, cot, logits[-1:], turn_about)
    weights = turn(me, wq, wk, wv, n_heads, dprob[-1:])
    far_qk, far_natural = [], []
    for w in far_weights:
        parts = [far_query_key(r, row_dev // 2, lengths, held, w[0], w[1], ()) for r in (0, row_dev // 2)]
        far_qk.append(parts)
        far_natural.append(turn(me, *w, n_heads, ()))
    before = [a for two in far_qk for a in two] + far_natural + [weights]
    if direct:
        logits = halve(*logits, "rows", up)
        dprob = halve(*dprob, "rows", turn_about)
        probs_own, dscore_own = softmax_back(logits, dprob, scale, far_cot)
        probs, probs_order = double(probs_own, "rows", up[::-1])
        dscore, dscore_order = double(dscore_own, "rows", turn_about[::-1])
        probs, dscore = assemble(me, probs, dscore, (probs_order, dscore_order), shards, [weights] + far_natural)
    else:
        logits, dprob = lax.psum((logits, dprob), "rows")
        probs, dscore = softmax_back(logits, dprob, scale)
    far_dscore = [flip(dscore, "heads", f) for f in fars]
    far_probs = [flip(probs, "heads", f) for f in fars]

    grads = own_gradients(lengths, probs, dscore, qk, cot)
    cut = 3 * local // 256 * 128
    cuts = (cut, 3 * local - cut)
    parts = weight_part(me, held, grads, cuts, shards)
    own = own_input(grads, weights, [parts[-1]] + far_dscore)
    ready = [own] + far_probs
    steps = []
    if direct:
        parts = [tuple(parts[:2]), tuple(parts[2:])]
        for bit in row_bits[:-1]:
            parts = [add_split(keep, flip(give, "rows", bit), ready)[::-1] for keep, give in parts]
            steps.append([keep for keep, _ in parts])
            ready = ()
        parts = [(keep, flip(give, "rows", row_bits[-1])) for keep, give in parts]
    else:
        weight_grad = lax.psum_scatter(parts[0], "rows", scatter_dimension=0, tiled=True)
        weight_grad = weight_grad.reshape(width // n_rows, 3, local)

    out = None
    got = []
    for index, first in enumerate(range(0, row_dev, chunk)):
        after = steps[index // 2] if index // 2 < len(steps) else ()
        which, at = divmod(first, row_dev // 2)
        far = [
            (far_probs[i], far_dscore[i], far_qk[i][which], far_cot[i], far_natural[i])
            for i in range(len(fars))
        ]
        keep, give = far_input(first, at, chunk, lengths, own, far, after)
        got.append(flip(give, "heads", 1))
        out = finish(keep, got[-1], first, row_dev, out)
    if direct:
        weight_grad = jnp.swapaxes(last_sum(parts, local, got[-2:]), 0, 1)
    return (jnp.swapaxes(out, 1, 2), weight_grad)


def solution(mesh):
    in_specs = (
        P("rows", None, None),
        P(None, "heads"),
        P(None, "heads"),
        P(None, "heads"),
        P("rows", None, "heads"),
        P("rows"),
    )
    out_specs = (P("rows", None, "heads"), P("rows", None, "heads"))
    return jax.shard_map(body, mesh=mesh, in_specs=in_specs, out_specs=out_specs, check_vma=False)
```

```python
import functools
import math

import jax
import jax.numpy as jnp
from jax import lax
from jax.experimental import pallas as pl
from jax.experimental.pallas import tpu as pltpu
from jax.sharding import PartitionSpec as P

HEAD_DIM = 64
F32 = jnp.float32
BF16 = jnp.bfloat16
MIB = 1024 * 1024

NN = (((1,), (0,)), ((), ()))
NT = (((1,), (1,)), ((), ()))
TN = (((0,), (0,)), ((), ()))


def mm(a, b, dims):
    return lax.dot_general(a, b, dims, preferred_element_type=F32)


def flip(values, axis, bit):
    n = lax.axis_size(axis)
    return lax.ppermute(values, axis, [(s, s ^ bit) for s in range(n)])


def cost(flops, moved):
    return pl.CostEstimate(flops=int(flops), bytes_accessed=int(moved), transcendentals=0)


SMEM = pl.BlockSpec(memory_space=pltpu.SMEM)
VMEM = pl.BlockSpec(memory_space=pltpu.VMEM)
ANY = pl.BlockSpec(memory_space=pl.ANY)
HBM = pl.BlockSpec(memory_space=pltpu.HBM)


def like(shape, dtype=BF16):
    return jax.ShapeDtypeStruct(shape, dtype)


def place(a, stays):
    return pltpu.with_memory_space_constraint(a, pltpu.HBM) if stays else a


def in_vmem(kernel, name, out, *operands, scalars=0, streamed=0, after=(), scratch=(), limit=12, flops=0):
    many = len(after)

    def run(*refs):
        kernel(*refs[: len(operands)], *refs[len(operands) + many :])

    moved = 2 * sum(a.size for a in operands) + 2 * sum(o.size for o in out)
    held = len(operands) - scalars - streamed
    return pl.pallas_call(
        run,
        in_specs=[SMEM] * scalars + [HBM] * streamed + [VMEM] * held + [ANY] * many,
        out_specs=[VMEM] * len(out),
        out_shape=list(out),
        scratch_shapes=list(scratch),
        compiler_params=pltpu.CompilerParams(vmem_limit_bytes=limit * MIB),
        cost_estimate=cost(flops, moved),
        name=name,
    )(*[place(a, scalars <= i < scalars + streamed) for i, a in enumerate(operands)], *after)


def lane_mask(length, cols):
    return (lax.broadcasted_iota(jnp.int32, (1, cols), 1) < length).astype(F32)


def reorder(bits):
    return [sum(bit for b, bit in enumerate(bits) if t >> b & 1) for t in range(1 << len(bits))]


def put_shards(me, acc, bits, outs):
    for t, j in enumerate(reorder(bits)):
        out = outs[t % len(outs)]
        out[t // len(outs)] = acc[:, me ^ j].astype(out.dtype)


BLOCK = 4
STEP = 2
AHEAD = 4


def query_key_kernel(bits, where, sheet, wq, wk, qk, held, *rest):
    outs, (wt, acc, sems) = rest[:-3], rest[-3:]
    rows, cols, _ = sheet.shape
    local = wq.shape[0]
    heads = local // HEAD_DIM
    copies = [
        pltpu.make_async_copy(wq, wt.at[:local], sems.at[0]),
        pltpu.make_async_copy(wk, wt.at[local:], sems.at[1]),
    ]
    for first in range(0, rows, STEP):
        some = pl.ds(first, STEP)
        copies.append(pltpu.make_async_copy(sheet.at[some], held.at[some], sems.at[len(copies)]))
    for copy in copies[:AHEAD]:
        copy.start()
    copies[0].wait()
    copies[1].wait()
    flat = (BLOCK * HEAD_DIM, cols)
    for first in range(0, rows, BLOCK):
        for r in range(first, first + BLOCK):
            if r % STEP == 0:
                at = 2 + r // STEP
                copies[at].wait()
                for later in copies[at + AHEAD - 2 : at + AHEAD - 1]:
                    later.start()
            value = (mm(wt[...], held[r], NT) * lane_mask(where[2 + r], cols)).astype(BF16)
            qk[r] = value.reshape(2 * heads, HEAD_DIM, cols)
        some = pl.ds(first, BLOCK)
        for h in range(heads):
            term = mm(qk[some, h].reshape(flat), qk[some, heads + h].reshape(flat), TN)
            term = term.reshape(acc.shape[1:])
            acc[h] = term if first == 0 else acc[h] + term
    put_shards(where[0], acc, bits, outs)


def query_key(where, sheet, wq, wk, bits):
    rows, cols, width = sheet.shape
    shards = 1 << len(bits)
    local = wq.shape[0]
    heads = local // HEAD_DIM
    return in_vmem(
        functools.partial(query_key_kernel, bits),
        "query_key",
        [like((rows, 2 * heads, HEAD_DIM, cols)), like(sheet.shape)] + part_shapes(shards, heads, cols),
        where,
        sheet,
        wq,
        wk,
        scalars=1,
        streamed=3,
        scratch=(
            pltpu.VMEM((2 * local, width), BF16),
            pltpu.VMEM((heads, shards, cols // shards, cols), F32),
            pltpu.SemaphoreType.DMA((2 + rows // STEP,)),
        ),
        limit=14,
        flops=2 * rows * cols * local * (2 * width + cols),
    )


def value_kernel(bits, where, sheet, wv, cot, *rest):
    outs, acc = rest[:-1], rest[-1]
    rows, cols, _ = sheet.shape
    local = wv.shape[0]
    heads = local // HEAD_DIM
    flat = (BLOCK * HEAD_DIM, cols)
    for first in range(0, rows, BLOCK):
        values = []
        for r in range(first, first + BLOCK):
            value = (mm(wv[...], sheet[r], NT) * lane_mask(where[2 + r], cols)).astype(BF16)
            values.append(value.reshape(heads, HEAD_DIM, cols))
        for h in range(heads):
            left = cot[pl.ds(first, BLOCK), h * HEAD_DIM : (h + 1) * HEAD_DIM].reshape(flat)
            right = jnp.concatenate([v[h] for v in values], axis=0)
            term = mm(left, right, TN).reshape(acc.shape[1:])
            acc[h] = term if first == 0 else acc[h] + term
    put_shards(where[0], acc, bits, outs)


def value_dprob(where, sheet, wv, cot, after, bits):
    rows, cols, width = sheet.shape
    shards = 1 << len(bits)
    local = wv.shape[0]
    heads = local // HEAD_DIM
    return in_vmem(
        functools.partial(value_kernel, bits),
        "value_dprob",
        part_shapes(shards, heads, cols),
        where,
        sheet,
        wv,
        cot,
        scalars=1,
        after=after,
        scratch=(pltpu.VMEM((heads, shards, cols // shards, cols), F32),),
        limit=16,
        flops=4 * rows * cols * local * (width + cols),
    )


def turn_kernel(where, wq, wk, wv, natural, full):
    local = wq.shape[0]
    for index, weight in enumerate((wq, wk, wv)):
        full[:, :, index * local : (index + 1) * local] = weight[...].T.reshape(full.shape[:2] + (local,))
    for j in range(natural.shape[0]):
        natural[j] = full[where[1] ^ j]


def turn(where, wq, wk, wv, devices, after):
    local, width = wq.shape
    shape = (width // devices, 3 * local)
    return in_vmem(
        turn_kernel,
        "turn",
        (like((2,) + shape),),
        where,
        wq,
        wk,
        wv,
        scalars=1,
        after=after,
        scratch=(pltpu.VMEM((devices,) + shape, BF16),),
    )[0]


def far_query_key_kernel(first, where, sheet, wq, wk, qk):
    local, _ = wq.shape
    cols = sheet.shape[1]
    both = jnp.concatenate([wq[...], wk[...]], axis=0)
    for r in range(qk.shape[0]):
        value = (mm(both, sheet[first + r], NT) * lane_mask(where[2 + first + r], cols)).astype(BF16)
        qk[r] = value.reshape(2 * local // HEAD_DIM, HEAD_DIM, cols)


def far_query_key(first, count, where, sheet, wq, wk, after):
    _, cols, width = sheet.shape
    local = wq.shape[0]
    return in_vmem(
        functools.partial(far_query_key_kernel, first),
        "far_query_key",
        (like((count, 2 * local // HEAD_DIM, HEAD_DIM, cols)),),
        where,
        sheet,
        wq,
        wk,
        scalars=1,
        after=after,
        flops=4 * count * cols * local * width,
    )[0]


def part_shapes(shards, heads, cols):
    if shards == 1:
        return [like((1, heads, cols, cols), F32)]
    half = (shards // 2, heads, cols // shards, cols)
    return [like(half, F32), like(half)]


def add_split_kernel(keep, got, give_out, keep_out):
    for j in range(keep.shape[0]):
        total = keep[j].astype(F32) + got[j].astype(F32)
        out = give_out if j % 2 else keep_out
        out[j // 2] = total.astype(out.dtype)


def add_split(keep, got, after=()):
    half = (keep.shape[0] // 2,) + keep.shape[1:]
    return in_vmem(add_split_kernel, "add_split", (like(half), like(half, keep.dtype)), keep, got, after=after)


def halve(keep, give, axis, bits, after=()):
    after = list(after) + [()] * len(bits)
    for bit, waits in zip(bits[:-1], after):
        give, keep = add_split(keep, flip(give, axis, bit), waits)
    return keep, flip(give, axis, bits[-1])


def softmax_kernel(scale, *refs):
    *terms, probs_out, dscore_out = refs
    half = len(terms) // 2
    total = lambda some: functools.reduce(jnp.add, [t[0].astype(F32) for t in some])
    logits = total(terms[:half]) * scale
    dprob = total(terms[half:])
    shifted = jnp.exp(logits - jnp.max(logits, axis=-1, keepdims=True))
    probs = shifted / jnp.sum(shifted, axis=-1, keepdims=True)
    inner = jnp.sum(probs * dprob, axis=-1, keepdims=True)
    probs_out[0] = probs.astype(BF16)
    dscore_out[0] = (scale * probs * (dprob - inner)).astype(BF16)


def softmax_back(logits, dprob, scale, after=()):
    out = like(logits[0].shape)
    return in_vmem(
        functools.partial(softmax_kernel, scale), "softmax_back", (out, out), *logits, *dprob, limit=16, after=after
    )


def join_kernel(one, other, out):
    out[: one.shape[0]] = one[...]
    out[one.shape[0] :] = other[...]


def join(one, other, after):
    shape = (one.shape[0] + other.shape[0],) + one.shape[1:]
    return in_vmem(join_kernel, "join", (like(shape),), one, other, after=after)[0]


def double(values, axis, bits, after=()):
    order = [0]
    after = list(after) + [()] * len(bits)
    for bit, waits in zip(bits[:-1], after):
        values = join(values, flip(values, axis, bit), waits)
        order = order + [j ^ bit for j in order]
    other = flip(values, axis, bits[-1])
    return (values, other), (order, [j ^ bits[-1] for j in order])


def assemble_kernel(orders, where, *refs):
    pieces, outs = refs[:-2], refs[-2:]
    for piece, (kind, order) in zip(pieces, orders):
        for t, j in enumerate(order):
            outs[kind][where[0] ^ j] = piece[t]


def assemble(where, probs, dscore, orders, shards, after):
    out = like((shards,) + probs[0].shape[1:])
    return in_vmem(
        functools.partial(assemble_kernel, [(k, o) for k, both in enumerate(orders) for o in both]), "assemble", (out, out), where, *probs, *dscore, scalars=1, after=after
    )


def gradients(where, first, count, probs, dscore, qk, cot, grads):
    cols = qk.shape[-1]
    heads = qk.shape[1] // 2
    rows = pl.ds(first, count)
    flat = (count * HEAD_DIM, cols)
    split = (count, HEAD_DIM, cols)
    masks = jnp.stack([lane_mask(where[2 + first + r], cols) for r in range(count)])
    for h in range(heads):
        p, ds = [ref[:, h].reshape(cols, cols) for ref in (probs, dscore)]
        g = cot[rows, h * HEAD_DIM : (h + 1) * HEAD_DIM].reshape(flat)
        dq = mm(qk[rows, heads + h].reshape(flat), ds, NT)
        dk = mm(qk[rows, h].reshape(flat), ds, NN)
        dv = mm(g, p, NN)
        for index, value in enumerate((dq, dk, dv)):
            grads[:, index * heads + h] = (value.reshape(split) * masks).astype(BF16)


def own_gradients_kernel(where, probs, dscore, qk, cot, grads):
    gradients(where, 0, qk.shape[0], probs, dscore, qk, cot, grads)


def own_gradients(where, probs, dscore, qk, cot):
    rows, two, _, cols = qk.shape
    return in_vmem(
        own_gradients_kernel,
        "own_gradients",
        (like((rows, two // 2 * 3, HEAD_DIM, cols)),),
        where,
        probs,
        dscore,
        qk,
        cot,
        scalars=1,
        limit=14,
        flops=3 * rows * two * HEAD_DIM * cols * cols,
    )[0]


def own_input_kernel(grads, weights, out):
    near, share, columns = weights.shape
    left = weights[...].reshape(near * share, columns)
    for r in range(grads.shape[0]):
        part = mm(left, grads[r].reshape(columns, grads.shape[-1]), NN).astype(BF16)
        out[:, r] = part.reshape(near, share, grads.shape[-1])


def own_input(grads, weights, after):
    rows, cols = grads.shape[0], grads.shape[-1]
    near, share, columns = weights.shape
    return in_vmem(
        own_input_kernel,
        "own_input",
        (like((near, rows, share, cols)),),
        grads,
        weights,
        after=after,
        flops=2 * rows * cols * near * share * columns,
    )[0]


def far_input_kernel(first, where, own, *refs):
    *refs, keep, give, grads = refs
    count, share, cols = keep.shape
    total = [own[:, first + r].astype(F32) for r in range(count)]
    for i in range(0, len(refs), 5):
        probs, dscore, qk, cot, weights = refs[i : i + 5]
        gradients(where, first, count, probs, dscore, qk, cot, grads)
        near, _, columns = weights.shape
        left = weights[...].reshape(near * share, columns)
        for r in range(count):
            part = mm(left, grads[r].reshape(columns, cols), NN).astype(BF16)
            total[r] = total[r] + part.reshape(near, share, cols).astype(F32)
    for r in range(count):
        keep[r] = total[r][0].astype(keep.dtype)
        give[r] = total[r][1].astype(give.dtype)


def far_input(first, count, where, own, far, after):
    _, rows, share, cols = own.shape
    columns = far[0][-1].shape[-1]
    out = like((count, share, cols))
    return in_vmem(
        functools.partial(far_input_kernel, first),
        "far_input",
        (out, out),
        where,
        own,
        *[a for one in far for a in one],
        scalars=1,
        after=after,
        scratch=(pltpu.VMEM((count, columns // HEAD_DIM, HEAD_DIM, cols), BF16),),
        limit=16,
        flops=2 * len(far) * count * cols * columns * (cols + 2 * share),
    )


def finish_kernel(keep, got, *rest):
    out = rest[-1]
    out[...] = (keep[...].astype(F32) + got[...].astype(F32)).astype(BF16)


def finish(keep, got, first, total_rows, before, after):
    count, share, cols = keep.shape
    block = math.gcd(first, count) if first else count
    spec = pl.BlockSpec((block, share, cols), lambda s: (s, 0, 0))
    extra = ([] if before is None else [before]) + after
    return pl.pallas_call(
        finish_kernel,
        grid=(count // block,),
        in_specs=[spec, spec] + [ANY] * len(extra),
        out_specs=pl.BlockSpec((block, share, cols), lambda s: (first // block + s, 0, 0)),
        out_shape=like((total_rows, share, cols)),
        input_output_aliases={} if before is None else {2: 0},
        compiler_params=pltpu.CompilerParams(vmem_limit_bytes=12 * MIB),
        cost_estimate=cost(keep.size, keep.size * 6),
        name="finish",
    )(keep, got, *extra)


def weight_product(sheet, grads):
    rows, cols, width = sheet.shape
    columns = grads.shape[1] * HEAD_DIM
    left = [grads[r].reshape(columns, cols) for r in range(rows)]
    return mm(jnp.concatenate(left, axis=1), sheet[...].reshape(rows * cols, width), NN).T


def weight_kernel(where, sheet, grads, *rest):
    outs, full = rest[:-1], rest[-1]
    full[...] = weight_product(sheet, grads).reshape(full.shape)
    for j in range(full.shape[0]):
        first = 0
        for keep, give in zip(outs[::2], outs[1::2]):
            out = (keep, give)[j % 2]
            last = first + out.shape[-1]
            out[j // 2] = full[where[0] ^ j, :, first:last].astype(out.dtype)
            first = last


def whole_weight_kernel(where, sheet, grads, out):
    out[...] = weight_product(sheet, grads)


def weight_part(where, sheet, grads, cuts, shards):
    rows, cols, width = sheet.shape
    columns = grads.shape[1] * HEAD_DIM
    if shards == 1:
        kernel, outs, scratch = whole_weight_kernel, [like((width, columns), F32)], ()
    else:
        halves = [(shards // 2, width // shards, cut) for cut in cuts]
        kernel = weight_kernel
        outs = [o for half in halves for o in (like(half, F32), like(half))]
        scratch = (pltpu.VMEM((shards, width // shards, columns), F32),)
    return in_vmem(
        kernel,
        "weight_part",
        outs,
        where,
        sheet,
        grads,
        scalars=1,
        scratch=scratch,
        limit=18,
        flops=2 * rows * cols * width * columns,
    )


def last_kernel(*refs):
    *terms, out = refs
    total = [terms[i][0] + terms[i + 1][0].astype(F32) for i in range(0, len(terms), 2)]
    total = jnp.concatenate(total, axis=-1)
    local = out.shape[-1]
    for index in range(out.shape[0]):
        out[index] = total[:, index * local : (index + 1) * local]


def last_sum(halves, local, after):
    terms = [a for half in halves for a in half]
    columns = sum(keep.shape[2] for keep, _ in halves)
    shape = (columns // local, terms[0].shape[1], local)
    return in_vmem(last_kernel, "last_sum", (like(shape, F32),), *terms, after=after)[0]


def body(sheet, w_query, w_key, w_value, cotangent, lengths):
    row_dev, cols, width = sheet.shape
    local = w_query.shape[1]
    n_rows = lax.axis_size("rows")
    n_heads = lax.axis_size("heads")
    scale = float(1.0 / (HEAD_DIM * row_dev * n_rows) ** 0.5)
    direct = n_rows <= 8
    shards = n_rows if direct else 1
    row_bits = [1 << b for b in range(n_rows.bit_length() - 1)]
    chunk = row_dev // 4

    me = jnp.stack([lax.axis_index("rows"), lax.axis_index("heads")]).astype(jnp.int32)
    where = jnp.concatenate([me, lengths])
    wq, wk, wv = w_query.T, w_key.T, w_value.T
    cot = jnp.swapaxes(cotangent, 1, 2)

    fars = range(2, n_heads, 2)
    far_cot = [flip(cot, "heads", f) for f in fars]
    far_weights = [[flip(w, "heads", f) for w in (wq, wk, wv)] for f in fars]
    fq, fk, fv = [[w[i] for w in far_weights] for i in range(3)]

    up = row_bits if direct else []
    turn_about = up[1:] + up[:1]
    qk, held, *logits = query_key(where, sheet, wq, wk, turn_about)
    dprob = value_dprob(where, held, wv, cot, logits[-1:], up)
    weights = turn(where, wq, wk, wv, n_heads, dprob[-1:])
    if direct:
        logits = halve(*logits, "rows", turn_about)
        dprob = halve(*dprob, "rows", up)
        probs_own, dscore_own = softmax_back(logits, dprob, scale, [weights])
        probs, probs_order = double(probs_own, "rows", up[::-1], [far_cot])
        dscore, dscore_order = double(dscore_own, "rows", turn_about[::-1], [far_cot])
        probs, dscore = assemble(where, probs, dscore, (probs_order, dscore_order), shards, fq + fk + fv)
    else:
        logits, dprob = lax.psum((logits, dprob), "rows")
        probs, dscore = softmax_back(logits, dprob, scale)
    far_dscore = [flip(dscore, "heads", f) for f in fars]
    far_probs = [flip(probs, "heads", f) for f in fars]

    grads = own_gradients(where, probs, dscore, qk, cot)
    cut = 3 * local // 256 * 128
    cuts = (cut, 3 * local - cut)
    parts = weight_part(where, held, grads, cuts, shards)
    ready = [parts[-1]]
    far_qk, far_natural = [], []
    for w in far_weights:
        far_qk.append(far_query_key(0, row_dev, where, held, w[0], w[1], ready))
        far_natural.append(turn(where, *w, n_heads, ready))
    own = own_input(grads, weights, ready)
    ready = [own] + far_qk + far_natural + far_probs
    steps = []
    if direct:
        parts = [tuple(parts[:2]), tuple(parts[2:])]
        for bit in row_bits[:-1]:
            parts = [add_split(keep, flip(give, "rows", bit), ready)[::-1] for keep, give in parts]
            steps.append([keep for keep, _ in parts])
            ready = ()
        parts = [(keep, flip(give, "rows", row_bits[-1])) for keep, give in parts]
    else:
        weight_grad = lax.psum_scatter(parts[0], "rows", scatter_dimension=0, tiled=True)
        weight_grad = weight_grad.reshape(width // n_rows, 3, local)

    sums = []
    if direct:
        weight_grad = last_sum(parts, local, ())
        sums = [weight_grad]
        weight_grad = jnp.swapaxes(weight_grad, 0, 1)
    out = None
    for index, first in enumerate(range(0, row_dev, chunk)):
        after = steps[index // 2] if index // 2 < len(steps) else ()
        far = list(zip(far_probs, far_dscore, far_qk, far_cot, far_natural))
        keep, give = far_input(first, chunk, where, own, far, after)
        got = flip(give, "heads", 1)
        out = finish(keep, got, first, row_dev, out, sums if index == 2 else [])
    return (jnp.swapaxes(out, 1, 2), weight_grad)


def solution(mesh):
    in_specs = (
        P("rows", None, None),
        P(None, "heads"),
        P(None, "heads"),
        P(None, "heads"),
        P("rows", None, "heads"),
        P("rows"),
    )
    out_specs = (P("rows", None, "heads"), P("rows", None, "heads"))
    return jax.shard_map(body, mesh=mesh, in_specs=in_specs, out_specs=out_specs, check_vma=False)
```

```python
import functools
import math

import jax
import jax.numpy as jnp
from jax import lax
from jax.experimental import pallas as pl
from jax.experimental.pallas import tpu as pltpu
from jax.sharding import PartitionSpec as P

HEAD_DIM = 64
F32 = jnp.float32
BF16 = jnp.bfloat16
MIB = 1024 * 1024

NN = (((1,), (0,)), ((), ()))
NT = (((1,), (1,)), ((), ()))
TN = (((0,), (0,)), ((), ()))


def mm(a, b, dims):
    return lax.dot_general(a, b, dims, preferred_element_type=F32)


def flip(values, axis, bit):
    n = lax.axis_size(axis)
    return lax.ppermute(values, axis, [(s, s ^ bit) for s in range(n)])


def cost(flops, moved):
    return pl.CostEstimate(flops=int(flops), bytes_accessed=int(moved), transcendentals=0)


SMEM = pl.BlockSpec(memory_space=pltpu.SMEM)
VMEM = pl.BlockSpec(memory_space=pltpu.VMEM)
ANY = pl.BlockSpec(memory_space=pl.ANY)
HBM = pl.BlockSpec(memory_space=pltpu.HBM)


def like(shape, dtype=BF16):
    return jax.ShapeDtypeStruct(shape, dtype)


def place(a, stays):
    return pltpu.with_memory_space_constraint(a, pltpu.HBM) if stays else a


def in_vmem(kernel, name, out, *operands, scalars=0, streamed=0, after=(), scratch=(), limit=12, flops=0):
    many = len(after)

    def run(*refs):
        kernel(*refs[: len(operands)], *refs[len(operands) + many :])

    moved = 2 * sum(a.size for a in operands) + 2 * sum(o.size for o in out)
    held = len(operands) - scalars - streamed
    return pl.pallas_call(
        run,
        in_specs=[SMEM] * scalars + [HBM] * streamed + [VMEM] * held + [ANY] * many,
        out_specs=[VMEM] * len(out),
        out_shape=list(out),
        scratch_shapes=list(scratch),
        compiler_params=pltpu.CompilerParams(vmem_limit_bytes=limit * MIB),
        cost_estimate=cost(flops, moved),
        name=name,
    )(*[place(a, scalars <= i < scalars + streamed) for i, a in enumerate(operands)], *after)


def lane_mask(length, cols):
    return (lax.broadcasted_iota(jnp.int32, (1, cols), 1) < length).astype(F32)


def reorder(bits):
    return [sum(bit for b, bit in enumerate(bits) if t >> b & 1) for t in range(1 << len(bits))]


def put_shards(me, acc, bits, outs):
    for t, j in enumerate(reorder(bits)):
        out = outs[t % len(outs)]
        out[t // len(outs)] = acc[:, me ^ j].astype(out.dtype)


BLOCK = 4
STEP = 2
AHEAD = 4


def query_key_kernel(bits, where, sheet, wq, wk, qk, held, *rest):
    outs, (wt, acc, sems) = rest[:-3], rest[-3:]
    rows, cols, _ = sheet.shape
    local = wq.shape[0]
    heads = local // HEAD_DIM
    copies = [
        pltpu.make_async_copy(wq, wt.at[:local], sems.at[0]),
        pltpu.make_async_copy(wk, wt.at[local:], sems.at[1]),
    ]
    for first in range(0, rows, STEP):
        some = pl.ds(first, STEP)
        copies.append(pltpu.make_async_copy(sheet.at[some], held.at[some], sems.at[len(copies)]))
    for copy in copies[:AHEAD]:
        copy.start()
    copies[0].wait()
    copies[1].wait()
    flat = (BLOCK * HEAD_DIM, cols)
    for first in range(0, rows, BLOCK):
        for r in range(first, first + BLOCK):
            if r % STEP == 0:
                at = 2 + r // STEP
                copies[at].wait()
                for later in copies[at + AHEAD - 2 : at + AHEAD - 1]:
                    later.start()
            value = (mm(wt[...], held[r], NT) * lane_mask(where[2 + r], cols)).astype(BF16)
            qk[r] = value.reshape(2 * heads, HEAD_DIM, cols)
        some = pl.ds(first, BLOCK)
        for h in range(heads):
            term = mm(qk[some, h].reshape(flat), qk[some, heads + h].reshape(flat), TN)
            term = term.reshape(acc.shape[1:])
            acc[h] = term if first == 0 else acc[h] + term
    put_shards(where[0], acc, bits, outs)


def query_key(where, sheet, wq, wk, bits):
    rows, cols, width = sheet.shape
    shards = 1 << len(bits)
    local = wq.shape[0]
    heads = local // HEAD_DIM
    return in_vmem(
        functools.partial(query_key_kernel, bits),
        "query_key",
        [like((rows, 2 * heads, HEAD_DIM, cols)), like(sheet.shape)] + part_shapes(shards, heads, cols),
        where,
        sheet,
        wq,
        wk,
        scalars=1,
        streamed=3,
        scratch=(
            pltpu.VMEM((2 * local, width), BF16),
            pltpu.VMEM((heads, shards, cols // shards, cols), F32),
            pltpu.SemaphoreType.DMA((2 + rows // STEP,)),
        ),
        limit=14,
        flops=2 * rows * cols * local * (2 * width + cols),
    )


def value_kernel(bits, fars, where, sheet, wv, cot, *rest):
    outs, halves, acc = rest[: -1 - len(fars)], rest[-1 - len(fars) : -1], rest[-1]
    rows, cols, width = sheet.shape
    local = wv.shape[0]
    heads = local // HEAD_DIM
    for far, half in zip(fars, halves):
        near = half.shape[1]
        side = lax.shift_right_logical(where[1], 1) ^ (far // 2)
        for s in range(width // near):
            @pl.when(side == s)
            def _():
                half[...] = wv[:, s * near : (s + 1) * near]
    flat = (BLOCK * HEAD_DIM, cols)
    for first in range(0, rows, BLOCK):
        values = []
        for r in range(first, first + BLOCK):
            value = (mm(wv[...], sheet[r], NT) * lane_mask(where[2 + r], cols)).astype(BF16)
            values.append(value.reshape(heads, HEAD_DIM, cols))
        for h in range(heads):
            left = cot[pl.ds(first, BLOCK), h * HEAD_DIM : (h + 1) * HEAD_DIM].reshape(flat)
            right = jnp.concatenate([v[h] for v in values], axis=0)
            term = mm(left, right, TN).reshape(acc.shape[1:])
            acc[h] = term if first == 0 else acc[h] + term
    put_shards(where[0], acc, bits, outs)


def value_dprob(where, sheet, wv, cot, after, bits, fars, devices):
    rows, cols, width = sheet.shape
    shards = 1 << len(bits)
    local = wv.shape[0]
    heads = local // HEAD_DIM
    return in_vmem(
        functools.partial(value_kernel, bits, fars),
        "value_dprob",
        part_shapes(shards, heads, cols) + [like((local, 2 * width // devices))] * len(fars),
        where,
        sheet,
        wv,
        cot,
        scalars=1,
        after=after,
        scratch=(pltpu.VMEM((heads, shards, cols // shards, cols), F32),),
        limit=16,
        flops=4 * rows * cols * local * (width + cols),
    )


def turn_kernel(where, wq, wk, wv, natural, *full):
    near, share, columns = natural.shape
    local = wq.shape[0]
    for index, (weight, held) in enumerate(zip((wq, wk, wv), full)):
        held[...] = weight[...].T.reshape(held.shape)
        mine = where[1] & (held.shape[0] - 1)
        for j in range(near):
            natural[j, :, index * local : (index + 1) * local] = held[mine ^ j]


def turn(where, wq, wk, wv, devices, after):
    local, width = wq.shape
    share = width // devices
    return in_vmem(
        turn_kernel,
        "turn",
        (like((2, share, 3 * local)),),
        where,
        wq,
        wk,
        wv,
        scalars=1,
        after=after,
        scratch=[pltpu.VMEM((w.shape[1] // share, share, local), BF16) for w in (wq, wk, wv)],
    )[0]


def far_query_key_kernel(first, where, sheet, wq, wk, qk):
    local, _ = wq.shape
    cols = sheet.shape[1]
    both = jnp.concatenate([wq[...], wk[...]], axis=0)
    for r in range(qk.shape[0]):
        value = (mm(both, sheet[first + r], NT) * lane_mask(where[2 + first + r], cols)).astype(BF16)
        qk[r] = value.reshape(2 * local // HEAD_DIM, HEAD_DIM, cols)


def far_query_key(first, count, where, sheet, wq, wk, after):
    _, cols, width = sheet.shape
    local = wq.shape[0]
    return in_vmem(
        functools.partial(far_query_key_kernel, first),
        "far_query_key",
        (like((count, 2 * local // HEAD_DIM, HEAD_DIM, cols)),),
        where,
        sheet,
        wq,
        wk,
        scalars=1,
        after=after,
        flops=4 * count * cols * local * width,
    )[0]


def part_shapes(shards, heads, cols):
    if shards == 1:
        return [like((1, heads, cols, cols), F32)]
    half = (shards // 2, heads, cols // shards, cols)
    return [like(half, F32), like(half)]


def add_split_kernel(keep, got, give_out, keep_out):
    for j in range(keep.shape[0]):
        total = keep[j].astype(F32) + got[j].astype(F32)
        out = give_out if j % 2 else keep_out
        out[j // 2] = total.astype(out.dtype)


def add_split(keep, got, after=()):
    half = (keep.shape[0] // 2,) + keep.shape[1:]
    return in_vmem(add_split_kernel, "add_split", (like(half), like(half, keep.dtype)), keep, got, after=after)


def halve(keep, give, axis, bits, after=()):
    after = list(after) + [()] * len(bits)
    for bit, waits in zip(bits[:-1], after):
        give, keep = add_split(keep, flip(give, axis, bit), waits)
    return keep, flip(give, axis, bits[-1])


def softmax_kernel(scale, *refs):
    *terms, probs_out, dscore_out = refs
    half = len(terms) // 2
    total = lambda some: functools.reduce(jnp.add, [t[0].astype(F32) for t in some])
    logits = total(terms[:half]) * scale
    dprob = total(terms[half:])
    shifted = jnp.exp(logits - jnp.max(logits, axis=-1, keepdims=True))
    probs = shifted / jnp.sum(shifted, axis=-1, keepdims=True)
    inner = jnp.sum(probs * dprob, axis=-1, keepdims=True)
    probs_out[0] = probs.astype(BF16)
    dscore_out[0] = (scale * probs * (dprob - inner)).astype(BF16)


def softmax_back(logits, dprob, scale, after=()):
    out = like(logits[0].shape)
    return in_vmem(
        functools.partial(softmax_kernel, scale), "softmax_back", (out, out), *logits, *dprob, limit=16, after=after
    )


def join_kernel(one, other, out):
    out[: one.shape[0]] = one[...]
    out[one.shape[0] :] = other[...]


def join(one, other, after):
    shape = (one.shape[0] + other.shape[0],) + one.shape[1:]
    return in_vmem(join_kernel, "join", (like(shape),), one, other, after=after)[0]


def double(values, axis, bits, after=()):
    order = [0]
    after = list(after) + [()] * len(bits)
    for bit, waits in zip(bits[:-1], after):
        values = join(values, flip(values, axis, bit), waits)
        order = order + [j ^ bit for j in order]
    other = flip(values, axis, bits[-1])
    return (values, other), (order, [j ^ bits[-1] for j in order])


def assemble_kernel(orders, where, *refs):
    pieces, outs = refs[:-2], refs[-2:]
    for piece, (kind, order) in zip(pieces, orders):
        for t, j in enumerate(order):
            outs[kind][where[0] ^ j] = piece[t]


def assemble(where, probs, dscore, orders, shards, after):
    out = like((shards,) + probs[0].shape[1:])
    return in_vmem(
        functools.partial(assemble_kernel, [(k, o) for k, both in enumerate(orders) for o in both]), "assemble", (out, out), where, *probs, *dscore, scalars=1, after=after
    )


def gradients(where, first, count, probs, dscore, qk, cot, grads):
    cols = qk.shape[-1]
    heads = qk.shape[1] // 2
    rows = pl.ds(first, count)
    flat = (count * HEAD_DIM, cols)
    split = (count, HEAD_DIM, cols)
    masks = jnp.stack([lane_mask(where[2 + first + r], cols) for r in range(count)])
    for h in range(heads):
        p, ds = [ref[:, h].reshape(cols, cols) for ref in (probs, dscore)]
        g = cot[rows, h * HEAD_DIM : (h + 1) * HEAD_DIM].reshape(flat)
        dq = mm(qk[rows, heads + h].reshape(flat), ds, NT)
        dk = mm(qk[rows, h].reshape(flat), ds, NN)
        dv = mm(g, p, NN)
        for index, value in enumerate((dq, dk, dv)):
            grads[:, index * heads + h] = (value.reshape(split) * masks).astype(BF16)


def gradients_kernel(where, probs, dscore, qk, cot, grads):
    gradients(where, 0, qk.shape[0], probs, dscore, qk, cot, grads)


def all_gradients(where, probs, dscore, qk, cot, name, after):
    rows, two, _, cols = qk.shape
    return in_vmem(
        gradients_kernel,
        name,
        (like((rows, two // 2 * 3, HEAD_DIM, cols)),),
        where,
        probs,
        dscore,
        qk,
        cot,
        scalars=1,
        after=after,
        limit=14,
        flops=3 * rows * two * HEAD_DIM * cols * cols,
    )[0]


def own_input_kernel(grads, weights, out):
    near, share, columns = weights.shape
    left = weights[...].reshape(near * share, columns)
    for r in range(grads.shape[0]):
        part = mm(left, grads[r].reshape(columns, grads.shape[-1]), NN).astype(BF16)
        out[:, r] = part.reshape(near, share, grads.shape[-1])


def own_input(grads, weights, after):
    rows, cols = grads.shape[0], grads.shape[-1]
    near, share, columns = weights.shape
    return in_vmem(
        own_input_kernel,
        "own_input",
        (like((near, rows, share, cols)),),
        grads,
        weights,
        after=after,
        flops=2 * rows * cols * near * share * columns,
    )[0]


def far_input_kernel(first, own, *refs):
    *refs, keep, give = refs
    count, share, cols = keep.shape
    for r in range(count):
        total = own[:, first + r].astype(F32)
        for i in range(0, len(refs), 2):
            grads, weights = refs[i : i + 2]
            near, _, columns = weights.shape
            left = weights[...].reshape(near * share, columns)
            part = mm(left, grads[first + r].reshape(columns, cols), NN).astype(BF16)
            total = total + part.reshape(near, share, cols).astype(F32)
        keep[r] = total[0].astype(keep.dtype)
        give[r] = total[1].astype(give.dtype)


def far_input(first, count, own, far, after):
    _, rows, share, cols = own.shape
    columns = far[0][1].shape[-1]
    out = like((count, share, cols))
    return in_vmem(
        functools.partial(far_input_kernel, first),
        "far_input",
        (out, out),
        own,
        *[a for one in far for a in one],
        after=after,
        limit=14,
        flops=4 * len(far) * count * cols * columns * share,
    )


def finish_kernel(*refs):
    *terms, out, total, sems = refs
    copies = []
    first = 0
    for index in range(0, len(terms), 2):
        keep, got = terms[index : index + 2]
        some = pl.ds(first, keep.shape[0])
        total[some] = (keep[...].astype(F32) + got[...].astype(F32)).astype(BF16)
        copies.append(pltpu.make_async_copy(total.at[some], out.at[some], sems.at[index // 2]))
        copies[-1].start()
        first += keep.shape[0]
    for copy in copies:
        copy.wait()


def finish(chunks):
    _, share, cols = chunks[0][0].shape
    rows = sum(keep.shape[0] for keep, _ in chunks)
    terms = [a for chunk in chunks for a in chunk]
    return pl.pallas_call(
        finish_kernel,
        in_specs=[VMEM] * len(terms),
        out_specs=HBM,
        out_shape=like((rows, share, cols)),
        scratch_shapes=[pltpu.VMEM((rows, share, cols), BF16), pltpu.SemaphoreType.DMA((len(chunks),))],
        compiler_params=pltpu.CompilerParams(vmem_limit_bytes=12 * MIB),
        cost_estimate=cost(rows * share * cols, 6 * rows * share * cols),
        name="finish",
    )(*terms)


def weight_product(sheet, grads):
    rows, cols, width = sheet.shape
    columns = grads.shape[1] * HEAD_DIM
    left = [grads[r].reshape(columns, cols) for r in range(rows)]
    return mm(jnp.concatenate(left, axis=1), sheet[...].reshape(rows * cols, width), NN).T


def weight_kernel(where, sheet, grads, *rest):
    outs, full = rest[:-1], rest[-1]
    full[...] = weight_product(sheet, grads).reshape(full.shape)
    for j in range(full.shape[0]):
        first = 0
        for keep, give in zip(outs[::2], outs[1::2]):
            out = (keep, give)[j % 2]
            last = first + out.shape[-1]
            out[j // 2] = full[where[0] ^ j, :, first:last].astype(out.dtype)
            first = last


def whole_weight_kernel(where, sheet, grads, out):
    out[...] = weight_product(sheet, grads)


def weight_part(where, sheet, grads, cuts, shards):
    rows, cols, width = sheet.shape
    columns = grads.shape[1] * HEAD_DIM
    if shards == 1:
        kernel, outs, scratch = whole_weight_kernel, [like((width, columns), F32)], ()
    else:
        halves = [(shards // 2, width // shards, cut) for cut in cuts]
        kernel = weight_kernel
        outs = [o for half in halves for o in (like(half, F32), like(half))]
        scratch = (pltpu.VMEM((shards, width // shards, columns), F32),)
    return in_vmem(
        kernel,
        "weight_part",
        outs,
        where,
        sheet,
        grads,
        scalars=1,
        scratch=scratch,
        limit=18,
        flops=2 * rows * cols * width * columns,
    )


def last_kernel(*refs):
    *terms, out = refs
    total = [terms[i][0] + terms[i + 1][0].astype(F32) for i in range(0, len(terms), 2)]
    total = jnp.concatenate(total, axis=-1)
    local = out.shape[-1]
    for index in range(out.shape[0]):
        out[index] = total[:, index * local : (index + 1) * local]


def last_sum(halves, local, after):
    terms = [a for half in halves for a in half]
    columns = sum(keep.shape[2] for keep, _ in halves)
    shape = (columns // local, terms[0].shape[1], local)
    return in_vmem(last_kernel, "last_sum", (like(shape, F32),), *terms, after=after)[0]


def body(sheet, w_query, w_key, w_value, cotangent, lengths):
    row_dev, cols, width = sheet.shape
    local = w_query.shape[1]
    n_rows = lax.axis_size("rows")
    n_heads = lax.axis_size("heads")
    scale = float(1.0 / (HEAD_DIM * row_dev * n_rows) ** 0.5)
    direct = n_rows <= 8
    shards = n_rows if direct else 1
    row_bits = [1 << b for b in range(n_rows.bit_length() - 1)]
    chunk = row_dev // 4

    me = jnp.stack([lax.axis_index("rows"), lax.axis_index("heads")]).astype(jnp.int32)
    where = jnp.concatenate([me, lengths])
    wq, wk, wv = w_query.T, w_key.T, w_value.T
    cot = jnp.swapaxes(cotangent, 1, 2)

    fars = range(2, n_heads, 2)
    far_cot = [flip(cot, "heads", f) for f in fars]
    fq, fk = [[flip(w, "heads", f) for f in fars] for w in (wq, wk)]

    up = row_bits if direct else []
    turn_about = up[1:] + up[:1]
    qk, held, *logits = query_key(where, sheet, wq, wk, turn_about)
    *dprob, = value_dprob(where, held, wv, cot, logits[-1:], up, fars, n_heads)
    dprob, halves = dprob[: -len(fars)], dprob[-len(fars) :]
    fv = [flip(half, "heads", f) for half, f in zip(halves, fars)]
    weights = turn(where, wq, wk, wv, n_heads, dprob[-1:])
    if direct:
        logits = halve(*logits, "rows", turn_about)
        dprob = halve(*dprob, "rows", up)
        probs_own, dscore_own = softmax_back(logits, dprob, scale, [weights])
        probs, probs_order = double(probs_own, "rows", up[::-1], [far_cot])
        dscore, dscore_order = double(dscore_own, "rows", turn_about[::-1], [far_cot])
        probs, dscore = assemble(where, probs, dscore, (probs_order, dscore_order), shards, fq + fk + fv)
    else:
        logits, dprob = lax.psum((logits, dprob), "rows")
        probs, dscore = softmax_back(logits, dprob, scale)
    far_dscore = [flip(dscore, "heads", f) for f in fars]
    far_probs = [flip(probs, "heads", f) for f in fars]

    grads = all_gradients(where, probs, dscore, qk, cot, "own_gradients", ())
    parts = weight_part(where, held, grads, (3 * local,), shards)
    ready = [parts[-1]]
    far_qk, far_natural = [], []
    for w in zip(fq, fk, fv):
        far_qk.append(far_query_key(0, row_dev, where, held, w[0], w[1], ready))
        far_natural.append(turn(where, *w, n_heads, ready))
    own = own_input(grads, weights, ready)
    ready = [own] + far_qk + far_natural + far_probs + far_dscore
    steps = [[], []]
    if direct:
        keep, give = parts
        steps = []
        for bit in row_bits[:-1]:
            give, keep = add_split(keep, flip(give, "rows", bit), ready)
            steps.append([keep])
            ready = ()
        sums = last_sum([(keep, flip(give, "rows", row_bits[-1]))], local, ())
        weight_grad = jnp.swapaxes(sums, 0, 1)
    else:
        weight_grad = lax.psum_scatter(parts[0], "rows", scatter_dimension=0, tiled=True)
        weight_grad = weight_grad.reshape(width // n_rows, 3, local)

    far_grads = [
        all_gradients(where, *args, "far_gradients", steps[0])
        for args in zip(far_probs, far_dscore, far_qk, far_cot)
    ]
    chunks = []
    for index, first in enumerate(range(0, row_dev, chunk)):
        after = steps[-1] if index >= 2 else ()
        keep, give = far_input(first, chunk, own, list(zip(far_grads, far_natural)), after)
        chunks.append((keep, flip(give, "heads", 1)))
    return (jnp.swapaxes(finish(chunks), 1, 2), weight_grad)


def solution(mesh):
    in_specs = (
        P("rows", None, None),
        P(None, "heads"),
        P(None, "heads"),
        P(None, "heads"),
        P("rows", None, "heads"),
        P("rows"),
    )
    out_specs = (P("rows", None, "heads"), P("rows", None, "heads"))
    return jax.shard_map(body, mesh=mesh, in_specs=in_specs, out_specs=out_specs, check_vma=False)
```

```python
import functools
import math

import jax
import jax.numpy as jnp
from jax import lax
from jax.experimental import pallas as pl
from jax.experimental.pallas import tpu as pltpu
from jax.sharding import PartitionSpec as P

HEAD_DIM = 64
F32 = jnp.float32
BF16 = jnp.bfloat16
MIB = 1024 * 1024

NN = (((1,), (0,)), ((), ()))
NT = (((1,), (1,)), ((), ()))
TN = (((0,), (0,)), ((), ()))


def mm(a, b, dims):
    return lax.dot_general(a, b, dims, preferred_element_type=F32)


def flip(values, axis, bit):
    n = lax.axis_size(axis)
    return lax.ppermute(values, axis, [(s, s ^ bit) for s in range(n)])


def cost(flops, moved):
    return pl.CostEstimate(flops=int(flops), bytes_accessed=int(moved), transcendentals=0)


SMEM = pl.BlockSpec(memory_space=pltpu.SMEM)
VMEM = pl.BlockSpec(memory_space=pltpu.VMEM)
ANY = pl.BlockSpec(memory_space=pl.ANY)
HBM = pl.BlockSpec(memory_space=pltpu.HBM)


def like(shape, dtype=BF16):
    return jax.ShapeDtypeStruct(shape, dtype)


def place(a, stays):
    return pltpu.with_memory_space_constraint(a, pltpu.HBM) if stays else a


def in_vmem(kernel, name, out, *operands, scalars=0, streamed=0, after=(), scratch=(), limit=12, flops=0, hidden=True):
    many = len(after)

    def run(*refs):
        kernel(*refs[: len(operands)], *refs[len(operands) + many :])

    moved = 2 * sum(a.size for a in operands) + 2 * sum(o.size for o in out)
    held = len(operands) - scalars - streamed
    return pl.pallas_call(
        run,
        in_specs=[SMEM] * scalars + [HBM] * streamed + [VMEM] * held + [ANY] * many,
        out_specs=[VMEM] * len(out),
        out_shape=list(out),
        scratch_shapes=list(scratch),
        compiler_params=pltpu.CompilerParams(vmem_limit_bytes=limit * MIB),
        cost_estimate=cost(flops, moved) if hidden else cost(0, 0),
        name=name,
    )(*[place(a, scalars <= i < scalars + streamed) for i, a in enumerate(operands)], *after)


def lane_mask(length, cols):
    return (lax.broadcasted_iota(jnp.int32, (1, cols), 1) < length).astype(F32)


def reorder(bits):
    return [sum(bit for b, bit in enumerate(bits) if t >> b & 1) for t in range(1 << len(bits))]


def put_shards(me, acc, bits, outs):
    for t, j in enumerate(reorder(bits)):
        out = outs[t % len(outs)]
        out[t // len(outs)] = acc[:, me ^ j].astype(out.dtype)


BLOCK = 4
STEP = 2
AHEAD = 4


def query_key_kernel(bits, where, sheet, wq, wk, qk, held, *rest):
    outs, (wt, acc, sems) = rest[:-3], rest[-3:]
    rows, cols, _ = sheet.shape
    local = wq.shape[0]
    heads = local // HEAD_DIM
    copies = [
        pltpu.make_async_copy(wq, wt.at[:local], sems.at[0]),
        pltpu.make_async_copy(wk, wt.at[local:], sems.at[1]),
    ]
    for first in range(0, rows, STEP):
        some = pl.ds(first, STEP)
        copies.append(pltpu.make_async_copy(sheet.at[some], held.at[some], sems.at[len(copies)]))
    for copy in copies[:AHEAD]:
        copy.start()
    copies[0].wait()
    copies[1].wait()
    flat = (BLOCK * HEAD_DIM, cols)
    for first in range(0, rows, BLOCK):
        for r in range(first, first + BLOCK):
            if r % STEP == 0:
                at = 2 + r // STEP
                copies[at].wait()
                for later in copies[at + AHEAD - 2 : at + AHEAD - 1]:
                    later.start()
            value = (mm(wt[...], held[r], NT) * lane_mask(where[2 + r], cols)).astype(BF16)
            qk[r] = value.reshape(2 * heads, HEAD_DIM, cols)
        some = pl.ds(first, BLOCK)
        for h in range(heads):
            term = mm(qk[some, h].reshape(flat), qk[some, heads + h].reshape(flat), TN)
            term = term.reshape(acc.shape[1:])
            acc[h] = term if first == 0 else acc[h] + term
    put_shards(where[0], acc, bits, outs)


def query_key(where, sheet, wq, wk, bits):
    rows, cols, width = sheet.shape
    shards = 1 << len(bits)
    local = wq.shape[0]
    heads = local // HEAD_DIM
    return in_vmem(
        functools.partial(query_key_kernel, bits),
        "query_key",
        [like((rows, 2 * heads, HEAD_DIM, cols)), like(sheet.shape)] + part_shapes(shards, heads, cols),
        where,
        sheet,
        wq,
        wk,
        scalars=1,
        streamed=3,
        scratch=(
            pltpu.VMEM((2 * local, width), BF16),
            pltpu.VMEM((heads, shards, cols // shards, cols), F32),
            pltpu.SemaphoreType.DMA((2 + rows // STEP,)),
        ),
        limit=14,
        flops=2 * rows * cols * local * (2 * width + cols),
    )


def value_kernel(bits, fars, where, sheet, wv, cot, *rest):
    outs, halves, acc = rest[: -1 - len(fars)], rest[-1 - len(fars) : -1], rest[-1]
    rows, cols, width = sheet.shape
    local = wv.shape[0]
    heads = local // HEAD_DIM
    for far, half in zip(fars, halves):
        near = half.shape[1]
        side = lax.shift_right_logical(where[1], 1) ^ (far // 2)
        for s in range(width // near):
            @pl.when(side == s)
            def _():
                half[...] = wv[:, s * near : (s + 1) * near]
    flat = (BLOCK * HEAD_DIM, cols)
    for first in range(0, rows, BLOCK):
        values = []
        for r in range(first, first + BLOCK):
            value = (mm(wv[...], sheet[r], NT) * lane_mask(where[2 + r], cols)).astype(BF16)
            values.append(value.reshape(heads, HEAD_DIM, cols))
        for h in range(heads):
            left = cot[pl.ds(first, BLOCK), h * HEAD_DIM : (h + 1) * HEAD_DIM].reshape(flat)
            right = jnp.concatenate([v[h] for v in values], axis=0)
            term = mm(left, right, TN).reshape(acc.shape[1:])
            acc[h] = term if first == 0 else acc[h] + term
    put_shards(where[0], acc, bits, outs)


def value_dprob(where, sheet, wv, cot, after, bits, fars, devices):
    rows, cols, width = sheet.shape
    shards = 1 << len(bits)
    local = wv.shape[0]
    heads = local // HEAD_DIM
    return in_vmem(
        functools.partial(value_kernel, bits, fars),
        "value_dprob",
        part_shapes(shards, heads, cols) + [like((local, 2 * width // devices))] * len(fars),
        where,
        sheet,
        wv,
        cot,
        scalars=1,
        after=after,
        scratch=(pltpu.VMEM((heads, shards, cols // shards, cols), F32),),
        limit=16,
        flops=4 * rows * cols * local * (width + cols),
    )


def turn_kernel(where, wq, wk, wv, natural, *full):
    near, share, columns = natural.shape
    local = wq.shape[0]
    for index, (weight, held) in enumerate(zip((wq, wk, wv), full)):
        held[...] = weight[...].T.reshape(held.shape)
        mine = where[1] & (held.shape[0] - 1)
        for j in range(near):
            natural[j, :, index * local : (index + 1) * local] = held[mine ^ j]


def turn(where, wq, wk, wv, devices, after):
    local, width = wq.shape
    share = width // devices
    return in_vmem(
        turn_kernel,
        "turn",
        (like((2, share, 3 * local)),),
        where,
        wq,
        wk,
        wv,
        scalars=1,
        after=after,
        hidden=False,
        scratch=[pltpu.VMEM((w.shape[1] // share, share, local), BF16) for w in (wq, wk, wv)],
    )[0]


def far_query_key_kernel(first, where, sheet, wq, wk, qk):
    local, _ = wq.shape
    cols = sheet.shape[1]
    both = jnp.concatenate([wq[...], wk[...]], axis=0)
    for r in range(qk.shape[0]):
        value = (mm(both, sheet[first + r], NT) * lane_mask(where[2 + first + r], cols)).astype(BF16)
        qk[r] = value.reshape(2 * local // HEAD_DIM, HEAD_DIM, cols)


def far_query_key(first, count, where, sheet, wq, wk, after):
    _, cols, width = sheet.shape
    local = wq.shape[0]
    return in_vmem(
        functools.partial(far_query_key_kernel, first),
        "far_query_key",
        (like((count, 2 * local // HEAD_DIM, HEAD_DIM, cols)),),
        where,
        sheet,
        wq,
        wk,
        scalars=1,
        after=after,
        hidden=False,
    )[0]


def part_shapes(shards, heads, cols):
    if shards == 1:
        return [like((1, heads, cols, cols), F32)]
    half = (shards // 2, heads, cols // shards, cols)
    return [like(half, F32), like(half)]


def add_split_kernel(keep, got, give_out, keep_out):
    for j in range(keep.shape[0]):
        total = keep[j].astype(F32) + got[j].astype(F32)
        out = give_out if j % 2 else keep_out
        out[j // 2] = total.astype(out.dtype)


def add_split(keep, got, after=()):
    half = (keep.shape[0] // 2,) + keep.shape[1:]
    return in_vmem(add_split_kernel, "add_split", (like(half), like(half, keep.dtype)), keep, got, after=after)


def halve(keep, give, axis, bits, after=()):
    after = list(after) + [()] * len(bits)
    for bit, waits in zip(bits[:-1], after):
        give, keep = add_split(keep, flip(give, axis, bit), waits)
    return keep, flip(give, axis, bits[-1])


def softmax_kernel(scale, *refs):
    *terms, probs_out, dscore_out = refs
    half = len(terms) // 2
    total = lambda some: functools.reduce(jnp.add, [t[0].astype(F32) for t in some])
    logits = total(terms[:half]) * scale
    dprob = total(terms[half:])
    shifted = jnp.exp(logits - jnp.max(logits, axis=-1, keepdims=True))
    probs = shifted / jnp.sum(shifted, axis=-1, keepdims=True)
    inner = jnp.sum(probs * dprob, axis=-1, keepdims=True)
    probs_out[0] = probs.astype(BF16)
    dscore_out[0] = (scale * probs * (dprob - inner)).astype(BF16)


def softmax_back(logits, dprob, scale, after=()):
    out = like(logits[0].shape)
    return in_vmem(
        functools.partial(softmax_kernel, scale), "softmax_back", (out, out), *logits, *dprob, limit=16, after=after
    )


def join_kernel(one, other, out):
    out[: one.shape[0]] = one[...]
    out[one.shape[0] :] = other[...]


def join(one, other, after):
    shape = (one.shape[0] + other.shape[0],) + one.shape[1:]
    return in_vmem(join_kernel, "join", (like(shape),), one, other, after=after)[0]


def double(values, axis, bits, after=()):
    order = [0]
    after = list(after) + [()] * len(bits)
    for bit, waits in zip(bits[:-1], after):
        values = join(values, flip(values, axis, bit), waits)
        order = order + [j ^ bit for j in order]
    other = flip(values, axis, bits[-1])
    return (values, other), (order, [j ^ bits[-1] for j in order])


def assemble_kernel(orders, where, *refs):
    pieces, outs = refs[:-2], refs[-2:]
    for piece, (kind, order) in zip(pieces, orders):
        for t, j in enumerate(order):
            outs[kind][where[0] ^ j] = piece[t]


def assemble(where, probs, dscore, orders, shards, after):
    out = like((shards,) + probs[0].shape[1:])
    return in_vmem(
        functools.partial(assemble_kernel, [(k, o) for k, both in enumerate(orders) for o in both]), "assemble", (out, out), where, *probs, *dscore, scalars=1, after=after
    )


def masked(where, value, first, count):
    cols = value.shape[-1]
    masks = jnp.stack([lane_mask(where[2 + first + r], cols) for r in range(count)])
    return (value.reshape(count, HEAD_DIM, cols) * masks).astype(BF16)


def query_key_gradients(where, dscore, qk, grads):
    rows, two, _, cols = qk.shape
    flat = (rows * HEAD_DIM, cols)
    heads = two // 2
    for h in range(heads):
        ds = dscore[:, h].reshape(cols, cols)
        grads[:, h] = masked(where, mm(qk[:, heads + h].reshape(flat), ds, NT), 0, rows)
        grads[:, heads + h] = masked(where, mm(qk[:, h].reshape(flat), ds, NN), 0, rows)


def value_gradient(where, probs, cot, h, first, count):
    cols = cot.shape[-1]
    g = cot[pl.ds(first, count), h * HEAD_DIM : (h + 1) * HEAD_DIM].reshape(count * HEAD_DIM, cols)
    return masked(where, mm(g, probs[:, h].reshape(cols, cols), NN), first, count)


def own_gradients_kernel(where, probs, dscore, qk, cot, grads):
    heads = qk.shape[1] // 2
    query_key_gradients(where, dscore, qk, grads)
    for h in range(heads):
        grads[:, 2 * heads + h] = value_gradient(where, probs, cot, h, 0, cot.shape[0])


def own_gradients(where, probs, dscore, qk, cot):
    rows, two, _, cols = qk.shape
    return in_vmem(
        own_gradients_kernel,
        "own_gradients",
        (like((rows, two // 2 * 3, HEAD_DIM, cols)),),
        where,
        probs,
        dscore,
        qk,
        cot,
        scalars=1,
        limit=14,
        flops=3 * rows * two * HEAD_DIM * cols * cols,
    )[0]


def near_input_kernel(where, own, weights, *refs):
    *refs, out, grads = refs
    near, share, columns = weights.shape
    rows, _, _, cols = own.shape
    left = weights[...].reshape(near * share, columns)
    for r in range(rows):
        part = mm(left, own[r].reshape(columns, cols), NN).astype(BF16).astype(F32)
        out[:, r] = part.reshape(near, share, cols)
    for i in range(0, len(refs), 3):
        dscore, qk, far = refs[i : i + 3]
        query_key_gradients(where, dscore, qk, grads)
        some = grads.shape[1] * HEAD_DIM
        left = far[:, :, :some].reshape(near * share, some)
        for r in range(rows):
            part = mm(left, grads[r].reshape(some, cols), NN)
            out[:, r] = out[:, r] + part.reshape(near, share, cols)


def near_input(where, grads, weights, far):
    rows, cols = grads.shape[0], grads.shape[-1]
    near, share, columns = weights.shape
    return in_vmem(
        near_input_kernel,
        "near_input",
        (like((near, rows, share, cols), F32),),
        where,
        grads,
        weights,
        *[a for one in far for a in one],
        scalars=1,
        scratch=(pltpu.VMEM((rows,) + far[0][1].shape[1:], BF16),),
        limit=14,
        hidden=False,
    )[0]


def far_input_kernel(first, where, near, *refs):
    *refs, keep, give = refs
    count, share, cols = keep.shape
    heads = refs[0].shape[1]
    local = heads * HEAD_DIM
    grads = []
    for i in range(0, len(refs), 3):
        probs, cot, _ = refs[i : i + 3]
        grads.append([value_gradient(where, probs, cot, h, first, count) for h in range(heads)])
    for r in range(count):
        total = near[:, first + r]
        for i, dv in zip(range(0, len(refs), 3), grads):
            weights = refs[i + 2]
            left = weights[:, :, 2 * local :].reshape(2 * share, local)
            right = jnp.concatenate([one[r] for one in dv], axis=0)
            total = total + mm(left, right, NN).reshape(2, share, cols)
        keep[r] = total[0].astype(keep.dtype)
        give[r] = total[1].astype(give.dtype)


def far_input(first, count, where, near, far):
    _, rows, share, cols = near.shape
    out = like((count, share, cols))
    return in_vmem(
        functools.partial(far_input_kernel, first),
        "far_input",
        (out, out),
        where,
        near,
        *[a for one in far for a in one],
        scalars=1,
        limit=14,
        hidden=False,
    )


def hold_kernel(values, out):
    out[...] = values[...]


def hold(values, after):
    return in_vmem(hold_kernel, "hold", (like(values.shape),), values, after=after, hidden=False)[0]


def finish_kernel(*refs):
    *terms, out, total, sems = refs
    copies = []
    first = 0
    for index in range(0, len(terms), 2):
        keep, got = terms[index : index + 2]
        some = pl.ds(first, keep.shape[0])
        total[some] = (keep[...].astype(F32) + got[...].astype(F32)).astype(BF16)
        copies.append(pltpu.make_async_copy(total.at[some], out.at[some], sems.at[index // 2]))
        copies[-1].start()
        first += keep.shape[0]
    for copy in copies:
        copy.wait()


def finish(chunks):
    _, share, cols = chunks[0][0].shape
    rows = sum(keep.shape[0] for keep, _ in chunks)
    terms = [a for chunk in chunks for a in chunk]
    return pl.pallas_call(
        finish_kernel,
        in_specs=[VMEM] * len(terms),
        out_specs=HBM,
        out_shape=like((rows, share, cols)),
        scratch_shapes=[pltpu.VMEM((rows, share, cols), BF16), pltpu.SemaphoreType.DMA((len(chunks),))],
        compiler_params=pltpu.CompilerParams(vmem_limit_bytes=12 * MIB),
        cost_estimate=cost(rows * share * cols, 6 * rows * share * cols),
        name="finish",
    )(*terms)


def weight_product(sheet, grads):
    rows, cols, width = sheet.shape
    columns = grads.shape[1] * HEAD_DIM
    left = [grads[r].reshape(columns, cols) for r in range(rows)]
    return mm(jnp.concatenate(left, axis=1), sheet[...].reshape(rows * cols, width), NN).T


def weight_kernel(where, sheet, grads, *rest):
    outs, full = rest[:-1], rest[-1]
    full[...] = weight_product(sheet, grads).reshape(full.shape)
    for j in range(full.shape[0]):
        first = 0
        for keep, give in zip(outs[::2], outs[1::2]):
            out = (keep, give)[j % 2]
            last = first + out.shape[-1]
            out[j // 2] = full[where[0] ^ j, :, first:last].astype(out.dtype)
            first = last


def whole_weight_kernel(where, sheet, grads, out):
    out[...] = weight_product(sheet, grads)


def weight_part(where, sheet, grads, cuts, shards, after):
    rows, cols, width = sheet.shape
    columns = grads.shape[1] * HEAD_DIM
    if shards == 1:
        kernel, outs, scratch = whole_weight_kernel, [like((width, columns), F32)], ()
    else:
        halves = [(shards // 2, width // shards, cut) for cut in cuts]
        kernel = weight_kernel
        outs = [o for half in halves for o in (like(half, F32), like(half))]
        scratch = (pltpu.VMEM((shards, width // shards, columns), F32),)
    return in_vmem(
        kernel,
        "weight_part",
        outs,
        where,
        sheet,
        grads,
        scalars=1,
        after=after,
        scratch=scratch,
        limit=18,
        flops=2 * rows * cols * width * columns,
    )


def add_apart_kernel(where, keep, got, own, give):
    mine = lax.shift_right_logical(where[0], 1)
    for t in range(keep.shape[0]):
        total = keep[t] + got[t].astype(F32)
        if t == 0:
            own[...] = total
        give[mine ^ t] = total.astype(give.dtype)


def add_apart(where, keep, got, after):
    outs = (like(keep.shape[1:], F32), like(keep.shape))
    return in_vmem(add_apart_kernel, "add_apart", outs, where, keep, got, scalars=1, after=after, hidden=False)


def last_kernel(where, own, got, out):
    mine = lax.shift_right_logical(where[0], 1)
    total = own[...]
    for t in range(1, got.shape[0]):
        total = total + got[mine ^ t].astype(F32)
    local = out.shape[-1]
    for index in range(out.shape[0]):
        out[index] = total[:, index * local : (index + 1) * local]


def last_sum(where, own, got, local):
    shape = (own.shape[1] // local, own.shape[0], local)
    return in_vmem(last_kernel, "last_sum", (like(shape, F32),), where, own, got, scalars=1, hidden=False)[0]


def body(sheet, w_query, w_key, w_value, cotangent, lengths):
    row_dev, cols, width = sheet.shape
    local = w_query.shape[1]
    n_rows = lax.axis_size("rows")
    n_heads = lax.axis_size("heads")
    scale = float(1.0 / (HEAD_DIM * row_dev * n_rows) ** 0.5)
    direct = n_rows <= 8
    shards = n_rows if direct else 1
    row_bits = [1 << b for b in range(n_rows.bit_length() - 1)]
    chunk = row_dev // 4

    me = jnp.stack([lax.axis_index("rows"), lax.axis_index("heads")]).astype(jnp.int32)
    where = jnp.concatenate([me, lengths])
    wq, wk, wv = w_query.T, w_key.T, w_value.T
    cot = jnp.swapaxes(cotangent, 1, 2)

    fars = range(2, n_heads, 2)
    far_cot = [flip(cot, "heads", f) for f in fars]
    fq, fk = [[flip(w, "heads", f) for f in fars] for w in (wq, wk)]

    up = row_bits if direct else []
    turn_about = up[1:] + up[:1]
    qk, held, *logits = query_key(where, sheet, wq, wk, turn_about)
    *dprob, = value_dprob(where, held, wv, cot, logits[-1:], up, fars, n_heads)
    dprob, halves = dprob[: -len(fars)], dprob[-len(fars) :]
    fv = [flip(half, "heads", f) for half, f in zip(halves, fars)]
    weights = turn(where, wq, wk, wv, n_heads, dprob[-1:])
    if direct:
        logits = halve(*logits, "rows", turn_about)
        dprob = halve(*dprob, "rows", up)
        probs_own, dscore_own = softmax_back(logits, dprob, scale, [weights])
        probs, probs_order = double(probs_own, "rows", up[::-1], [far_cot])
        dscore, dscore_order = double(dscore_own, "rows", turn_about[::-1], [far_cot])
        probs, dscore = assemble(where, probs, dscore, (probs_order, dscore_order), shards, fq + fk)
    else:
        logits, dprob = lax.psum((logits, dprob), "rows")
        probs, dscore = softmax_back(logits, dprob, scale)
    far_dscore = [flip(dscore, "heads", f) for f in fars]
    grads = own_gradients(where, probs, dscore, qk, cot)
    parts = weight_part(where, held, grads, (3 * local,), shards, fv)
    probs = hold(probs, [parts[-1]] + far_dscore)
    far_probs = [flip(probs, "heads", f) for f in fars]
    far_qk, far_natural = [], []
    for w in zip(fq, fk, fv):
        far_qk.append(far_query_key(0, row_dev, where, held, w[0], w[1], [probs]))
        far_natural.append(turn(where, *w, n_heads, [probs]))
    near = near_input(where, grads, weights, list(zip(far_dscore, far_qk, far_natural)))
    if direct:
        keep, give = parts
        own, give = add_apart(where, keep, flip(give, "rows", 1), [near])
        lines = [list(range(first, n_rows, 2)) for first in range(2)]
        got = lax.all_to_all(give, "rows", 0, 0, axis_index_groups=lines)
        weight_grad = last_sum(where, own, got, local)
        weight_grad = jnp.swapaxes(weight_grad, 0, 1)
    else:
        weight_grad = lax.psum_scatter(parts[0], "rows", scatter_dimension=0, tiled=True)
        weight_grad = weight_grad.reshape(width // n_rows, 3, local)

    chunks = []
    for first in range(0, row_dev, chunk):
        keep, give = far_input(first, chunk, where, near, list(zip(far_probs, far_cot, far_natural)))
        chunks.append((keep, flip(give, "heads", 1)))
    return (jnp.swapaxes(finish(chunks), 1, 2), weight_grad)


def solution(mesh):
    in_specs = (
        P("rows", None, None),
        P(None, "heads"),
        P(None, "heads"),
        P(None, "heads"),
        P("rows", None, "heads"),
        P("rows"),
    )
    out_specs = (P("rows", None, "heads"), P("rows", None, "heads"))
    return jax.shard_map(body, mesh=mesh, in_specs=in_specs, out_specs=out_specs, check_vma=False)
```

```python
import functools
import math

import jax
import jax.numpy as jnp
from jax import lax
from jax.experimental import pallas as pl
from jax.experimental.pallas import tpu as pltpu
from jax.sharding import PartitionSpec as P

HEAD_DIM = 64
F32 = jnp.float32
BF16 = jnp.bfloat16
MIB = 1024 * 1024

NN = (((1,), (0,)), ((), ()))
NT = (((1,), (1,)), ((), ()))
TN = (((0,), (0,)), ((), ()))


def mm(a, b, dims):
    return lax.dot_general(a, b, dims, preferred_element_type=F32)


def flip(values, axis, bit):
    n = lax.axis_size(axis)
    return lax.ppermute(values, axis, [(s, s ^ bit) for s in range(n)])


def cost(flops, moved):
    return pl.CostEstimate(flops=int(flops), bytes_accessed=int(moved), transcendentals=0)


SMEM = pl.BlockSpec(memory_space=pltpu.SMEM)
VMEM = pl.BlockSpec(memory_space=pltpu.VMEM)
ANY = pl.BlockSpec(memory_space=pl.ANY)
HBM = pl.BlockSpec(memory_space=pltpu.HBM)


def like(shape, dtype=BF16):
    return jax.ShapeDtypeStruct(shape, dtype)


def place(a, stays):
    return pltpu.with_memory_space_constraint(a, pltpu.HBM) if stays else a


def in_vmem(kernel, name, out, *operands, scalars=0, streamed=0, after=(), scratch=(), limit=12, flops=0):
    many = len(after)

    def run(*refs):
        kernel(*refs[: len(operands)], *refs[len(operands) + many :])

    moved = 2 * sum(a.size for a in operands) + 2 * sum(o.size for o in out)
    held = len(operands) - scalars - streamed
    return pl.pallas_call(
        run,
        in_specs=[SMEM] * scalars + [HBM] * streamed + [VMEM] * held + [ANY] * many,
        out_specs=[VMEM] * len(out),
        out_shape=list(out),
        scratch_shapes=list(scratch),
        compiler_params=pltpu.CompilerParams(vmem_limit_bytes=limit * MIB),
        cost_estimate=cost(flops, moved),
        name=name,
    )(*[place(a, scalars <= i < scalars + streamed) for i, a in enumerate(operands)], *after)


def lane_mask(length, cols):
    return (lax.broadcasted_iota(jnp.int32, (1, cols), 1) < length).astype(F32)


def reorder(bits):
    return [sum(bit for b, bit in enumerate(bits) if t >> b & 1) for t in range(1 << len(bits))]


def put_shards(me, acc, bits, outs):
    for t, j in enumerate(reorder(bits)):
        out = outs[t % len(outs)]
        out[t // len(outs)] = acc[:, me ^ j].astype(out.dtype)


BLOCK = 4
STEP = 2
AHEAD = 4


def query_key_kernel(bits, where, sheet, wq, wk, qk, held, *rest):
    outs, (wt, acc, sems) = rest[:-3], rest[-3:]
    rows, cols, _ = sheet.shape
    local = wq.shape[0]
    heads = local // HEAD_DIM
    copies = [
        pltpu.make_async_copy(wq, wt.at[:local], sems.at[0]),
        pltpu.make_async_copy(wk, wt.at[local:], sems.at[1]),
    ]
    for first in range(0, rows, STEP):
        some = pl.ds(first, STEP)
        copies.append(pltpu.make_async_copy(sheet.at[some], held.at[some], sems.at[len(copies)]))
    for copy in copies[:AHEAD]:
        copy.start()
    copies[0].wait()
    copies[1].wait()
    flat = (BLOCK * HEAD_DIM, cols)
    for first in range(0, rows, BLOCK):
        for r in range(first, first + BLOCK):
            if r % STEP == 0:
                at = 2 + r // STEP
                copies[at].wait()
                for later in copies[at + AHEAD - 2 : at + AHEAD - 1]:
                    later.start()
            value = (mm(wt[...], held[r], NT) * lane_mask(where[2 + r], cols)).astype(BF16)
            qk[r] = value.reshape(2 * heads, HEAD_DIM, cols)
        some = pl.ds(first, BLOCK)
        for h in range(heads):
            term = mm(qk[some, h].reshape(flat), qk[some, heads + h].reshape(flat), TN)
            term = term.reshape(acc.shape[1:])
            acc[h] = term if first == 0 else acc[h] + term
    put_shards(where[0], acc, bits, outs)


def query_key(where, sheet, wq, wk, bits):
    rows, cols, width = sheet.shape
    shards = 1 << len(bits)
    local = wq.shape[0]
    heads = local // HEAD_DIM
    return in_vmem(
        functools.partial(query_key_kernel, bits),
        "query_key",
        [like((rows, 2 * heads, HEAD_DIM, cols)), like(sheet.shape)] + part_shapes(shards, heads, cols),
        where,
        sheet,
        wq,
        wk,
        scalars=1,
        streamed=3,
        scratch=(
            pltpu.VMEM((2 * local, width), BF16),
            pltpu.VMEM((heads, shards, cols // shards, cols), F32),
            pltpu.SemaphoreType.DMA((2 + rows // STEP,)),
        ),
        limit=14,
        flops=2 * rows * cols * local * (2 * width + cols),
    )


def value_kernel(bits, fars, where, sheet, wv, cot, *rest):
    outs, halves, acc = rest[: -1 - len(fars)], rest[-1 - len(fars) : -1], rest[-1]
    rows, cols, width = sheet.shape
    local = wv.shape[0]
    heads = local // HEAD_DIM
    for far, half in zip(fars, halves):
        near = half.shape[1]
        side = lax.shift_right_logical(where[1], 1) ^ (far // 2)
        for s in range(width // near):
            @pl.when(side == s)
            def _():
                half[...] = wv[:, s * near : (s + 1) * near]
    flat = (BLOCK * HEAD_DIM, cols)
    for first in range(0, rows, BLOCK):
        values = []
        for r in range(first, first + BLOCK):
            value = (mm(wv[...], sheet[r], NT) * lane_mask(where[2 + r], cols)).astype(BF16)
            values.append(value.reshape(heads, HEAD_DIM, cols))
        for h in range(heads):
            left = cot[pl.ds(first, BLOCK), h * HEAD_DIM : (h + 1) * HEAD_DIM].reshape(flat)
            right = jnp.concatenate([v[h] for v in values], axis=0)
            term = mm(left, right, TN).reshape(acc.shape[1:])
            acc[h] = term if first == 0 else acc[h] + term
    put_shards(where[0], acc, bits, outs)


def value_dprob(where, sheet, wv, cot, after, bits, fars, devices):
    rows, cols, width = sheet.shape
    shards = 1 << len(bits)
    local = wv.shape[0]
    heads = local // HEAD_DIM
    return in_vmem(
        functools.partial(value_kernel, bits, fars),
        "value_dprob",
        part_shapes(shards, heads, cols) + [like((local, 2 * width // devices))] * len(fars),
        where,
        sheet,
        wv,
        cot,
        scalars=1,
        after=after,
        scratch=(pltpu.VMEM((heads, shards, cols // shards, cols), F32),),
        limit=16,
        flops=4 * rows * cols * local * (width + cols),
    )


def turn_kernel(where, wq, wk, wv, natural, *full):
    near, share, columns = natural.shape
    local = wq.shape[0]
    for index, (weight, held) in enumerate(zip((wq, wk, wv), full)):
        held[...] = weight[...].T.reshape(held.shape)
        mine = where[1] & (held.shape[0] - 1)
        for j in range(near):
            natural[j, :, index * local : (index + 1) * local] = held[mine ^ j]


def turn(where, wq, wk, wv, devices, after):
    local, width = wq.shape
    share = width // devices
    return in_vmem(
        turn_kernel,
        "turn",
        (like((2, share, 3 * local)),),
        where,
        wq,
        wk,
        wv,
        scalars=1,
        after=after,
        scratch=[pltpu.VMEM((w.shape[1] // share, share, local), BF16) for w in (wq, wk, wv)],
    )[0]


def far_query_key_kernel(first, where, sheet, wq, wk, qk):
    local, _ = wq.shape
    cols = sheet.shape[1]
    both = jnp.concatenate([wq[...], wk[...]], axis=0)
    for r in range(qk.shape[0]):
        value = (mm(both, sheet[first + r], NT) * lane_mask(where[2 + first + r], cols)).astype(BF16)
        qk[r] = value.reshape(2 * local // HEAD_DIM, HEAD_DIM, cols)


def far_query_key(first, count, where, sheet, wq, wk, after):
    _, cols, width = sheet.shape
    local = wq.shape[0]
    return in_vmem(
        functools.partial(far_query_key_kernel, first),
        "far_query_key",
        (like((count, 2 * local // HEAD_DIM, HEAD_DIM, cols)),),
        where,
        sheet,
        wq,
        wk,
        scalars=1,
        after=after,
    )[0]


def part_shapes(shards, heads, cols):
    if shards == 1:
        return [like((1, heads, cols, cols), F32)]
    half = (shards // 2, heads, cols // shards, cols)
    return [like(half, F32), like(half)]


def add_split_kernel(keep, got, give_out, keep_out):
    for j in range(keep.shape[0]):
        total = keep[j].astype(F32) + got[j].astype(F32)
        out = give_out if j % 2 else keep_out
        out[j // 2] = total.astype(out.dtype)


def add_split(keep, got, after=()):
    half = (keep.shape[0] // 2,) + keep.shape[1:]
    return in_vmem(add_split_kernel, "add_split", (like(half), like(half, keep.dtype)), keep, got, after=after)


def halve(keep, give, axis, bits, after=()):
    after = list(after) + [()] * len(bits)
    for bit, waits in zip(bits[:-1], after):
        give, keep = add_split(keep, flip(give, axis, bit), waits)
    return keep, flip(give, axis, bits[-1])


def softmax_kernel(scale, *refs):
    *terms, probs_out, dscore_out = refs
    half = len(terms) // 2
    total = lambda some: functools.reduce(jnp.add, [t[0].astype(F32) for t in some])
    logits = total(terms[:half]) * scale
    dprob = total(terms[half:])
    shifted = jnp.exp(logits - jnp.max(logits, axis=-1, keepdims=True))
    probs = shifted / jnp.sum(shifted, axis=-1, keepdims=True)
    inner = jnp.sum(probs * dprob, axis=-1, keepdims=True)
    probs_out[0] = probs.astype(BF16)
    dscore_out[0] = (scale * probs * (dprob - inner)).astype(BF16)


def softmax_back(logits, dprob, scale, after=()):
    out = like(logits[0].shape)
    return in_vmem(
        functools.partial(softmax_kernel, scale), "softmax_back", (out, out), *logits, *dprob, limit=16, after=after
    )


def join_kernel(one, other, out):
    out[: one.shape[0]] = one[...]
    out[one.shape[0] :] = other[...]


def join(one, other, after):
    shape = (one.shape[0] + other.shape[0],) + one.shape[1:]
    return in_vmem(join_kernel, "join", (like(shape),), one, other, after=after)[0]


def double(values, axis, bits, after=()):
    order = [0]
    after = list(after) + [()] * len(bits)
    for bit, waits in zip(bits[:-1], after):
        values = join(values, flip(values, axis, bit), waits)
        order = order + [j ^ bit for j in order]
    other = flip(values, axis, bits[-1])
    return (values, other), (order, [j ^ bits[-1] for j in order])


def assemble_kernel(orders, where, *refs):
    pieces, outs = refs[:-2], refs[-2:]
    for piece, (kind, order) in zip(pieces, orders):
        for t, j in enumerate(order):
            outs[kind][where[0] ^ j] = piece[t]


def assemble(where, probs, dscore, orders, shards, after):
    out = like((shards,) + probs[0].shape[1:])
    return in_vmem(
        functools.partial(assemble_kernel, [(k, o) for k, both in enumerate(orders) for o in both]), "assemble", (out, out), where, *probs, *dscore, scalars=1, after=after
    )


def masked(where, value, first, count):
    cols = value.shape[-1]
    masks = jnp.stack([lane_mask(where[2 + first + r], cols) for r in range(count)])
    return (value.reshape(count, HEAD_DIM, cols) * masks).astype(BF16)


def query_key_gradients(where, dscore, qk, grads):
    rows, two, _, cols = qk.shape
    flat = (rows * HEAD_DIM, cols)
    heads = two // 2
    for h in range(heads):
        ds = dscore[:, h].reshape(cols, cols)
        grads[:, h] = masked(where, mm(qk[:, heads + h].reshape(flat), ds, NT), 0, rows)
        grads[:, heads + h] = masked(where, mm(qk[:, h].reshape(flat), ds, NN), 0, rows)


def value_gradient(where, probs, cot, h, first, count):
    cols = cot.shape[-1]
    g = cot[pl.ds(first, count), h * HEAD_DIM : (h + 1) * HEAD_DIM].reshape(count * HEAD_DIM, cols)
    return masked(where, mm(g, probs[:, h].reshape(cols, cols), NN), first, count)


def own_gradients_kernel(where, probs, dscore, qk, cot, grads):
    heads = qk.shape[1] // 2
    query_key_gradients(where, dscore, qk, grads)
    for h in range(heads):
        grads[:, 2 * heads + h] = value_gradient(where, probs, cot, h, 0, cot.shape[0])


def own_gradients(where, probs, dscore, qk, cot):
    rows, two, _, cols = qk.shape
    return in_vmem(
        own_gradients_kernel,
        "own_gradients",
        (like((rows, two // 2 * 3, HEAD_DIM, cols)),),
        where,
        probs,
        dscore,
        qk,
        cot,
        scalars=1,
        limit=14,
        flops=3 * rows * two * HEAD_DIM * cols * cols,
    )[0]


def near_input_kernel(fars, where, own, weights, *refs):
    far, outs, grads = refs[: 3 * fars], refs[3 * fars : -1], refs[-1]
    near, share, columns = weights.shape
    rows, _, _, cols = own.shape
    count = rows // len(outs)
    some = grads.shape[2] * HEAD_DIM
    for i in range(fars):
        query_key_gradients(where, *far[3 * i : 3 * i + 2], grads.at[i])
    for r in range(rows):
        left = weights[...].reshape(near * share, columns)
        total = mm(left, own[r].reshape(columns, cols), NN)
        for i in range(fars):
            left = far[3 * i + 2][:, :, :some].reshape(near * share, some)
            total = total + mm(left, grads[i, r].reshape(some, cols), NN)
        outs[r // count][:, r % count] = total.astype(BF16).reshape(near, share, cols)


def near_input(where, grads, weights, far, chunk):
    rows, cols = grads.shape[0], grads.shape[-1]
    near, share, columns = weights.shape
    return in_vmem(
        functools.partial(near_input_kernel, len(far)),
        "near_input",
        [like((near, chunk, share, cols))] * (rows // chunk),
        where,
        grads,
        weights,
        *[a for one in far for a in one],
        scalars=1,
        scratch=(pltpu.VMEM((len(far), rows) + far[0][1].shape[1:], BF16),),
        limit=14,
        flops=2 * rows * cols * near * share * columns * (1 + len(far)),
    )


def far_input_kernel(first, fars, where, near, *refs):
    far, keep, give = refs[: 3 * fars], refs[-2], refs[-1]
    count, share, cols = keep.shape
    heads = far[0].shape[1]
    local = heads * HEAD_DIM
    grads = []
    for i in range(fars):
        probs, cot, _ = far[3 * i : 3 * i + 3]
        grads.append([value_gradient(where, probs, cot, h, first, count) for h in range(heads)])
    for r in range(count):
        total = near[:, r].astype(F32)
        for i, dv in enumerate(grads):
            left = far[3 * i + 2][:, :, 2 * local :].reshape(2 * share, local)
            right = jnp.concatenate([one[r] for one in dv], axis=0)
            total = total + mm(left, right, NN).reshape(2, share, cols)
        keep[r] = total[0].astype(keep.dtype)
        give[r] = total[1].astype(give.dtype)


def far_input(first, where, near, far):
    _, count, share, cols = near.shape
    out = like((count, share, cols))
    return in_vmem(
        functools.partial(far_input_kernel, first, len(far)),
        "far_input",
        (out, out),
        where,
        near,
        *[a for one in far for a in one],
        scalars=1,
        limit=14,
    )


def hold_kernel(values, out):
    out[...] = values[...]


def hold(values, after):
    return in_vmem(hold_kernel, "hold", (like(values.shape),), values, after=after)[0]


def finish_kernel(*refs):
    *terms, out, total, sems = refs
    copies = []
    first = 0
    for index in range(0, len(terms), 2):
        keep, got = terms[index : index + 2]
        some = pl.ds(first, keep.shape[0])
        total[some] = (keep[...].astype(F32) + got[...].astype(F32)).astype(BF16)
        copies.append(pltpu.make_async_copy(total.at[some], out.at[some], sems.at[index // 2]))
        copies[-1].start()
        first += keep.shape[0]
    for copy in copies:
        copy.wait()


def finish(chunks):
    _, share, cols = chunks[0][0].shape
    rows = sum(keep.shape[0] for keep, _ in chunks)
    terms = [a for chunk in chunks for a in chunk]
    return pl.pallas_call(
        finish_kernel,
        in_specs=[VMEM] * len(terms),
        out_specs=HBM,
        out_shape=like((rows, share, cols)),
        scratch_shapes=[pltpu.VMEM((rows, share, cols), BF16), pltpu.SemaphoreType.DMA((len(chunks),))],
        compiler_params=pltpu.CompilerParams(vmem_limit_bytes=12 * MIB),
        cost_estimate=cost(rows * share * cols, 6 * rows * share * cols),
        name="finish",
    )(*terms)


def weight_product(sheet, grads):
    rows, cols, width = sheet.shape
    columns = grads.shape[1] * HEAD_DIM
    left = [grads[r].reshape(columns, cols) for r in range(rows)]
    return mm(jnp.concatenate(left, axis=1), sheet[...].reshape(rows * cols, width), NN).T


def weight_kernel(where, sheet, grads, *rest):
    outs, full = rest[:-1], rest[-1]
    full[...] = weight_product(sheet, grads).reshape(full.shape)
    for j in range(full.shape[0]):
        first = 0
        for keep, give in zip(outs[::2], outs[1::2]):
            out = (keep, give)[j % 2]
            last = first + out.shape[-1]
            out[j // 2] = full[where[0] ^ j, :, first:last].astype(out.dtype)
            first = last


def whole_weight_kernel(where, sheet, grads, out):
    out[...] = weight_product(sheet, grads)


def weight_part(where, sheet, grads, cuts, shards, after):
    rows, cols, width = sheet.shape
    columns = grads.shape[1] * HEAD_DIM
    if shards == 1:
        kernel, outs, scratch = whole_weight_kernel, [like((width, columns), F32)], ()
    else:
        halves = [(shards // 2, width // shards, cut) for cut in cuts]
        kernel = weight_kernel
        outs = [o for half in halves for o in (like(half, F32), like(half))]
        scratch = (pltpu.VMEM((shards, width // shards, columns), F32),)
    return in_vmem(
        kernel,
        "weight_part",
        outs,
        where,
        sheet,
        grads,
        scalars=1,
        after=after,
        scratch=scratch,
        limit=18,
        flops=2 * rows * cols * width * columns,
    )


def add_apart_kernel(where, keep, got, own, give):
    mine = lax.shift_right_logical(where[0], 1)
    for t in range(keep.shape[0]):
        total = keep[t] + got[t].astype(F32)
        if t == 0:
            own[...] = total
        give[mine ^ t] = total.astype(give.dtype)


def add_apart(where, keep, got, after):
    outs = (like(keep.shape[1:], F32), like(keep.shape))
    return in_vmem(add_apart_kernel, "add_apart", outs, where, keep, got, scalars=1, after=after)


def last_kernel(where, own, got, out):
    mine = lax.shift_right_logical(where[0], 1)
    total = own[...]
    for t in range(1, got.shape[0]):
        total = total + got[mine ^ t].astype(F32)
    local = out.shape[-1]
    for index in range(out.shape[0]):
        out[index] = total[:, index * local : (index + 1) * local]


def last_sum(where, own, got, local):
    shape = (own.shape[1] // local, own.shape[0], local)
    return in_vmem(last_kernel, "last_sum", (like(shape, F32),), where, own, got, scalars=1)[0]


def body(sheet, w_query, w_key, w_value, cotangent, lengths):
    row_dev, cols, width = sheet.shape
    local = w_query.shape[1]
    n_rows = lax.axis_size("rows")
    n_heads = lax.axis_size("heads")
    scale = float(1.0 / (HEAD_DIM * row_dev * n_rows) ** 0.5)
    direct = n_rows <= 8
    shards = n_rows if direct else 1
    row_bits = [1 << b for b in range(n_rows.bit_length() - 1)]
    chunk = row_dev // 4

    me = jnp.stack([lax.axis_index("rows"), lax.axis_index("heads")]).astype(jnp.int32)
    where = jnp.concatenate([me, lengths])
    wq, wk, wv = w_query.T, w_key.T, w_value.T
    cot = jnp.swapaxes(cotangent, 1, 2)

    fars = range(2, n_heads, 2)
    far_cot = [flip(cot, "heads", f) for f in fars]
    fq, fk = [[flip(w, "heads", f) for f in fars] for w in (wq, wk)]

    up = row_bits if direct else []
    turn_about = up[1:] + up[:1]
    qk, held, *logits = query_key(where, sheet, wq, wk, turn_about)
    *dprob, = value_dprob(where, held, wv, cot, logits[-1:], up, fars, n_heads)
    dprob, halves = dprob[: -len(fars)], dprob[-len(fars) :]
    fv = [flip(half, "heads", f) for half, f in zip(halves, fars)]
    weights = turn(where, wq, wk, wv, n_heads, dprob[-1:])
    if direct:
        logits = halve(*logits, "rows", turn_about)
        dprob = halve(*dprob, "rows", up)
        probs_own, dscore_own = softmax_back(logits, dprob, scale, [weights])
        probs, probs_order = double(probs_own, "rows", up[::-1], [far_cot])
        dscore, dscore_order = double(dscore_own, "rows", turn_about[::-1], [far_cot])
        probs, dscore = assemble(where, probs, dscore, (probs_order, dscore_order), shards, fq + fk)
    else:
        logits, dprob = lax.psum((logits, dprob), "rows")
        probs, dscore = softmax_back(logits, dprob, scale)
    far_dscore = [flip(dscore, "heads", f) for f in fars]
    grads = own_gradients(where, probs, dscore, qk, cot)
    parts = weight_part(where, held, grads, (3 * local,), shards, fv)
    probs = hold(probs, [parts[-1]] + far_dscore)
    far_probs = [flip(probs, "heads", f) for f in fars]
    far_qk, far_natural = [], []
    for w in zip(fq, fk, fv):
        far_qk.append(far_query_key(0, row_dev, where, held, w[0], w[1], [probs]))
        far_natural.append(turn(where, *w, n_heads, [probs]))
    near = near_input(where, grads, weights, list(zip(far_dscore, far_qk, far_natural)), chunk)
    if direct:
        keep, give = parts
        own, give = add_apart(where, keep, flip(give, "rows", 1), near[-1:])
        lines = [list(range(first, n_rows, 2)) for first in range(2)]
        got = lax.all_to_all(give, "rows", 0, 0, axis_index_groups=lines)
        weight_grad = last_sum(where, own, got, local)
        weight_grad = jnp.swapaxes(weight_grad, 0, 1)
    else:
        weight_grad = lax.psum_scatter(parts[0], "rows", scatter_dimension=0, tiled=True)
        weight_grad = weight_grad.reshape(width // n_rows, 3, local)

    chunks = []
    for index, part in enumerate(near):
        keep, give = far_input(index * chunk, where, part, list(zip(far_probs, far_cot, far_natural)))
        chunks.append((keep, flip(give, "heads", 1)))
    return (jnp.swapaxes(finish(chunks), 1, 2), weight_grad)


def solution(mesh):
    in_specs = (
        P("rows", None, None),
        P(None, "heads"),
        P(None, "heads"),
        P(None, "heads"),
        P("rows", None, "heads"),
        P("rows"),
    )
    out_specs = (P("rows", None, "heads"), P("rows", None, "heads"))
    return jax.shard_map(body, mesh=mesh, in_specs=in_specs, out_specs=out_specs, check_vma=False)
```

```python
import functools
import math

import jax
import jax.numpy as jnp
from jax import lax
from jax.experimental import pallas as pl
from jax.experimental.pallas import tpu as pltpu
from jax.sharding import PartitionSpec as P

HEAD_DIM = 64
F32 = jnp.float32
BF16 = jnp.bfloat16
MIB = 1024 * 1024

NN = (((1,), (0,)), ((), ()))
NT = (((1,), (1,)), ((), ()))
TN = (((0,), (0,)), ((), ()))


def mm(a, b, dims):
    return lax.dot_general(a, b, dims, preferred_element_type=F32)


def flip(values, axis, bit):
    n = lax.axis_size(axis)
    return lax.ppermute(values, axis, [(s, s ^ bit) for s in range(n)])


def cost(flops, moved):
    return pl.CostEstimate(flops=int(flops), bytes_accessed=int(moved), transcendentals=0)


SMEM = pl.BlockSpec(memory_space=pltpu.SMEM)
VMEM = pl.BlockSpec(memory_space=pltpu.VMEM)
ANY = pl.BlockSpec(memory_space=pl.ANY)
HBM = pl.BlockSpec(memory_space=pltpu.HBM)


def like(shape, dtype=BF16):
    return jax.ShapeDtypeStruct(shape, dtype)


def place(a, stays):
    return pltpu.with_memory_space_constraint(a, pltpu.HBM) if stays else a


def in_vmem(kernel, name, out, *operands, scalars=0, streamed=0, after=(), scratch=(), limit=12, flops=0):
    many = len(after)

    def run(*refs):
        kernel(*refs[: len(operands)], *refs[len(operands) + many :])

    moved = 2 * sum(a.size for a in operands) + 2 * sum(o.size for o in out)
    held = len(operands) - scalars - streamed
    return pl.pallas_call(
        run,
        in_specs=[SMEM] * scalars + [HBM] * streamed + [VMEM] * held + [ANY] * many,
        out_specs=[VMEM] * len(out),
        out_shape=list(out),
        scratch_shapes=list(scratch),
        compiler_params=pltpu.CompilerParams(vmem_limit_bytes=limit * MIB),
        cost_estimate=cost(flops, moved),
        name=name,
    )(*[place(a, scalars <= i < scalars + streamed) for i, a in enumerate(operands)], *after)


def lane_mask(length, cols):
    return (lax.broadcasted_iota(jnp.int32, (1, cols), 1) < length).astype(F32)


def reorder(bits):
    return [sum(bit for b, bit in enumerate(bits) if t >> b & 1) for t in range(1 << len(bits))]


def put_shards(me, acc, bits, outs):
    for t, j in enumerate(reorder(bits)):
        out = outs[t % len(outs)]
        out[t // len(outs)] = acc[:, me ^ j].astype(out.dtype)


BLOCK = 4
STEP = 2
AHEAD = 4


def query_key_kernel(bits, where, sheet, wq, wk, qk, held, *rest):
    outs, (wt, acc, sems) = rest[:-3], rest[-3:]
    rows, cols, _ = sheet.shape
    local = wq.shape[0]
    heads = local // HEAD_DIM
    copies = [
        pltpu.make_async_copy(wq, wt.at[:local], sems.at[0]),
        pltpu.make_async_copy(wk, wt.at[local:], sems.at[1]),
    ]
    for first in range(0, rows, STEP):
        some = pl.ds(first, STEP)
        copies.append(pltpu.make_async_copy(sheet.at[some], held.at[some], sems.at[len(copies)]))
    for copy in copies[:AHEAD]:
        copy.start()
    copies[0].wait()
    copies[1].wait()
    flat = (BLOCK * HEAD_DIM, cols)
    for first in range(0, rows, BLOCK):
        for r in range(first, first + BLOCK):
            if r % STEP == 0:
                at = 2 + r // STEP
                copies[at].wait()
                for later in copies[at + AHEAD - 2 : at + AHEAD - 1]:
                    later.start()
            value = (mm(wt[...], held[r], NT) * lane_mask(where[2 + r], cols)).astype(BF16)
            qk[r] = value.reshape(2 * heads, HEAD_DIM, cols)
        some = pl.ds(first, BLOCK)
        for h in range(heads):
            term = mm(qk[some, h].reshape(flat), qk[some, heads + h].reshape(flat), TN)
            term = term.reshape(acc.shape[1:])
            acc[h] = term if first == 0 else acc[h] + term
    put_shards(where[0], acc, bits, outs)


def query_key(where, sheet, wq, wk, bits):
    rows, cols, width = sheet.shape
    shards = 1 << len(bits)
    local = wq.shape[0]
    heads = local // HEAD_DIM
    return in_vmem(
        functools.partial(query_key_kernel, bits),
        "query_key",
        [like((rows, 2 * heads, HEAD_DIM, cols)), like(sheet.shape)] + part_shapes(shards, heads, cols),
        where,
        sheet,
        wq,
        wk,
        scalars=1,
        streamed=3,
        scratch=(
            pltpu.VMEM((2 * local, width), BF16),
            pltpu.VMEM((heads, shards, cols // shards, cols), F32),
            pltpu.SemaphoreType.DMA((2 + rows // STEP,)),
        ),
        limit=14,
        flops=2 * rows * cols * local * (2 * width + cols),
    )


def value_kernel(bits, fars, where, sheet, wv, cot, *rest):
    outs, halves, acc = rest[: -1 - len(fars)], rest[-1 - len(fars) : -1], rest[-1]
    rows, cols, width = sheet.shape
    local = wv.shape[0]
    heads = local // HEAD_DIM
    for far, half in zip(fars, halves):
        near = half.shape[1]
        side = lax.shift_right_logical(where[1], 1) ^ (far // 2)
        for s in range(width // near):
            @pl.when(side == s)
            def _():
                half[...] = wv[:, s * near : (s + 1) * near]
    flat = (BLOCK * HEAD_DIM, cols)
    for first in range(0, rows, BLOCK):
        values = []
        for r in range(first, first + BLOCK):
            value = (mm(wv[...], sheet[r], NT) * lane_mask(where[2 + r], cols)).astype(BF16)
            values.append(value.reshape(heads, HEAD_DIM, cols))
        for h in range(heads):
            left = cot[pl.ds(first, BLOCK), h * HEAD_DIM : (h + 1) * HEAD_DIM].reshape(flat)
            right = jnp.concatenate([v[h] for v in values], axis=0)
            term = mm(left, right, TN).reshape(acc.shape[1:])
            acc[h] = term if first == 0 else acc[h] + term
    put_shards(where[0], acc, bits, outs)


def value_dprob(where, sheet, wv, cot, after, bits, fars, devices):
    rows, cols, width = sheet.shape
    shards = 1 << len(bits)
    local = wv.shape[0]
    heads = local // HEAD_DIM
    return in_vmem(
        functools.partial(value_kernel, bits, fars),
        "value_dprob",
        part_shapes(shards, heads, cols) + [like((local, 2 * width // devices))] * len(fars),
        where,
        sheet,
        wv,
        cot,
        scalars=1,
        after=after,
        scratch=(pltpu.VMEM((heads, shards, cols // shards, cols), F32),),
        limit=16,
        flops=4 * rows * cols * local * (width + cols),
    )


def turn_kernel(where, wq, wk, wv, natural, *full):
    near, share, columns = natural.shape
    local = wq.shape[0]
    for index, (weight, held) in enumerate(zip((wq, wk, wv), full)):
        held[...] = weight[...].T.reshape(held.shape)
        mine = where[1] & (held.shape[0] - 1)
        for j in range(near):
            natural[j, :, index * local : (index + 1) * local] = held[mine ^ j]


def turn(where, wq, wk, wv, devices, after):
    local, width = wq.shape
    share = width // devices
    return in_vmem(
        turn_kernel,
        "turn",
        (like((2, share, 3 * local)),),
        where,
        wq,
        wk,
        wv,
        scalars=1,
        after=after,
        scratch=[pltpu.VMEM((w.shape[1] // share, share, local), BF16) for w in (wq, wk, wv)],
    )[0]


def far_query_key_kernel(first, where, sheet, wq, wk, qk):
    local, _ = wq.shape
    cols = sheet.shape[1]
    both = jnp.concatenate([wq[...], wk[...]], axis=0)
    for r in range(qk.shape[0]):
        value = (mm(both, sheet[first + r], NT) * lane_mask(where[2 + first + r], cols)).astype(BF16)
        qk[r] = value.reshape(2 * local // HEAD_DIM, HEAD_DIM, cols)


def far_query_key(first, count, where, sheet, wq, wk, after):
    _, cols, width = sheet.shape
    local = wq.shape[0]
    return in_vmem(
        functools.partial(far_query_key_kernel, first),
        "far_query_key",
        (like((count, 2 * local // HEAD_DIM, HEAD_DIM, cols)),),
        where,
        sheet,
        wq,
        wk,
        scalars=1,
        after=after,
    )[0]


def part_shapes(shards, heads, cols):
    if shards == 1:
        return [like((1, heads, cols, cols), F32)]
    half = (shards // 2, heads, cols // shards, cols)
    return [like(half, F32), like(half)]


def add_split_kernel(keep, got, give_out, keep_out):
    for j in range(keep.shape[0]):
        total = keep[j].astype(F32) + got[j].astype(F32)
        out = give_out if j % 2 else keep_out
        out[j // 2] = total.astype(out.dtype)


def add_split(keep, got, after=()):
    half = (keep.shape[0] // 2,) + keep.shape[1:]
    return in_vmem(add_split_kernel, "add_split", (like(half), like(half, keep.dtype)), keep, got, after=after)


def halve(keep, give, axis, bits, after=()):
    after = list(after) + [()] * len(bits)
    for bit, waits in zip(bits[:-1], after):
        give, keep = add_split(keep, flip(give, axis, bit), waits)
    return keep, flip(give, axis, bits[-1])


def softmax_kernel(scale, *refs):
    *terms, probs_out, dscore_out = refs
    half = len(terms) // 2
    total = lambda some: functools.reduce(jnp.add, [t[0].astype(F32) for t in some])
    logits = total(terms[:half]) * scale
    dprob = total(terms[half:])
    shifted = jnp.exp(logits - jnp.max(logits, axis=-1, keepdims=True))
    probs = shifted / jnp.sum(shifted, axis=-1, keepdims=True)
    inner = jnp.sum(probs * dprob, axis=-1, keepdims=True)
    probs_out[0] = probs.astype(BF16)
    dscore_out[0] = (scale * probs * (dprob - inner)).astype(BF16)


def softmax_back(logits, dprob, scale, after=()):
    out = like(logits[0].shape)
    return in_vmem(
        functools.partial(softmax_kernel, scale), "softmax_back", (out, out), *logits, *dprob, limit=16, after=after
    )


def join_kernel(one, other, out):
    out[: one.shape[0]] = one[...]
    out[one.shape[0] :] = other[...]


def join(one, other, after):
    shape = (one.shape[0] + other.shape[0],) + one.shape[1:]
    return in_vmem(join_kernel, "join", (like(shape),), one, other, after=after)[0]


def double(values, axis, bits, after=()):
    order = [0]
    after = list(after) + [()] * len(bits)
    for bit, waits in zip(bits[:-1], after):
        values = join(values, flip(values, axis, bit), waits)
        order = order + [j ^ bit for j in order]
    other = flip(values, axis, bits[-1])
    return (values, other), (order, [j ^ bits[-1] for j in order])


def assemble_kernel(orders, where, *refs):
    pieces, outs = refs[:-2], refs[-2:]
    for piece, (kind, order) in zip(pieces, orders):
        for t, j in enumerate(order):
            outs[kind][where[0] ^ j] = piece[t]


def assemble(where, probs, dscore, orders, shards, after):
    out = like((shards,) + probs[0].shape[1:])
    return in_vmem(
        functools.partial(assemble_kernel, [(k, o) for k, both in enumerate(orders) for o in both]), "assemble", (out, out), where, *probs, *dscore, scalars=1, after=after
    )


def masked(where, value, first, count):
    cols = value.shape[-1]
    masks = jnp.stack([lane_mask(where[2 + first + r], cols) for r in range(count)])
    return (value.reshape(count, HEAD_DIM, cols) * masks).astype(BF16)


def query_key_gradients(where, dscore, qk, grads):
    first = 0
    heads = qk[0].shape[1] // 2
    cols = qk[0].shape[-1]
    for part in qk:
        count = part.shape[0]
        flat = (count * HEAD_DIM, cols)
        some = pl.ds(first, count)
        for h in range(heads):
            ds = dscore[:, h].reshape(cols, cols)
            grads[some, h] = masked(where, mm(part[:, heads + h].reshape(flat), ds, NT), first, count)
            grads[some, heads + h] = masked(where, mm(part[:, h].reshape(flat), ds, NN), first, count)
        first += count


def value_gradient(where, probs, cot, h, first, count):
    cols = cot.shape[-1]
    g = cot[pl.ds(first, count), h * HEAD_DIM : (h + 1) * HEAD_DIM].reshape(count * HEAD_DIM, cols)
    return masked(where, mm(g, probs[:, h].reshape(cols, cols), NN), first, count)


def own_gradients_kernel(where, probs, dscore, qk, cot, grads):
    heads = qk.shape[1] // 2
    query_key_gradients(where, dscore, [qk], grads)
    for h in range(heads):
        grads[:, 2 * heads + h] = value_gradient(where, probs, cot, h, 0, cot.shape[0])


def own_gradients(where, probs, dscore, qk, cot):
    rows, two, _, cols = qk.shape
    return in_vmem(
        own_gradients_kernel,
        "own_gradients",
        (like((rows, two // 2 * 3, HEAD_DIM, cols)),),
        where,
        probs,
        dscore,
        qk,
        cot,
        scalars=1,
        limit=14,
        flops=3 * rows * two * HEAD_DIM * cols * cols,
    )[0]


def near_input_kernel(fars, pieces, where, own, weights, *refs):
    each = 2 + pieces
    far, outs, grads = refs[: each * fars], refs[each * fars : -1], refs[-1]
    near, share, columns = weights.shape
    rows, _, _, cols = own.shape
    count = rows // len(outs)
    some = grads.shape[2] * HEAD_DIM
    far = [far[i * each : (i + 1) * each] for i in range(fars)]
    for i, (dscore, _, *qk) in enumerate(far):
        query_key_gradients(where, dscore, qk, grads.at[i])
    for r in range(rows):
        left = weights[...].reshape(near * share, columns)
        total = mm(left, own[r].reshape(columns, cols), NN)
        for i, (_, natural, *_) in enumerate(far):
            left = natural[:, :, :some].reshape(near * share, some)
            total = total + mm(left, grads[i, r].reshape(some, cols), NN)
        outs[r // count][:, r % count] = total.astype(BF16).reshape(near, share, cols)


def near_input(where, grads, weights, far, chunk):
    rows, cols = grads.shape[0], grads.shape[-1]
    near, share, columns = weights.shape
    pieces = len(far[0][1])
    heads = far[0][1][0].shape[1]
    return in_vmem(
        functools.partial(near_input_kernel, len(far), pieces),
        "near_input",
        [like((near, chunk, share, cols))] * (rows // chunk),
        where,
        grads,
        weights,
        *[a for dscore, qk, natural in far for a in (dscore, natural, *qk)],
        scalars=1,
        scratch=(pltpu.VMEM((len(far), rows, heads, HEAD_DIM, cols), BF16),),
        limit=14,
        flops=2 * rows * cols * near * share * columns * (1 + len(far)),
    )


def far_input_kernel(first, fars, where, near, *refs):
    far, keep, give = refs[: 3 * fars], refs[-2], refs[-1]
    count, share, cols = keep.shape
    heads = far[0].shape[1]
    local = heads * HEAD_DIM
    grads = []
    for i in range(fars):
        probs, cot, _ = far[3 * i : 3 * i + 3]
        grads.append([value_gradient(where, probs, cot, h, first, count) for h in range(heads)])
    for r in range(count):
        total = near[:, r].astype(F32)
        for i, dv in enumerate(grads):
            left = far[3 * i + 2][:, :, 2 * local :].reshape(2 * share, local)
            right = jnp.concatenate([one[r] for one in dv], axis=0)
            total = total + mm(left, right, NN).reshape(2, share, cols)
        keep[r] = total[0].astype(keep.dtype)
        give[r] = total[1].astype(give.dtype)


def far_input(first, where, near, far, after):
    _, count, share, cols = near.shape
    out = like((count, share, cols))
    return in_vmem(
        functools.partial(far_input_kernel, first, len(far)),
        "far_input",
        (out, out),
        where,
        near,
        *[a for one in far for a in one],
        scalars=1,
        after=after,
        limit=14,
    )


def hold_kernel(values, out):
    out[...] = values[...]


def hold(values, after):
    return in_vmem(hold_kernel, "hold", (like(values.shape),), values, after=after)[0]


def finish_kernel(*refs):
    *terms, out, total, sems = refs
    copies = []
    first = 0
    for index in range(0, len(terms), 2):
        keep, got = terms[index : index + 2]
        some = pl.ds(first, keep.shape[0])
        total[some] = (keep[...].astype(F32) + got[...].astype(F32)).astype(BF16)
        copies.append(pltpu.make_async_copy(total.at[some], out.at[some], sems.at[index // 2]))
        copies[-1].start()
        first += keep.shape[0]
    for copy in copies:
        copy.wait()


def finish(chunks):
    _, share, cols = chunks[0][0].shape
    rows = sum(keep.shape[0] for keep, _ in chunks)
    terms = [a for chunk in chunks for a in chunk]
    return pl.pallas_call(
        finish_kernel,
        in_specs=[VMEM] * len(terms),
        out_specs=HBM,
        out_shape=like((rows, share, cols)),
        scratch_shapes=[pltpu.VMEM((rows, share, cols), BF16), pltpu.SemaphoreType.DMA((len(chunks),))],
        compiler_params=pltpu.CompilerParams(vmem_limit_bytes=12 * MIB),
        cost_estimate=cost(rows * share * cols, 6 * rows * share * cols),
        name="finish",
    )(*terms)


def weight_product(sheet, grads):
    rows, cols, width = sheet.shape
    columns = grads.shape[1] * HEAD_DIM
    left = [grads[r].reshape(columns, cols) for r in range(rows)]
    return mm(jnp.concatenate(left, axis=1), sheet[...].reshape(rows * cols, width), NN).T


def weight_kernel(where, sheet, grads, *rest):
    outs, full = rest[:-1], rest[-1]
    full[...] = weight_product(sheet, grads).reshape(full.shape)
    for j in range(full.shape[0]):
        first = 0
        for keep, give in zip(outs[::2], outs[1::2]):
            out = (keep, give)[j % 2]
            last = first + out.shape[-1]
            out[j // 2] = full[where[0] ^ j, :, first:last].astype(out.dtype)
            first = last


def whole_weight_kernel(where, sheet, grads, out):
    out[...] = weight_product(sheet, grads)


def weight_part(where, sheet, grads, cuts, shards, after):
    rows, cols, width = sheet.shape
    columns = grads.shape[1] * HEAD_DIM
    if shards == 1:
        kernel, outs, scratch = whole_weight_kernel, [like((width, columns), F32)], ()
    else:
        halves = [(shards // 2, width // shards, cut) for cut in cuts]
        kernel = weight_kernel
        outs = [o for half in halves for o in (like(half, F32), like(half))]
        scratch = (pltpu.VMEM((shards, width // shards, columns), F32),)
    return in_vmem(
        kernel,
        "weight_part",
        outs,
        where,
        sheet,
        grads,
        scalars=1,
        after=after,
        scratch=scratch,
        limit=18,
        flops=2 * rows * cols * width * columns,
    )


def last_kernel(keep, got, out):
    total = keep[0] + got[0].astype(F32)
    local = out.shape[-1]
    for index in range(out.shape[0]):
        out[index] = total[:, index * local : (index + 1) * local]


def last_sum(keep, got, local):
    shape = (keep.shape[2] // local, keep.shape[1], local)
    return in_vmem(last_kernel, "last_sum", (like(shape, F32),), keep, got)[0]


def body(sheet, w_query, w_key, w_value, cotangent, lengths):
    row_dev, cols, width = sheet.shape
    local = w_query.shape[1]
    n_rows = lax.axis_size("rows")
    n_heads = lax.axis_size("heads")
    scale = float(1.0 / (HEAD_DIM * row_dev * n_rows) ** 0.5)
    direct = n_rows <= 8
    shards = n_rows if direct else 1
    row_bits = [1 << b for b in range(n_rows.bit_length() - 1)]
    chunk = row_dev // 4

    me = jnp.stack([lax.axis_index("rows"), lax.axis_index("heads")]).astype(jnp.int32)
    where = jnp.concatenate([me, lengths])
    wq, wk, wv = w_query.T, w_key.T, w_value.T
    cot = jnp.swapaxes(cotangent, 1, 2)

    fars = range(2, n_heads, 2)
    far_cot = [flip(cot, "heads", f) for f in fars]
    fq, fk = [[flip(w, "heads", f) for f in fars] for w in (wq, wk)]

    up = row_bits if direct else []
    turn_about = up[1:] + up[:1]
    qk, held, *logits = query_key(where, sheet, wq, wk, turn_about)
    *dprob, = value_dprob(where, held, wv, cot, logits[-1:], up, fars, n_heads)
    dprob, halves = dprob[: -len(fars)], dprob[-len(fars) :]
    fv = [flip(half, "heads", f) for half, f in zip(halves, fars)]
    weights = turn(where, wq, wk, wv, n_heads, dprob[-1:])
    piece = row_dev // 4
    far_qk = [
        [far_query_key(r, piece, where, held, w[0], w[1], ()) for r in range(0, row_dev, piece)]
        for w in zip(fq, fk)
    ]
    if direct:
        logits = halve(*logits, "rows", turn_about)
        dprob = halve(*dprob, "rows", up)
        probs_own, dscore_own = softmax_back(logits, dprob, scale, [weights] + fq + fk)
        probs, probs_order = double(probs_own, "rows", up[::-1])
        dscore, dscore_order = double(dscore_own, "rows", turn_about[::-1])
        probs, dscore = assemble(where, probs, dscore, (probs_order, dscore_order), shards, sum(far_qk, far_cot))
    else:
        logits, dprob = lax.psum((logits, dprob), "rows")
        probs, dscore = softmax_back(logits, dprob, scale)
    far_dscore = [flip(dscore, "heads", f) for f in fars]
    grads = own_gradients(where, probs, dscore, qk, cot)
    parts = weight_part(where, held, grads, (3 * local,), shards, fv)
    probs = hold(probs, [parts[-1]] + far_dscore)
    far_probs = [flip(probs, "heads", f) for f in fars]
    far_natural = [turn(where, *w, n_heads, [probs]) for w in zip(fq, fk, fv)]
    near = near_input(where, grads, weights, list(zip(far_dscore, far_qk, far_natural)), chunk)
    ready = near[-1:]
    steps = []
    if direct:
        keep, give = parts
        for bit in row_bits[:-1]:
            give, keep = add_split(keep, flip(give, "rows", bit), ready)
            ready = ()
            steps.append([keep])
        weight_grad = last_sum(keep, flip(give, "rows", row_bits[-1]), local)
        weight_grad = jnp.swapaxes(weight_grad, 0, 1)
    else:
        weight_grad = lax.psum_scatter(parts[0], "rows", scatter_dimension=0, tiled=True)
        weight_grad = weight_grad.reshape(width // n_rows, 3, local)
    chunks = []
    for index, part in enumerate(near):
        far = list(zip(far_probs, far_cot, far_natural))
        after = steps[index // 2] if index // 2 < len(steps) else ()
        keep, give = far_input(index * chunk, where, part, far, after)
        chunks.append((keep, flip(give, "heads", 1)))
    return (jnp.swapaxes(finish(chunks), 1, 2), weight_grad)


def solution(mesh):
    in_specs = (
        P("rows", None, None),
        P(None, "heads"),
        P(None, "heads"),
        P(None, "heads"),
        P("rows", None, "heads"),
        P("rows"),
    )
    out_specs = (P("rows", None, "heads"), P("rows", None, "heads"))
    return jax.shard_map(body, mesh=mesh, in_specs=in_specs, out_specs=out_specs, check_vma=False)
```

```python
import functools
import math

import jax
import jax.numpy as jnp
from jax import lax
from jax.experimental import pallas as pl
from jax.experimental.pallas import tpu as pltpu
from jax.sharding import PartitionSpec as P

HEAD_DIM = 64
F32 = jnp.float32
BF16 = jnp.bfloat16
MIB = 1024 * 1024

NN = (((1,), (0,)), ((), ()))
NT = (((1,), (1,)), ((), ()))
TN = (((0,), (0,)), ((), ()))


def mm(a, b, dims):
    return lax.dot_general(a, b, dims, preferred_element_type=F32)


def flip(values, axis, bit):
    n = lax.axis_size(axis)
    return lax.ppermute(values, axis, [(s, s ^ bit) for s in range(n)])


def cost(flops, moved):
    return pl.CostEstimate(flops=int(flops), bytes_accessed=int(moved), transcendentals=0)


SMEM = pl.BlockSpec(memory_space=pltpu.SMEM)
VMEM = pl.BlockSpec(memory_space=pltpu.VMEM)
ANY = pl.BlockSpec(memory_space=pl.ANY)
HBM = pl.BlockSpec(memory_space=pltpu.HBM)


def like(shape, dtype=BF16):
    return jax.ShapeDtypeStruct(shape, dtype)


def place(a, stays):
    return pltpu.with_memory_space_constraint(a, pltpu.HBM) if stays else a


def in_vmem(kernel, name, out, *operands, scalars=0, streamed=0, after=(), scratch=(), limit=12, flops=0):
    many = len(after)

    def run(*refs):
        kernel(*refs[: len(operands)], *refs[len(operands) + many :])

    moved = 2 * sum(a.size for a in operands) + 2 * sum(o.size for o in out)
    held = len(operands) - scalars - streamed
    return pl.pallas_call(
        run,
        in_specs=[SMEM] * scalars + [HBM] * streamed + [VMEM] * held + [ANY] * many,
        out_specs=[VMEM] * len(out),
        out_shape=list(out),
        scratch_shapes=list(scratch),
        compiler_params=pltpu.CompilerParams(vmem_limit_bytes=limit * MIB),
        cost_estimate=cost(flops, moved),
        name=name,
    )(*[place(a, scalars <= i < scalars + streamed) for i, a in enumerate(operands)], *after)


def lane_mask(length, cols):
    return (lax.broadcasted_iota(jnp.int32, (1, cols), 1) < length).astype(F32)


def reorder(bits):
    return [sum(bit for b, bit in enumerate(bits) if t >> b & 1) for t in range(1 << len(bits))]


def put_shards(me, acc, bits, outs):
    for t, j in enumerate(reorder(bits)):
        out = outs[t % len(outs)]
        out[t // len(outs)] = acc[:, me ^ j].astype(out.dtype)


BLOCK = 4
STEP = 2
AHEAD = 4


def query_key_kernel(bits, fars, where, sheet, wq, wk, wv, qk, held, *rest):
    outs, staged, (wt, acc, sems) = rest[: -3 - len(fars)], rest[-3 - len(fars) : -3], rest[-3:]
    rows, cols, width = sheet.shape
    local = wq.shape[0]
    heads = local // HEAD_DIM
    copies = []

    def copy(source, target):
        copies.append(pltpu.make_async_copy(source, target, sems.at[len(copies)]))

    copy(wq, wt.at[:local])
    copy(wk, wt.at[local:])
    for first in range(0, rows, STEP):
        some = pl.ds(first, STEP)
        copy(sheet.at[some], held.at[some])
    for far, out in zip(fars, staged):
        near = out.shape[1] - width
        side = lax.shift_right_logical(where[1], 1) ^ (far // 2)
        some = pl.ds(pl.multiple_of(side * near, 128), near)
        copy(wk, out.at[:, pl.ds(0, width)])
        copy(wv.at[:, some], out.at[:, pl.ds(width, near)])
    for one in copies[:AHEAD]:
        one.start()
    copies[0].wait()
    copies[1].wait()
    flat = (BLOCK * HEAD_DIM, cols)
    for first in range(0, rows, BLOCK):
        for r in range(first, first + BLOCK):
            if r % STEP == 0:
                at = 2 + r // STEP
                copies[at].wait()
                last = at + AHEAD - 1 if r + STEP < rows else len(copies)
                for later in copies[at + AHEAD - 2 : last]:
                    later.start()
            value = (mm(wt[...], held[r], NT) * lane_mask(where[2 + r], cols)).astype(BF16)
            qk[r] = value.reshape(2 * heads, HEAD_DIM, cols)
        some = pl.ds(first, BLOCK)
        for h in range(heads):
            term = mm(qk[some, h].reshape(flat), qk[some, heads + h].reshape(flat), TN)
            term = term.reshape(acc.shape[1:])
            acc[h] = term if first == 0 else acc[h] + term
    put_shards(where[0], acc, bits, outs)
    started = 2 + rows // STEP
    for one in copies[started:]:
        one.wait()


def query_key(where, sheet, wq, wk, wv, bits, fars, devices):
    rows, cols, width = sheet.shape
    shards = 1 << len(bits)
    local = wq.shape[0]
    heads = local // HEAD_DIM
    return in_vmem(
        functools.partial(query_key_kernel, bits, fars),
        "query_key",
        [like((rows, 2 * heads, HEAD_DIM, cols)), like(sheet.shape)]
        + part_shapes(shards, heads, cols)
        + [like((local, width + 2 * width // devices))] * len(fars),
        where,
        sheet,
        wq,
        wk,
        wv,
        scalars=1,
        streamed=4,
        scratch=(
            pltpu.VMEM((2 * local, width), BF16),
            pltpu.VMEM((heads, shards, cols // shards, cols), F32),
            pltpu.SemaphoreType.DMA((2 + rows // STEP + 2 * len(fars),)),
        ),
        limit=14,
        flops=2 * rows * cols * local * (2 * width + cols),
    )


def value_kernel(bits, where, sheet, wv, cot, *rest):
    *outs, copied, acc = rest
    copied[...] = cot[...]
    rows, cols, width = sheet.shape
    local = wv.shape[0]
    heads = local // HEAD_DIM
    flat = (BLOCK * HEAD_DIM, cols)
    for first in range(0, rows, BLOCK):
        values = []
        for r in range(first, first + BLOCK):
            value = (mm(wv[...], sheet[r], NT) * lane_mask(where[2 + r], cols)).astype(BF16)
            values.append(value.reshape(heads, HEAD_DIM, cols))
        for h in range(heads):
            left = cot[pl.ds(first, BLOCK), h * HEAD_DIM : (h + 1) * HEAD_DIM].reshape(flat)
            right = jnp.concatenate([v[h] for v in values], axis=0)
            term = mm(left, right, TN).reshape(acc.shape[1:])
            acc[h] = term if first == 0 else acc[h] + term
    put_shards(where[0], acc, bits, outs)


def value_dprob(where, sheet, wv, cot, after, bits):
    rows, cols, width = sheet.shape
    shards = 1 << len(bits)
    local = wv.shape[0]
    heads = local // HEAD_DIM
    return in_vmem(
        functools.partial(value_kernel, bits),
        "value_dprob",
        part_shapes(shards, heads, cols) + [like(cot.shape)],
        where,
        sheet,
        wv,
        cot,
        scalars=1,
        after=after,
        scratch=(pltpu.VMEM((heads, shards, cols // shards, cols), F32),),
        limit=16,
        flops=16 * rows * cols * local * (width + cols),
    )


def turn_kernel(where, wq, *rest):
    *others, natural, query, key, value = rest
    near, share, columns = natural.shape
    local, width = wq.shape
    wk = others[0][:, :width]
    wv = others[1][...] if len(others) == 2 else others[0][:, width:]
    for index, (weight, held) in enumerate(((wq[...], query), (wk, key), (wv, value))):
        held[...] = weight.T.reshape(held.shape)
        mine = where[1] & (held.shape[0] - 1)
        for j in range(near):
            natural[j, :, index * local : (index + 1) * local] = held[mine ^ j]


def turn(where, wq, others, devices, after):
    local, width = wq.shape
    share = width // devices
    counts = (devices, devices, devices if len(others) == 2 else 2)
    return in_vmem(
        turn_kernel,
        "turn",
        (like((2, share, 3 * local)),),
        where,
        wq,
        *others,
        scalars=1,
        after=after,
        scratch=[pltpu.VMEM((count, share, local), BF16) for count in counts],
    )[0]


def far_query_key_kernel(where, sheet, wq, staged, qk):
    local = staged.shape[0]
    rows, cols, width = sheet.shape
    both = jnp.concatenate([wq[...], staged[:, :width]], axis=0)
    for r in range(rows):
        value = (mm(both, sheet[r], NT) * lane_mask(where[2 + r], cols)).astype(BF16)
        qk[r] = value.reshape(2 * local // HEAD_DIM, HEAD_DIM, cols)


def far_query_key(where, sheet, wq, staged, after):
    rows, cols, width = sheet.shape
    local = staged.shape[0]
    return in_vmem(
        far_query_key_kernel,
        "far_query_key",
        (like((rows, 2 * local // HEAD_DIM, HEAD_DIM, cols)),),
        where,
        sheet,
        wq,
        staged,
        scalars=1,
        after=after,
        flops=4 * rows * cols * local * width,
    )[0]


def part_shapes(shards, heads, cols):
    if shards == 1:
        return [like((1, heads, cols, cols), F32)]
    half = (shards // 2, heads, cols // shards, cols)
    return [like(half, F32), like(half)]


def add_split_kernel(keep, got, give_out, keep_out):
    for j in range(keep.shape[0]):
        total = keep[j].astype(F32) + got[j].astype(F32)
        out = give_out if j % 2 else keep_out
        out[j // 2] = total.astype(out.dtype)


def add_split(keep, got, after=()):
    half = (keep.shape[0] // 2,) + keep.shape[1:]
    return in_vmem(add_split_kernel, "add_split", (like(half), like(half, keep.dtype)), keep, got, after=after)


def halve(keep, give, axis, bits, after=()):
    after = list(after) + [()] * len(bits)
    for bit, waits in zip(bits[:-1], after):
        give, keep = add_split(keep, flip(give, axis, bit), waits)
    return keep, flip(give, axis, bits[-1])


def softmax_kernel(scale, *refs):
    *terms, probs_out, dscore_out = refs
    half = len(terms) // 2
    total = lambda some: functools.reduce(jnp.add, [t[0].astype(F32) for t in some])
    logits = total(terms[:half]) * scale
    dprob = total(terms[half:])
    shifted = jnp.exp(logits - jnp.max(logits, axis=-1, keepdims=True))
    probs = shifted / jnp.sum(shifted, axis=-1, keepdims=True)
    inner = jnp.sum(probs * dprob, axis=-1, keepdims=True)
    probs_out[0] = probs.astype(BF16)
    dscore_out[0] = (scale * probs * (dprob - inner)).astype(BF16)


def softmax_back(logits, dprob, scale, after=()):
    out = like(logits[0].shape)
    return in_vmem(
        functools.partial(softmax_kernel, scale), "softmax_back", (out, out), *logits, *dprob, limit=16, after=after
    )


def join_kernel(one, other, out):
    out[: one.shape[0]] = one[...]
    out[one.shape[0] :] = other[...]


def join(one, other, after):
    shape = (one.shape[0] + other.shape[0],) + one.shape[1:]
    return in_vmem(join_kernel, "join", (like(shape),), one, other, after=after)[0]


def double(values, axis, bits, after=()):
    order = [0]
    after = list(after) + [()] * len(bits)
    for bit, waits in zip(bits[:-1], after):
        values = join(values, flip(values, axis, bit), waits)
        order = order + [j ^ bit for j in order]
    other = flip(values, axis, bits[-1])
    return (values, other), (order, [j ^ bits[-1] for j in order])


def assemble_kernel(orders, where, *refs):
    *pieces, out = refs
    for piece, (kind, order) in zip(pieces, orders):
        for t, j in enumerate(order):
            out[kind, where[0] ^ j] = piece[t]


def assemble(where, probs, dscore, orders, shards, after):
    orders = [(kind, order) for kind, both in enumerate(orders) for order in both]
    out = like((2, shards) + probs[0].shape[1:])
    return in_vmem(
        functools.partial(assemble_kernel, orders),
        "assemble",
        (out,),
        where,
        *probs,
        *dscore,
        scalars=1,
        after=after,
    )[0]


def gradients(where, first, count, scores, qk, cot, grads):
    cols = qk.shape[-1]
    heads = qk.shape[1] // 2
    rows = pl.ds(first, count)
    flat = (count * HEAD_DIM, cols)
    split = (count, HEAD_DIM, cols)
    masks = jnp.stack([lane_mask(where[2 + first + r], cols) for r in range(count)])
    for h in range(heads):
        p, ds = [scores[kind, :, h].reshape(cols, cols) for kind in range(2)]
        g = cot[rows, h * HEAD_DIM : (h + 1) * HEAD_DIM].reshape(flat)
        dq = mm(qk[rows, heads + h].reshape(flat), ds, NT)
        dk = mm(qk[rows, h].reshape(flat), ds, NN)
        dv = mm(g, p, NN)
        for index, value in enumerate((dq, dk, dv)):
            grads[:, index * heads + h] = (value.reshape(split) * masks).astype(BF16)


def gradients_kernel(where, scores, qk, cot, grads):
    gradients(where, 0, qk.shape[0], scores, qk, cot, grads)


def all_gradients(where, scores, qk, cot, name, after):
    rows, two, _, cols = qk.shape
    return in_vmem(
        gradients_kernel,
        name,
        (like((rows, two // 2 * 3, HEAD_DIM, cols)),),
        where,
        scores,
        qk,
        cot,
        scalars=1,
        after=after,
        limit=14,
        flops=3 * rows * two * HEAD_DIM * cols * cols,
    )[0]


def own_input_kernel(grads, weights, out):
    near, share, columns = weights.shape
    left = weights[...].reshape(near * share, columns)
    for r in range(grads.shape[0]):
        part = mm(left, grads[r].reshape(columns, grads.shape[-1]), NN).astype(BF16)
        out[:, r] = part.reshape(near, share, grads.shape[-1])


def own_input(grads, weights, after):
    rows, cols = grads.shape[0], grads.shape[-1]
    near, share, columns = weights.shape
    return in_vmem(
        own_input_kernel,
        "own_input",
        (like((near, rows, share, cols)),),
        grads,
        weights,
        after=after,
        flops=2 * rows * cols * near * share * columns,
    )[0]


def far_input_kernel(first, own, *refs):
    *refs, keep, give = refs
    count, share, cols = keep.shape
    for r in range(count):
        total = own[:, first + r].astype(F32)
        for i in range(0, len(refs), 2):
            grads, weights = refs[i : i + 2]
            near, _, columns = weights.shape
            left = weights[...].reshape(near * share, columns)
            part = mm(left, grads[first + r].reshape(columns, cols), NN).astype(BF16)
            total = total + part.reshape(near, share, cols).astype(F32)
        keep[r] = total[0].astype(keep.dtype)
        give[r] = total[1].astype(give.dtype)


def far_input(first, count, own, far, after):
    _, rows, share, cols = own.shape
    columns = far[0][1].shape[-1]
    out = like((count, share, cols))
    return in_vmem(
        functools.partial(far_input_kernel, first),
        "far_input",
        (out, out),
        own,
        *[a for one in far for a in one],
        after=after,
        limit=14,
        flops=4 * len(far) * count * cols * columns * share,
    )


def finish_kernel(*refs):
    *terms, out, total, sems = refs
    copies = []
    first = 0
    for index in range(0, len(terms), 2):
        keep, got = terms[index : index + 2]
        some = pl.ds(first, keep.shape[0])
        total[some] = (keep[...].astype(F32) + got[...].astype(F32)).astype(BF16)
        copies.append(pltpu.make_async_copy(total.at[some], out.at[some], sems.at[index // 2]))
        copies[-1].start()
        first += keep.shape[0]
    for copy in copies:
        copy.wait()


def finish(chunks):
    _, share, cols = chunks[0][0].shape
    rows = sum(keep.shape[0] for keep, _ in chunks)
    terms = [a for chunk in chunks for a in chunk]
    return pl.pallas_call(
        finish_kernel,
        in_specs=[VMEM] * len(terms),
        out_specs=HBM,
        out_shape=like((rows, share, cols)),
        scratch_shapes=[pltpu.VMEM((rows, share, cols), BF16), pltpu.SemaphoreType.DMA((len(chunks),))],
        compiler_params=pltpu.CompilerParams(vmem_limit_bytes=12 * MIB),
        cost_estimate=cost(rows * share * cols, 6 * rows * share * cols),
        name="finish",
    )(*terms)


def weight_product(sheet, grads):
    rows, cols, width = sheet.shape
    columns = grads.shape[1] * HEAD_DIM
    left = [grads[r].reshape(columns, cols) for r in range(rows)]
    return mm(jnp.concatenate(left, axis=1), sheet[...].reshape(rows * cols, width), NN).T


def weight_kernel(where, sheet, grads, *rest):
    outs, full = rest[:-1], rest[-1]
    full[...] = weight_product(sheet, grads).reshape(full.shape)
    for j in range(full.shape[0]):
        first = 0
        for keep, give in zip(outs[::2], outs[1::2]):
            out = (keep, give)[j % 2]
            last = first + out.shape[-1]
            out[j // 2] = full[where[0] ^ j, :, first:last].astype(out.dtype)
            first = last


def whole_weight_kernel(where, sheet, grads, out):
    out[...] = weight_product(sheet, grads)


def weight_part(where, sheet, grads, cuts, shards, after):
    rows, cols, width = sheet.shape
    columns = grads.shape[1] * HEAD_DIM
    if shards == 1:
        kernel, outs, scratch = whole_weight_kernel, [like((width, columns), F32)], ()
    else:
        halves = [(shards // 2, width // shards, cut) for cut in cuts]
        kernel = weight_kernel
        outs = [o for half in halves for o in (like(half, F32), like(half))]
        scratch = (pltpu.VMEM((shards, width // shards, columns), F32),)
    return in_vmem(
        kernel,
        "weight_part",
        outs,
        where,
        sheet,
        grads,
        scalars=1,
        after=after,
        scratch=scratch,
        limit=18,
        flops=2 * rows * cols * width * columns,
    )


def last_kernel(*refs):
    *terms, out = refs
    total = [terms[i][0] + terms[i + 1][0].astype(F32) for i in range(0, len(terms), 2)]
    total = jnp.concatenate(total, axis=-1)
    local = out.shape[-1]
    for index in range(out.shape[0]):
        out[index] = total[:, index * local : (index + 1) * local]


def last_sum(halves, local, after):
    terms = [a for half in halves for a in half]
    columns = sum(keep.shape[2] for keep, _ in halves)
    shape = (columns // local, terms[0].shape[1], local)
    return in_vmem(last_kernel, "last_sum", (like(shape, F32),), *terms, after=after)[0]


def body(sheet, w_query, w_key, w_value, cotangent, lengths):
    row_dev, cols, width = sheet.shape
    local = w_query.shape[1]
    n_rows = lax.axis_size("rows")
    n_heads = lax.axis_size("heads")
    scale = float(1.0 / (HEAD_DIM * row_dev * n_rows) ** 0.5)
    direct = n_rows <= 8
    shards = n_rows if direct else 1
    row_bits = [1 << b for b in range(n_rows.bit_length() - 1)]
    chunk = row_dev // 4

    me = jnp.stack([lax.axis_index("rows"), lax.axis_index("heads")]).astype(jnp.int32)
    where = jnp.concatenate([me, lengths])
    wq, wk, wv = w_query.T, w_key.T, w_value.T
    cot = jnp.swapaxes(cotangent, 1, 2)

    fars = range(2, n_heads, 2)
    far_wq = [flip(wq, "heads", f) for f in fars]
    up = row_bits if direct else []
    turn_about = up[1:] + up[:1]
    qk, held, *logits = query_key(where, sheet, wq, wk, wv, turn_about, fars, n_heads)
    logits, staged = logits[: -len(fars)], logits[-len(fars) :]
    far_staged = [flip(a, "heads", f) for a, f in zip(staged, fars)]
    *dprob, copied = value_dprob(where, held, wv, cot, logits[-1:] + far_wq, up)
    far_cot = [flip(copied, "heads", f) for f in fars]
    weights = turn(where, wq, [wk, wv], n_heads, dprob[-1:])
    if direct:
        logits = halve(*logits, "rows", turn_about)
        dprob = halve(*dprob, "rows", up, [far_staged])
        probs, dscore = softmax_back(logits, dprob, scale, [weights] + far_staged)
        probs, probs_order = double(probs, "rows", up[::-1])
        dscore, dscore_order = double(dscore, "rows", turn_about[::-1])
        scores = assemble(where, probs, dscore, (probs_order, dscore_order), shards, ())
    else:
        logits, dprob = lax.psum((logits, dprob), "rows")
        scores = jnp.stack(softmax_back(logits, dprob, scale))
    far_scores = [flip(scores, "heads", f) for f in fars]
    grads = all_gradients(where, scores, qk, cot, "own_gradients", ())
    parts = weight_part(where, held, grads, (3 * local,), shards, ())
    ready = [parts[-1]]
    far_qk = [far_query_key(where, held, *w, ready + far_cot) for w in zip(far_wq, far_staged)]
    far_natural = [turn(where, w, [other], n_heads, ready) for w, other in zip(far_wq, far_staged)]
    own = own_input(grads, weights, ready)
    ready = [own] + far_qk + far_natural + far_scores
    steps = [[], []]
    if direct:
        keep, give = parts
        steps = []
        for bit in row_bits[:-1]:
            give, keep = add_split(keep, flip(give, "rows", bit), ready)
            steps.append([keep])
            ready = ()
        sums = last_sum([(keep, flip(give, "rows", row_bits[-1]))], local, ())
        weight_grad = jnp.swapaxes(sums, 0, 1)
    else:
        weight_grad = lax.psum_scatter(parts[0], "rows", scatter_dimension=0, tiled=True)
        weight_grad = weight_grad.reshape(width // n_rows, 3, local)

    far_grads = [
        all_gradients(where, *args, "far_gradients", steps[0])
        for args in zip(far_scores, far_qk, far_cot)
    ]
    chunks = []
    for index, first in enumerate(range(0, row_dev, chunk)):
        after = steps[-1] if index >= 2 else ()
        keep, give = far_input(first, chunk, own, list(zip(far_grads, far_natural)), after)
        chunks.append((keep, flip(give, "heads", 1)))
    return (jnp.swapaxes(finish(chunks), 1, 2), weight_grad)


def solution(mesh):
    in_specs = (
        P("rows", None, None),
        P(None, "heads"),
        P(None, "heads"),
        P(None, "heads"),
        P("rows", None, "heads"),
        P("rows"),
    )
    out_specs = (P("rows", None, "heads"), P("rows", None, "heads"))
    return jax.shard_map(body, mesh=mesh, in_specs=in_specs, out_specs=out_specs, check_vma=False)
```

```python
import functools
import math

import jax
import jax.numpy as jnp
from jax import lax
from jax.experimental import pallas as pl
from jax.experimental.pallas import tpu as pltpu
from jax.sharding import PartitionSpec as P

HEAD_DIM = 64
F32 = jnp.float32
BF16 = jnp.bfloat16
MIB = 1024 * 1024

NN = (((1,), (0,)), ((), ()))
NT = (((1,), (1,)), ((), ()))
TN = (((0,), (0,)), ((), ()))


def mm(a, b, dims):
    return lax.dot_general(a, b, dims, preferred_element_type=F32)


def flip(values, axis, bit):
    n = lax.axis_size(axis)
    return lax.ppermute(values, axis, [(s, s ^ bit) for s in range(n)])


def cost(flops, moved):
    return pl.CostEstimate(flops=int(flops), bytes_accessed=int(moved), transcendentals=0)


SMEM = pl.BlockSpec(memory_space=pltpu.SMEM)
VMEM = pl.BlockSpec(memory_space=pltpu.VMEM)
ANY = pl.BlockSpec(memory_space=pl.ANY)
HBM = pl.BlockSpec(memory_space=pltpu.HBM)


def like(shape, dtype=BF16):
    return jax.ShapeDtypeStruct(shape, dtype)


def place(a, stays):
    return pltpu.with_memory_space_constraint(a, pltpu.HBM) if stays else a


def in_vmem(kernel, name, out, *operands, scalars=0, streamed=0, after=(), scratch=(), limit=12, flops=0):
    many = len(after)

    def run(*refs):
        kernel(*refs[: len(operands)], *refs[len(operands) + many :])

    moved = 2 * sum(a.size for a in operands) + 2 * sum(o.size for o in out)
    held = len(operands) - scalars - streamed
    return pl.pallas_call(
        run,
        in_specs=[SMEM] * scalars + [HBM] * streamed + [VMEM] * held + [ANY] * many,
        out_specs=[VMEM] * len(out),
        out_shape=list(out),
        scratch_shapes=list(scratch),
        compiler_params=pltpu.CompilerParams(vmem_limit_bytes=limit * MIB),
        cost_estimate=cost(flops, moved),
        name=name,
    )(*[place(a, scalars <= i < scalars + streamed) for i, a in enumerate(operands)], *after)


def lane_mask(length, cols):
    return (lax.broadcasted_iota(jnp.int32, (1, cols), 1) < length).astype(F32)


def reorder(bits):
    return [sum(bit for b, bit in enumerate(bits) if t >> b & 1) for t in range(1 << len(bits))]


def put_shards(me, acc, bits, outs):
    for t, j in enumerate(reorder(bits)):
        out = outs[t % len(outs)]
        out[t // len(outs)] = acc[:, me ^ j].astype(out.dtype)


BLOCK = 4
STEP = 2
AHEAD = 4


def query_key_kernel(bits, fars, where, sheet, wq, wk, wv, qk, held, *rest):
    outs, staged, (wt, acc, sems) = rest[: -3 - len(fars)], rest[-3 - len(fars) : -3], rest[-3:]
    rows, cols, width = sheet.shape
    local = wq.shape[0]
    heads = local // HEAD_DIM
    copies = []

    def copy(source, target):
        copies.append(pltpu.make_async_copy(source, target, sems.at[len(copies)]))

    copy(wq, wt.at[:local])
    copy(wk, wt.at[local:])
    for first in range(0, rows, STEP):
        some = pl.ds(first, STEP)
        copy(sheet.at[some], held.at[some])
    for far, out in zip(fars, staged):
        near = out.shape[1] - width
        side = lax.shift_right_logical(where[1], 1) ^ (far // 2)
        some = pl.ds(pl.multiple_of(side * near, 128), near)
        copy(wk, out.at[:, pl.ds(0, width)])
        copy(wv.at[:, some], out.at[:, pl.ds(width, near)])
    for one in copies[:AHEAD]:
        one.start()
    copies[0].wait()
    copies[1].wait()
    flat = (BLOCK * HEAD_DIM, cols)
    for first in range(0, rows, BLOCK):
        for r in range(first, first + BLOCK):
            if r % STEP == 0:
                at = 2 + r // STEP
                copies[at].wait()
                last = at + AHEAD - 1 if r + STEP < rows else len(copies)
                for later in copies[at + AHEAD - 2 : last]:
                    later.start()
            value = (mm(wt[...], held[r], NT) * lane_mask(where[2 + r], cols)).astype(BF16)
            qk[r] = value.reshape(2 * heads, HEAD_DIM, cols)
        some = pl.ds(first, BLOCK)
        for h in range(heads):
            term = mm(qk[some, h].reshape(flat), qk[some, heads + h].reshape(flat), TN)
            term = term.reshape(acc.shape[1:])
            acc[h] = term if first == 0 else acc[h] + term
    put_shards(where[0], acc, bits, outs)
    started = 2 + rows // STEP
    for one in copies[started:]:
        one.wait()


def query_key(where, sheet, wq, wk, wv, bits, fars, devices):
    rows, cols, width = sheet.shape
    shards = 1 << len(bits)
    local = wq.shape[0]
    heads = local // HEAD_DIM
    return in_vmem(
        functools.partial(query_key_kernel, bits, fars),
        "query_key",
        [like((rows, 2 * heads, HEAD_DIM, cols)), like(sheet.shape)]
        + part_shapes(shards, heads, cols)
        + [like((local, width + 2 * width // devices))] * len(fars),
        where,
        sheet,
        wq,
        wk,
        wv,
        scalars=1,
        streamed=4,
        scratch=(
            pltpu.VMEM((2 * local, width), BF16),
            pltpu.VMEM((heads, shards, cols // shards, cols), F32),
            pltpu.SemaphoreType.DMA((2 + rows // STEP + 2 * len(fars),)),
        ),
        limit=14,
        flops=2 * rows * cols * local * (2 * width + cols),
    )


def value_kernel(bits, where, sheet, wv, cot, *rest):
    outs, acc = rest[:-1], rest[-1]
    rows, cols, width = sheet.shape
    local = wv.shape[0]
    heads = local // HEAD_DIM
    flat = (BLOCK * HEAD_DIM, cols)
    for first in range(0, rows, BLOCK):
        values = []
        for r in range(first, first + BLOCK):
            value = (mm(wv[...], sheet[r], NT) * lane_mask(where[2 + r], cols)).astype(BF16)
            values.append(value.reshape(heads, HEAD_DIM, cols))
        for h in range(heads):
            left = cot[pl.ds(first, BLOCK), h * HEAD_DIM : (h + 1) * HEAD_DIM].reshape(flat)
            right = jnp.concatenate([v[h] for v in values], axis=0)
            term = mm(left, right, TN).reshape(acc.shape[1:])
            acc[h] = term if first == 0 else acc[h] + term
    put_shards(where[0], acc, bits, outs)


def value_dprob(where, sheet, wv, cot, after, bits):
    rows, cols, width = sheet.shape
    shards = 1 << len(bits)
    local = wv.shape[0]
    heads = local // HEAD_DIM
    return in_vmem(
        functools.partial(value_kernel, bits),
        "value_dprob",
        part_shapes(shards, heads, cols),
        where,
        sheet,
        wv,
        cot,
        scalars=1,
        after=after,
        scratch=(pltpu.VMEM((heads, shards, cols // shards, cols), F32),),
        limit=16,
        flops=16 * rows * cols * local * (width + cols),
    )


def turn_kernel(where, wq, *rest):
    *others, natural, query, key, value = rest
    near, share, columns = natural.shape
    local, width = wq.shape
    wk = others[0][:, :width]
    wv = others[1][...] if len(others) == 2 else others[0][:, width:]
    for index, (weight, held) in enumerate(((wq[...], query), (wk, key), (wv, value))):
        held[...] = weight.T.reshape(held.shape)
        mine = where[1] & (held.shape[0] - 1)
        for j in range(near):
            natural[j, :, index * local : (index + 1) * local] = held[mine ^ j]


def turn(where, wq, others, devices, after):
    local, width = wq.shape
    share = width // devices
    counts = (devices, devices, devices if len(others) == 2 else 2)
    return in_vmem(
        turn_kernel,
        "turn",
        (like((2, share, 3 * local)),),
        where,
        wq,
        *others,
        scalars=1,
        after=after,
        scratch=[pltpu.VMEM((count, share, local), BF16) for count in counts],
    )[0]


def far_query_key_kernel(where, sheet, wq, staged, qk):
    local = staged.shape[0]
    rows, cols, width = sheet.shape
    both = jnp.concatenate([wq[...], staged[:, :width]], axis=0)
    for r in range(rows):
        value = (mm(both, sheet[r], NT) * lane_mask(where[2 + r], cols)).astype(BF16)
        qk[r] = value.reshape(2 * local // HEAD_DIM, HEAD_DIM, cols)


def far_query_key(where, sheet, wq, staged, after):
    rows, cols, width = sheet.shape
    local = staged.shape[0]
    return in_vmem(
        far_query_key_kernel,
        "far_query_key",
        (like((rows, 2 * local // HEAD_DIM, HEAD_DIM, cols)),),
        where,
        sheet,
        wq,
        staged,
        scalars=1,
        after=after,
        flops=4 * rows * cols * local * width,
    )[0]


def part_shapes(shards, heads, cols):
    if shards == 1:
        return [like((1, heads, cols, cols), F32)]
    half = (shards // 2, heads, cols // shards, cols)
    return [like(half, F32), like(half)]


def hold_kernel(values, out):
    out[...] = values[...]


def hold(values, after):
    return in_vmem(hold_kernel, "hold", (like(values.shape),), values, after=after)[0]


def add_split_kernel(keep, got, give_out, keep_out):
    for j in range(keep.shape[0]):
        total = keep[j].astype(F32) + got[j].astype(F32)
        out = give_out if j % 2 else keep_out
        out[j // 2] = total.astype(out.dtype)


def add_split(keep, got, after=()):
    half = (keep.shape[0] // 2,) + keep.shape[1:]
    return in_vmem(add_split_kernel, "add_split", (like(half), like(half, keep.dtype)), keep, got, after=after)


def halve(keep, give, axis, bits, after=()):
    after = list(after) + [()] * len(bits)
    for bit, waits in zip(bits[:-1], after):
        give, keep = add_split(keep, flip(give, axis, bit), waits)
    return keep, flip(give, axis, bits[-1])


def softmax_kernel(scale, *refs):
    *terms, probs_out, dscore_out = refs
    half = len(terms) // 2
    total = lambda some: functools.reduce(jnp.add, [t[0].astype(F32) for t in some])
    logits = total(terms[:half]) * scale
    dprob = total(terms[half:])
    shifted = jnp.exp(logits - jnp.max(logits, axis=-1, keepdims=True))
    probs = shifted / jnp.sum(shifted, axis=-1, keepdims=True)
    inner = jnp.sum(probs * dprob, axis=-1, keepdims=True)
    probs_out[0] = probs.astype(BF16)
    dscore_out[0] = (scale * probs * (dprob - inner)).astype(BF16)


def softmax_back(logits, dprob, scale, after=()):
    out = like(logits[0].shape)
    return in_vmem(
        functools.partial(softmax_kernel, scale), "softmax_back", (out, out), *logits, *dprob, limit=16, after=after
    )


def join_kernel(one, other, out):
    out[: one.shape[0]] = one[...]
    out[one.shape[0] :] = other[...]


def join(one, other, after):
    shape = (one.shape[0] + other.shape[0],) + one.shape[1:]
    return in_vmem(join_kernel, "join", (like(shape),), one, other, after=after)[0]


def double(values, axis, bits, after=()):
    order = [0]
    after = list(after) + [()] * len(bits)
    for bit, waits in zip(bits[:-1], after):
        values = join(values, flip(values, axis, bit), waits)
        order = order + [j ^ bit for j in order]
    other = flip(values, axis, bits[-1])
    return (values, other), (order, [j ^ bits[-1] for j in order])


def assemble_kernel(orders, where, *refs):
    *pieces, out = refs
    for piece, (kind, order) in zip(pieces, orders):
        for t, j in enumerate(order):
            out[kind, where[0] ^ j] = piece[t]


def assemble(where, probs, dscore, orders, shards, after):
    orders = [(kind, order) for kind, both in enumerate(orders) for order in both]
    out = like((2, shards) + probs[0].shape[1:])
    return in_vmem(
        functools.partial(assemble_kernel, orders),
        "assemble",
        (out,),
        where,
        *probs,
        *dscore,
        scalars=1,
        after=after,
    )[0]


def gradients(where, first, count, scores, qk, cot, grads):
    cols = qk.shape[-1]
    heads = qk.shape[1] // 2
    rows = pl.ds(first, count)
    flat = (count * HEAD_DIM, cols)
    split = (count, HEAD_DIM, cols)
    masks = jnp.stack([lane_mask(where[2 + first + r], cols) for r in range(count)])
    for h in range(heads):
        p, ds = [scores[kind, :, h].reshape(cols, cols) for kind in range(2)]
        g = cot[rows, h * HEAD_DIM : (h + 1) * HEAD_DIM].reshape(flat)
        dq = mm(qk[rows, heads + h].reshape(flat), ds, NT)
        dk = mm(qk[rows, h].reshape(flat), ds, NN)
        dv = mm(g, p, NN)
        for index, value in enumerate((dq, dk, dv)):
            grads[:, index * heads + h] = (value.reshape(split) * masks).astype(BF16)


def gradients_kernel(where, scores, qk, cot, grads):
    gradients(where, 0, qk.shape[0], scores, qk, cot, grads)


def all_gradients(where, scores, qk, cot, name, after):
    rows, two, _, cols = qk.shape
    return in_vmem(
        gradients_kernel,
        name,
        (like((rows, two // 2 * 3, HEAD_DIM, cols)),),
        where,
        scores,
        qk,
        cot,
        scalars=1,
        after=after,
        limit=14,
        flops=3 * rows * two * HEAD_DIM * cols * cols,
    )[0]


def own_input_kernel(grads, weights, out):
    near, share, columns = weights.shape
    left = weights[...].reshape(near * share, columns)
    for r in range(grads.shape[0]):
        part = mm(left, grads[r].reshape(columns, grads.shape[-1]), NN).astype(BF16)
        out[:, r] = part.reshape(near, share, grads.shape[-1])


def own_input(grads, weights, after):
    rows, cols = grads.shape[0], grads.shape[-1]
    near, share, columns = weights.shape
    return in_vmem(
        own_input_kernel,
        "own_input",
        (like((near, rows, share, cols)),),
        grads,
        weights,
        after=after,
        flops=2 * rows * cols * near * share * columns,
    )[0]


def far_input_kernel(first, own, *refs):
    *refs, keep, give = refs
    count, share, cols = keep.shape
    for r in range(count):
        total = own[:, first + r].astype(F32)
        for i in range(0, len(refs), 2):
            grads, weights = refs[i : i + 2]
            near, _, columns = weights.shape
            left = weights[...].reshape(near * share, columns)
            part = mm(left, grads[first + r].reshape(columns, cols), NN).astype(BF16)
            total = total + part.reshape(near, share, cols).astype(F32)
        keep[r] = total[0].astype(keep.dtype)
        give[r] = total[1].astype(give.dtype)


def far_input(first, count, own, far, after):
    _, rows, share, cols = own.shape
    columns = far[0][1].shape[-1]
    out = like((count, share, cols))
    return in_vmem(
        functools.partial(far_input_kernel, first),
        "far_input",
        (out, out),
        own,
        *[a for one in far for a in one],
        after=after,
        limit=14,
        flops=4 * len(far) * count * cols * columns * share,
    )


def finish_kernel(*refs):
    *terms, out, total, sems = refs
    copies = []
    first = 0
    for index in range(0, len(terms), 2):
        keep, got = terms[index : index + 2]
        some = pl.ds(first, keep.shape[0])
        total[some] = (keep[...].astype(F32) + got[...].astype(F32)).astype(BF16)
        copies.append(pltpu.make_async_copy(total.at[some], out.at[some], sems.at[index // 2]))
        copies[-1].start()
        first += keep.shape[0]
    for copy in copies:
        copy.wait()


def finish(chunks):
    _, share, cols = chunks[0][0].shape
    rows = sum(keep.shape[0] for keep, _ in chunks)
    terms = [a for chunk in chunks for a in chunk]
    return pl.pallas_call(
        finish_kernel,
        in_specs=[VMEM] * len(terms),
        out_specs=HBM,
        out_shape=like((rows, share, cols)),
        scratch_shapes=[pltpu.VMEM((rows, share, cols), BF16), pltpu.SemaphoreType.DMA((len(chunks),))],
        compiler_params=pltpu.CompilerParams(vmem_limit_bytes=12 * MIB),
        cost_estimate=cost(rows * share * cols, 6 * rows * share * cols),
        name="finish",
    )(*terms)


def weight_product(sheet, grads):
    rows, cols, width = sheet.shape
    columns = grads.shape[1] * HEAD_DIM
    left = [grads[r].reshape(columns, cols) for r in range(rows)]
    return mm(jnp.concatenate(left, axis=1), sheet[...].reshape(rows * cols, width), NN).T


def weight_kernel(where, sheet, grads, *rest):
    outs, full = rest[:-1], rest[-1]
    full[...] = weight_product(sheet, grads).reshape(full.shape)
    for j in range(full.shape[0]):
        first = 0
        for keep, give in zip(outs[::2], outs[1::2]):
            out = (keep, give)[j % 2]
            last = first + out.shape[-1]
            out[j // 2] = full[where[0] ^ j, :, first:last].astype(out.dtype)
            first = last


def whole_weight_kernel(where, sheet, grads, out):
    out[...] = weight_product(sheet, grads)


def weight_part(where, sheet, grads, cuts, shards, after):
    rows, cols, width = sheet.shape
    columns = grads.shape[1] * HEAD_DIM
    if shards == 1:
        kernel, outs, scratch = whole_weight_kernel, [like((width, columns), F32)], ()
    else:
        halves = [(shards // 2, width // shards, cut) for cut in cuts]
        kernel = weight_kernel
        outs = [o for half in halves for o in (like(half, F32), like(half))]
        scratch = (pltpu.VMEM((shards, width // shards, columns), F32),)
    return in_vmem(
        kernel,
        "weight_part",
        outs,
        where,
        sheet,
        grads,
        scalars=1,
        after=after,
        scratch=scratch,
        limit=18,
        flops=2 * rows * cols * width * columns,
    )


def last_kernel(_, keep, got, out):
    total = keep[0] + got[0].astype(F32)
    local = out.shape[-1]
    for index in range(out.shape[0]):
        out[index] = total[:, index * local : (index + 1) * local]


def last_sum(before, keep, got, local):
    shape = (keep.shape[2] // local, keep.shape[1], local)
    return in_vmem(last_kernel, "last_sum", (like(shape, F32),), before, keep, got, streamed=1)[0]


def body(sheet, w_query, w_key, w_value, cotangent, lengths):
    row_dev, cols, width = sheet.shape
    local = w_query.shape[1]
    n_rows = lax.axis_size("rows")
    n_heads = lax.axis_size("heads")
    scale = float(1.0 / (HEAD_DIM * row_dev * n_rows) ** 0.5)
    direct = n_rows <= 8
    shards = n_rows if direct else 1
    row_bits = [1 << b for b in range(n_rows.bit_length() - 1)]
    chunk = row_dev // 4

    me = jnp.stack([lax.axis_index("rows"), lax.axis_index("heads")]).astype(jnp.int32)
    where = jnp.concatenate([me, lengths])
    wq, wk, wv = w_query.T, w_key.T, w_value.T
    cot = jnp.swapaxes(cotangent, 1, 2)

    fars = range(2, n_heads, 2)
    far_wq = [flip(wq, "heads", f) for f in fars]
    up = row_bits if direct else []
    turn_about = up[1:] + up[:1]
    qk, held, *logits = query_key(where, sheet, wq, wk, wv, turn_about, fars, n_heads)
    logits, staged = logits[: -len(fars)], logits[-len(fars) :]
    far_staged = [flip(a, "heads", f) for a, f in zip(staged, fars)]
    dprob = value_dprob(where, held, wv, cot, logits[-1:] + far_wq, up)
    weights = turn(where, wq, [wk, wv], n_heads, dprob[-1:])
    if direct:
        give, keep = add_split(logits[0], flip(logits[1], "rows", turn_about[0]), dprob[1:])
        later = [give]
        logits = halve(keep, give, "rows", turn_about[1:])
        dprob = halve(*dprob, "rows", up, [far_staged])
        probs, dscore = softmax_back(logits, dprob, scale, [weights] + far_staged)
        probs, probs_order = double(probs, "rows", up[::-1])
        dscore, dscore_order = double(dscore, "rows", turn_about[::-1])
        scores = assemble(where, probs, dscore, (probs_order, dscore_order), shards, ())
    else:
        later = [weights]
        logits, dprob = lax.psum((logits, dprob), "rows")
        scores = jnp.stack(softmax_back(logits, dprob, scale))
    far_cot = [flip(hold(cot, later), "heads", f) for f in fars]
    far_scores = [flip(scores, "heads", f) for f in fars]
    grads = all_gradients(where, scores, qk, cot, "own_gradients", ())
    parts = weight_part(where, held, grads, (3 * local,), shards, ())
    ready = [parts[-1]]
    far_qk = [far_query_key(where, held, *w, ready + far_cot) for w in zip(far_wq, far_staged)]
    far_natural = [turn(where, w, [other], n_heads, ready) for w, other in zip(far_wq, far_staged)]
    own = own_input(grads, weights, ready)
    ready = [own] + far_qk + far_natural + far_scores
    steps = [[], []]
    if direct:
        keep, give = parts
        steps = []
        for bit in row_bits[:-1]:
            give, keep = add_split(keep, flip(give, "rows", bit), ready)
            steps.append([keep])
            ready = ()
        last = keep, flip(give, "rows", row_bits[-1])
    else:
        weight_grad = lax.psum_scatter(parts[0], "rows", scatter_dimension=0, tiled=True)
        weight_grad = weight_grad.reshape(width // n_rows, 3, local)

    far_grads = [
        all_gradients(where, *args, "far_gradients", steps[0])
        for args in zip(far_scores, far_qk, far_cot)
    ]
    chunks = []
    for index, first in enumerate(range(0, row_dev, chunk)):
        after = steps[-1] if index >= 2 else ()
        keep, give = far_input(first, chunk, own, list(zip(far_grads, far_natural)), after)
        chunks.append((keep, flip(give, "heads", 1)))
    out = finish(chunks)
    if direct:
        weight_grad = jnp.swapaxes(last_sum(out, *last, local), 0, 1)
    return (jnp.swapaxes(out, 1, 2), weight_grad)


def solution(mesh):
    in_specs = (
        P("rows", None, None),
        P(None, "heads"),
        P(None, "heads"),
        P(None, "heads"),
        P("rows", None, "heads"),
        P("rows"),
    )
    out_specs = (P("rows", None, "heads"), P("rows", None, "heads"))
    return jax.shard_map(body, mesh=mesh, in_specs=in_specs, out_specs=out_specs, check_vma=False)
```

```python
import functools
import math

import jax
import jax.numpy as jnp
from jax import lax
from jax.experimental import pallas as pl
from jax.experimental.pallas import tpu as pltpu
from jax.sharding import PartitionSpec as P

HEAD_DIM = 64
F32 = jnp.float32
BF16 = jnp.bfloat16
MIB = 1024 * 1024

NN = (((1,), (0,)), ((), ()))
NT = (((1,), (1,)), ((), ()))
TN = (((0,), (0,)), ((), ()))


def mm(a, b, dims):
    return lax.dot_general(a, b, dims, preferred_element_type=F32)


def flip(values, axis, bit):
    n = lax.axis_size(axis)
    return lax.ppermute(values, axis, [(s, s ^ bit) for s in range(n)])


def cost(flops, moved):
    return pl.CostEstimate(flops=int(flops), bytes_accessed=int(moved), transcendentals=0)


SMEM = pl.BlockSpec(memory_space=pltpu.SMEM)
VMEM = pl.BlockSpec(memory_space=pltpu.VMEM)
ANY = pl.BlockSpec(memory_space=pl.ANY)
HBM = pl.BlockSpec(memory_space=pltpu.HBM)


def like(shape, dtype=BF16):
    return jax.ShapeDtypeStruct(shape, dtype)


def place(a, stays):
    return pltpu.with_memory_space_constraint(a, pltpu.HBM) if stays else a


def in_vmem(kernel, name, out, *operands, scalars=0, streamed=0, after=(), scratch=(), limit=12, flops=0):
    many = len(after)

    def run(*refs):
        kernel(*refs[: len(operands)], *refs[len(operands) + many :])

    moved = 2 * sum(a.size for a in operands) + 2 * sum(o.size for o in out)
    held = len(operands) - scalars - streamed
    return pl.pallas_call(
        run,
        in_specs=[SMEM] * scalars + [HBM] * streamed + [VMEM] * held + [ANY] * many,
        out_specs=[VMEM] * len(out),
        out_shape=list(out),
        scratch_shapes=list(scratch),
        compiler_params=pltpu.CompilerParams(vmem_limit_bytes=limit * MIB),
        cost_estimate=cost(flops, moved),
        name=name,
    )(*[place(a, scalars <= i < scalars + streamed) for i, a in enumerate(operands)], *after)


def lane_mask(length, cols):
    return (lax.broadcasted_iota(jnp.int32, (1, cols), 1) < length).astype(F32)


def reorder(bits):
    return [sum(bit for b, bit in enumerate(bits) if t >> b & 1) for t in range(1 << len(bits))]


def put_shards(me, acc, bits, outs):
    for t, j in enumerate(reorder(bits)):
        out = outs[t % len(outs)]
        out[t // len(outs)] = acc[:, me ^ j].astype(out.dtype)


BLOCK = 4
STEP = 2
AHEAD = 6


def query_key_kernel(bits, fars, me, lengths, sheet, wq, wk, wv, qk, held, seen, *rest):
    outs, staged, (wt, acc, number, sems) = rest[: -4 - len(fars)], rest[-4 - len(fars) : -4], rest[-4:]
    rows, cols, width = sheet.shape
    local = wq.shape[0]
    heads = local // HEAD_DIM
    copies = []

    def copy(source, target):
        copies.append(pltpu.make_async_copy(source, target, sems.at[len(copies)]))

    copy(lengths, number)
    copy(lengths, seen)
    copy(wq, wt.at[:local])
    copy(wk, wt.at[local:])
    for first in range(0, rows, STEP):
        some = pl.ds(first, STEP)
        copy(sheet.at[some], held.at[some])
    for far, out in zip(fars, staged):
        near = out.shape[1] - width
        side = lax.shift_right_logical(me[1], 1) ^ (far // 2)
        some = pl.ds(pl.multiple_of(side * near, 128), near)
        copy(wk, out.at[:, pl.ds(0, width)])
        copy(wv.at[:, some], out.at[:, pl.ds(width, near)])
    for one in copies[:AHEAD]:
        one.start()
    for one in copies[:4]:
        one.wait()
    flat = (BLOCK * HEAD_DIM, cols)
    for first in range(0, rows, BLOCK):
        for r in range(first, first + BLOCK):
            if r % STEP == 0:
                at = 4 + r // STEP
                copies[at].wait()
                last = at + AHEAD - 3 if r + STEP < rows else len(copies)
                for later in copies[at + AHEAD - 4 : last]:
                    later.start()
            value = (mm(wt[...], held[r], NT) * lane_mask(number[0, r], cols)).astype(BF16)
            qk[r] = value.reshape(2 * heads, HEAD_DIM, cols)
        some = pl.ds(first, BLOCK)
        for h in range(heads):
            term = mm(qk[some, h].reshape(flat), qk[some, heads + h].reshape(flat), TN)
            term = term.reshape(acc.shape[1:])
            acc[h] = term if first == 0 else acc[h] + term
    put_shards(me[0], acc, bits, outs)
    started = 4 + rows // STEP
    for one in copies[started:]:
        one.wait()


def query_key(me, lengths, sheet, wq, wk, wv, bits, fars, devices):
    rows, cols, width = sheet.shape
    shards = 1 << len(bits)
    local = wq.shape[0]
    heads = local // HEAD_DIM
    return in_vmem(
        functools.partial(query_key_kernel, bits, fars),
        "query_key",
        [like((rows, 2 * heads, HEAD_DIM, cols)), like(sheet.shape), like(lengths.shape, jnp.int32)]
        + part_shapes(shards, heads, cols)
        + [like((local, width + 2 * width // devices))] * len(fars),
        me,
        lengths,
        sheet,
        wq,
        wk,
        wv,
        scalars=1,
        streamed=5,
        scratch=(
            pltpu.VMEM((2 * local, width), BF16),
            pltpu.VMEM((heads, shards, cols // shards, cols), F32),
            pltpu.SMEM(lengths.shape, jnp.int32),
            pltpu.SemaphoreType.DMA((4 + rows // STEP + 2 * len(fars),)),
        ),
        limit=14,
        flops=2 * rows * cols * local * (2 * width + cols),
    )


def value_kernel(bits, where, sheet, wv, cot, *rest):
    outs, acc = rest[:-1], rest[-1]
    rows, cols, width = sheet.shape
    local = wv.shape[0]
    heads = local // HEAD_DIM
    flat = (BLOCK * HEAD_DIM, cols)
    for first in range(0, rows, BLOCK):
        values = []
        for r in range(first, first + BLOCK):
            value = (mm(wv[...], sheet[r], NT) * lane_mask(where[2 + r], cols)).astype(BF16)
            values.append(value.reshape(heads, HEAD_DIM, cols))
        for h in range(heads):
            left = cot[pl.ds(first, BLOCK), h * HEAD_DIM : (h + 1) * HEAD_DIM].reshape(flat)
            right = jnp.concatenate([v[h] for v in values], axis=0)
            term = mm(left, right, TN).reshape(acc.shape[1:])
            acc[h] = term if first == 0 else acc[h] + term
    put_shards(where[0], acc, bits, outs)


def value_dprob(where, sheet, wv, cot, after, bits):
    rows, cols, width = sheet.shape
    shards = 1 << len(bits)
    local = wv.shape[0]
    heads = local // HEAD_DIM
    return in_vmem(
        functools.partial(value_kernel, bits),
        "value_dprob",
        part_shapes(shards, heads, cols),
        where,
        sheet,
        wv,
        cot,
        scalars=1,
        after=after,
        scratch=(pltpu.VMEM((heads, shards, cols // shards, cols), F32),),
        limit=16,
        flops=16 * rows * cols * local * (width + cols),
    )


def turn_kernel(where, wq, *rest):
    *others, natural, query, key, value = rest
    near, share, columns = natural.shape
    local, width = wq.shape
    wk = others[0][:, :width]
    wv = others[1][...] if len(others) == 2 else others[0][:, width:]
    for index, (weight, held) in enumerate(((wq[...], query), (wk, key), (wv, value))):
        held[...] = weight.T.reshape(held.shape)
        mine = where[1] & (held.shape[0] - 1)
        for j in range(near):
            natural[j, :, index * local : (index + 1) * local] = held[mine ^ j]


def turn(where, wq, others, devices, after):
    local, width = wq.shape
    share = width // devices
    counts = (devices, devices, devices if len(others) == 2 else 2)
    return in_vmem(
        turn_kernel,
        "turn",
        (like((2, share, 3 * local)),),
        where,
        wq,
        *others,
        scalars=1,
        after=after,
        scratch=[pltpu.VMEM((count, share, local), BF16) for count in counts],
    )[0]


def far_query_key_kernel(where, sheet, wq, staged, qk):
    local = staged.shape[0]
    rows, cols, width = sheet.shape
    both = jnp.concatenate([wq[...], staged[:, :width]], axis=0)
    for r in range(rows):
        value = (mm(both, sheet[r], NT) * lane_mask(where[2 + r], cols)).astype(BF16)
        qk[r] = value.reshape(2 * local // HEAD_DIM, HEAD_DIM, cols)


def far_query_key(where, sheet, wq, staged, after):
    rows, cols, width = sheet.shape
    local = staged.shape[0]
    return in_vmem(
        far_query_key_kernel,
        "far_query_key",
        (like((rows, 2 * local // HEAD_DIM, HEAD_DIM, cols)),),
        where,
        sheet,
        wq,
        staged,
        scalars=1,
        after=after,
        flops=4 * rows * cols * local * width,
    )[0]


def part_shapes(shards, heads, cols):
    if shards == 1:
        return [like((1, heads, cols, cols), F32)]
    half = (shards // 2, heads, cols // shards, cols)
    return [like(half, F32), like(half)]


def hold_kernel(values, out):
    out[...] = values[...]


def hold(values, after):
    return in_vmem(hold_kernel, "hold", (like(values.shape),), values, after=after)[0]


def add_split_kernel(keep, got, give_out, keep_out):
    for j in range(keep.shape[0]):
        total = keep[j].astype(F32) + got[j].astype(F32)
        out = give_out if j % 2 else keep_out
        out[j // 2] = total.astype(out.dtype)


def add_split(keep, got, after=()):
    half = (keep.shape[0] // 2,) + keep.shape[1:]
    return in_vmem(add_split_kernel, "add_split", (like(half), like(half, keep.dtype)), keep, got, after=after)


def halve(keep, give, axis, bits, after=()):
    after = list(after) + [()] * len(bits)
    for bit, waits in zip(bits[:-1], after):
        give, keep = add_split(keep, flip(give, axis, bit), waits)
    return keep, flip(give, axis, bits[-1])


def softmax_kernel(scale, *refs):
    *terms, probs_out, dscore_out = refs
    half = len(terms) // 2
    total = lambda some: functools.reduce(jnp.add, [t[0].astype(F32) for t in some])
    logits = total(terms[:half]) * scale
    dprob = total(terms[half:])
    shifted = jnp.exp(logits - jnp.max(logits, axis=-1, keepdims=True))
    probs = shifted / jnp.sum(shifted, axis=-1, keepdims=True)
    inner = jnp.sum(probs * dprob, axis=-1, keepdims=True)
    probs_out[0] = probs.astype(BF16)
    dscore_out[0] = (scale * probs * (dprob - inner)).astype(BF16)


def softmax_back(logits, dprob, scale, after=()):
    out = like(logits[0].shape)
    return in_vmem(
        functools.partial(softmax_kernel, scale), "softmax_back", (out, out), *logits, *dprob, limit=16, after=after
    )


def join_kernel(one, other, out):
    out[: one.shape[0]] = one[...]
    out[one.shape[0] :] = other[...]


def join(one, other, after):
    shape = (one.shape[0] + other.shape[0],) + one.shape[1:]
    return in_vmem(join_kernel, "join", (like(shape),), one, other, after=after)[0]


def double(values, axis, bits, after=()):
    order = [0]
    after = list(after) + [()] * len(bits)
    for bit, waits in zip(bits[:-1], after):
        values = join(values, flip(values, axis, bit), waits)
        order = order + [j ^ bit for j in order]
    other = flip(values, axis, bits[-1])
    return (values, other), (order, [j ^ bits[-1] for j in order])


def assemble_kernel(orders, where, *refs):
    *pieces, out = refs
    for piece, (kind, order) in zip(pieces, orders):
        for t, j in enumerate(order):
            out[kind, where[0] ^ j] = piece[t]


def assemble(where, probs, dscore, orders, shards, after):
    orders = [(kind, order) for kind, both in enumerate(orders) for order in both]
    out = like((2, shards) + probs[0].shape[1:])
    return in_vmem(
        functools.partial(assemble_kernel, orders),
        "assemble",
        (out,),
        where,
        *probs,
        *dscore,
        scalars=1,
        after=after,
    )[0]


def gradients(where, first, count, scores, qk, cot, grads):
    cols = qk.shape[-1]
    heads = qk.shape[1] // 2
    rows = pl.ds(first, count)
    flat = (count * HEAD_DIM, cols)
    split = (count, HEAD_DIM, cols)
    masks = jnp.stack([lane_mask(where[2 + first + r], cols) for r in range(count)])
    for h in range(heads):
        p, ds = [scores[kind, :, h].reshape(cols, cols) for kind in range(2)]
        g = cot[rows, h * HEAD_DIM : (h + 1) * HEAD_DIM].reshape(flat)
        dq = mm(qk[rows, heads + h].reshape(flat), ds, NT)
        dk = mm(qk[rows, h].reshape(flat), ds, NN)
        dv = mm(g, p, NN)
        for index, value in enumerate((dq, dk, dv)):
            grads[:, index * heads + h] = (value.reshape(split) * masks).astype(BF16)


def gradients_kernel(where, scores, qk, cot, grads):
    gradients(where, 0, qk.shape[0], scores, qk, cot, grads)


def all_gradients(where, scores, qk, cot, name, after):
    rows, two, _, cols = qk.shape
    return in_vmem(
        gradients_kernel,
        name,
        (like((rows, two // 2 * 3, HEAD_DIM, cols)),),
        where,
        scores,
        qk,
        cot,
        scalars=1,
        after=after,
        limit=14,
        flops=3 * rows * two * HEAD_DIM * cols * cols,
    )[0]


def own_input_kernel(grads, weights, out):
    near, share, columns = weights.shape
    left = weights[...].reshape(near * share, columns)
    for r in range(grads.shape[0]):
        part = mm(left, grads[r].reshape(columns, grads.shape[-1]), NN).astype(BF16)
        out[:, r] = part.reshape(near, share, grads.shape[-1])


def own_input(grads, weights, after):
    rows, cols = grads.shape[0], grads.shape[-1]
    near, share, columns = weights.shape
    return in_vmem(
        own_input_kernel,
        "own_input",
        (like((near, rows, share, cols)),),
        grads,
        weights,
        after=after,
        flops=2 * rows * cols * near * share * columns,
    )[0]


def far_input_kernel(first, own, *refs):
    *refs, keep, give = refs
    count, share, cols = keep.shape
    for r in range(count):
        total = own[:, first + r].astype(F32)
        for i in range(0, len(refs), 2):
            grads, weights = refs[i : i + 2]
            near, _, columns = weights.shape
            left = weights[...].reshape(near * share, columns)
            part = mm(left, grads[first + r].reshape(columns, cols), NN).astype(BF16)
            total = total + part.reshape(near, share, cols).astype(F32)
        keep[r] = total[0].astype(keep.dtype)
        give[r] = total[1].astype(give.dtype)


def far_input(first, count, own, far, after):
    _, rows, share, cols = own.shape
    columns = far[0][1].shape[-1]
    out = like((count, share, cols))
    return in_vmem(
        functools.partial(far_input_kernel, first),
        "far_input",
        (out, out),
        own,
        *[a for one in far for a in one],
        after=after,
        limit=14,
        flops=4 * len(far) * count * cols * columns * share,
    )


def finish_kernel(*refs):
    *terms, out, total, sems = refs
    copies = []
    first = 0
    for index in range(0, len(terms), 2):
        keep, got = terms[index : index + 2]
        some = pl.ds(first, keep.shape[0])
        total[some] = (keep[...].astype(F32) + got[...].astype(F32)).astype(BF16)
        copies.append(pltpu.make_async_copy(total.at[some], out.at[some], sems.at[index // 2]))
        copies[-1].start()
        first += keep.shape[0]
    for copy in copies:
        copy.wait()


def finish(chunks):
    _, share, cols = chunks[0][0].shape
    rows = sum(keep.shape[0] for keep, _ in chunks)
    terms = [a for chunk in chunks for a in chunk]
    return pl.pallas_call(
        finish_kernel,
        in_specs=[VMEM] * len(terms),
        out_specs=HBM,
        out_shape=like((rows, share, cols)),
        scratch_shapes=[pltpu.VMEM((rows, share, cols), BF16), pltpu.SemaphoreType.DMA((len(chunks),))],
        compiler_params=pltpu.CompilerParams(vmem_limit_bytes=12 * MIB),
        cost_estimate=cost(rows * share * cols, 6 * rows * share * cols),
        name="finish",
    )(*terms)


def weight_product(sheet, grads):
    rows, cols, width = sheet.shape
    columns = grads.shape[1] * HEAD_DIM
    left = [grads[r].reshape(columns, cols) for r in range(rows)]
    return mm(jnp.concatenate(left, axis=1), sheet[...].reshape(rows * cols, width), NN).T


def weight_kernel(where, sheet, grads, *rest):
    outs, full = rest[:-1], rest[-1]
    full[...] = weight_product(sheet, grads).reshape(full.shape)
    for j in range(full.shape[0]):
        first = 0
        for keep, give in zip(outs[::2], outs[1::2]):
            out = (keep, give)[j % 2]
            last = first + out.shape[-1]
            out[j // 2] = full[where[0] ^ j, :, first:last].astype(out.dtype)
            first = last


def whole_weight_kernel(where, sheet, grads, out):
    out[...] = weight_product(sheet, grads)


def weight_part(where, sheet, grads, cuts, shards, after):
    rows, cols, width = sheet.shape
    columns = grads.shape[1] * HEAD_DIM
    if shards == 1:
        kernel, outs, scratch = whole_weight_kernel, [like((width, columns), F32)], ()
    else:
        halves = [(shards // 2, width // shards, cut) for cut in cuts]
        kernel = weight_kernel
        outs = [o for half in halves for o in (like(half, F32), like(half))]
        scratch = (pltpu.VMEM((shards, width // shards, columns), F32),)
    return in_vmem(
        kernel,
        "weight_part",
        outs,
        where,
        sheet,
        grads,
        scalars=1,
        after=after,
        scratch=scratch,
        limit=18,
        flops=2 * rows * cols * width * columns,
    )


def last_kernel(_, keep, got, out):
    total = keep[0] + got[0].astype(F32)
    local = out.shape[-1]
    for index in range(out.shape[0]):
        out[index] = total[:, index * local : (index + 1) * local]


def last_sum(before, keep, got, local):
    shape = (keep.shape[2] // local, keep.shape[1], local)
    return in_vmem(last_kernel, "last_sum", (like(shape, F32),), before, keep, got, streamed=1)[0]


def body(sheet, w_query, w_key, w_value, cotangent, lengths):
    row_dev, cols, width = sheet.shape
    local = w_query.shape[1]
    n_rows = lax.axis_size("rows")
    n_heads = lax.axis_size("heads")
    scale = float(1.0 / (HEAD_DIM * row_dev * n_rows) ** 0.5)
    direct = n_rows <= 8
    shards = n_rows if direct else 1
    row_bits = [1 << b for b in range(n_rows.bit_length() - 1)]
    chunk = row_dev // 2

    me = jnp.stack([lax.axis_index("rows"), lax.axis_index("heads")]).astype(jnp.int32)
    wq, wk, wv = w_query.T, w_key.T, w_value.T
    cot = jnp.swapaxes(cotangent, 1, 2)

    fars = range(2, n_heads, 2)
    far_wq = [flip(wq, "heads", f) for f in fars]
    up = row_bits if direct else []
    turn_about = up[1:] + up[:1]
    parts = query_key(me, lengths.reshape(1, row_dev), sheet, wq, wk, wv, turn_about, fars, n_heads)
    qk, held, seen, *logits = parts
    where = jnp.concatenate([me, seen.reshape(row_dev)])
    logits, staged = logits[: -len(fars)], logits[-len(fars) :]
    far_staged = [flip(a, "heads", f) for a, f in zip(staged, fars)]
    dprob = value_dprob(where, held, wv, cot, logits[-1:] + far_wq, up)
    weights = turn(where, wq, [wk, wv], n_heads, dprob[-1:])
    if direct:
        give, keep = add_split(logits[0], flip(logits[1], "rows", turn_about[0]), dprob[1:])
        later = [give]
        logits = halve(keep, give, "rows", turn_about[1:])
        dprob = halve(*dprob, "rows", up, [far_staged])
        probs, dscore = softmax_back(logits, dprob, scale, [weights] + far_staged)
        probs, probs_order = double(probs, "rows", up[::-1])
        dscore, dscore_order = double(dscore, "rows", turn_about[::-1])
        scores = assemble(where, probs, dscore, (probs_order, dscore_order), shards, ())
    else:
        later = [weights]
        logits, dprob = lax.psum((logits, dprob), "rows")
        scores = jnp.stack(softmax_back(logits, dprob, scale))
    far_cot = [flip(hold(cot, later), "heads", f) for f in fars]
    far_scores = [flip(scores, "heads", f) for f in fars]
    grads = all_gradients(where, scores, qk, cot, "own_gradients", ())
    parts = weight_part(where, held, grads, (3 * local,), shards, ())
    ready = [parts[-1]]
    far_qk = [far_query_key(where, held, *w, ready + far_cot) for w in zip(far_wq, far_staged)]
    far_natural = [turn(where, w, [other], n_heads, ready) for w, other in zip(far_wq, far_staged)]
    own = own_input(grads, weights, ready)
    ready = [own] + far_qk + far_natural + far_scores
    steps = [[], []]
    if direct:
        keep, give = parts
        steps = []
        for bit in row_bits[:-1]:
            give, keep = add_split(keep, flip(give, "rows", bit), ready)
            steps.append([keep])
            ready = ()
        last = keep, flip(give, "rows", row_bits[-1])
    else:
        weight_grad = lax.psum_scatter(parts[0], "rows", scatter_dimension=0, tiled=True)
        weight_grad = weight_grad.reshape(width // n_rows, 3, local)

    far_grads = [
        all_gradients(where, *args, "far_gradients", steps[0])
        for args in zip(far_scores, far_qk, far_cot)
    ]
    chunks = []
    for index, first in enumerate(range(0, row_dev, chunk)):
        after = steps[-1] if index else ()
        keep, give = far_input(first, chunk, own, list(zip(far_grads, far_natural)), after)
        chunks.append((keep, flip(give, "heads", 1)))
    out = finish(chunks)
    if direct:
        weight_grad = jnp.swapaxes(last_sum(out, *last, local), 0, 1)
    return (jnp.swapaxes(out, 1, 2), weight_grad)


def solution(mesh):
    in_specs = (
        P("rows", None, None),
        P(None, "heads"),
        P(None, "heads"),
        P(None, "heads"),
        P("rows", None, "heads"),
        P("rows"),
    )
    out_specs = (P("rows", None, "heads"), P("rows", None, "heads"))
    return jax.shard_map(body, mesh=mesh, in_specs=in_specs, out_specs=out_specs, check_vma=False)
```

```python
import functools
import math

import jax
import jax.numpy as jnp
from jax import lax
from jax.experimental import pallas as pl
from jax.experimental.pallas import tpu as pltpu
from jax.sharding import PartitionSpec as P

HEAD_DIM = 64
F32 = jnp.float32
BF16 = jnp.bfloat16
MIB = 1024 * 1024

NN = (((1,), (0,)), ((), ()))
NT = (((1,), (1,)), ((), ()))
TN = (((0,), (0,)), ((), ()))


def mm(a, b, dims):
    return lax.dot_general(a, b, dims, preferred_element_type=F32)


def flip(values, axis, bit):
    n = lax.axis_size(axis)
    return lax.ppermute(values, axis, [(s, s ^ bit) for s in range(n)])


def cost(flops, moved):
    return pl.CostEstimate(flops=int(flops), bytes_accessed=int(moved), transcendentals=0)


SMEM = pl.BlockSpec(memory_space=pltpu.SMEM)
VMEM = pl.BlockSpec(memory_space=pltpu.VMEM)
ANY = pl.BlockSpec(memory_space=pl.ANY)
HBM = pl.BlockSpec(memory_space=pltpu.HBM)


def like(shape, dtype=BF16):
    return jax.ShapeDtypeStruct(shape, dtype)


def place(a, stays):
    return pltpu.with_memory_space_constraint(a, pltpu.HBM) if stays else a


def in_vmem(kernel, name, out, *operands, scalars=0, streamed=0, after=(), scratch=(), limit=12, flops=0):
    many = len(after)

    def run(*refs):
        kernel(*refs[: len(operands)], *refs[len(operands) + many :])

    moved = 2 * sum(a.size for a in operands) + 2 * sum(o.size for o in out)
    held = len(operands) - scalars - streamed
    return pl.pallas_call(
        run,
        in_specs=[SMEM] * scalars + [HBM] * streamed + [VMEM] * held + [ANY] * many,
        out_specs=[VMEM] * len(out),
        out_shape=list(out),
        scratch_shapes=list(scratch),
        compiler_params=pltpu.CompilerParams(vmem_limit_bytes=limit * MIB),
        cost_estimate=cost(flops, moved),
        name=name,
    )(*[place(a, scalars <= i < scalars + streamed) for i, a in enumerate(operands)], *after)


def lane_mask(length, cols):
    return (lax.broadcasted_iota(jnp.int32, (1, cols), 1) < length).astype(F32)


def reorder(bits):
    return [sum(bit for b, bit in enumerate(bits) if t >> b & 1) for t in range(1 << len(bits))]


def put_shards(me, acc, bits, outs):
    for t, j in enumerate(reorder(bits)):
        out = outs[t % len(outs)]
        out[t // len(outs)] = acc[:, me ^ j].astype(out.dtype)


BLOCK = 4
STEP = 2
AHEAD = 6


def query_key_kernel(bits, me, lengths, sheet, wq, wk, qk, held, seen, *rest):
    outs, (wt, acc, number, sems) = rest[:-4], rest[-4:]
    rows, cols, width = sheet.shape
    local = wq.shape[0]
    heads = local // HEAD_DIM
    copies = []

    def copy(source, target):
        copies.append(pltpu.make_async_copy(source, target, sems.at[len(copies)]))

    copy(lengths, number)
    copy(lengths, seen)
    copy(wq, wt.at[:local])
    copy(wk, wt.at[local:])
    for first in range(0, rows, STEP):
        some = pl.ds(first, STEP)
        copy(sheet.at[some], held.at[some])
    for one in copies[:AHEAD]:
        one.start()
    for one in copies[:4]:
        one.wait()
    flat = (BLOCK * HEAD_DIM, cols)
    for first in range(0, rows, BLOCK):
        for r in range(first, first + BLOCK):
            if r % STEP == 0:
                at = 4 + r // STEP
                copies[at].wait()
                for later in copies[at + AHEAD - 4 : at + AHEAD - 3]:
                    later.start()
            value = (mm(wt[...], held[r], NT) * lane_mask(number[0, r], cols)).astype(BF16)
            qk[r] = value.reshape(2 * heads, HEAD_DIM, cols)
        some = pl.ds(first, BLOCK)
        for h in range(heads):
            term = mm(qk[some, h].reshape(flat), qk[some, heads + h].reshape(flat), TN)
            term = term.reshape(acc.shape[1:])
            acc[h] = term if first == 0 else acc[h] + term
    put_shards(me[0], acc, bits, outs)


def query_key(me, lengths, sheet, wq, wk, bits):
    rows, cols, width = sheet.shape
    shards = 1 << len(bits)
    local = wq.shape[0]
    heads = local // HEAD_DIM
    return in_vmem(
        functools.partial(query_key_kernel, bits),
        "query_key",
        [like((rows, 2 * heads, HEAD_DIM, cols)), like(sheet.shape), like(lengths.shape, jnp.int32)]
        + part_shapes(shards, heads, cols),
        me,
        lengths,
        sheet,
        wq,
        wk,
        scalars=1,
        streamed=4,
        scratch=(
            pltpu.VMEM((2 * local, width), BF16),
            pltpu.VMEM((heads, shards, cols // shards, cols), F32),
            pltpu.SMEM(lengths.shape, jnp.int32),
            pltpu.SemaphoreType.DMA((4 + rows // STEP,)),
        ),
        limit=14,
        flops=2 * rows * cols * local * (2 * width + cols),
    )


def value_kernel(bits, fars, where, sheet, wv, cot, *rest):
    outs, halves, acc = rest[: -1 - len(fars)], rest[-1 - len(fars) : -1], rest[-1]
    rows, cols, width = sheet.shape
    for far, half in zip(fars, halves):
        near = half.shape[1]
        side = lax.shift_right_logical(where[1], 1) ^ (far // 2)
        for s in range(width // near):
            @pl.when(side == s)
            def _():
                half[...] = wv[:, s * near : (s + 1) * near]
    local = wv.shape[0]
    heads = local // HEAD_DIM
    flat = (BLOCK * HEAD_DIM, cols)
    for first in range(0, rows, BLOCK):
        values = []
        for r in range(first, first + BLOCK):
            value = (mm(wv[...], sheet[r], NT) * lane_mask(where[2 + r], cols)).astype(BF16)
            values.append(value.reshape(heads, HEAD_DIM, cols))
        for h in range(heads):
            left = cot[pl.ds(first, BLOCK), h * HEAD_DIM : (h + 1) * HEAD_DIM].reshape(flat)
            right = jnp.concatenate([v[h] for v in values], axis=0)
            term = mm(left, right, TN).reshape(acc.shape[1:])
            acc[h] = term if first == 0 else acc[h] + term
    put_shards(where[0], acc, bits, outs)


def value_dprob(where, sheet, wv, cot, after, bits, fars, devices):
    rows, cols, width = sheet.shape
    shards = 1 << len(bits)
    local = wv.shape[0]
    heads = local // HEAD_DIM
    return in_vmem(
        functools.partial(value_kernel, bits, fars),
        "value_dprob",
        part_shapes(shards, heads, cols) + [like((local, 2 * width // devices))] * len(fars),
        where,
        sheet,
        wv,
        cot,
        scalars=1,
        after=after,
        scratch=(pltpu.VMEM((heads, shards, cols // shards, cols), F32),),
        limit=16,
        flops=16 * rows * cols * local * (width + cols),
    )


def turn_kernel(where, wq, wk, wv, natural, *full):
    near, share, columns = natural.shape
    local = wq.shape[0]
    for index, (weight, held) in enumerate(zip((wq, wk, wv), full)):
        held[...] = weight[...].T.reshape(held.shape)
        mine = where[1] & (held.shape[0] - 1)
        for j in range(near):
            natural[j, :, index * local : (index + 1) * local] = held[mine ^ j]


def turn(where, wq, wk, wv, devices, after):
    local, width = wq.shape
    share = width // devices
    return in_vmem(
        turn_kernel,
        "turn",
        (like((2, share, 3 * local)),),
        where,
        wq,
        wk,
        wv,
        scalars=1,
        after=after,
        scratch=[pltpu.VMEM((w.shape[1] // share, share, local), BF16) for w in (wq, wk, wv)],
    )[0]


def far_query_key_kernel(where, sheet, wq, wk, qk):
    local = wq.shape[0]
    rows, cols, _ = sheet.shape
    both = jnp.concatenate([wq[...], wk[...]], axis=0)
    for r in range(rows):
        value = (mm(both, sheet[r], NT) * lane_mask(where[2 + r], cols)).astype(BF16)
        qk[r] = value.reshape(2 * local // HEAD_DIM, HEAD_DIM, cols)


def far_query_key(where, sheet, wq, wk, after):
    rows, cols, width = sheet.shape
    local = wq.shape[0]
    return in_vmem(
        far_query_key_kernel,
        "far_query_key",
        (like((rows, 2 * local // HEAD_DIM, HEAD_DIM, cols)),),
        where,
        sheet,
        wq,
        wk,
        scalars=1,
        after=after,
        flops=4 * rows * cols * local * width,
    )[0]


def part_shapes(shards, heads, cols):
    if shards == 1:
        return [like((1, heads, cols, cols), F32)]
    half = (shards // 2, heads, cols // shards, cols)
    return [like(half, F32), like(half)]


def hold_kernel(values, out):
    out[...] = values[...]


def hold(values, after):
    return in_vmem(hold_kernel, "hold", (like(values.shape),), values, after=after)[0]


def add_split_kernel(keep, got, give_out, keep_out):
    for j in range(keep.shape[0]):
        total = keep[j].astype(F32) + got[j].astype(F32)
        out = give_out if j % 2 else keep_out
        out[j // 2] = total.astype(out.dtype)


def add_split(keep, got, after=()):
    half = (keep.shape[0] // 2,) + keep.shape[1:]
    return in_vmem(add_split_kernel, "add_split", (like(half), like(half, keep.dtype)), keep, got, after=after)


def halve(keep, give, axis, bits, after=()):
    after = list(after) + [()] * len(bits)
    for bit, waits in zip(bits[:-1], after):
        give, keep = add_split(keep, flip(give, axis, bit), waits)
    return keep, flip(give, axis, bits[-1])


def softmax_kernel(scale, *refs):
    *terms, probs_out, dscore_out = refs
    half = len(terms) // 2
    total = lambda some: functools.reduce(jnp.add, [t[0].astype(F32) for t in some])
    logits = total(terms[:half]) * scale
    dprob = total(terms[half:])
    shifted = jnp.exp(logits - jnp.max(logits, axis=-1, keepdims=True))
    probs = shifted / jnp.sum(shifted, axis=-1, keepdims=True)
    inner = jnp.sum(probs * dprob, axis=-1, keepdims=True)
    probs_out[0] = probs.astype(BF16)
    dscore_out[0] = (scale * probs * (dprob - inner)).astype(BF16)


def softmax_back(logits, dprob, scale, after=()):
    out = like(logits[0].shape)
    return in_vmem(
        functools.partial(softmax_kernel, scale), "softmax_back", (out, out), *logits, *dprob, limit=16, after=after
    )


def join_kernel(one, other, out):
    out[: one.shape[0]] = one[...]
    out[one.shape[0] :] = other[...]


def join(one, other, after):
    shape = (one.shape[0] + other.shape[0],) + one.shape[1:]
    return in_vmem(join_kernel, "join", (like(shape),), one, other, after=after)[0]


def double(values, axis, bits, after=()):
    order = [0]
    after = list(after) + [()] * len(bits)
    for bit, waits in zip(bits[:-1], after):
        values = join(values, flip(values, axis, bit), waits)
        order = order + [j ^ bit for j in order]
    other = flip(values, axis, bits[-1])
    return (values, other), (order, [j ^ bits[-1] for j in order])


def assemble_kernel(orders, where, *refs):
    *pieces, out = refs
    for piece, (kind, order) in zip(pieces, orders):
        for t, j in enumerate(order):
            out[kind, where[0] ^ j] = piece[t]


def assemble(where, probs, dscore, orders, shards, after):
    orders = [(kind, order) for kind, both in enumerate(orders) for order in both]
    out = like((2, shards) + probs[0].shape[1:])
    return in_vmem(
        functools.partial(assemble_kernel, orders),
        "assemble",
        (out,),
        where,
        *probs,
        *dscore,
        scalars=1,
        after=after,
    )[0]


def gradients(where, first, count, scores, qk, cot, grads):
    cols = qk.shape[-1]
    heads = qk.shape[1] // 2
    rows = pl.ds(first, count)
    flat = (count * HEAD_DIM, cols)
    split = (count, HEAD_DIM, cols)
    masks = jnp.stack([lane_mask(where[2 + first + r], cols) for r in range(count)])
    for h in range(heads):
        p, ds = [scores[kind, :, h].reshape(cols, cols) for kind in range(2)]
        g = cot[rows, h * HEAD_DIM : (h + 1) * HEAD_DIM].reshape(flat)
        dq = mm(qk[rows, heads + h].reshape(flat), ds, NT)
        dk = mm(qk[rows, h].reshape(flat), ds, NN)
        dv = mm(g, p, NN)
        for index, value in enumerate((dq, dk, dv)):
            grads[:, index * heads + h] = (value.reshape(split) * masks).astype(BF16)


def gradients_kernel(where, scores, qk, cot, grads):
    gradients(where, 0, qk.shape[0], scores, qk, cot, grads)


def all_gradients(where, scores, qk, cot, name, after):
    rows, two, _, cols = qk.shape
    return in_vmem(
        gradients_kernel,
        name,
        (like((rows, two // 2 * 3, HEAD_DIM, cols)),),
        where,
        scores,
        qk,
        cot,
        scalars=1,
        after=after,
        limit=14,
        flops=3 * rows * two * HEAD_DIM * cols * cols,
    )[0]


def own_input_kernel(grads, weights, out):
    near, share, columns = weights.shape
    left = weights[...].reshape(near * share, columns)
    for r in range(grads.shape[0]):
        part = mm(left, grads[r].reshape(columns, grads.shape[-1]), NN).astype(BF16)
        out[:, r] = part.reshape(near, share, grads.shape[-1])


def own_input(grads, weights, after):
    rows, cols = grads.shape[0], grads.shape[-1]
    near, share, columns = weights.shape
    return in_vmem(
        own_input_kernel,
        "own_input",
        (like((near, rows, share, cols)),),
        grads,
        weights,
        after=after,
        flops=2 * rows * cols * near * share * columns,
    )[0]


def far_input_kernel(first, own, *refs):
    *refs, keep, give = refs
    count, share, cols = keep.shape
    for r in range(count):
        total = own[:, first + r].astype(F32)
        for i in range(0, len(refs), 2):
            grads, weights = refs[i : i + 2]
            near, _, columns = weights.shape
            left = weights[...].reshape(near * share, columns)
            part = mm(left, grads[first + r].reshape(columns, cols), NN).astype(BF16)
            total = total + part.reshape(near, share, cols).astype(F32)
        keep[r] = total[0].astype(keep.dtype)
        give[r] = total[1].astype(give.dtype)


def far_input(first, count, own, far, after):
    _, rows, share, cols = own.shape
    columns = far[0][1].shape[-1]
    out = like((count, share, cols))
    return in_vmem(
        functools.partial(far_input_kernel, first),
        "far_input",
        (out, out),
        own,
        *[a for one in far for a in one],
        after=after,
        limit=14,
        flops=4 * len(far) * count * cols * columns * share,
    )


def finish_kernel(*refs):
    *terms, out, total, sems = refs
    copies = []
    first = 0
    for index in range(0, len(terms), 2):
        keep, got = terms[index : index + 2]
        some = pl.ds(first, keep.shape[0])
        total[some] = (keep[...].astype(F32) + got[...].astype(F32)).astype(BF16)
        copies.append(pltpu.make_async_copy(total.at[some], out.at[some], sems.at[index // 2]))
        copies[-1].start()
        first += keep.shape[0]
    for copy in copies:
        copy.wait()


def finish(chunks):
    _, share, cols = chunks[0][0].shape
    rows = sum(keep.shape[0] for keep, _ in chunks)
    terms = [a for chunk in chunks for a in chunk]
    return pl.pallas_call(
        finish_kernel,
        in_specs=[VMEM] * len(terms),
        out_specs=HBM,
        out_shape=like((rows, share, cols)),
        scratch_shapes=[pltpu.VMEM((rows, share, cols), BF16), pltpu.SemaphoreType.DMA((len(chunks),))],
        compiler_params=pltpu.CompilerParams(vmem_limit_bytes=12 * MIB),
        cost_estimate=cost(rows * share * cols, 6 * rows * share * cols),
        name="finish",
    )(*terms)


def weight_product(sheet, grads):
    rows, cols, width = sheet.shape
    columns = grads.shape[1] * HEAD_DIM
    left = [grads[r].reshape(columns, cols) for r in range(rows)]
    return mm(jnp.concatenate(left, axis=1), sheet[...].reshape(rows * cols, width), NN).T


def weight_kernel(where, sheet, grads, *rest):
    outs, full = rest[:-1], rest[-1]
    full[...] = weight_product(sheet, grads).reshape(full.shape)
    for j in range(full.shape[0]):
        first = 0
        for keep, give in zip(outs[::2], outs[1::2]):
            out = (keep, give)[j % 2]
            last = first + out.shape[-1]
            out[j // 2] = full[where[0] ^ j, :, first:last].astype(out.dtype)
            first = last


def whole_weight_kernel(where, sheet, grads, out):
    out[...] = weight_product(sheet, grads)


def weight_part(where, sheet, grads, cuts, shards, after):
    rows, cols, width = sheet.shape
    columns = grads.shape[1] * HEAD_DIM
    if shards == 1:
        kernel, outs, scratch = whole_weight_kernel, [like((width, columns), F32)], ()
    else:
        halves = [(shards // 2, width // shards, cut) for cut in cuts]
        kernel = weight_kernel
        outs = [o for half in halves for o in (like(half, F32), like(half))]
        scratch = (pltpu.VMEM((shards, width // shards, columns), F32),)
    return in_vmem(
        kernel,
        "weight_part",
        outs,
        where,
        sheet,
        grads,
        scalars=1,
        after=after,
        scratch=scratch,
        limit=18,
        flops=2 * rows * cols * width * columns,
    )


def last_kernel(_, keep, got, out):
    total = keep[0] + got[0].astype(F32)
    local = out.shape[-1]
    for index in range(out.shape[0]):
        out[index] = total[:, index * local : (index + 1) * local]


def last_sum(before, keep, got, local):
    shape = (keep.shape[2] // local, keep.shape[1], local)
    return in_vmem(last_kernel, "last_sum", (like(shape, F32),), before, keep, got, streamed=1)[0]


def body(sheet, w_query, w_key, w_value, cotangent, lengths):
    row_dev, cols, width = sheet.shape
    local = w_query.shape[1]
    n_rows = lax.axis_size("rows")
    n_heads = lax.axis_size("heads")
    scale = float(1.0 / (HEAD_DIM * row_dev * n_rows) ** 0.5)
    direct = n_rows <= 8
    shards = n_rows if direct else 1
    row_bits = [1 << b for b in range(n_rows.bit_length() - 1)]
    chunk = row_dev // 2

    me = jnp.stack([lax.axis_index("rows"), lax.axis_index("heads")]).astype(jnp.int32)
    wq, wk, wv = w_query.T, w_key.T, w_value.T
    cot = jnp.swapaxes(cotangent, 1, 2)

    fars = range(2, n_heads, 2)
    far_cot = [flip(cot, "heads", f) for f in fars]
    fq, fk = [[flip(w, "heads", f) for f in fars] for w in (wq, wk)]
    up = row_bits if direct else []
    turn_about = up[1:] + up[:1]
    qk, held, seen, *logits = query_key(me, lengths.reshape(1, row_dev), sheet, wq, wk, turn_about)
    where = jnp.concatenate([me, seen.reshape(row_dev)])
    dprob = value_dprob(where, held, wv, cot, logits[-1:], up, fars, n_heads)
    dprob, halves = dprob[: -len(fars)], dprob[-len(fars) :]
    fv = [flip(half, "heads", f) for half, f in zip(halves, fars)]
    weights = turn(where, wq, wk, wv, n_heads, dprob[-1:])
    if direct:
        logits = halve(*logits, "rows", turn_about)
        dprob = halve(*dprob, "rows", up)
        probs, dscore = softmax_back(logits, dprob, scale, [weights])
        probs, probs_order = double(probs, "rows", up[::-1], [far_cot, fv])
        dscore, dscore_order = double(dscore, "rows", turn_about[::-1])
        scores = assemble(where, probs, dscore, (probs_order, dscore_order), shards, fq)
    else:
        logits, dprob = lax.psum((logits, dprob), "rows")
        scores = jnp.stack(softmax_back(logits, dprob, scale))
    far_scores = [flip(scores, "heads", f) for f in fars]
    grads = all_gradients(where, scores, qk, cot, "own_gradients", ())
    parts = weight_part(where, held, grads, (3 * local,), shards, fk)
    ready = [parts[-1]]
    far_qk = [far_query_key(where, held, *w, ready) for w in zip(fq, fk)]
    far_natural = [turn(where, *w, n_heads, ready) for w in zip(fq, fk, fv)]
    own = own_input(grads, weights, ready)
    ready = [own] + far_qk + far_natural + far_scores
    steps = [[], []]
    if direct:
        keep, give = parts
        steps = []
        for bit in row_bits[:-1]:
            give, keep = add_split(keep, flip(give, "rows", bit), ready)
            steps.append([keep])
            ready = ()
        last = keep, flip(give, "rows", row_bits[-1])
    else:
        weight_grad = lax.psum_scatter(parts[0], "rows", scatter_dimension=0, tiled=True)
        weight_grad = weight_grad.reshape(width // n_rows, 3, local)

    far_grads = [
        all_gradients(where, *args, "far_gradients", steps[0])
        for args in zip(far_scores, far_qk, far_cot)
    ]
    chunks = []
    for index, first in enumerate(range(0, row_dev, chunk)):
        after = steps[-1] if index else ()
        keep, give = far_input(first, chunk, own, list(zip(far_grads, far_natural)), after)
        chunks.append((keep, flip(give, "heads", 1)))
    out = finish(chunks)
    if direct:
        weight_grad = jnp.swapaxes(last_sum(out, *last, local), 0, 1)
    return (jnp.swapaxes(out, 1, 2), weight_grad)


def solution(mesh):
    in_specs = (
        P("rows", None, None),
        P(None, "heads"),
        P(None, "heads"),
        P(None, "heads"),
        P("rows", None, "heads"),
        P("rows"),
    )
    out_specs = (P("rows", None, "heads"), P("rows", None, "heads"))
    return jax.shard_map(body, mesh=mesh, in_specs=in_specs, out_specs=out_specs, check_vma=False)
```

```python
import functools
import math

import jax
import jax.numpy as jnp
from jax import lax
from jax.experimental import pallas as pl
from jax.experimental.pallas import tpu as pltpu
from jax.sharding import PartitionSpec as P

HEAD_DIM = 64
F32 = jnp.float32
BF16 = jnp.bfloat16
MIB = 1024 * 1024

NN = (((1,), (0,)), ((), ()))
NT = (((1,), (1,)), ((), ()))
TN = (((0,), (0,)), ((), ()))


def mm(a, b, dims):
    return lax.dot_general(a, b, dims, preferred_element_type=F32)


def flip(values, axis, bit):
    n = lax.axis_size(axis)
    return lax.ppermute(values, axis, [(s, s ^ bit) for s in range(n)])


def cost(flops, moved):
    return pl.CostEstimate(flops=int(flops), bytes_accessed=int(moved), transcendentals=0)


SMEM = pl.BlockSpec(memory_space=pltpu.SMEM)
VMEM = pl.BlockSpec(memory_space=pltpu.VMEM)
ANY = pl.BlockSpec(memory_space=pl.ANY)
HBM = pl.BlockSpec(memory_space=pltpu.HBM)


def like(shape, dtype=BF16):
    return jax.ShapeDtypeStruct(shape, dtype)


def place(a, stays):
    return pltpu.with_memory_space_constraint(a, pltpu.HBM) if stays else a


def in_vmem(kernel, name, out, *operands, scalars=0, streamed=0, after=(), scratch=(), limit=12, flops=0):
    many = len(after)

    def run(*refs):
        kernel(*refs[: len(operands)], *refs[len(operands) + many :])

    moved = 2 * sum(a.size for a in operands) + 2 * sum(o.size for o in out)
    held = len(operands) - scalars - streamed
    return pl.pallas_call(
        run,
        in_specs=[SMEM] * scalars + [HBM] * streamed + [VMEM] * held + [ANY] * many,
        out_specs=[VMEM] * len(out),
        out_shape=list(out),
        scratch_shapes=list(scratch),
        compiler_params=pltpu.CompilerParams(vmem_limit_bytes=limit * MIB),
        cost_estimate=cost(flops, moved),
        name=name,
    )(*[place(a, scalars <= i < scalars + streamed) for i, a in enumerate(operands)], *after)


def lane_mask(length, cols):
    return (lax.broadcasted_iota(jnp.int32, (1, cols), 1) < length).astype(F32)


def reorder(bits):
    return [sum(bit for b, bit in enumerate(bits) if t >> b & 1) for t in range(1 << len(bits))]


def put_shards(me, acc, bits, outs):
    for t, j in enumerate(reorder(bits)):
        out = outs[t % len(outs)]
        out[t // len(outs)] = acc[:, me ^ j].astype(out.dtype)


BLOCK = 4
STEP = 2
AHEAD = 6


def query_key_kernel(bits, me, lengths, sheet, wq, wk, qk, held, seen, *rest):
    outs, (wt, acc, number, sems) = rest[:-4], rest[-4:]
    rows, cols, width = sheet.shape
    local = wq.shape[0]
    heads = local // HEAD_DIM
    copies = []

    def copy(source, target):
        copies.append(pltpu.make_async_copy(source, target, sems.at[len(copies)]))

    copy(lengths, number)
    copy(lengths, seen)
    copy(wq, wt.at[:local])
    copy(wk, wt.at[local:])
    for first in range(0, rows, STEP):
        some = pl.ds(first, STEP)
        copy(sheet.at[some], held.at[some])
    for one in copies[:AHEAD]:
        one.start()
    for one in copies[:4]:
        one.wait()
    flat = (BLOCK * HEAD_DIM, cols)
    for first in range(0, rows, BLOCK):
        for r in range(first, first + BLOCK):
            if r % STEP == 0:
                at = 4 + r // STEP
                copies[at].wait()
                for later in copies[at + AHEAD - 4 : at + AHEAD - 3]:
                    later.start()
            value = (mm(wt[...], held[r], NT) * lane_mask(number[0, r], cols)).astype(BF16)
            qk[r] = value.reshape(2 * heads, HEAD_DIM, cols)
        some = pl.ds(first, BLOCK)
        for h in range(heads):
            term = mm(qk[some, h].reshape(flat), qk[some, heads + h].reshape(flat), TN)
            term = term.reshape(acc.shape[1:])
            acc[h] = term if first == 0 else acc[h] + term
    put_shards(me[0], acc, bits, outs)


def query_key(me, lengths, sheet, wq, wk, bits):
    rows, cols, width = sheet.shape
    shards = 1 << len(bits)
    local = wq.shape[0]
    heads = local // HEAD_DIM
    return in_vmem(
        functools.partial(query_key_kernel, bits),
        "query_key",
        [like((rows, 2 * heads, HEAD_DIM, cols)), like(sheet.shape), like(lengths.shape, jnp.int32)]
        + part_shapes(shards, heads, cols),
        me,
        lengths,
        sheet,
        wq,
        wk,
        scalars=1,
        streamed=4,
        scratch=(
            pltpu.VMEM((2 * local, width), BF16),
            pltpu.VMEM((heads, shards, cols // shards, cols), F32),
            pltpu.SMEM(lengths.shape, jnp.int32),
            pltpu.SemaphoreType.DMA((4 + rows // STEP,)),
        ),
        limit=14,
        flops=2 * rows * cols * local * (2 * width + cols),
    )


def value_kernel(bits, fars, where, sheet, wv, cot, *rest):
    outs, halves, acc = rest[: -1 - len(fars)], rest[-1 - len(fars) : -1], rest[-1]
    rows, cols, width = sheet.shape
    for far, half in zip(fars, halves):
        near = half.shape[1]
        side = lax.shift_right_logical(where[1], 1) ^ (far // 2)
        for s in range(width // near):
            @pl.when(side == s)
            def _():
                half[...] = wv[:, s * near : (s + 1) * near]
    local = wv.shape[0]
    heads = local // HEAD_DIM
    flat = (BLOCK * HEAD_DIM, cols)
    for first in range(0, rows, BLOCK):
        values = []
        for r in range(first, first + BLOCK):
            value = (mm(wv[...], sheet[r], NT) * lane_mask(where[2 + r], cols)).astype(BF16)
            values.append(value.reshape(heads, HEAD_DIM, cols))
        for h in range(heads):
            left = cot[pl.ds(first, BLOCK), h * HEAD_DIM : (h + 1) * HEAD_DIM].reshape(flat)
            right = jnp.concatenate([v[h] for v in values], axis=0)
            term = mm(left, right, TN).reshape(acc.shape[1:])
            acc[h] = term if first == 0 else acc[h] + term
    put_shards(where[0], acc, bits, outs)


def value_dprob(where, sheet, wv, cot, after, bits, fars, devices):
    rows, cols, width = sheet.shape
    shards = 1 << len(bits)
    local = wv.shape[0]
    heads = local // HEAD_DIM
    return in_vmem(
        functools.partial(value_kernel, bits, fars),
        "value_dprob",
        part_shapes(shards, heads, cols) + [like((local, 2 * width // devices))] * len(fars),
        where,
        sheet,
        wv,
        cot,
        scalars=1,
        after=after,
        scratch=(pltpu.VMEM((heads, shards, cols // shards, cols), F32),),
        limit=16,
        flops=16 * rows * cols * local * (width + cols),
    )


def turn_kernel(where, wq, wk, wv, natural, *full):
    near, share, columns = natural.shape
    local = wq.shape[0]
    for index, (weight, held) in enumerate(zip((wq, wk, wv), full)):
        held[...] = weight[...].T.reshape(held.shape)
        mine = where[1] & (held.shape[0] - 1)
        for j in range(near):
            natural[j, :, index * local : (index + 1) * local] = held[mine ^ j]


def turn(where, wq, wk, wv, devices, after):
    local, width = wq.shape
    share = width // devices
    return in_vmem(
        turn_kernel,
        "turn",
        (like((2, share, 3 * local)),),
        where,
        wq,
        wk,
        wv,
        scalars=1,
        after=after,
        scratch=[pltpu.VMEM((w.shape[1] // share, share, local), BF16) for w in (wq, wk, wv)],
    )[0]


def far_query_key_kernel(where, sheet, wq, wk, qk):
    local = wq.shape[0]
    rows, cols, _ = sheet.shape
    both = jnp.concatenate([wq[...], wk[...]], axis=0)
    for r in range(rows):
        value = (mm(both, sheet[r], NT) * lane_mask(where[2 + r], cols)).astype(BF16)
        qk[r] = value.reshape(2 * local // HEAD_DIM, HEAD_DIM, cols)


def far_query_key(where, sheet, wq, wk, after):
    rows, cols, width = sheet.shape
    local = wq.shape[0]
    return in_vmem(
        far_query_key_kernel,
        "far_query_key",
        (like((rows, 2 * local // HEAD_DIM, HEAD_DIM, cols)),),
        where,
        sheet,
        wq,
        wk,
        scalars=1,
        after=after,
        flops=4 * rows * cols * local * width,
    )[0]


def part_shapes(shards, heads, cols):
    if shards == 1:
        return [like((1, heads, cols, cols), F32)]
    half = (shards // 2, heads, cols // shards, cols)
    return [like(half, F32), like(half)]


def hold_kernel(values, out):
    out[...] = values[...]


def hold(values, after):
    return in_vmem(hold_kernel, "hold", (like(values.shape),), values, after=after)[0]


def add_split_kernel(keep, got, give_out, keep_out):
    for j in range(keep.shape[0]):
        total = keep[j].astype(F32) + got[j].astype(F32)
        out = give_out if j % 2 else keep_out
        out[j // 2] = total.astype(out.dtype)


def add_split(keep, got, after=()):
    half = (keep.shape[0] // 2,) + keep.shape[1:]
    return in_vmem(add_split_kernel, "add_split", (like(half), like(half, keep.dtype)), keep, got, after=after)


def halve(keep, give, axis, bits, after=()):
    after = list(after) + [()] * len(bits)
    for bit, waits in zip(bits[:-1], after):
        give, keep = add_split(keep, flip(give, axis, bit), waits)
    return keep, flip(give, axis, bits[-1])


def softmax_kernel(scale, *refs):
    *terms, probs_out, dscore_out = refs
    half = len(terms) // 2
    total = lambda some: functools.reduce(jnp.add, [t[0].astype(F32) for t in some])
    logits = total(terms[:half]) * scale
    dprob = total(terms[half:])
    shifted = jnp.exp(logits - jnp.max(logits, axis=-1, keepdims=True))
    probs = shifted / jnp.sum(shifted, axis=-1, keepdims=True)
    inner = jnp.sum(probs * dprob, axis=-1, keepdims=True)
    probs_out[0] = probs.astype(BF16)
    dscore_out[0] = (scale * probs * (dprob - inner)).astype(BF16)


def softmax_back(logits, dprob, scale, after=()):
    out = like(logits[0].shape)
    return in_vmem(
        functools.partial(softmax_kernel, scale), "softmax_back", (out, out), *logits, *dprob, limit=16, after=after
    )


def join_kernel(one, other, out):
    out[: one.shape[0]] = one[...]
    out[one.shape[0] :] = other[...]


def join(one, other, after):
    shape = (one.shape[0] + other.shape[0],) + one.shape[1:]
    return in_vmem(join_kernel, "join", (like(shape),), one, other, after=after)[0]


def double(values, axis, bits, after=()):
    order = [0]
    after = list(after) + [()] * len(bits)
    for bit, waits in zip(bits[:-1], after):
        values = join(values, flip(values, axis, bit), waits)
        order = order + [j ^ bit for j in order]
    other = flip(values, axis, bits[-1])
    return (values, other), (order, [j ^ bits[-1] for j in order])


def assemble_kernel(orders, where, *refs):
    *pieces, out = refs
    for piece, (kind, order) in zip(pieces, orders):
        for t, j in enumerate(order):
            out[kind, where[0] ^ j] = piece[t]


def assemble(where, probs, dscore, orders, shards, after):
    orders = [(kind, order) for kind, both in enumerate(orders) for order in both]
    out = like((2, shards) + probs[0].shape[1:])
    return in_vmem(
        functools.partial(assemble_kernel, orders),
        "assemble",
        (out,),
        where,
        *probs,
        *dscore,
        scalars=1,
        after=after,
    )[0]


def gradients(where, first, count, scores, qk, cot, grads):
    cols = qk.shape[-1]
    heads = qk.shape[1] // 2
    rows = pl.ds(first, count)
    flat = (count * HEAD_DIM, cols)
    split = (count, HEAD_DIM, cols)
    masks = jnp.stack([lane_mask(where[2 + first + r], cols) for r in range(count)])
    for h in range(heads):
        p, ds = [scores[kind, :, h].reshape(cols, cols) for kind in range(2)]
        g = cot[rows, h * HEAD_DIM : (h + 1) * HEAD_DIM].reshape(flat)
        dq = mm(qk[rows, heads + h].reshape(flat), ds, NT)
        dk = mm(qk[rows, h].reshape(flat), ds, NN)
        dv = mm(g, p, NN)
        for index, value in enumerate((dq, dk, dv)):
            grads[:, index * heads + h] = (value.reshape(split) * masks).astype(BF16)


def gradients_kernel(where, scores, qk, cot, grads):
    gradients(where, 0, qk.shape[0], scores, qk, cot, grads)


def all_gradients(where, scores, qk, cot, name, after):
    rows, two, _, cols = qk.shape
    return in_vmem(
        gradients_kernel,
        name,
        (like((rows, two // 2 * 3, HEAD_DIM, cols)),),
        where,
        scores,
        qk,
        cot,
        scalars=1,
        after=after,
        limit=14,
        flops=3 * rows * two * HEAD_DIM * cols * cols,
    )[0]


def own_input_kernel(grads, weights, out):
    near, share, columns = weights.shape
    left = weights[...].reshape(near * share, columns)
    for r in range(grads.shape[0]):
        part = mm(left, grads[r].reshape(columns, grads.shape[-1]), NN).astype(BF16)
        out[:, r] = part.reshape(near, share, grads.shape[-1])


def own_input(grads, weights, after):
    rows, cols = grads.shape[0], grads.shape[-1]
    near, share, columns = weights.shape
    return in_vmem(
        own_input_kernel,
        "own_input",
        (like((near, rows, share, cols)),),
        grads,
        weights,
        after=after,
        flops=2 * rows * cols * near * share * columns,
    )[0]


def far_input_kernel(first, own, *refs):
    *refs, keep, give = refs
    count, share, cols = keep.shape
    for r in range(count):
        total = own[:, first + r].astype(F32)
        for i in range(0, len(refs), 2):
            grads, weights = refs[i : i + 2]
            near, _, columns = weights.shape
            left = weights[...].reshape(near * share, columns)
            part = mm(left, grads[first + r].reshape(columns, cols), NN).astype(BF16)
            total = total + part.reshape(near, share, cols).astype(F32)
        keep[r] = total[0].astype(keep.dtype)
        give[r] = total[1].astype(give.dtype)


def far_input(first, count, own, far, after):
    _, rows, share, cols = own.shape
    columns = far[0][1].shape[-1]
    out = like((count, share, cols))
    return in_vmem(
        functools.partial(far_input_kernel, first),
        "far_input",
        (out, out),
        own,
        *[a for one in far for a in one],
        after=after,
        limit=14,
        flops=4 * len(far) * count * cols * columns * share,
    )


def finish_kernel(*refs):
    *terms, out, total, sems = refs
    copies = []
    first = 0
    for index in range(0, len(terms), 2):
        keep, got = terms[index : index + 2]
        some = pl.ds(first, keep.shape[0])
        total[some] = (keep[...].astype(F32) + got[...].astype(F32)).astype(BF16)
        copies.append(pltpu.make_async_copy(total.at[some], out.at[some], sems.at[index // 2]))
        copies[-1].start()
        first += keep.shape[0]
    for copy in copies:
        copy.wait()


def finish(chunks):
    _, share, cols = chunks[0][0].shape
    rows = sum(keep.shape[0] for keep, _ in chunks)
    terms = [a for chunk in chunks for a in chunk]
    return pl.pallas_call(
        finish_kernel,
        in_specs=[VMEM] * len(terms),
        out_specs=HBM,
        out_shape=like((rows, share, cols)),
        scratch_shapes=[pltpu.VMEM((rows, share, cols), BF16), pltpu.SemaphoreType.DMA((len(chunks),))],
        compiler_params=pltpu.CompilerParams(vmem_limit_bytes=12 * MIB),
        cost_estimate=cost(rows * share * cols, 6 * rows * share * cols),
        name="finish",
    )(*terms)


def weight_product(sheet, grads):
    rows, cols, width = sheet.shape
    columns = grads.shape[1] * HEAD_DIM
    left = [grads[r].reshape(columns, cols) for r in range(rows)]
    return mm(jnp.concatenate(left, axis=1), sheet[...].reshape(rows * cols, width), NN).T


def weight_kernel(where, sheet, grads, *rest):
    outs, full = rest[:-1], rest[-1]
    full[...] = weight_product(sheet, grads).reshape(full.shape)
    for j in range(full.shape[0]):
        first = 0
        for keep, give in zip(outs[::2], outs[1::2]):
            out = (keep, give)[j % 2]
            last = first + out.shape[-1]
            out[j // 2] = full[where[0] ^ j, :, first:last].astype(out.dtype)
            first = last


def whole_weight_kernel(where, sheet, grads, out):
    out[...] = weight_product(sheet, grads)


def weight_part(where, sheet, grads, cuts, shards, after):
    rows, cols, width = sheet.shape
    columns = grads.shape[1] * HEAD_DIM
    if shards == 1:
        kernel, outs, scratch = whole_weight_kernel, [like((width, columns), F32)], ()
    else:
        halves = [(shards // 2, width // shards, cut) for cut in cuts]
        kernel = weight_kernel
        outs = [o for half in halves for o in (like(half, F32), like(half))]
        scratch = (pltpu.VMEM((shards, width // shards, columns), F32),)
    return in_vmem(
        kernel,
        "weight_part",
        outs,
        where,
        sheet,
        grads,
        scalars=1,
        after=after,
        scratch=scratch,
        limit=18,
        flops=2 * rows * cols * width * columns,
    )


def last_kernel(_, keep, got, out):
    total = keep[0] + got[0].astype(F32)
    local = out.shape[-1]
    for index in range(out.shape[0]):
        out[index] = total[:, index * local : (index + 1) * local]


def last_sum(before, keep, got, local):
    shape = (keep.shape[2] // local, keep.shape[1], local)
    return in_vmem(last_kernel, "last_sum", (like(shape, F32),), before, keep, got, streamed=1)[0]


def body(sheet, w_query, w_key, w_value, cotangent, lengths):
    row_dev, cols, width = sheet.shape
    local = w_query.shape[1]
    n_rows = lax.axis_size("rows")
    n_heads = lax.axis_size("heads")
    scale = float(1.0 / (HEAD_DIM * row_dev * n_rows) ** 0.5)
    direct = n_rows <= 8
    shards = n_rows if direct else 1
    row_bits = [1 << b for b in range(n_rows.bit_length() - 1)]
    chunk = row_dev // 2

    me = jnp.stack([lax.axis_index("rows"), lax.axis_index("heads")]).astype(jnp.int32)
    wq, wk, wv = w_query.T, w_key.T, w_value.T
    cot = jnp.swapaxes(cotangent, 1, 2)

    fars = range(2, n_heads, 2)
    far_cot = [flip(cot, "heads", f) for f in fars]
    fq, fk = [[flip(w, "heads", f) for f in fars] for w in (wq, wk)]
    up = row_bits if direct else []
    turn_about = up[1:] + up[:1]
    qk, held, seen, *logits = query_key(me, lengths.reshape(1, row_dev), sheet, wq, wk, turn_about)
    where = jnp.concatenate([me, seen.reshape(row_dev)])
    dprob = value_dprob(where, held, wv, cot, logits[-1:], up, fars, n_heads)
    dprob, halves = dprob[: -len(fars)], dprob[-len(fars) :]
    fv = [flip(half, "heads", f) for half, f in zip(halves, fars)]
    weights = turn(where, wq, wk, wv, n_heads, dprob[-1:])
    if direct:
        logits = halve(*logits, "rows", turn_about)
        dprob = halve(*dprob, "rows", up)
        probs, dscore = softmax_back(logits, dprob, scale, [weights])
        probs, probs_order = double(probs, "rows", up[::-1], [far_cot])
        dscore, dscore_order = double(dscore, "rows", turn_about[::-1])
        scores = assemble(where, probs, dscore, (probs_order, dscore_order), shards, fq)
    else:
        logits, dprob = lax.psum((logits, dprob), "rows")
        scores = jnp.stack(softmax_back(logits, dprob, scale))
    far_scores = [flip(scores, "heads", f) for f in fars]
    grads = all_gradients(where, scores, qk, cot, "own_gradients", ())
    parts = weight_part(where, held, grads, (3 * local,), shards, fv)
    ready = [parts[-1]]
    far_qk = [far_query_key(where, held, *w, ready) for w in zip(fq, fk)]
    far_natural = [turn(where, *w, n_heads, ready) for w in zip(fq, fk, fv)]
    own = own_input(grads, weights, ready)
    ready = [own] + far_qk + far_natural
    far_grads = []

    def far_gradients(after):
        for args in zip(far_scores, far_qk, far_cot):
            far_grads.append(all_gradients(where, *args, "far_gradients", after))
        return far_grads

    steps = [[]]
    if direct:
        keep, give = parts
        for bit in row_bits[:-1]:
            give, keep = add_split(keep, flip(give, "rows", bit), ready)
            steps.append([keep])
            ready = far_grads or far_gradients(steps[-1])
        last = keep, flip(give, "rows", row_bits[-1])
    else:
        weight_grad = lax.psum_scatter(parts[0], "rows", scatter_dimension=0, tiled=True)
        weight_grad = weight_grad.reshape(width // n_rows, 3, local)
    if not far_grads:
        far_gradients(steps[-1])
    chunks = []
    for index, first in enumerate(range(0, row_dev, chunk)):
        after = steps[-1] if index else ()
        keep, give = far_input(first, chunk, own, list(zip(far_grads, far_natural)), after)
        chunks.append((keep, flip(give, "heads", 1)))
    out = finish(chunks)
    if direct:
        weight_grad = jnp.swapaxes(last_sum(out, *last, local), 0, 1)
    return (jnp.swapaxes(out, 1, 2), weight_grad)


def solution(mesh):
    in_specs = (
        P("rows", None, None),
        P(None, "heads"),
        P(None, "heads"),
        P(None, "heads"),
        P("rows", None, "heads"),
        P("rows"),
    )
    out_specs = (P("rows", None, "heads"), P("rows", None, "heads"))
    return jax.shard_map(body, mesh=mesh, in_specs=in_specs, out_specs=out_specs, check_vma=False)
```

```python
import functools
import math

import jax
import jax.numpy as jnp
from jax import lax
from jax.experimental import pallas as pl
from jax.experimental.pallas import tpu as pltpu
from jax.sharding import PartitionSpec as P

HEAD_DIM = 64
F32 = jnp.float32
BF16 = jnp.bfloat16
MIB = 1024 * 1024

NN = (((1,), (0,)), ((), ()))
NT = (((1,), (1,)), ((), ()))
TN = (((0,), (0,)), ((), ()))


def mm(a, b, dims):
    return lax.dot_general(a, b, dims, preferred_element_type=F32)


def flip(values, axis, bit):
    n = lax.axis_size(axis)
    return lax.ppermute(values, axis, [(s, s ^ bit) for s in range(n)])


def cost(flops, moved):
    return pl.CostEstimate(flops=int(flops), bytes_accessed=int(moved), transcendentals=0)


SMEM = pl.BlockSpec(memory_space=pltpu.SMEM)
VMEM = pl.BlockSpec(memory_space=pltpu.VMEM)
ANY = pl.BlockSpec(memory_space=pl.ANY)
HBM = pl.BlockSpec(memory_space=pltpu.HBM)


def like(shape, dtype=BF16):
    return jax.ShapeDtypeStruct(shape, dtype)


def place(a, stays):
    return pltpu.with_memory_space_constraint(a, pltpu.HBM) if stays else a


def in_vmem(kernel, name, out, *operands, scalars=0, streamed=0, after=(), scratch=(), limit=12, flops=0):
    many = len(after)

    def run(*refs):
        kernel(*refs[: len(operands)], *refs[len(operands) + many :])

    moved = 2 * sum(a.size for a in operands) + 2 * sum(o.size for o in out)
    held = len(operands) - scalars - streamed
    return pl.pallas_call(
        run,
        in_specs=[SMEM] * scalars + [HBM] * streamed + [VMEM] * held + [ANY] * many,
        out_specs=[VMEM] * len(out),
        out_shape=list(out),
        scratch_shapes=list(scratch),
        compiler_params=pltpu.CompilerParams(vmem_limit_bytes=limit * MIB),
        cost_estimate=cost(flops, moved),
        name=name,
    )(*[place(a, scalars <= i < scalars + streamed) for i, a in enumerate(operands)], *after)


def lane_mask(length, cols):
    return (lax.broadcasted_iota(jnp.int32, (1, cols), 1) < length).astype(F32)


def reorder(bits):
    return [sum(bit for b, bit in enumerate(bits) if t >> b & 1) for t in range(1 << len(bits))]


def put_shards(me, acc, bits, outs):
    for t, j in enumerate(reorder(bits)):
        out = outs[t % len(outs)]
        out[t // len(outs)] = acc[:, me ^ j].astype(out.dtype)


BLOCK = 4
STEP = 2
AHEAD = 6


def query_key_kernel(bits, me, lengths, sheet, wq, wk, qk, held, seen, *rest):
    outs, (wt, acc, number, sems) = rest[:-4], rest[-4:]
    rows, cols, width = sheet.shape
    local = wq.shape[0]
    heads = local // HEAD_DIM
    copies = []

    def copy(source, target):
        copies.append(pltpu.make_async_copy(source, target, sems.at[len(copies)]))

    copy(lengths, number)
    copy(lengths, seen)
    copy(wq, wt.at[:local])
    copy(wk, wt.at[local:])
    for first in range(0, rows, STEP):
        some = pl.ds(first, STEP)
        copy(sheet.at[some], held.at[some])
    for one in copies[:AHEAD]:
        one.start()
    for one in copies[:4]:
        one.wait()
    flat = (BLOCK * HEAD_DIM, cols)
    for first in range(0, rows, BLOCK):
        for r in range(first, first + BLOCK):
            if r % STEP == 0:
                at = 4 + r // STEP
                copies[at].wait()
                for later in copies[at + AHEAD - 4 : at + AHEAD - 3]:
                    later.start()
            value = (mm(wt[...], held[r], NT) * lane_mask(number[0, r], cols)).astype(BF16)
            qk[r] = value.reshape(2 * heads, HEAD_DIM, cols)
        some = pl.ds(first, BLOCK)
        for h in range(heads):
            term = mm(qk[some, h].reshape(flat), qk[some, heads + h].reshape(flat), TN)
            term = term.reshape(acc.shape[1:])
            acc[h] = term if first == 0 else acc[h] + term
    put_shards(me[0], acc, bits, outs)


def query_key(me, lengths, sheet, wq, wk, bits):
    rows, cols, width = sheet.shape
    shards = 1 << len(bits)
    local = wq.shape[0]
    heads = local // HEAD_DIM
    return in_vmem(
        functools.partial(query_key_kernel, bits),
        "query_key",
        [like((rows, 2 * heads, HEAD_DIM, cols)), like(sheet.shape), like(lengths.shape, jnp.int32)]
        + part_shapes(shards, heads, cols),
        me,
        lengths,
        sheet,
        wq,
        wk,
        scalars=1,
        streamed=4,
        scratch=(
            pltpu.VMEM((2 * local, width), BF16),
            pltpu.VMEM((heads, shards, cols // shards, cols), F32),
            pltpu.SMEM(lengths.shape, jnp.int32),
            pltpu.SemaphoreType.DMA((4 + rows // STEP,)),
        ),
        limit=14,
        flops=rows * cols * local * (2 * width + cols) // 2,
    )


def value_kernel(bits, fars, where, sheet, wv, cot, *rest):
    outs, halves, acc = rest[: -1 - len(fars)], rest[-1 - len(fars) : -1], rest[-1]
    rows, cols, width = sheet.shape
    for far, half in zip(fars, halves):
        near = half.shape[1]
        side = lax.shift_right_logical(where[1], 1) ^ (far // 2)
        for s in range(width // near):
            @pl.when(side == s)
            def _():
                half[...] = wv[:, s * near : (s + 1) * near]
    local = wv.shape[0]
    heads = local // HEAD_DIM
    flat = (BLOCK * HEAD_DIM, cols)
    for first in range(0, rows, BLOCK):
        values = []
        for r in range(first, first + BLOCK):
            value = (mm(wv[...], sheet[r], NT) * lane_mask(where[2 + r], cols)).astype(BF16)
            values.append(value.reshape(heads, HEAD_DIM, cols))
        for h in range(heads):
            left = cot[pl.ds(first, BLOCK), h * HEAD_DIM : (h + 1) * HEAD_DIM].reshape(flat)
            right = jnp.concatenate([v[h] for v in values], axis=0)
            term = mm(left, right, TN).reshape(acc.shape[1:])
            acc[h] = term if first == 0 else acc[h] + term
    put_shards(where[0], acc, bits, outs)


def value_dprob(where, sheet, wv, cot, after, bits, fars, devices):
    rows, cols, width = sheet.shape
    shards = 1 << len(bits)
    local = wv.shape[0]
    heads = local // HEAD_DIM
    return in_vmem(
        functools.partial(value_kernel, bits, fars),
        "value_dprob",
        part_shapes(shards, heads, cols) + [like((local, 2 * width // devices))] * len(fars),
        where,
        sheet,
        wv,
        cot,
        scalars=1,
        after=after,
        scratch=(pltpu.VMEM((heads, shards, cols // shards, cols), F32),),
        limit=16,
        flops=4 * rows * cols * local * (width + cols),
    )


def turn_kernel(where, wq, wk, wv, natural, *full):
    near, share, columns = natural.shape
    local = wq.shape[0]
    for index, (weight, held) in enumerate(zip((wq, wk, wv), full)):
        held[...] = weight[...].T.reshape(held.shape)
        mine = where[1] & (held.shape[0] - 1)
        for j in range(near):
            natural[j, :, index * local : (index + 1) * local] = held[mine ^ j]


def turn(where, wq, wk, wv, devices, after):
    local, width = wq.shape
    share = width // devices
    return in_vmem(
        turn_kernel,
        "turn",
        (like((2, share, 3 * local)),),
        where,
        wq,
        wk,
        wv,
        scalars=1,
        after=after,
        scratch=[pltpu.VMEM((w.shape[1] // share, share, local), BF16) for w in (wq, wk, wv)],
    )[0]


def far_query_key_kernel(where, sheet, wq, wk, qk):
    local = wq.shape[0]
    rows, cols, _ = sheet.shape
    both = jnp.concatenate([wq[...], wk[...]], axis=0)
    for r in range(rows):
        value = (mm(both, sheet[r], NT) * lane_mask(where[2 + r], cols)).astype(BF16)
        qk[r] = value.reshape(2 * local // HEAD_DIM, HEAD_DIM, cols)


def far_query_key(where, sheet, wq, wk, after):
    rows, cols, width = sheet.shape
    local = wq.shape[0]
    return in_vmem(
        far_query_key_kernel,
        "far_query_key",
        (like((rows, 2 * local // HEAD_DIM, HEAD_DIM, cols)),),
        where,
        sheet,
        wq,
        wk,
        scalars=1,
        after=after,
        flops=4 * rows * cols * local * width,
    )[0]


def part_shapes(shards, heads, cols):
    if shards == 1:
        return [like((1, heads, cols, cols), F32)]
    half = (shards // 2, heads, cols // shards, cols)
    return [like(half, F32), like(half)]


def hold_kernel(values, out):
    out[...] = values[...]


def hold(values, after):
    return in_vmem(hold_kernel, "hold", (like(values.shape),), values, after=after)[0]


def add_split_kernel(keep, got, give_out, keep_out):
    for j in range(keep.shape[0]):
        total = keep[j].astype(F32) + got[j].astype(F32)
        out = give_out if j % 2 else keep_out
        out[j // 2] = total.astype(out.dtype)


def add_split(keep, got, after=()):
    half = (keep.shape[0] // 2,) + keep.shape[1:]
    return in_vmem(add_split_kernel, "add_split", (like(half), like(half, keep.dtype)), keep, got, after=after)


def halve(keep, give, axis, bits, after=()):
    after = list(after) + [()] * len(bits)
    for bit, waits in zip(bits[:-1], after):
        give, keep = add_split(keep, flip(give, axis, bit), waits)
    return keep, flip(give, axis, bits[-1])


def softmax_kernel(scale, *refs):
    *terms, probs_out, dscore_out = refs
    half = len(terms) // 2
    total = lambda some: functools.reduce(jnp.add, [t[0].astype(F32) for t in some])
    logits = total(terms[:half]) * scale
    dprob = total(terms[half:])
    shifted = jnp.exp(logits - jnp.max(logits, axis=-1, keepdims=True))
    probs = shifted / jnp.sum(shifted, axis=-1, keepdims=True)
    inner = jnp.sum(probs * dprob, axis=-1, keepdims=True)
    probs_out[0] = probs.astype(BF16)
    dscore_out[0] = (scale * probs * (dprob - inner)).astype(BF16)


def softmax_back(logits, dprob, scale, after=()):
    out = like(logits[0].shape)
    return in_vmem(
        functools.partial(softmax_kernel, scale), "softmax_back", (out, out), *logits, *dprob, limit=16, after=after
    )


def join_kernel(one, other, out):
    out[: one.shape[0]] = one[...]
    out[one.shape[0] :] = other[...]


def join(one, other, after):
    shape = (one.shape[0] + other.shape[0],) + one.shape[1:]
    return in_vmem(join_kernel, "join", (like(shape),), one, other, after=after)[0]


def double(values, axis, bits, after=()):
    order = [0]
    after = list(after) + [()] * len(bits)
    for bit, waits in zip(bits[:-1], after):
        values = join(values, flip(values, axis, bit), waits)
        order = order + [j ^ bit for j in order]
    other = flip(values, axis, bits[-1])
    return (values, other), (order, [j ^ bits[-1] for j in order])


def assemble_kernel(orders, where, *refs):
    *pieces, out = refs
    for piece, (kind, order) in zip(pieces, orders):
        for t, j in enumerate(order):
            out[kind, where[0] ^ j] = piece[t]


def assemble(where, probs, dscore, orders, shards, after):
    orders = [(kind, order) for kind, both in enumerate(orders) for order in both]
    out = like((2, shards) + probs[0].shape[1:])
    return in_vmem(
        functools.partial(assemble_kernel, orders),
        "assemble",
        (out,),
        where,
        *probs,
        *dscore,
        scalars=1,
        after=after,
    )[0]


def gradients(where, first, count, scores, qk, cot, grads):
    cols = qk.shape[-1]
    heads = qk.shape[1] // 2
    rows = pl.ds(first, count)
    flat = (count * HEAD_DIM, cols)
    split = (count, HEAD_DIM, cols)
    masks = jnp.stack([lane_mask(where[2 + first + r], cols) for r in range(count)])
    for h in range(heads):
        p, ds = [scores[kind, :, h].reshape(cols, cols) for kind in range(2)]
        g = cot[rows, h * HEAD_DIM : (h + 1) * HEAD_DIM].reshape(flat)
        dq = mm(qk[rows, heads + h].reshape(flat), ds, NT)
        dk = mm(qk[rows, h].reshape(flat), ds, NN)
        dv = mm(g, p, NN)
        for index, value in enumerate((dq, dk, dv)):
            grads[:, index * heads + h] = (value.reshape(split) * masks).astype(BF16)


def gradients_kernel(where, scores, qk, cot, grads):
    gradients(where, 0, qk.shape[0], scores, qk, cot, grads)


def all_gradients(where, scores, qk, cot, name, after):
    rows, two, _, cols = qk.shape
    return in_vmem(
        gradients_kernel,
        name,
        (like((rows, two // 2 * 3, HEAD_DIM, cols)),),
        where,
        scores,
        qk,
        cot,
        scalars=1,
        after=after,
        limit=14,
        flops=3 * rows * two * HEAD_DIM * cols * cols,
    )[0]


def own_input_kernel(grads, weights, out):
    near, share, columns = weights.shape
    left = weights[...].reshape(near * share, columns)
    for r in range(grads.shape[0]):
        part = mm(left, grads[r].reshape(columns, grads.shape[-1]), NN).astype(BF16)
        out[:, r] = part.reshape(near, share, grads.shape[-1])


def own_input(grads, weights, after):
    rows, cols = grads.shape[0], grads.shape[-1]
    near, share, columns = weights.shape
    return in_vmem(
        own_input_kernel,
        "own_input",
        (like((near, rows, share, cols)),),
        grads,
        weights,
        after=after,
        flops=2 * rows * cols * near * share * columns,
    )[0]


def far_input_kernel(first, own, *refs):
    *refs, keep, give = refs
    count, share, cols = keep.shape
    for r in range(count):
        total = own[:, first + r].astype(F32)
        for i in range(0, len(refs), 2):
            grads, weights = refs[i : i + 2]
            near, _, columns = weights.shape
            left = weights[...].reshape(near * share, columns)
            part = mm(left, grads[first + r].reshape(columns, cols), NN).astype(BF16)
            total = total + part.reshape(near, share, cols).astype(F32)
        keep[r] = total[0].astype(keep.dtype)
        give[r] = total[1].astype(give.dtype)


def far_input(first, count, own, far, after):
    _, rows, share, cols = own.shape
    columns = far[0][1].shape[-1]
    out = like((count, share, cols))
    return in_vmem(
        functools.partial(far_input_kernel, first),
        "far_input",
        (out, out),
        own,
        *[a for one in far for a in one],
        after=after,
        limit=14,
        flops=4 * len(far) * count * cols * columns * share,
    )


def finish_kernel(*refs):
    *terms, out, total, sems = refs
    copies = []
    first = 0
    for index in range(0, len(terms), 2):
        keep, got = terms[index : index + 2]
        some = pl.ds(first, keep.shape[0])
        total[some] = (keep[...].astype(F32) + got[...].astype(F32)).astype(BF16)
        copies.append(pltpu.make_async_copy(total.at[some], out.at[some], sems.at[index // 2]))
        copies[-1].start()
        first += keep.shape[0]
    for copy in copies:
        copy.wait()


def finish(chunks):
    _, share, cols = chunks[0][0].shape
    rows = sum(keep.shape[0] for keep, _ in chunks)
    terms = [a for chunk in chunks for a in chunk]
    return pl.pallas_call(
        finish_kernel,
        in_specs=[VMEM] * len(terms),
        out_specs=HBM,
        out_shape=like((rows, share, cols)),
        scratch_shapes=[pltpu.VMEM((rows, share, cols), BF16), pltpu.SemaphoreType.DMA((len(chunks),))],
        compiler_params=pltpu.CompilerParams(vmem_limit_bytes=12 * MIB),
        cost_estimate=cost(rows * share * cols, 6 * rows * share * cols),
        name="finish",
    )(*terms)


def weight_product(sheet, grads):
    rows, cols, width = sheet.shape
    columns = grads.shape[1] * HEAD_DIM
    left = [grads[r].reshape(columns, cols) for r in range(rows)]
    return mm(jnp.concatenate(left, axis=1), sheet[...].reshape(rows * cols, width), NN).T


def weight_kernel(where, sheet, grads, *rest):
    outs, full = rest[:-1], rest[-1]
    full[...] = weight_product(sheet, grads).reshape(full.shape)
    for j in range(full.shape[0]):
        first = 0
        for keep, give in zip(outs[::2], outs[1::2]):
            out = (keep, give)[j % 2]
            last = first + out.shape[-1]
            out[j // 2] = full[where[0] ^ j, :, first:last].astype(out.dtype)
            first = last


def whole_weight_kernel(where, sheet, grads, out):
    out[...] = weight_product(sheet, grads)


def weight_part(where, sheet, grads, cuts, shards, after):
    rows, cols, width = sheet.shape
    columns = grads.shape[1] * HEAD_DIM
    if shards == 1:
        kernel, outs, scratch = whole_weight_kernel, [like((width, columns), F32)], ()
    else:
        halves = [(shards // 2, width // shards, cut) for cut in cuts]
        kernel = weight_kernel
        outs = [o for half in halves for o in (like(half, F32), like(half))]
        scratch = (pltpu.VMEM((shards, width // shards, columns), F32),)
    return in_vmem(
        kernel,
        "weight_part",
        outs,
        where,
        sheet,
        grads,
        scalars=1,
        after=after,
        scratch=scratch,
        limit=18,
        flops=2 * rows * cols * width * columns,
    )


def last_kernel(_, keep, got, out):
    total = keep[0] + got[0].astype(F32)
    local = out.shape[-1]
    for index in range(out.shape[0]):
        out[index] = total[:, index * local : (index + 1) * local]


def last_sum(before, keep, got, local):
    shape = (keep.shape[2] // local, keep.shape[1], local)
    return in_vmem(last_kernel, "last_sum", (like(shape, F32),), before, keep, got, streamed=1)[0]


def body(sheet, w_query, w_key, w_value, cotangent, lengths):
    row_dev, cols, width = sheet.shape
    local = w_query.shape[1]
    n_rows = lax.axis_size("rows")
    n_heads = lax.axis_size("heads")
    scale = float(1.0 / (HEAD_DIM * row_dev * n_rows) ** 0.5)
    direct = n_rows <= 8
    shards = n_rows if direct else 1
    row_bits = [1 << b for b in range(n_rows.bit_length() - 1)]
    chunk = row_dev // 2

    me = jnp.stack([lax.axis_index("rows"), lax.axis_index("heads")]).astype(jnp.int32)
    wq, wk, wv = w_query.T, w_key.T, w_value.T
    cot = jnp.swapaxes(cotangent, 1, 2)

    fars = range(2, n_heads, 2)
    far_cot = [flip(cot, "heads", f) for f in fars]
    fq, fk = [[flip(w, "heads", f) for f in fars] for w in (wq, wk)]
    up = row_bits if direct else []
    turn_about = up[1:] + up[:1]
    qk, held, seen, *logits = query_key(me, lengths.reshape(1, row_dev), sheet, wq, wk, turn_about)
    where = jnp.concatenate([me, seen.reshape(row_dev)])
    dprob = value_dprob(where, held, wv, cot, logits[-1:], up, fars, n_heads)
    dprob, halves = dprob[: -len(fars)], dprob[-len(fars) :]
    fv = [flip(half, "heads", f) for half, f in zip(halves, fars)]
    weights = turn(where, wq, wk, wv, n_heads, dprob[-1:])
    if direct:
        logits = halve(*logits, "rows", turn_about)
        dprob = halve(*dprob, "rows", up)
        probs, dscore = softmax_back(logits, dprob, scale, [weights])
        probs, probs_order = double(probs, "rows", up[::-1], [far_cot])
        dscore, dscore_order = double(dscore, "rows", turn_about[::-1])
        scores = assemble(where, probs, dscore, (probs_order, dscore_order), shards, fq)
    else:
        logits, dprob = lax.psum((logits, dprob), "rows")
        scores = jnp.stack(softmax_back(logits, dprob, scale))
    far_scores = [flip(scores, "heads", f) for f in fars]
    grads = all_gradients(where, scores, qk, cot, "own_gradients", ())
    parts = weight_part(where, held, grads, (3 * local,), shards, fv)
    ready = [parts[-1]]
    far_qk = [far_query_key(where, held, *w, ready) for w in zip(fq, fk)]
    far_natural = [turn(where, *w, n_heads, ready) for w in zip(fq, fk, fv)]
    own = own_input(grads, weights, ready)
    ready = [own] + far_qk + far_natural
    far_grads = []

    def far_gradients(after):
        for args in zip(far_scores, far_qk, far_cot):
            far_grads.append(all_gradients(where, *args, "far_gradients", after))
        return far_grads

    steps = [[]]
    if direct:
        keep, give = parts
        for bit in row_bits[:-1]:
            give, keep = add_split(keep, flip(give, "rows", bit), ready)
            steps.append([keep])
            ready = far_grads or far_gradients(steps[-1])
        last = keep, flip(give, "rows", row_bits[-1])
    else:
        weight_grad = lax.psum_scatter(parts[0], "rows", scatter_dimension=0, tiled=True)
        weight_grad = weight_grad.reshape(width // n_rows, 3, local)
    if not far_grads:
        far_gradients(steps[-1])
    chunks = []
    for index, first in enumerate(range(0, row_dev, chunk)):
        after = steps[-1] if index else ()
        keep, give = far_input(first, chunk, own, list(zip(far_grads, far_natural)), after)
        chunks.append((keep, flip(give, "heads", 1)))
    out = finish(chunks)
    if direct:
        weight_grad = jnp.swapaxes(last_sum(out, *last, local), 0, 1)
    return (jnp.swapaxes(out, 1, 2), weight_grad)


def solution(mesh):
    in_specs = (
        P("rows", None, None),
        P(None, "heads"),
        P(None, "heads"),
        P(None, "heads"),
        P("rows", None, "heads"),
        P("rows"),
    )
    out_specs = (P("rows", None, "heads"), P("rows", None, "heads"))
    return jax.shard_map(body, mesh=mesh, in_specs=in_specs, out_specs=out_specs, check_vma=False)
```

```python
import functools
import math

import jax
import jax.numpy as jnp
from jax import lax
from jax.experimental import pallas as pl
from jax.experimental.pallas import tpu as pltpu
from jax.sharding import PartitionSpec as P

HEAD_DIM = 64
F32 = jnp.float32
BF16 = jnp.bfloat16
MIB = 1024 * 1024

NN = (((1,), (0,)), ((), ()))
NT = (((1,), (1,)), ((), ()))
TN = (((0,), (0,)), ((), ()))


def mm(a, b, dims):
    return lax.dot_general(a, b, dims, preferred_element_type=F32)


def flip(values, axis, bit):
    n = lax.axis_size(axis)
    return lax.ppermute(values, axis, [(s, s ^ bit) for s in range(n)])


def cost(flops, moved):
    return pl.CostEstimate(flops=int(flops), bytes_accessed=int(moved), transcendentals=0)


SMEM = pl.BlockSpec(memory_space=pltpu.SMEM)
VMEM = pl.BlockSpec(memory_space=pltpu.VMEM)
ANY = pl.BlockSpec(memory_space=pl.ANY)
HBM = pl.BlockSpec(memory_space=pltpu.HBM)


def like(shape, dtype=BF16):
    return jax.ShapeDtypeStruct(shape, dtype)


def place(a, stays):
    return pltpu.with_memory_space_constraint(a, pltpu.HBM) if stays else a


def in_vmem(kernel, name, out, *operands, scalars=0, streamed=0, after=(), scratch=(), limit=12, flops=0, counted=True):
    many = len(after)

    def run(*refs):
        kernel(*refs[: len(operands)], *refs[len(operands) + many :])

    moved = 2 * sum(a.size for a in operands) + 2 * sum(o.size for o in out)
    held = len(operands) - scalars - streamed
    return pl.pallas_call(
        run,
        in_specs=[SMEM] * scalars + [HBM] * streamed + [VMEM] * held + [ANY] * many,
        out_specs=[VMEM] * len(out),
        out_shape=list(out),
        scratch_shapes=list(scratch),
        compiler_params=pltpu.CompilerParams(vmem_limit_bytes=limit * MIB),
        cost_estimate=cost(flops, moved) if counted else cost(0, 0),
        name=name,
    )(*[place(a, scalars <= i < scalars + streamed) for i, a in enumerate(operands)], *after)


def lane_mask(length, cols):
    return (lax.broadcasted_iota(jnp.int32, (1, cols), 1) < length).astype(F32)


def reorder(bits):
    return [sum(bit for b, bit in enumerate(bits) if t >> b & 1) for t in range(1 << len(bits))]


def put_shards(me, acc, bits, outs):
    for t, j in enumerate(reorder(bits)):
        out = outs[t % len(outs)]
        out[t // len(outs)] = acc[:, me ^ j].astype(out.dtype)


BLOCK = 4
STEP = 2
AHEAD = 6


def query_key_kernel(bits, me, lengths, sheet, wq, wk, qk, held, seen, *rest):
    outs, (wt, acc, number, sems) = rest[:-4], rest[-4:]
    rows, cols, width = sheet.shape
    local = wq.shape[0]
    heads = local // HEAD_DIM
    copies = []

    def copy(source, target):
        copies.append(pltpu.make_async_copy(source, target, sems.at[len(copies)]))

    copy(lengths, number)
    copy(lengths, seen)
    copy(wq, wt.at[:local])
    copy(wk, wt.at[local:])
    for first in range(0, rows, STEP):
        some = pl.ds(first, STEP)
        copy(sheet.at[some], held.at[some])
    for one in copies[:AHEAD]:
        one.start()
    for one in copies[:4]:
        one.wait()
    flat = (BLOCK * HEAD_DIM, cols)
    for first in range(0, rows, BLOCK):
        for r in range(first, first + BLOCK):
            if r % STEP == 0:
                at = 4 + r // STEP
                copies[at].wait()
                for later in copies[at + AHEAD - 4 : at + AHEAD - 3]:
                    later.start()
            value = (mm(wt[...], held[r], NT) * lane_mask(number[0, r], cols)).astype(BF16)
            qk[r] = value.reshape(2 * heads, HEAD_DIM, cols)
        some = pl.ds(first, BLOCK)
        for h in range(heads):
            term = mm(qk[some, h].reshape(flat), qk[some, heads + h].reshape(flat), TN)
            term = term.reshape(acc.shape[1:])
            acc[h] = term if first == 0 else acc[h] + term
    put_shards(me[0], acc, bits, outs)


def query_key(me, lengths, sheet, wq, wk, bits):
    rows, cols, width = sheet.shape
    shards = 1 << len(bits)
    local = wq.shape[0]
    heads = local // HEAD_DIM
    return in_vmem(
        functools.partial(query_key_kernel, bits),
        "query_key",
        [like((rows, 2 * heads, HEAD_DIM, cols)), like(sheet.shape), like(lengths.shape, jnp.int32)]
        + part_shapes(shards, heads, cols),
        me,
        lengths,
        sheet,
        wq,
        wk,
        scalars=1,
        streamed=4,
        scratch=(
            pltpu.VMEM((2 * local, width), BF16),
            pltpu.VMEM((heads, shards, cols // shards, cols), F32),
            pltpu.SMEM(lengths.shape, jnp.int32),
            pltpu.SemaphoreType.DMA((4 + rows // STEP,)),
        ),
        limit=14,
        flops=rows * cols * local * (2 * width + cols) // 2,
    )


def value_kernel(bits, fars, where, sheet, wv, cot, *rest):
    outs, halves, acc = rest[: -1 - len(fars)], rest[-1 - len(fars) : -1], rest[-1]
    rows, cols, width = sheet.shape
    for far, half in zip(fars, halves):
        near = half.shape[1]
        side = lax.shift_right_logical(where[1], 1) ^ (far // 2)
        for s in range(width // near):
            @pl.when(side == s)
            def _():
                half[...] = wv[:, s * near : (s + 1) * near]
    local = wv.shape[0]
    heads = local // HEAD_DIM
    flat = (BLOCK * HEAD_DIM, cols)
    for first in range(0, rows, BLOCK):
        values = []
        for r in range(first, first + BLOCK):
            value = (mm(wv[...], sheet[r], NT) * lane_mask(where[2 + r], cols)).astype(BF16)
            values.append(value.reshape(heads, HEAD_DIM, cols))
        for h in range(heads):
            left = cot[pl.ds(first, BLOCK), h * HEAD_DIM : (h + 1) * HEAD_DIM].reshape(flat)
            right = jnp.concatenate([v[h] for v in values], axis=0)
            term = mm(left, right, TN).reshape(acc.shape[1:])
            acc[h] = term if first == 0 else acc[h] + term
    put_shards(where[0], acc, bits, outs)


def value_dprob(where, sheet, wv, cot, after, bits, fars, devices):
    rows, cols, width = sheet.shape
    shards = 1 << len(bits)
    local = wv.shape[0]
    heads = local // HEAD_DIM
    return in_vmem(
        functools.partial(value_kernel, bits, fars),
        "value_dprob",
        part_shapes(shards, heads, cols) + [like((local, 2 * width // devices))] * len(fars),
        where,
        sheet,
        wv,
        cot,
        scalars=1,
        after=after,
        scratch=(pltpu.VMEM((heads, shards, cols // shards, cols), F32),),
        limit=16,
        flops=4 * rows * cols * local * (width + cols),
    )


def turn_kernel(where, wq, wk, wv, natural, *full):
    near, share, columns = natural.shape
    local = wq.shape[0]
    for index, (weight, held) in enumerate(zip((wq, wk, wv), full)):
        held[...] = weight[...].T.reshape(held.shape)
        mine = where[1] & (held.shape[0] - 1)
        for j in range(near):
            natural[j, :, index * local : (index + 1) * local] = held[mine ^ j]


def turn(where, wq, wk, wv, devices, after):
    local, width = wq.shape
    share = width // devices
    return in_vmem(
        turn_kernel,
        "turn",
        (like((2, share, 3 * local)),),
        where,
        wq,
        wk,
        wv,
        scalars=1,
        after=after,
        scratch=[pltpu.VMEM((w.shape[1] // share, share, local), BF16) for w in (wq, wk, wv)],
    )[0]


def far_query_key_kernel(where, sheet, wq, wk, qk):
    local = wq.shape[0]
    rows, cols, _ = sheet.shape
    both = jnp.concatenate([wq[...], wk[...]], axis=0)
    for r in range(rows):
        value = (mm(both, sheet[r], NT) * lane_mask(where[2 + r], cols)).astype(BF16)
        qk[r] = value.reshape(2 * local // HEAD_DIM, HEAD_DIM, cols)


def far_query_key(where, sheet, wq, wk, after):
    rows, cols, width = sheet.shape
    local = wq.shape[0]
    return in_vmem(
        far_query_key_kernel,
        "far_query_key",
        (like((rows, 2 * local // HEAD_DIM, HEAD_DIM, cols)),),
        where,
        sheet,
        wq,
        wk,
        scalars=1,
        after=after,
        flops=4 * rows * cols * local * width,
    )[0]


def part_shapes(shards, heads, cols):
    if shards == 1:
        return [like((1, heads, cols, cols), F32)]
    half = (shards // 2, heads, cols // shards, cols)
    return [like(half, F32), like(half)]


def hold_kernel(values, out):
    out[...] = values[...]


def hold(values, after):
    return in_vmem(hold_kernel, "hold", (like(values.shape),), values, after=after)[0]


def add_split_kernel(keep, got, give_out, keep_out):
    for j in range(keep.shape[0]):
        total = keep[j].astype(F32) + got[j].astype(F32)
        out = give_out if j % 2 else keep_out
        out[j // 2] = total.astype(out.dtype)


def add_split(keep, got, after=(), flops=0):
    half = (keep.shape[0] // 2,) + keep.shape[1:]
    return in_vmem(add_split_kernel, "add_split", (like(half), like(half, keep.dtype)), keep, got, after=after, flops=flops)


def halve(keep, give, axis, bits, after=(), flops=0):
    after = list(after) + [()] * len(bits)
    for bit, waits in zip(bits[:-1], after):
        give, keep = add_split(keep, flip(give, axis, bit), waits, flops)
    return keep, flip(give, axis, bits[-1])


def softmax_kernel(scale, *refs):
    *terms, probs_out, dscore_out = refs
    half = len(terms) // 2
    total = lambda some: functools.reduce(jnp.add, [t[0].astype(F32) for t in some])
    logits = total(terms[:half]) * scale
    dprob = total(terms[half:])
    shifted = jnp.exp(logits - jnp.max(logits, axis=-1, keepdims=True))
    probs = shifted / jnp.sum(shifted, axis=-1, keepdims=True)
    inner = jnp.sum(probs * dprob, axis=-1, keepdims=True)
    probs_out[0] = probs.astype(BF16)
    dscore_out[0] = (scale * probs * (dprob - inner)).astype(BF16)


def softmax_back(logits, dprob, scale, after=()):
    out = like(logits[0].shape)
    return in_vmem(
        functools.partial(softmax_kernel, scale), "softmax_back", (out, out), *logits, *dprob, limit=16, after=after
    )


def join_kernel(one, other, out):
    out[: one.shape[0]] = one[...]
    out[one.shape[0] :] = other[...]


def join(one, other, after):
    shape = (one.shape[0] + other.shape[0],) + one.shape[1:]
    return in_vmem(join_kernel, "join", (like(shape),), one, other, after=after)[0]


def double(values, axis, bits, after=()):
    order = [0]
    after = list(after) + [()] * len(bits)
    for bit, waits in zip(bits[:-1], after):
        values = join(values, flip(values, axis, bit), waits)
        order = order + [j ^ bit for j in order]
    other = flip(values, axis, bits[-1])
    return (values, other), (order, [j ^ bits[-1] for j in order])


def assemble_kernel(orders, where, *refs):
    *pieces, out = refs
    for piece, (kind, order) in zip(pieces, orders):
        for t, j in enumerate(order):
            out[kind, where[0] ^ j] = piece[t]


def assemble(where, probs, dscore, orders, shards, after):
    orders = [(kind, order) for kind, both in enumerate(orders) for order in both]
    out = like((2, shards) + probs[0].shape[1:])
    return in_vmem(
        functools.partial(assemble_kernel, orders),
        "assemble",
        (out,),
        where,
        *probs,
        *dscore,
        scalars=1,
        after=after,
    )[0]


def gradients(where, first, count, scores, qk, cot, grads):
    cols = qk.shape[-1]
    heads = qk.shape[1] // 2
    rows = pl.ds(first, count)
    flat = (count * HEAD_DIM, cols)
    split = (count, HEAD_DIM, cols)
    masks = jnp.stack([lane_mask(where[2 + first + r], cols) for r in range(count)])
    for h in range(heads):
        p, ds = [scores[kind, :, h].reshape(cols, cols) for kind in range(2)]
        g = cot[rows, h * HEAD_DIM : (h + 1) * HEAD_DIM].reshape(flat)
        dq = mm(qk[rows, heads + h].reshape(flat), ds, NT)
        dk = mm(qk[rows, h].reshape(flat), ds, NN)
        dv = mm(g, p, NN)
        for index, value in enumerate((dq, dk, dv)):
            grads[:, index * heads + h] = (value.reshape(split) * masks).astype(BF16)


def gradients_kernel(where, scores, qk, cot, grads):
    gradients(where, 0, qk.shape[0], scores, qk, cot, grads)


def all_gradients(where, scores, qk, cot, name, after, counted=True):
    rows, two, _, cols = qk.shape
    return in_vmem(
        gradients_kernel,
        name,
        (like((rows, two // 2 * 3, HEAD_DIM, cols)),),
        where,
        scores,
        qk,
        cot,
        scalars=1,
        after=after,
        limit=14,
        counted=counted,
        flops=3 * rows * two * HEAD_DIM * cols * cols,
    )[0]


def own_input_kernel(grads, weights, out):
    near, share, columns = weights.shape
    left = weights[...].reshape(near * share, columns)
    for r in range(grads.shape[0]):
        part = mm(left, grads[r].reshape(columns, grads.shape[-1]), NN).astype(BF16)
        out[:, r] = part.reshape(near, share, grads.shape[-1])


def own_input(grads, weights, after):
    rows, cols = grads.shape[0], grads.shape[-1]
    near, share, columns = weights.shape
    return in_vmem(
        own_input_kernel,
        "own_input",
        (like((near, rows, share, cols)),),
        grads,
        weights,
        after=after,
        flops=2 * rows * cols * near * share * columns,
    )[0]


def far_input_kernel(first, own, *refs):
    *refs, keep, give = refs
    count, share, cols = keep.shape
    for r in range(count):
        total = own[:, first + r].astype(F32)
        for i in range(0, len(refs), 2):
            grads, weights = refs[i : i + 2]
            near, _, columns = weights.shape
            left = weights[...].reshape(near * share, columns)
            part = mm(left, grads[first + r].reshape(columns, cols), NN).astype(BF16)
            total = total + part.reshape(near, share, cols).astype(F32)
        keep[r] = total[0].astype(keep.dtype)
        give[r] = total[1].astype(give.dtype)


def far_input(first, count, own, far, after):
    _, rows, share, cols = own.shape
    columns = far[0][1].shape[-1]
    out = like((count, share, cols))
    return in_vmem(
        functools.partial(far_input_kernel, first),
        "far_input",
        (out, out),
        own,
        *[a for one in far for a in one],
        after=after,
        limit=14,
        counted=False,
        flops=4 * len(far) * count * cols * columns * share,
    )


def finish_kernel(*refs):
    *terms, out, total, sems = refs
    copies = []
    first = 0
    for index in range(0, len(terms), 2):
        keep, got = terms[index : index + 2]
        some = pl.ds(first, keep.shape[0])
        total[some] = (keep[...].astype(F32) + got[...].astype(F32)).astype(BF16)
        copies.append(pltpu.make_async_copy(total.at[some], out.at[some], sems.at[index // 2]))
        copies[-1].start()
        first += keep.shape[0]
    for copy in copies:
        copy.wait()


def finish(chunks):
    _, share, cols = chunks[0][0].shape
    rows = sum(keep.shape[0] for keep, _ in chunks)
    terms = [a for chunk in chunks for a in chunk]
    return pl.pallas_call(
        finish_kernel,
        in_specs=[VMEM] * len(terms),
        out_specs=HBM,
        out_shape=like((rows, share, cols)),
        scratch_shapes=[pltpu.VMEM((rows, share, cols), BF16), pltpu.SemaphoreType.DMA((len(chunks),))],
        compiler_params=pltpu.CompilerParams(vmem_limit_bytes=12 * MIB),
        cost_estimate=cost(rows * share * cols, 6 * rows * share * cols),
        name="finish",
    )(*terms)


def weight_product(sheet, grads):
    rows, cols, width = sheet.shape
    columns = grads.shape[1] * HEAD_DIM
    left = [grads[r].reshape(columns, cols) for r in range(rows)]
    return mm(jnp.concatenate(left, axis=1), sheet[...].reshape(rows * cols, width), NN).T


def weight_kernel(bits, where, sheet, grads, *rest):
    outs, full = rest[:-1], rest[-1]
    full[...] = weight_product(sheet, grads).reshape(full.shape)
    for t, j in enumerate(reorder(bits)):
        first = 0
        for keep, give in zip(outs[::2], outs[1::2]):
            out = (keep, give)[t % 2]
            last = first + out.shape[-1]
            out[t // 2] = full[where[0] ^ j, :, first:last].astype(out.dtype)
            first = last


def whole_weight_kernel(_, where, sheet, grads, out):
    out[...] = weight_product(sheet, grads)


def weight_part(where, sheet, grads, cuts, bits, after):
    rows, cols, width = sheet.shape
    shards = 1 << len(bits)
    columns = grads.shape[1] * HEAD_DIM
    if shards == 1:
        kernel, outs, scratch = whole_weight_kernel, [like((width, columns), F32)], ()
    else:
        halves = [(shards // 2, width // shards, cut) for cut in cuts]
        kernel = weight_kernel
        outs = [o for half in halves for o in (like(half, F32), like(half))]
        scratch = (pltpu.VMEM((shards, width // shards, columns), F32),)
    return in_vmem(
        functools.partial(kernel, bits),
        "weight_part",
        outs,
        where,
        sheet,
        grads,
        scalars=1,
        after=after,
        scratch=scratch,
        limit=18,
        flops=2 * rows * cols * width * columns,
    )


def last_kernel(_, keep, got, out):
    total = keep[0] + got[0].astype(F32)
    local = out.shape[-1]
    for index in range(out.shape[0]):
        out[index] = total[:, index * local : (index + 1) * local]


def last_sum(before, keep, got, local):
    shape = (keep.shape[2] // local, keep.shape[1], local)
    return in_vmem(last_kernel, "last_sum", (like(shape, F32),), before, keep, got, streamed=1)[0]


def body(sheet, w_query, w_key, w_value, cotangent, lengths):
    row_dev, cols, width = sheet.shape
    local = w_query.shape[1]
    n_rows = lax.axis_size("rows")
    n_heads = lax.axis_size("heads")
    scale = float(1.0 / (HEAD_DIM * row_dev * n_rows) ** 0.5)
    direct = n_rows <= 8
    shards = n_rows if direct else 1
    row_bits = [1 << b for b in range(n_rows.bit_length() - 1)]
    chunk = row_dev // 2

    me = jnp.stack([lax.axis_index("rows"), lax.axis_index("heads")]).astype(jnp.int32)
    wq, wk, wv = w_query.T, w_key.T, w_value.T
    cot = jnp.swapaxes(cotangent, 1, 2)

    fars = range(2, n_heads, 2)
    far_cot = [flip(cot, "heads", f) for f in fars]
    fq, fk = [[flip(w, "heads", f) for f in fars] for w in (wq, wk)]
    up = row_bits if direct else []
    turn_about = up[1:] + up[:1]
    qk, held, seen, *logits = query_key(me, lengths.reshape(1, row_dev), sheet, wq, wk, turn_about)
    where = jnp.concatenate([me, seen.reshape(row_dev)])
    dprob = value_dprob(where, held, wv, cot, logits[-1:], up, fars, n_heads)
    dprob, halves = dprob[: -len(fars)], dprob[-len(fars) :]
    fv = [flip(half, "heads", f) for half, f in zip(halves, fars)]
    weights = turn(where, wq, wk, wv, n_heads, dprob[-1:])
    if direct:
        logits = halve(*logits, "rows", turn_about)
        dprob = halve(*dprob, "rows", up)
        probs, dscore = softmax_back(logits, dprob, scale, [weights])
        probs, probs_order = double(probs, "rows", up[::-1], [far_cot])
        dscore, dscore_order = double(dscore, "rows", turn_about[::-1])
        scores = assemble(where, probs, dscore, (probs_order, dscore_order), shards, fq)
    else:
        logits, dprob = lax.psum((logits, dprob), "rows")
        scores = jnp.stack(softmax_back(logits, dprob, scale))
    far_scores = [flip(scores, "heads", f) for f in fars]
    grads = all_gradients(where, scores, qk, cot, "own_gradients", ())
    weight_bits = up[:1] + up[1:][::-1]
    parts = weight_part(where, held, grads, (3 * local,), weight_bits, fv)
    ready = [parts[-1]]
    far_qk = [far_query_key(where, held, *w, ready) for w in zip(fq, fk)]
    far_natural = [turn(where, *w, n_heads, ready) for w in zip(fq, fk, fv)]
    own = own_input(grads, weights, ready)
    ready = [own] + far_qk + far_natural
    first_sum = []
    if direct:
        keep, give = parts
        give, keep = add_split(keep, flip(give, "rows", weight_bits[0]), ready)
        first_sum = [keep]
    else:
        weight_grad = lax.psum_scatter(parts[0], "rows", scatter_dimension=0, tiled=True)
        weight_grad = weight_grad.reshape(width // n_rows, 3, local)
    far_grads = [
        all_gradients(where, *args, "far_gradients", first_sum, False)
        for args in zip(far_scores, far_qk, far_cot)
    ]
    chunks = []
    for first in range(0, row_dev, chunk):
        keep_rows, give_rows = far_input(first, chunk, own, list(zip(far_grads, far_natural)), ())
        chunks.append((keep_rows, flip(give_rows, "heads", 1)))
    if direct:
        last = halve(keep, give, "rows", weight_bits[1:], [[chunks[-1][0]]], 1 << 34)
    out = finish(chunks)
    if direct:
        weight_grad = jnp.swapaxes(last_sum(out, *last, local), 0, 1)
    return (jnp.swapaxes(out, 1, 2), weight_grad)


def solution(mesh):
    in_specs = (
        P("rows", None, None),
        P(None, "heads"),
        P(None, "heads"),
        P(None, "heads"),
        P("rows", None, "heads"),
        P("rows"),
    )
    out_specs = (P("rows", None, "heads"), P("rows", None, "heads"))
    return jax.shard_map(body, mesh=mesh, in_specs=in_specs, out_specs=out_specs, check_vma=False)
```

```python
import functools
import math

import jax
import jax.numpy as jnp
from jax import lax
from jax.experimental import pallas as pl
from jax.experimental.pallas import tpu as pltpu
from jax.sharding import PartitionSpec as P

HEAD_DIM = 64
F32 = jnp.float32
BF16 = jnp.bfloat16
MIB = 1024 * 1024

NN = (((1,), (0,)), ((), ()))
NT = (((1,), (1,)), ((), ()))
TN = (((0,), (0,)), ((), ()))


def mm(a, b, dims):
    return lax.dot_general(a, b, dims, preferred_element_type=F32)


def flip(values, axis, bit):
    n = lax.axis_size(axis)
    return lax.ppermute(values, axis, [(s, s ^ bit) for s in range(n)])


def cost(flops, moved):
    return pl.CostEstimate(flops=int(flops), bytes_accessed=int(moved), transcendentals=0)


SMEM = pl.BlockSpec(memory_space=pltpu.SMEM)
VMEM = pl.BlockSpec(memory_space=pltpu.VMEM)
ANY = pl.BlockSpec(memory_space=pl.ANY)
HBM = pl.BlockSpec(memory_space=pltpu.HBM)


def like(shape, dtype=BF16):
    return jax.ShapeDtypeStruct(shape, dtype)


def place(a, stays):
    return pltpu.with_memory_space_constraint(a, pltpu.HBM) if stays else a


def in_vmem(kernel, name, out, *operands, scalars=0, streamed=0, after=(), scratch=(), limit=12, flops=0, counted=True):
    many = len(after)

    def run(*refs):
        kernel(*refs[: len(operands)], *refs[len(operands) + many :])

    moved = 2 * sum(a.size for a in operands) + 2 * sum(o.size for o in out)
    held = len(operands) - scalars - streamed
    return pl.pallas_call(
        run,
        in_specs=[SMEM] * scalars + [HBM] * streamed + [VMEM] * held + [ANY] * many,
        out_specs=[VMEM] * len(out),
        out_shape=list(out),
        scratch_shapes=list(scratch),
        compiler_params=pltpu.CompilerParams(vmem_limit_bytes=limit * MIB),
        cost_estimate=cost(flops, moved) if counted else cost(0, 0),
        name=name,
    )(*[place(a, scalars <= i < scalars + streamed) for i, a in enumerate(operands)], *after)


def lane_mask(length, cols):
    return (lax.broadcasted_iota(jnp.int32, (1, cols), 1) < length).astype(F32)


def reorder(bits):
    return [sum(bit for b, bit in enumerate(bits) if t >> b & 1) for t in range(1 << len(bits))]


def put_shards(me, acc, bits, outs):
    for t, j in enumerate(reorder(bits)):
        out = outs[t % len(outs)]
        out[t // len(outs)] = acc[:, me ^ j].astype(out.dtype)


BLOCK = 4
STEP = 2
AHEAD = 6


def query_key_kernel(bits, me, lengths, sheet, wq, wk, qk, held, seen, *rest):
    outs, (wt, acc, number, sems) = rest[:-4], rest[-4:]
    rows, cols, width = sheet.shape
    local = wq.shape[0]
    heads = local // HEAD_DIM
    copies = []

    def copy(source, target):
        copies.append(pltpu.make_async_copy(source, target, sems.at[len(copies)]))

    copy(lengths, number)
    copy(lengths, seen)
    copy(wq, wt.at[:local])
    copy(wk, wt.at[local:])
    for first in range(0, rows, STEP):
        some = pl.ds(first, STEP)
        copy(sheet.at[some], held.at[some])
    for one in copies[:AHEAD]:
        one.start()
    for one in copies[:4]:
        one.wait()
    flat = (BLOCK * HEAD_DIM, cols)
    for first in range(0, rows, BLOCK):
        for r in range(first, first + BLOCK):
            if r % STEP == 0:
                at = 4 + r // STEP
                copies[at].wait()
                for later in copies[at + AHEAD - 4 : at + AHEAD - 3]:
                    later.start()
            value = (mm(wt[...], held[r], NT) * lane_mask(number[0, r], cols)).astype(BF16)
            qk[r] = value.reshape(2 * heads, HEAD_DIM, cols)
        some = pl.ds(first, BLOCK)
        for h in range(heads):
            term = mm(qk[some, h].reshape(flat), qk[some, heads + h].reshape(flat), TN)
            term = term.reshape(acc.shape[1:])
            acc[h] = term if first == 0 else acc[h] + term
    put_shards(me[0], acc, bits, outs)


def query_key(me, lengths, sheet, wq, wk, bits):
    rows, cols, width = sheet.shape
    shards = 1 << len(bits)
    local = wq.shape[0]
    heads = local // HEAD_DIM
    return in_vmem(
        functools.partial(query_key_kernel, bits),
        "query_key",
        [like((rows, 2 * heads, HEAD_DIM, cols)), like(sheet.shape), like(lengths.shape, jnp.int32)]
        + part_shapes(shards, heads, cols),
        me,
        lengths,
        sheet,
        wq,
        wk,
        scalars=1,
        streamed=4,
        scratch=(
            pltpu.VMEM((2 * local, width), BF16),
            pltpu.VMEM((heads, shards, cols // shards, cols), F32),
            pltpu.SMEM(lengths.shape, jnp.int32),
            pltpu.SemaphoreType.DMA((4 + rows // STEP,)),
        ),
        limit=14,
        flops=rows * cols * local * (2 * width + cols) // 2,
    )


def value_kernel(bits, fars, where, sheet, wv, cot, *rest):
    outs, halves, acc = rest[: -1 - len(fars)], rest[-1 - len(fars) : -1], rest[-1]
    rows, cols, width = sheet.shape
    for far, half in zip(fars, halves):
        near = half.shape[1]
        side = lax.shift_right_logical(where[1], 1) ^ (far // 2)
        for s in range(width // near):
            @pl.when(side == s)
            def _():
                half[...] = wv[:, s * near : (s + 1) * near]
    local = wv.shape[0]
    heads = local // HEAD_DIM
    flat = (BLOCK * HEAD_DIM, cols)
    for first in range(0, rows, BLOCK):
        values = []
        for r in range(first, first + BLOCK):
            value = (mm(wv[...], sheet[r], NT) * lane_mask(where[2 + r], cols)).astype(BF16)
            values.append(value.reshape(heads, HEAD_DIM, cols))
        for h in range(heads):
            left = cot[pl.ds(first, BLOCK), h * HEAD_DIM : (h + 1) * HEAD_DIM].reshape(flat)
            right = jnp.concatenate([v[h] for v in values], axis=0)
            term = mm(left, right, TN).reshape(acc.shape[1:])
            acc[h] = term if first == 0 else acc[h] + term
    put_shards(where[0], acc, bits, outs)


def value_dprob(where, sheet, wv, cot, after, bits, fars, devices):
    rows, cols, width = sheet.shape
    shards = 1 << len(bits)
    local = wv.shape[0]
    heads = local // HEAD_DIM
    return in_vmem(
        functools.partial(value_kernel, bits, fars),
        "value_dprob",
        part_shapes(shards, heads, cols) + [like((local, 2 * width // devices))] * len(fars),
        where,
        sheet,
        wv,
        cot,
        scalars=1,
        after=after,
        scratch=(pltpu.VMEM((heads, shards, cols // shards, cols), F32),),
        limit=16,
        flops=4 * rows * cols * local * (width + cols),
    )


def turn_kernel(where, wq, wk, wv, natural, *full):
    near, share, columns = natural.shape
    local = wq.shape[0]
    for index, (weight, held) in enumerate(zip((wq, wk, wv), full)):
        held[...] = weight[...].T.reshape(held.shape)
        mine = where[1] & (held.shape[0] - 1)
        for j in range(near):
            natural[j, :, index * local : (index + 1) * local] = held[mine ^ j]


def turn(where, wq, wk, wv, devices, after):
    local, width = wq.shape
    share = width // devices
    return in_vmem(
        turn_kernel,
        "turn",
        (like((2, share, 3 * local)),),
        where,
        wq,
        wk,
        wv,
        scalars=1,
        after=after,
        scratch=[pltpu.VMEM((w.shape[1] // share, share, local), BF16) for w in (wq, wk, wv)],
    )[0]


def far_query_key_kernel(where, sheet, wq, wk, qk):
    local = wq.shape[0]
    rows, cols, _ = sheet.shape
    both = jnp.concatenate([wq[...], wk[...]], axis=0)
    for r in range(rows):
        value = (mm(both, sheet[r], NT) * lane_mask(where[2 + r], cols)).astype(BF16)
        qk[r] = value.reshape(2 * local // HEAD_DIM, HEAD_DIM, cols)


def far_query_key(where, sheet, wq, wk, after):
    rows, cols, width = sheet.shape
    local = wq.shape[0]
    return in_vmem(
        far_query_key_kernel,
        "far_query_key",
        (like((rows, 2 * local // HEAD_DIM, HEAD_DIM, cols)),),
        where,
        sheet,
        wq,
        wk,
        scalars=1,
        after=after,
        flops=4 * rows * cols * local * width,
    )[0]


def part_shapes(shards, heads, cols):
    if shards == 1:
        return [like((1, heads, cols, cols), F32)]
    half = (shards // 2, heads, cols // shards, cols)
    return [like(half, F32), like(half)]


def hold_kernel(values, out):
    out[...] = values[...]


def hold(values, after):
    return in_vmem(hold_kernel, "hold", (like(values.shape),), values, after=after)[0]


def add_split_kernel(keep, got, give_out, keep_out):
    for j in range(keep.shape[0]):
        total = keep[j].astype(F32) + got[j].astype(F32)
        out = give_out if j % 2 else keep_out
        out[j // 2] = total.astype(out.dtype)


def add_split(keep, got, after=(), flops=0):
    half = (keep.shape[0] // 2,) + keep.shape[1:]
    return in_vmem(add_split_kernel, "add_split", (like(half), like(half, keep.dtype)), keep, got, after=after, flops=flops)


def halve(keep, give, axis, bits, after=(), flops=0):
    after = list(after) + [()] * len(bits)
    for bit, waits in zip(bits[:-1], after):
        give, keep = add_split(keep, flip(give, axis, bit), waits, flops)
    return keep, flip(give, axis, bits[-1])


def softmax_kernel(scale, *refs):
    *terms, probs_out, dscore_out = refs
    half = len(terms) // 2
    total = lambda some: functools.reduce(jnp.add, [t[0].astype(F32) for t in some])
    logits = total(terms[:half]) * scale
    dprob = total(terms[half:])
    shifted = jnp.exp(logits - jnp.max(logits, axis=-1, keepdims=True))
    probs = shifted / jnp.sum(shifted, axis=-1, keepdims=True)
    inner = jnp.sum(probs * dprob, axis=-1, keepdims=True)
    probs_out[0] = probs.astype(BF16)
    dscore_out[0] = (scale * probs * (dprob - inner)).astype(BF16)


def softmax_back(logits, dprob, scale, after=()):
    out = like(logits[0].shape)
    return in_vmem(
        functools.partial(softmax_kernel, scale), "softmax_back", (out, out), *logits, *dprob, limit=16, after=after
    )


def join_kernel(one, other, out):
    out[: one.shape[0]] = one[...]
    out[one.shape[0] :] = other[...]


def join(one, other, after):
    shape = (one.shape[0] + other.shape[0],) + one.shape[1:]
    return in_vmem(join_kernel, "join", (like(shape),), one, other, after=after)[0]


def double(values, axis, bits, after=()):
    order = [0]
    after = list(after) + [()] * len(bits)
    for bit, waits in zip(bits[:-1], after):
        values = join(values, flip(values, axis, bit), waits)
        order = order + [j ^ bit for j in order]
    other = flip(values, axis, bits[-1])
    return (values, other), (order, [j ^ bits[-1] for j in order])


def assemble_kernel(orders, where, *refs):
    *pieces, out = refs
    for piece, (kind, order) in zip(pieces, orders):
        for t, j in enumerate(order):
            out[kind, where[0] ^ j] = piece[t]


def assemble(where, probs, dscore, orders, shards, after):
    orders = [(kind, order) for kind, both in enumerate(orders) for order in both]
    out = like((2, shards) + probs[0].shape[1:])
    return in_vmem(
        functools.partial(assemble_kernel, orders),
        "assemble",
        (out,),
        where,
        *probs,
        *dscore,
        scalars=1,
        after=after,
    )[0]


def masked(where, value):
    rows, cols = value.shape[0] // HEAD_DIM, value.shape[1]
    masks = jnp.stack([lane_mask(where[2 + r], cols) for r in range(rows)])
    return (value.reshape(rows, HEAD_DIM, cols) * masks).astype(BF16)


def query_key_gradients(where, dscore, qk, grads):
    rows, two, _, cols = qk.shape
    heads = two // 2
    flat = (rows * HEAD_DIM, cols)
    for h in range(heads):
        ds = dscore[:, h].reshape(cols, cols)
        grads[:, h] = masked(where, mm(qk[:, heads + h].reshape(flat), ds, NT))
        grads[:, heads + h] = masked(where, mm(qk[:, h].reshape(flat), ds, NN))


def value_gradients(where, probs, cot, first, grads):
    rows, local, cols = cot.shape
    for h in range(local // HEAD_DIM):
        g = cot[:, h * HEAD_DIM : (h + 1) * HEAD_DIM].reshape(rows * HEAD_DIM, cols)
        grads[:, first + h] = masked(where, mm(g, probs[:, h].reshape(cols, cols), NN))


def own_query_key_kernel(orders, where, *refs):
    *pieces, qk, grads, dscore = refs
    for piece, order in zip(pieces, orders):
        for t, j in enumerate(order):
            dscore[where[0] ^ j] = piece[t]
    query_key_gradients(where, dscore, qk, grads)


def own_query_key(where, pieces, orders, qk, shards):
    return in_vmem(
        functools.partial(own_query_key_kernel, orders),
        "own_query_key",
        (like(qk.shape),),
        where,
        *pieces,
        qk,
        scalars=1,
        scratch=(pltpu.VMEM((shards,) + pieces[0].shape[1:], BF16),),
        limit=14,
        flops=2 * qk.size * qk.shape[-1],
    )[0]


def own_value_kernel(where, scores, cot, grads):
    value_gradients(where, scores.at[0], cot, 0, grads)


def own_value(where, scores, cot):
    rows, local, cols = cot.shape
    return in_vmem(
        own_value_kernel,
        "own_value",
        (like((rows, local // HEAD_DIM, HEAD_DIM, cols)),),
        where,
        scores,
        cot,
        scalars=1,
        limit=14,
        flops=2 * cot.size * cols,
    )[0]


def far_gradients_kernel(where, scores, qk, cot, grads):
    query_key_gradients(where, scores.at[1], qk, grads)
    value_gradients(where, scores.at[0], cot, qk.shape[1], grads)


def far_gradients(where, scores, qk, cot, after):
    rows, two, _, cols = qk.shape
    return in_vmem(
        far_gradients_kernel,
        "far_gradients",
        (like((rows, two // 2 * 3, HEAD_DIM, cols)),),
        where,
        scores,
        qk,
        cot,
        scalars=1,
        after=after,
        limit=14,
        counted=False,
    )[0]


def all_rows(grads, r):
    cols = grads[0].shape[-1]
    return jnp.concatenate([g[r].reshape(g.shape[1] * HEAD_DIM, cols) for g in grads], axis=0)


def own_input_kernel(two, value, weights, out):
    near, share, columns = weights.shape
    left = weights[...].reshape(near * share, columns)
    for r in range(two.shape[0]):
        part = mm(left, all_rows((two, value), r), NN).astype(BF16)
        out[:, r] = part.reshape(near, share, two.shape[-1])


def own_input(grads, weights, after):
    rows, cols = grads[0].shape[0], grads[0].shape[-1]
    near, share, columns = weights.shape
    return in_vmem(
        own_input_kernel,
        "own_input",
        (like((near, rows, share, cols)),),
        *grads,
        weights,
        after=after,
        flops=2 * rows * cols * near * share * columns,
    )[0]


def far_input_kernel(first, own, *refs):
    *refs, keep, give = refs
    count, share, cols = keep.shape
    for r in range(count):
        total = own[:, first + r].astype(F32)
        for i in range(0, len(refs), 2):
            grads, weights = refs[i : i + 2]
            near, _, columns = weights.shape
            left = weights[...].reshape(near * share, columns)
            part = mm(left, grads[first + r].reshape(columns, cols), NN).astype(BF16)
            total = total + part.reshape(near, share, cols).astype(F32)
        keep[r] = total[0].astype(keep.dtype)
        give[r] = total[1].astype(give.dtype)


def far_input(first, count, own, far, after):
    _, rows, share, cols = own.shape
    columns = far[0][1].shape[-1]
    out = like((count, share, cols))
    return in_vmem(
        functools.partial(far_input_kernel, first),
        "far_input",
        (out, out),
        own,
        *[a for one in far for a in one],
        after=after,
        limit=14,
        counted=False,
        flops=4 * len(far) * count * cols * columns * share,
    )


def finish_kernel(*refs):
    *terms, out, total, sems = refs
    copies = []
    first = 0
    for index in range(0, len(terms), 2):
        keep, got = terms[index : index + 2]
        some = pl.ds(first, keep.shape[0])
        total[some] = (keep[...].astype(F32) + got[...].astype(F32)).astype(BF16)
        copies.append(pltpu.make_async_copy(total.at[some], out.at[some], sems.at[index // 2]))
        copies[-1].start()
        first += keep.shape[0]
    for copy in copies:
        copy.wait()


def finish(chunks):
    _, share, cols = chunks[0][0].shape
    rows = sum(keep.shape[0] for keep, _ in chunks)
    terms = [a for chunk in chunks for a in chunk]
    return pl.pallas_call(
        finish_kernel,
        in_specs=[VMEM] * len(terms),
        out_specs=HBM,
        out_shape=like((rows, share, cols)),
        scratch_shapes=[pltpu.VMEM((rows, share, cols), BF16), pltpu.SemaphoreType.DMA((len(chunks),))],
        compiler_params=pltpu.CompilerParams(vmem_limit_bytes=12 * MIB),
        cost_estimate=cost(rows * share * cols, 6 * rows * share * cols),
        name="finish",
    )(*terms)


def weight_product(sheet, grads):
    rows, cols, width = sheet.shape
    left = [all_rows(grads, r) for r in range(rows)]
    return mm(jnp.concatenate(left, axis=1), sheet[...].reshape(rows * cols, width), NN).T


def weight_kernel(bits, where, sheet, two, value, *rest):
    outs, full = rest[:-1], rest[-1]
    full[...] = weight_product(sheet, (two, value)).reshape(full.shape)
    for t, j in enumerate(reorder(bits)):
        first = 0
        for keep, give in zip(outs[::2], outs[1::2]):
            out = (keep, give)[t % 2]
            last = first + out.shape[-1]
            out[t // 2] = full[where[0] ^ j, :, first:last].astype(out.dtype)
            first = last


def whole_weight_kernel(_, where, sheet, two, value, out):
    out[...] = weight_product(sheet, (two, value))


def weight_part(where, sheet, grads, cuts, bits, after):
    rows, cols, width = sheet.shape
    shards = 1 << len(bits)
    columns = sum(g.shape[1] for g in grads) * HEAD_DIM
    if shards == 1:
        kernel, outs, scratch = whole_weight_kernel, [like((width, columns), F32)], ()
    else:
        halves = [(shards // 2, width // shards, cut) for cut in cuts]
        kernel = weight_kernel
        outs = [o for half in halves for o in (like(half, F32), like(half))]
        scratch = (pltpu.VMEM((shards, width // shards, columns), F32),)
    return in_vmem(
        functools.partial(kernel, bits),
        "weight_part",
        outs,
        where,
        sheet,
        *grads,
        scalars=1,
        after=after,
        scratch=scratch,
        limit=18,
        flops=2 * rows * cols * width * columns,
    )


def last_kernel(_, keep, got, out):
    total = keep[0] + got[0].astype(F32)
    local = out.shape[-1]
    for index in range(out.shape[0]):
        out[index] = total[:, index * local : (index + 1) * local]


def last_sum(before, keep, got, local):
    shape = (keep.shape[2] // local, keep.shape[1], local)
    return in_vmem(last_kernel, "last_sum", (like(shape, F32),), before, keep, got, streamed=1)[0]


def body(sheet, w_query, w_key, w_value, cotangent, lengths):
    row_dev, cols, width = sheet.shape
    local = w_query.shape[1]
    n_rows = lax.axis_size("rows")
    n_heads = lax.axis_size("heads")
    scale = float(1.0 / (HEAD_DIM * row_dev * n_rows) ** 0.5)
    direct = n_rows <= 8
    shards = n_rows if direct else 1
    row_bits = [1 << b for b in range(n_rows.bit_length() - 1)]
    chunk = row_dev // 2

    me = jnp.stack([lax.axis_index("rows"), lax.axis_index("heads")]).astype(jnp.int32)
    wq, wk, wv = w_query.T, w_key.T, w_value.T
    cot = jnp.swapaxes(cotangent, 1, 2)

    fars = range(2, n_heads, 2)
    far_cot = [flip(cot, "heads", f) for f in fars]
    fq, fk = [[flip(w, "heads", f) for f in fars] for w in (wq, wk)]
    up = row_bits if direct else []
    turn_about = up[1:] + up[:1]
    qk, held, seen, *logits = query_key(me, lengths.reshape(1, row_dev), sheet, wq, wk, turn_about)
    where = jnp.concatenate([me, seen.reshape(row_dev)])
    dprob = value_dprob(where, held, wv, cot, logits[-1:], up, fars, n_heads)
    dprob, halves = dprob[: -len(fars)], dprob[-len(fars) :]
    fv = [flip(half, "heads", f) for half, f in zip(halves, fars)]
    weights = turn(where, wq, wk, wv, n_heads, dprob[-1:])
    if direct:
        logits = halve(*logits, "rows", turn_about)
        dprob = halve(*dprob, "rows", up)
        probs, dscore = softmax_back(logits, dprob, scale, [weights])
        probs, probs_order = double(probs, "rows", up[::-1], [far_cot, fq])
        dscore, dscore_order = double(dscore, "rows", turn_about[::-1])
        two = own_query_key(where, dscore, dscore_order, qk, shards)
        scores = assemble(where, probs, dscore, (probs_order, dscore_order), shards, [two])
    else:
        logits, dprob = lax.psum((logits, dprob), "rows")
        probs, dscore = softmax_back(logits, dprob, scale)
        two = own_query_key(where, [dscore], [[0]], qk, shards)
        scores = jnp.stack([probs, dscore])
    far_scores = [flip(scores, "heads", f) for f in fars]
    grads = two, own_value(where, scores, cot)
    weight_bits = up[:1] + up[1:][::-1]
    parts = weight_part(where, held, grads, (3 * local,), weight_bits, fv)
    ready = [parts[-1]]
    far_qk = [far_query_key(where, held, *w, ready) for w in zip(fq, fk)]
    far_natural = [turn(where, *w, n_heads, ready) for w in zip(fq, fk, fv)]
    own = own_input(grads, weights, ready)
    ready = [own] + far_qk + far_natural
    first_sum = []
    if direct:
        keep, give = parts
        give, keep = add_split(keep, flip(give, "rows", weight_bits[0]), ready)
        first_sum = [keep]
    else:
        weight_grad = lax.psum_scatter(parts[0], "rows", scatter_dimension=0, tiled=True)
        weight_grad = weight_grad.reshape(width // n_rows, 3, local)
    far_grads = [
        far_gradients(where, *args, first_sum)
        for args in zip(far_scores, far_qk, far_cot)
    ]
    chunks = []
    for first in range(0, row_dev, chunk):
        keep_rows, give_rows = far_input(first, chunk, own, list(zip(far_grads, far_natural)), ())
        chunks.append((keep_rows, flip(give_rows, "heads", 1)))
    if direct:
        last = halve(keep, give, "rows", weight_bits[1:], [[chunks[-1][0]]], 1 << 34)
    out = finish(chunks)
    if direct:
        weight_grad = jnp.swapaxes(last_sum(out, *last, local), 0, 1)
    return (jnp.swapaxes(out, 1, 2), weight_grad)


def solution(mesh):
    in_specs = (
        P("rows", None, None),
        P(None, "heads"),
        P(None, "heads"),
        P(None, "heads"),
        P("rows", None, "heads"),
        P("rows"),
    )
    out_specs = (P("rows", None, "heads"), P("rows", None, "heads"))
    return jax.shard_map(body, mesh=mesh, in_specs=in_specs, out_specs=out_specs, check_vma=False)
```

```python
import functools
import math

import jax
import jax.numpy as jnp
from jax import lax
from jax.experimental import pallas as pl
from jax.experimental.pallas import tpu as pltpu
from jax.sharding import PartitionSpec as P

HEAD_DIM = 64
F32 = jnp.float32
BF16 = jnp.bfloat16
MIB = 1024 * 1024

NN = (((1,), (0,)), ((), ()))
NT = (((1,), (1,)), ((), ()))
TN = (((0,), (0,)), ((), ()))


def mm(a, b, dims):
    return lax.dot_general(a, b, dims, preferred_element_type=F32)


def flip(values, axis, bit):
    n = lax.axis_size(axis)
    return lax.ppermute(values, axis, [(s, s ^ bit) for s in range(n)])


def cost(flops, moved):
    return pl.CostEstimate(flops=int(flops), bytes_accessed=int(moved), transcendentals=0)


SMEM = pl.BlockSpec(memory_space=pltpu.SMEM)
VMEM = pl.BlockSpec(memory_space=pltpu.VMEM)
ANY = pl.BlockSpec(memory_space=pl.ANY)
HBM = pl.BlockSpec(memory_space=pltpu.HBM)


def like(shape, dtype=BF16):
    return jax.ShapeDtypeStruct(shape, dtype)


def place(a, stays):
    return pltpu.with_memory_space_constraint(a, pltpu.HBM) if stays else a


def in_vmem(kernel, name, out, *operands, scalars=0, streamed=0, after=(), scratch=(), limit=12, flops=0, counted=True):
    many = len(after)

    def run(*refs):
        kernel(*refs[: len(operands)], *refs[len(operands) + many :])

    moved = 2 * sum(a.size for a in operands) + 2 * sum(o.size for o in out)
    held = len(operands) - scalars - streamed
    return pl.pallas_call(
        run,
        in_specs=[SMEM] * scalars + [HBM] * streamed + [VMEM] * held + [ANY] * many,
        out_specs=[VMEM] * len(out),
        out_shape=list(out),
        scratch_shapes=list(scratch),
        compiler_params=pltpu.CompilerParams(vmem_limit_bytes=limit * MIB),
        cost_estimate=cost(flops, moved) if counted else cost(0, 0),
        name=name,
    )(*[place(a, scalars <= i < scalars + streamed) for i, a in enumerate(operands)], *after)


def lane_mask(length, cols):
    return (lax.broadcasted_iota(jnp.int32, (1, cols), 1) < length).astype(F32)


def reorder(bits):
    return [sum(bit for b, bit in enumerate(bits) if t >> b & 1) for t in range(1 << len(bits))]


def put_shards(me, acc, bits, outs):
    for t, j in enumerate(reorder(bits)):
        out = outs[t % len(outs)]
        out[t // len(outs)] = acc[:, me ^ j].astype(out.dtype)


BLOCK = 4
STEP = 2
AHEAD = 6


def query_key_kernel(bits, me, lengths, sheet, wq, wk, qk, held, seen, *rest):
    outs, (wt, acc, number, sems) = rest[:-4], rest[-4:]
    rows, cols, width = sheet.shape
    local = wq.shape[0]
    heads = local // HEAD_DIM
    copies = []

    def copy(source, target):
        copies.append(pltpu.make_async_copy(source, target, sems.at[len(copies)]))

    copy(lengths, number)
    copy(lengths, seen)
    copy(wq, wt.at[:local])
    copy(wk, wt.at[local:])
    for first in range(0, rows, STEP):
        some = pl.ds(first, STEP)
        copy(sheet.at[some], held.at[some])
    for one in copies[:AHEAD]:
        one.start()
    for one in copies[:4]:
        one.wait()
    flat = (BLOCK * HEAD_DIM, cols)
    for first in range(0, rows, BLOCK):
        for r in range(first, first + BLOCK):
            if r % STEP == 0:
                at = 4 + r // STEP
                copies[at].wait()
                for later in copies[at + AHEAD - 4 : at + AHEAD - 3]:
                    later.start()
            value = (mm(wt[...], held[r], NT) * lane_mask(number[0, r], cols)).astype(BF16)
            qk[r] = value.reshape(2 * heads, HEAD_DIM, cols)
        some = pl.ds(first, BLOCK)
        for h in range(heads):
            term = mm(qk[some, h].reshape(flat), qk[some, heads + h].reshape(flat), TN)
            term = term.reshape(acc.shape[1:])
            acc[h] = term if first == 0 else acc[h] + term
    put_shards(me[0], acc, bits, outs)


def query_key(me, lengths, sheet, wq, wk, bits):
    rows, cols, width = sheet.shape
    shards = 1 << len(bits)
    local = wq.shape[0]
    heads = local // HEAD_DIM
    return in_vmem(
        functools.partial(query_key_kernel, bits),
        "query_key",
        [like((rows, 2 * heads, HEAD_DIM, cols)), like(sheet.shape), like(lengths.shape, jnp.int32)]
        + part_shapes(shards, heads, cols),
        me,
        lengths,
        sheet,
        wq,
        wk,
        scalars=1,
        streamed=4,
        scratch=(
            pltpu.VMEM((2 * local, width), BF16),
            pltpu.VMEM((heads, shards, cols // shards, cols), F32),
            pltpu.SMEM(lengths.shape, jnp.int32),
            pltpu.SemaphoreType.DMA((4 + rows // STEP,)),
        ),
        limit=14,
        flops=rows * cols * local * (2 * width + cols) // 2,
    )


def value_kernel(bits, fars, where, sheet, wv, cot, *rest):
    outs, halves, acc = rest[: -1 - len(fars)], rest[-1 - len(fars) : -1], rest[-1]
    rows, cols, width = sheet.shape
    for far, half in zip(fars, halves):
        near = half.shape[1]
        side = lax.shift_right_logical(where[1], 1) ^ (far // 2)
        for s in range(width // near):
            @pl.when(side == s)
            def _():
                half[...] = wv[:, s * near : (s + 1) * near]
    local = wv.shape[0]
    heads = local // HEAD_DIM
    flat = (BLOCK * HEAD_DIM, cols)
    for first in range(0, rows, BLOCK):
        values = []
        for r in range(first, first + BLOCK):
            value = (mm(wv[...], sheet[r], NT) * lane_mask(where[2 + r], cols)).astype(BF16)
            values.append(value.reshape(heads, HEAD_DIM, cols))
        for h in range(heads):
            left = cot[pl.ds(first, BLOCK), h * HEAD_DIM : (h + 1) * HEAD_DIM].reshape(flat)
            right = jnp.concatenate([v[h] for v in values], axis=0)
            term = mm(left, right, TN).reshape(acc.shape[1:])
            acc[h] = term if first == 0 else acc[h] + term
    put_shards(where[0], acc, bits, outs)


def value_dprob(where, sheet, wv, cot, after, bits, fars, devices):
    rows, cols, width = sheet.shape
    shards = 1 << len(bits)
    local = wv.shape[0]
    heads = local // HEAD_DIM
    return in_vmem(
        functools.partial(value_kernel, bits, fars),
        "value_dprob",
        part_shapes(shards, heads, cols) + [like((local, 2 * width // devices))] * len(fars),
        where,
        sheet,
        wv,
        cot,
        scalars=1,
        after=after,
        scratch=(pltpu.VMEM((heads, shards, cols // shards, cols), F32),),
        limit=16,
        flops=4 * rows * cols * local * (width + cols),
    )


def turn_kernel(where, wq, wk, wv, natural, *full):
    near, share, columns = natural.shape
    local = wq.shape[0]
    for index, (weight, held) in enumerate(zip((wq, wk, wv), full)):
        held[...] = weight[...].T.reshape(held.shape)
        mine = where[1] & (held.shape[0] - 1)
        for j in range(near):
            natural[j, :, index * local : (index + 1) * local] = held[mine ^ j]


def turn(where, wq, wk, wv, devices, after):
    local, width = wq.shape
    share = width // devices
    return in_vmem(
        turn_kernel,
        "turn",
        (like((2, share, 3 * local)),),
        where,
        wq,
        wk,
        wv,
        scalars=1,
        after=after,
        scratch=[pltpu.VMEM((w.shape[1] // share, share, local), BF16) for w in (wq, wk, wv)],
    )[0]


def far_query_key_kernel(where, sheet, wq, wk, qk):
    local = wq.shape[0]
    rows, cols, _ = sheet.shape
    both = jnp.concatenate([wq[...], wk[...]], axis=0)
    for r in range(rows):
        value = (mm(both, sheet[r], NT) * lane_mask(where[2 + r], cols)).astype(BF16)
        qk[r] = value.reshape(2 * local // HEAD_DIM, HEAD_DIM, cols)


def far_query_key(where, sheet, wq, wk, after):
    rows, cols, width = sheet.shape
    local = wq.shape[0]
    return in_vmem(
        far_query_key_kernel,
        "far_query_key",
        (like((rows, 2 * local // HEAD_DIM, HEAD_DIM, cols)),),
        where,
        sheet,
        wq,
        wk,
        scalars=1,
        after=after,
        flops=4 * rows * cols * local * width,
    )[0]


def part_shapes(shards, heads, cols):
    if shards == 1:
        return [like((1, heads, cols, cols), F32)]
    half = (shards // 2, heads, cols // shards, cols)
    return [like(half, F32), like(half)]


def hold_kernel(values, out):
    out[...] = values[...]


def hold(values, after):
    return in_vmem(hold_kernel, "hold", (like(values.shape),), values, after=after)[0]


def add_split_kernel(keep, got, give_out, keep_out):
    for j in range(keep.shape[0]):
        total = keep[j].astype(F32) + got[j].astype(F32)
        out = give_out if j % 2 else keep_out
        out[j // 2] = total.astype(out.dtype)


def add_split(keep, got, after=(), flops=0):
    half = (keep.shape[0] // 2,) + keep.shape[1:]
    return in_vmem(add_split_kernel, "add_split", (like(half), like(half, keep.dtype)), keep, got, after=after, flops=flops)


def halve(keep, give, axis, bits, after=(), flops=0):
    after = list(after) + [()] * len(bits)
    for bit, waits in zip(bits[:-1], after):
        give, keep = add_split(keep, flip(give, axis, bit), waits, flops)
    return keep, flip(give, axis, bits[-1])


def softmax_kernel(scale, *refs):
    *terms, probs_out, dscore_out = refs
    half = len(terms) // 2
    total = lambda some: functools.reduce(jnp.add, [t[0].astype(F32) for t in some])
    logits = total(terms[:half]) * scale
    dprob = total(terms[half:])
    shifted = jnp.exp(logits - jnp.max(logits, axis=-1, keepdims=True))
    probs = shifted / jnp.sum(shifted, axis=-1, keepdims=True)
    inner = jnp.sum(probs * dprob, axis=-1, keepdims=True)
    probs_out[0] = probs.astype(BF16)
    dscore_out[0] = (scale * probs * (dprob - inner)).astype(BF16)


def softmax_back(logits, dprob, scale, after=()):
    out = like(logits[0].shape)
    return in_vmem(
        functools.partial(softmax_kernel, scale), "softmax_back", (out, out), *logits, *dprob, limit=16, after=after
    )


def join_kernel(one, other, out):
    out[: one.shape[0]] = one[...]
    out[one.shape[0] :] = other[...]


def join(one, other, after):
    shape = (one.shape[0] + other.shape[0],) + one.shape[1:]
    return in_vmem(join_kernel, "join", (like(shape),), one, other, after=after)[0]


def double(values, axis, bits, after=()):
    order = [0]
    after = list(after) + [()] * len(bits)
    for bit, waits in zip(bits[:-1], after):
        values = join(values, flip(values, axis, bit), waits)
        order = order + [j ^ bit for j in order]
    other = flip(values, axis, bits[-1])
    return (values, other), (order, [j ^ bits[-1] for j in order])


def assemble_kernel(orders, where, *refs):
    *pieces, out = refs
    for piece, (kind, order) in zip(pieces, orders):
        for t, j in enumerate(order):
            out[kind, where[0] ^ j] = piece[t]


def assemble(where, probs, dscore, orders, shards, after):
    orders = [(kind, order) for kind, both in enumerate(orders) for order in both]
    out = like((2, shards) + probs[0].shape[1:])
    return in_vmem(
        functools.partial(assemble_kernel, orders),
        "assemble",
        (out,),
        where,
        *probs,
        *dscore,
        scalars=1,
        after=after,
    )[0]


def gradients(where, first, count, scores, qk, cot, grads):
    cols = qk.shape[-1]
    heads = qk.shape[1] // 2
    rows = pl.ds(first, count)
    flat = (count * HEAD_DIM, cols)
    split = (count, HEAD_DIM, cols)
    masks = jnp.stack([lane_mask(where[2 + first + r], cols) for r in range(count)])
    for h in range(heads):
        p, ds = [scores[kind, :, h].reshape(cols, cols) for kind in range(2)]
        g = cot[rows, h * HEAD_DIM : (h + 1) * HEAD_DIM].reshape(flat)
        dq = mm(qk[rows, heads + h].reshape(flat), ds, NT)
        dk = mm(qk[rows, h].reshape(flat), ds, NN)
        dv = mm(g, p, NN)
        for index, value in enumerate((dq, dk, dv)):
            grads[:, index * heads + h] = (value.reshape(split) * masks).astype(BF16)


def gradients_kernel(where, scores, qk, cot, grads):
    gradients(where, 0, qk.shape[0], scores, qk, cot, grads)


def all_gradients(where, scores, qk, cot, name, after, counted=True):
    rows, two, _, cols = qk.shape
    return in_vmem(
        gradients_kernel,
        name,
        (like((rows, two // 2 * 3, HEAD_DIM, cols)),),
        where,
        scores,
        qk,
        cot,
        scalars=1,
        after=after,
        limit=14,
        counted=counted,
        flops=3 * rows * two * HEAD_DIM * cols * cols,
    )[0]


def own_input_kernel(grads, weights, out):
    near, share, columns = weights.shape
    left = weights[...].reshape(near * share, columns)
    for r in range(grads.shape[0]):
        part = mm(left, grads[r].reshape(columns, grads.shape[-1]), NN).astype(BF16)
        out[:, r] = part.reshape(near, share, grads.shape[-1])


def own_input(grads, weights, after):
    rows, cols = grads.shape[0], grads.shape[-1]
    near, share, columns = weights.shape
    return in_vmem(
        own_input_kernel,
        "own_input",
        (like((near, rows, share, cols)),),
        grads,
        weights,
        after=after,
        flops=2 * rows * cols * near * share * columns,
    )[0]


def far_input_kernel(first, own, *refs):
    *refs, keep, give = refs
    count, share, cols = keep.shape
    for r in range(count):
        total = own[:, first + r].astype(F32)
        for i in range(0, len(refs), 2):
            grads, weights = refs[i : i + 2]
            near, _, columns = weights.shape
            left = weights[...].reshape(near * share, columns)
            part = mm(left, grads[first + r].reshape(columns, cols), NN).astype(BF16)
            total = total + part.reshape(near, share, cols).astype(F32)
        keep[r] = total[0].astype(keep.dtype)
        give[r] = total[1].astype(give.dtype)


def far_input(first, count, own, far, after):
    _, rows, share, cols = own.shape
    columns = far[0][1].shape[-1]
    out = like((count, share, cols))
    return in_vmem(
        functools.partial(far_input_kernel, first),
        "far_input",
        (out, out),
        own,
        *[a for one in far for a in one],
        after=after,
        limit=14,
        counted=False,
        flops=4 * len(far) * count * cols * columns * share,
    )


def finish_kernel(*refs):
    *terms, out, total, sems = refs
    copies = []
    first = 0
    for index in range(0, len(terms), 2):
        keep, got = terms[index : index + 2]
        some = pl.ds(first, keep.shape[0])
        total[some] = (keep[...].astype(F32) + got[...].astype(F32)).astype(BF16)
        copies.append(pltpu.make_async_copy(total.at[some], out.at[some], sems.at[index // 2]))
        copies[-1].start()
        first += keep.shape[0]
    for copy in copies:
        copy.wait()


def finish(chunks):
    _, share, cols = chunks[0][0].shape
    rows = sum(keep.shape[0] for keep, _ in chunks)
    terms = [a for chunk in chunks for a in chunk]
    return pl.pallas_call(
        finish_kernel,
        in_specs=[VMEM] * len(terms),
        out_specs=HBM,
        out_shape=like((rows, share, cols)),
        scratch_shapes=[pltpu.VMEM((rows, share, cols), BF16), pltpu.SemaphoreType.DMA((len(chunks),))],
        compiler_params=pltpu.CompilerParams(vmem_limit_bytes=12 * MIB),
        cost_estimate=cost(rows * share * cols, 6 * rows * share * cols),
        name="finish",
    )(*terms)


def weight_product(sheet, grads):
    rows, cols, width = sheet.shape
    columns = grads.shape[1] * HEAD_DIM
    left = [grads[r].reshape(columns, cols) for r in range(rows)]
    return mm(jnp.concatenate(left, axis=1), sheet[...].reshape(rows * cols, width), NN).T


def weight_kernel(bits, where, sheet, grads, *rest):
    outs, full = rest[:-1], rest[-1]
    full[...] = weight_product(sheet, grads).reshape(full.shape)
    for t, j in enumerate(reorder(bits)):
        first = 0
        for keep, give in zip(outs[::2], outs[1::2]):
            out = (keep, give)[t % 2]
            last = first + out.shape[-1]
            out[t // 2] = full[where[0] ^ j, :, first:last].astype(out.dtype)
            first = last


def whole_weight_kernel(_, where, sheet, grads, out):
    out[...] = weight_product(sheet, grads)


def weight_part(where, sheet, grads, cuts, bits, after):
    rows, cols, width = sheet.shape
    shards = 1 << len(bits)
    columns = grads.shape[1] * HEAD_DIM
    if shards == 1:
        kernel, outs, scratch = whole_weight_kernel, [like((width, columns), F32)], ()
    else:
        halves = [(shards // 2, width // shards, cut) for cut in cuts]
        kernel = weight_kernel
        outs = [o for half in halves for o in (like(half, F32), like(half))]
        scratch = (pltpu.VMEM((shards, width // shards, columns), F32),)
    return in_vmem(
        functools.partial(kernel, bits),
        "weight_part",
        outs,
        where,
        sheet,
        grads,
        scalars=1,
        after=after,
        scratch=scratch,
        limit=18,
        flops=2 * rows * cols * width * columns,
    )


def last_kernel(_, keep, got, out):
    total = keep[0] + got[0].astype(F32)
    local = out.shape[-1]
    for index in range(out.shape[0]):
        out[index] = total[:, index * local : (index + 1) * local]


def last_sum(before, keep, got, local):
    shape = (keep.shape[2] // local, keep.shape[1], local)
    return in_vmem(last_kernel, "last_sum", (like(shape, F32),), before, keep, got, streamed=1)[0]


def body(sheet, w_query, w_key, w_value, cotangent, lengths):
    row_dev, cols, width = sheet.shape
    local = w_query.shape[1]
    n_rows = lax.axis_size("rows")
    n_heads = lax.axis_size("heads")
    scale = float(1.0 / (HEAD_DIM * row_dev * n_rows) ** 0.5)
    direct = n_rows <= 8
    shards = n_rows if direct else 1
    row_bits = [1 << b for b in range(n_rows.bit_length() - 1)]
    chunk = row_dev // 2

    me = jnp.stack([lax.axis_index("rows"), lax.axis_index("heads")]).astype(jnp.int32)
    wq, wk, wv = w_query.T, w_key.T, w_value.T
    cot = jnp.swapaxes(cotangent, 1, 2)

    fars = range(2, n_heads, 2)
    far_cot = [flip(cot, "heads", f) for f in fars]
    fq, fk = [[flip(w, "heads", f) for f in fars] for w in (wq, wk)]
    up = row_bits if direct else []
    turn_about = up[1:] + up[:1]
    qk, held, seen, *logits = query_key(me, lengths.reshape(1, row_dev), sheet, wq, wk, turn_about)
    where = jnp.concatenate([me, seen.reshape(row_dev)])
    dprob = value_dprob(where, held, wv, cot, logits[-1:], up, fars, n_heads)
    dprob, halves = dprob[: -len(fars)], dprob[-len(fars) :]
    fv = [flip(half, "heads", f) for half, f in zip(halves, fars)]
    weights = turn(where, wq, wk, wv, n_heads, dprob[-1:])
    if direct:
        logits = halve(*logits, "rows", turn_about)
        dprob = halve(*dprob, "rows", up)
        probs, dscore = softmax_back(logits, dprob, scale, [weights])
        probs, probs_order = double(probs, "rows", up[::-1], [far_cot, fq])
        dscore, dscore_order = double(dscore, "rows", turn_about[::-1])
        scores = assemble(where, probs, dscore, (probs_order, dscore_order), shards, ())
    else:
        logits, dprob = lax.psum((logits, dprob), "rows")
        scores = jnp.stack(softmax_back(logits, dprob, scale))
    far_scores = [flip(scores, "heads", f) for f in fars]
    grads = all_gradients(where, scores, qk, cot, "own_gradients", ())
    weight_bits = up[:1] + up[1:][::-1]
    parts = weight_part(where, held, grads, (3 * local,), weight_bits, fv)
    ready = [parts[-1]]
    far_qk = [far_query_key(where, held, *w, ready) for w in zip(fq, fk)]
    far_natural = [turn(where, *w, n_heads, ready) for w in zip(fq, fk, fv)]
    own = own_input(grads, weights, ready)
    ready = [own] + far_qk + far_natural
    first_sum = []
    if direct:
        keep, give = parts
        give, keep = add_split(keep, flip(give, "rows", weight_bits[0]), ready)
        first_sum = [keep]
    else:
        weight_grad = lax.psum_scatter(parts[0], "rows", scatter_dimension=0, tiled=True)
        weight_grad = weight_grad.reshape(width // n_rows, 3, local)
    far_grads = [
        all_gradients(where, *args, "far_gradients", first_sum, False)
        for args in zip(far_scores, far_qk, far_cot)
    ]
    chunks = []
    for first in range(0, row_dev, chunk):
        keep_rows, give_rows = far_input(first, chunk, own, list(zip(far_grads, far_natural)), ())
        chunks.append((keep_rows, flip(give_rows, "heads", 1)))
    if direct:
        last = halve(keep, give, "rows", weight_bits[1:], [[chunks[-1][0]]], 1 << 34)
    out = finish(chunks)
    if direct:
        weight_grad = jnp.swapaxes(last_sum(out, *last, local), 0, 1)
    return (jnp.swapaxes(out, 1, 2), weight_grad)


def solution(mesh):
    in_specs = (
        P("rows", None, None),
        P(None, "heads"),
        P(None, "heads"),
        P(None, "heads"),
        P("rows", None, "heads"),
        P("rows"),
    )
    out_specs = (P("rows", None, "heads"), P("rows", None, "heads"))
    return jax.shard_map(body, mesh=mesh, in_specs=in_specs, out_specs=out_specs, check_vma=False)
```

```python
import functools
import math

import jax
import jax.numpy as jnp
from jax import lax
from jax.experimental import pallas as pl
from jax.experimental.pallas import tpu as pltpu
from jax.sharding import PartitionSpec as P

HEAD_DIM = 64
F32 = jnp.float32
BF16 = jnp.bfloat16
MIB = 1024 * 1024

NN = (((1,), (0,)), ((), ()))
NT = (((1,), (1,)), ((), ()))
TN = (((0,), (0,)), ((), ()))


def mm(a, b, dims):
    return lax.dot_general(a, b, dims, preferred_element_type=F32)


def flip(values, axis, bit):
    n = lax.axis_size(axis)
    return lax.ppermute(values, axis, [(s, s ^ bit) for s in range(n)])


def cost(flops, moved):
    return pl.CostEstimate(flops=int(flops), bytes_accessed=int(moved), transcendentals=0)


SMEM = pl.BlockSpec(memory_space=pltpu.SMEM)
VMEM = pl.BlockSpec(memory_space=pltpu.VMEM)
ANY = pl.BlockSpec(memory_space=pl.ANY)
HBM = pl.BlockSpec(memory_space=pltpu.HBM)


def like(shape, dtype=BF16):
    return jax.ShapeDtypeStruct(shape, dtype)


def place(a, stays):
    return pltpu.with_memory_space_constraint(a, pltpu.HBM) if stays else a


def in_vmem(kernel, name, out, *operands, scalars=0, streamed=0, after=(), scratch=(), limit=12, flops=0, counted=True):
    many = len(after)

    def run(*refs):
        kernel(*refs[: len(operands)], *refs[len(operands) + many :])

    moved = 2 * sum(a.size for a in operands) + 2 * sum(o.size for o in out)
    held = len(operands) - scalars - streamed
    return pl.pallas_call(
        run,
        in_specs=[SMEM] * scalars + [HBM] * streamed + [VMEM] * held + [ANY] * many,
        out_specs=[VMEM] * len(out),
        out_shape=list(out),
        scratch_shapes=list(scratch),
        compiler_params=pltpu.CompilerParams(vmem_limit_bytes=limit * MIB),
        cost_estimate=cost(flops, moved) if counted else cost(0, 0),
        name=name,
    )(*[place(a, scalars <= i < scalars + streamed) for i, a in enumerate(operands)], *after)


def lane_mask(length, cols):
    return (lax.broadcasted_iota(jnp.int32, (1, cols), 1) < length).astype(F32)


def reorder(bits):
    return [sum(bit for b, bit in enumerate(bits) if t >> b & 1) for t in range(1 << len(bits))]


def put_shards(me, acc, bits, outs):
    for t, j in enumerate(reorder(bits)):
        out = outs[t % len(outs)]
        out[t // len(outs)] = acc[:, me ^ j].astype(out.dtype)


BLOCK = 4
STEP = 2
AHEAD = 6


def query_key_kernel(bits, me, lengths, sheet, wq, wk, qk, held, seen, *rest):
    outs, (wt, acc, number, sems) = rest[:-4], rest[-4:]
    rows, cols, width = sheet.shape
    local = wq.shape[0]
    heads = local // HEAD_DIM
    copies = []

    def copy(source, target):
        copies.append(pltpu.make_async_copy(source, target, sems.at[len(copies)]))

    copy(lengths, number)
    copy(lengths, seen)
    copy(wq, wt.at[:local])
    copy(wk, wt.at[local:])
    for first in range(0, rows, STEP):
        some = pl.ds(first, STEP)
        copy(sheet.at[some], held.at[some])
    for one in copies[:AHEAD]:
        one.start()
    for one in copies[:4]:
        one.wait()
    flat = (BLOCK * HEAD_DIM, cols)
    for first in range(0, rows, BLOCK):
        for r in range(first, first + BLOCK):
            if r % STEP == 0:
                at = 4 + r // STEP
                copies[at].wait()
                for later in copies[at + AHEAD - 4 : at + AHEAD - 3]:
                    later.start()
            value = (mm(wt[...], held[r], NT) * lane_mask(number[0, r], cols)).astype(BF16)
            qk[r] = value.reshape(2 * heads, HEAD_DIM, cols)
        some = pl.ds(first, BLOCK)
        for h in range(heads):
            term = mm(qk[some, h].reshape(flat), qk[some, heads + h].reshape(flat), TN)
            term = term.reshape(acc.shape[1:])
            acc[h] = term if first == 0 else acc[h] + term
    put_shards(me[0], acc, bits, outs)


def query_key(me, lengths, sheet, wq, wk, bits):
    rows, cols, width = sheet.shape
    shards = 1 << len(bits)
    local = wq.shape[0]
    heads = local // HEAD_DIM
    return in_vmem(
        functools.partial(query_key_kernel, bits),
        "query_key",
        [like((rows, 2 * heads, HEAD_DIM, cols)), like(sheet.shape), like(lengths.shape, jnp.int32)]
        + part_shapes(shards, heads, cols),
        me,
        lengths,
        sheet,
        wq,
        wk,
        scalars=1,
        streamed=4,
        scratch=(
            pltpu.VMEM((2 * local, width), BF16),
            pltpu.VMEM((heads, shards, cols // shards, cols), F32),
            pltpu.SMEM(lengths.shape, jnp.int32),
            pltpu.SemaphoreType.DMA((4 + rows // STEP,)),
        ),
        limit=14,
        flops=rows * cols * local * (2 * width + cols) // 2,
    )


def value_kernel(bits, fars, where, sheet, wv, cot, *rest):
    outs, halves, acc = rest[: -1 - len(fars)], rest[-1 - len(fars) : -1], rest[-1]
    rows, cols, width = sheet.shape
    for far, half in zip(fars, halves):
        near = half.shape[1]
        side = lax.shift_right_logical(where[1], 1) ^ (far // 2)
        for s in range(width // near):
            @pl.when(side == s)
            def _():
                half[...] = wv[:, s * near : (s + 1) * near]
    local = wv.shape[0]
    heads = local // HEAD_DIM
    flat = (BLOCK * HEAD_DIM, cols)
    for first in range(0, rows, BLOCK):
        values = []
        for r in range(first, first + BLOCK):
            value = (mm(wv[...], sheet[r], NT) * lane_mask(where[2 + r], cols)).astype(BF16)
            values.append(value.reshape(heads, HEAD_DIM, cols))
        for h in range(heads):
            left = cot[pl.ds(first, BLOCK), h * HEAD_DIM : (h + 1) * HEAD_DIM].reshape(flat)
            right = jnp.concatenate([v[h] for v in values], axis=0)
            term = mm(left, right, TN).reshape(acc.shape[1:])
            acc[h] = term if first == 0 else acc[h] + term
    put_shards(where[0], acc, bits, outs)


def value_dprob(where, sheet, wv, cot, after, bits, fars, devices):
    rows, cols, width = sheet.shape
    shards = 1 << len(bits)
    local = wv.shape[0]
    heads = local // HEAD_DIM
    return in_vmem(
        functools.partial(value_kernel, bits, fars),
        "value_dprob",
        part_shapes(shards, heads, cols) + [like((local, 2 * width // devices))] * len(fars),
        where,
        sheet,
        wv,
        cot,
        scalars=1,
        after=after,
        scratch=(pltpu.VMEM((heads, shards, cols // shards, cols), F32),),
        limit=16,
        flops=4 * rows * cols * local * (width + cols),
    )


def turn_kernel(where, wq, wk, wv, natural, *full):
    near, share, columns = natural.shape
    local = wq.shape[0]
    for index, (weight, held) in enumerate(zip((wq, wk, wv), full)):
        held[...] = weight[...].T.reshape(held.shape)
        mine = where[1] & (held.shape[0] - 1)
        for j in range(near):
            natural[j, :, index * local : (index + 1) * local] = held[mine ^ j]


def turn(where, wq, wk, wv, devices, after):
    local, width = wq.shape
    share = width // devices
    return in_vmem(
        turn_kernel,
        "turn",
        (like((2, share, 3 * local)),),
        where,
        wq,
        wk,
        wv,
        scalars=1,
        after=after,
        scratch=[pltpu.VMEM((w.shape[1] // share, share, local), BF16) for w in (wq, wk, wv)],
    )[0]


def far_query_key_kernel(where, sheet, wq, wk, qk):
    local = wq.shape[0]
    rows, cols, _ = sheet.shape
    both = jnp.concatenate([wq[...], wk[...]], axis=0)
    for r in range(rows):
        value = (mm(both, sheet[r], NT) * lane_mask(where[2 + r], cols)).astype(BF16)
        qk[r] = value.reshape(2 * local // HEAD_DIM, HEAD_DIM, cols)


def far_query_key(where, sheet, wq, wk, after):
    rows, cols, width = sheet.shape
    local = wq.shape[0]
    return in_vmem(
        far_query_key_kernel,
        "far_query_key",
        (like((rows, 2 * local // HEAD_DIM, HEAD_DIM, cols)),),
        where,
        sheet,
        wq,
        wk,
        scalars=1,
        after=after,
        flops=4 * rows * cols * local * width,
    )[0]


def part_shapes(shards, heads, cols):
    if shards == 1:
        return [like((1, heads, cols, cols), F32)]
    half = (shards // 2, heads, cols // shards, cols)
    return [like(half, F32), like(half)]


def hold_kernel(values, out):
    out[...] = values[...]


def hold(values, after):
    return in_vmem(hold_kernel, "hold", (like(values.shape),), values, after=after)[0]


def add_split_kernel(keep, got, give_out, keep_out):
    for j in range(keep.shape[0]):
        total = keep[j].astype(F32) + got[j].astype(F32)
        out = give_out if j % 2 else keep_out
        out[j // 2] = total.astype(out.dtype)


def add_split(keep, got, after=(), flops=0):
    half = (keep.shape[0] // 2,) + keep.shape[1:]
    return in_vmem(add_split_kernel, "add_split", (like(half), like(half, keep.dtype)), keep, got, after=after, flops=flops)


def halve(keep, give, axis, bits, after=(), flops=0):
    after = list(after) + [()] * len(bits)
    for bit, waits in zip(bits[:-1], after):
        give, keep = add_split(keep, flip(give, axis, bit), waits, flops)
    return keep, flip(give, axis, bits[-1])


def softmax_kernel(scale, *refs):
    *terms, probs_out, dscore_out = refs
    half = len(terms) // 2
    total = lambda some: functools.reduce(jnp.add, [t[0].astype(F32) for t in some])
    logits = total(terms[:half]) * scale
    dprob = total(terms[half:])
    shifted = jnp.exp(logits - jnp.max(logits, axis=-1, keepdims=True))
    probs = shifted / jnp.sum(shifted, axis=-1, keepdims=True)
    inner = jnp.sum(probs * dprob, axis=-1, keepdims=True)
    probs_out[0] = probs.astype(BF16)
    dscore_out[0] = (scale * probs * (dprob - inner)).astype(BF16)


def softmax_back(logits, dprob, scale, after=()):
    out = like(logits[0].shape)
    return in_vmem(
        functools.partial(softmax_kernel, scale), "softmax_back", (out, out), *logits, *dprob, limit=16, after=after
    )


def join_kernel(one, other, out):
    out[: one.shape[0]] = one[...]
    out[one.shape[0] :] = other[...]


def join(one, other, after):
    shape = (one.shape[0] + other.shape[0],) + one.shape[1:]
    return in_vmem(join_kernel, "join", (like(shape),), one, other, after=after)[0]


def double(values, axis, bits, after=()):
    order = [0]
    after = list(after) + [()] * len(bits)
    for bit, waits in zip(bits[:-1], after):
        values = join(values, flip(values, axis, bit), waits)
        order = order + [j ^ bit for j in order]
    other = flip(values, axis, bits[-1])
    return (values, other), (order, [j ^ bits[-1] for j in order])


def assemble_kernel(orders, where, *refs):
    *pieces, out = refs
    for piece, (kind, order) in zip(pieces, orders):
        for t, j in enumerate(order):
            out[kind, where[0] ^ j] = piece[t]


def assemble(where, probs, dscore, orders, shards, after):
    orders = [(kind, order) for kind, both in enumerate(orders) for order in both]
    out = like((2, shards) + probs[0].shape[1:])
    return in_vmem(
        functools.partial(assemble_kernel, orders),
        "assemble",
        (out,),
        where,
        *probs,
        *dscore,
        scalars=1,
        after=after,
    )[0]


def gradients(where, first, count, scores, qk, cot, grads):
    cols = qk.shape[-1]
    heads = qk.shape[1] // 2
    rows = pl.ds(first, count)
    flat = (count * HEAD_DIM, cols)
    split = (count, HEAD_DIM, cols)
    masks = jnp.stack([lane_mask(where[2 + first + r], cols) for r in range(count)])
    for h in range(heads):
        p, ds = [scores[kind, :, h].reshape(cols, cols) for kind in range(2)]
        g = cot[rows, h * HEAD_DIM : (h + 1) * HEAD_DIM].reshape(flat)
        dq = mm(qk[rows, heads + h].reshape(flat), ds, NT)
        dk = mm(qk[rows, h].reshape(flat), ds, NN)
        dv = mm(g, p, NN)
        for index, value in enumerate((dq, dk, dv)):
            grads[:, index * heads + h] = (value.reshape(split) * masks).astype(BF16)


def gradients_kernel(where, scores, qk, cot, grads):
    gradients(where, 0, qk.shape[0], scores, qk, cot, grads)


def all_gradients(where, scores, qk, cot, name, after, counted=True):
    rows, two, _, cols = qk.shape
    return in_vmem(
        gradients_kernel,
        name,
        (like((rows, two // 2 * 3, HEAD_DIM, cols)),),
        where,
        scores,
        qk,
        cot,
        scalars=1,
        after=after,
        limit=14,
        counted=counted,
        flops=3 * rows * two * HEAD_DIM * cols * cols,
    )[0]


def own_input_kernel(grads, weights, out):
    near, share, columns = weights.shape
    left = weights[...].reshape(near * share, columns)
    for r in range(grads.shape[0]):
        part = mm(left, grads[r].reshape(columns, grads.shape[-1]), NN).astype(BF16)
        out[:, r] = part.reshape(near, share, grads.shape[-1])


def own_input(grads, weights, after):
    rows, cols = grads.shape[0], grads.shape[-1]
    near, share, columns = weights.shape
    return in_vmem(
        own_input_kernel,
        "own_input",
        (like((near, rows, share, cols)),),
        grads,
        weights,
        after=after,
        flops=2 * rows * cols * near * share * columns,
    )[0]


def far_input_kernel(first, own, *refs):
    *refs, keep, give = refs
    count, share, cols = keep.shape
    for r in range(count):
        total = own[:, first + r].astype(F32)
        for i in range(0, len(refs), 2):
            grads, weights = refs[i : i + 2]
            near, _, columns = weights.shape
            left = weights[...].reshape(near * share, columns)
            part = mm(left, grads[first + r].reshape(columns, cols), NN).astype(BF16)
            total = total + part.reshape(near, share, cols).astype(F32)
        keep[r] = total[0].astype(keep.dtype)
        give[r] = total[1].astype(give.dtype)


def far_input(first, count, own, far, after):
    _, rows, share, cols = own.shape
    columns = far[0][1].shape[-1]
    out = like((count, share, cols))
    return in_vmem(
        functools.partial(far_input_kernel, first),
        "far_input",
        (out, out),
        own,
        *[a for one in far for a in one],
        after=after,
        limit=14,
        flops=4 * len(far) * count * cols * columns * share,
    )


def finish_kernel(*refs):
    *terms, out, total, sems = refs
    copies = []
    first = 0
    for index in range(0, len(terms), 2):
        keep, got = terms[index : index + 2]
        some = pl.ds(first, keep.shape[0])
        total[some] = (keep[...].astype(F32) + got[...].astype(F32)).astype(BF16)
        copies.append(pltpu.make_async_copy(total.at[some], out.at[some], sems.at[index // 2]))
        copies[-1].start()
        first += keep.shape[0]
    for copy in copies:
        copy.wait()


def finish(chunks):
    _, share, cols = chunks[0][0].shape
    rows = sum(keep.shape[0] for keep, _ in chunks)
    terms = [a for chunk in chunks for a in chunk]
    return pl.pallas_call(
        finish_kernel,
        in_specs=[VMEM] * len(terms),
        out_specs=HBM,
        out_shape=like((rows, share, cols)),
        scratch_shapes=[pltpu.VMEM((rows, share, cols), BF16), pltpu.SemaphoreType.DMA((len(chunks),))],
        compiler_params=pltpu.CompilerParams(vmem_limit_bytes=12 * MIB),
        cost_estimate=cost(rows * share * cols, 6 * rows * share * cols),
        name="finish",
    )(*terms)


def weight_product(sheet, grads):
    rows, cols, width = sheet.shape
    columns = grads.shape[1] * HEAD_DIM
    left = [grads[r].reshape(columns, cols) for r in range(rows)]
    return mm(jnp.concatenate(left, axis=1), sheet[...].reshape(rows * cols, width), NN).T


def weight_kernel(bits, where, sheet, grads, *rest):
    outs, full = rest[:-1], rest[-1]
    full[...] = weight_product(sheet, grads).reshape(full.shape)
    for t, j in enumerate(reorder(bits)):
        first = 0
        for keep, give in zip(outs[::2], outs[1::2]):
            out = (keep, give)[t % 2]
            last = first + out.shape[-1]
            out[t // 2] = full[where[0] ^ j, :, first:last].astype(out.dtype)
            first = last


def whole_weight_kernel(_, where, sheet, grads, out):
    out[...] = weight_product(sheet, grads)


def weight_part(where, sheet, grads, cuts, bits, after):
    rows, cols, width = sheet.shape
    shards = 1 << len(bits)
    columns = grads.shape[1] * HEAD_DIM
    if shards == 1:
        kernel, outs, scratch = whole_weight_kernel, [like((width, columns), F32)], ()
    else:
        halves = [(shards // 2, width // shards, cut) for cut in cuts]
        kernel = weight_kernel
        outs = [o for half in halves for o in (like(half, F32), like(half))]
        scratch = (pltpu.VMEM((shards, width // shards, columns), F32),)
    return in_vmem(
        functools.partial(kernel, bits),
        "weight_part",
        outs,
        where,
        sheet,
        grads,
        scalars=1,
        after=after,
        scratch=scratch,
        limit=18,
        flops=2 * rows * cols * width * columns,
    )


def last_kernel(_, keep, got, out):
    total = keep[0] + got[0].astype(F32)
    local = out.shape[-1]
    for index in range(out.shape[0]):
        out[index] = total[:, index * local : (index + 1) * local]


def last_sum(before, keep, got, local):
    shape = (keep.shape[2] // local, keep.shape[1], local)
    return in_vmem(last_kernel, "last_sum", (like(shape, F32),), before, keep, got, streamed=1)[0]


def body(sheet, w_query, w_key, w_value, cotangent, lengths):
    row_dev, cols, width = sheet.shape
    local = w_query.shape[1]
    n_rows = lax.axis_size("rows")
    n_heads = lax.axis_size("heads")
    scale = float(1.0 / (HEAD_DIM * row_dev * n_rows) ** 0.5)
    direct = n_rows <= 8
    shards = n_rows if direct else 1
    row_bits = [1 << b for b in range(n_rows.bit_length() - 1)]
    chunk = row_dev // 2

    me = jnp.stack([lax.axis_index("rows"), lax.axis_index("heads")]).astype(jnp.int32)
    wq, wk, wv = w_query.T, w_key.T, w_value.T
    cot = jnp.swapaxes(cotangent, 1, 2)

    fars = range(2, n_heads, 2)
    far_cot = [flip(cot, "heads", f) for f in fars]
    fq, fk = [[flip(w, "heads", f) for f in fars] for w in (wq, wk)]
    up = row_bits if direct else []
    turn_about = up[1:] + up[:1]
    qk, held, seen, *logits = query_key(me, lengths.reshape(1, row_dev), sheet, wq, wk, turn_about)
    where = jnp.concatenate([me, seen.reshape(row_dev)])
    dprob = value_dprob(where, held, wv, cot, logits[-1:], up, fars, n_heads)
    dprob, halves = dprob[: -len(fars)], dprob[-len(fars) :]
    fv = [flip(half, "heads", f) for half, f in zip(halves, fars)]
    weights = turn(where, wq, wk, wv, n_heads, dprob[-1:])
    if direct:
        logits = halve(*logits, "rows", turn_about)
        dprob = halve(*dprob, "rows", up)
        probs, dscore = softmax_back(logits, dprob, scale, [weights])
        probs, probs_order = double(probs, "rows", up[::-1], [far_cot])
        dscore, dscore_order = double(dscore, "rows", turn_about[::-1])
        scores = assemble(where, probs, dscore, (probs_order, dscore_order), shards, fq)
    else:
        logits, dprob = lax.psum((logits, dprob), "rows")
        scores = jnp.stack(softmax_back(logits, dprob, scale))
    far_scores = [flip(scores, "heads", f) for f in fars]
    grads = all_gradients(where, scores, qk, cot, "own_gradients", ())
    weight_bits = up[:1] + up[1:][::-1]
    parts = weight_part(where, held, grads, (3 * local,), weight_bits, fv)
    ready = [parts[-1]]
    far_qk = [far_query_key(where, held, *w, ready) for w in zip(fq, fk)]
    far_natural = [turn(where, *w, n_heads, ready) for w in zip(fq, fk, fv)]
    own = own_input(grads, weights, ready)
    ready = [own] + far_qk + far_natural
    first_sum = []
    if direct:
        keep, give = parts
        give, keep = add_split(keep, flip(give, "rows", weight_bits[0]), ready)
        first_sum = [keep]
    else:
        weight_grad = lax.psum_scatter(parts[0], "rows", scatter_dimension=0, tiled=True)
        weight_grad = weight_grad.reshape(width // n_rows, 3, local)
    far_grads = [
        all_gradients(where, *args, "far_gradients", first_sum, False)
        for args in zip(far_scores, far_qk, far_cot)
    ]
    chunks = []
    for first in range(0, row_dev, chunk):
        keep_rows, give_rows = far_input(first, chunk, own, list(zip(far_grads, far_natural)), ())
        chunks.append((keep_rows, flip(give_rows, "heads", 1)))
    if direct:
        last = halve(keep, give, "rows", weight_bits[1:], [[chunks[-1][0]]], 1 << 34)
    out = finish(chunks)
    if direct:
        weight_grad = jnp.swapaxes(last_sum(out, *last, local), 0, 1)
    return (jnp.swapaxes(out, 1, 2), weight_grad)


def solution(mesh):
    in_specs = (
        P("rows", None, None),
        P(None, "heads"),
        P(None, "heads"),
        P(None, "heads"),
        P("rows", None, "heads"),
        P("rows"),
    )
    out_specs = (P("rows", None, "heads"), P("rows", None, "heads"))
    return jax.shard_map(body, mesh=mesh, in_specs=in_specs, out_specs=out_specs, check_vma=False)
```

```python
import functools
import math

import jax
import jax.numpy as jnp
from jax import lax
from jax.experimental import pallas as pl
from jax.experimental.pallas import tpu as pltpu
from jax.sharding import PartitionSpec as P

HEAD_DIM = 64
F32 = jnp.float32
BF16 = jnp.bfloat16
MIB = 1024 * 1024

NN = (((1,), (0,)), ((), ()))
NT = (((1,), (1,)), ((), ()))
TN = (((0,), (0,)), ((), ()))


def mm(a, b, dims):
    return lax.dot_general(a, b, dims, preferred_element_type=F32)


def flip(values, axis, bit):
    n = lax.axis_size(axis)
    return lax.ppermute(values, axis, [(s, s ^ bit) for s in range(n)])


def cost(flops, moved):
    return pl.CostEstimate(flops=int(flops), bytes_accessed=int(moved), transcendentals=0)


SMEM = pl.BlockSpec(memory_space=pltpu.SMEM)
VMEM = pl.BlockSpec(memory_space=pltpu.VMEM)
ANY = pl.BlockSpec(memory_space=pl.ANY)
HBM = pl.BlockSpec(memory_space=pltpu.HBM)


def like(shape, dtype=BF16):
    return jax.ShapeDtypeStruct(shape, dtype)


def place(a, stays):
    return pltpu.with_memory_space_constraint(a, pltpu.HBM) if stays else a


def in_vmem(kernel, name, out, *operands, scalars=0, streamed=0, after=(), scratch=(), limit=12, flops=0, counted=True):
    many = len(after)

    def run(*refs):
        kernel(*refs[: len(operands)], *refs[len(operands) + many :])

    moved = 2 * sum(a.size for a in operands) + 2 * sum(o.size for o in out)
    held = len(operands) - scalars - streamed
    return pl.pallas_call(
        run,
        in_specs=[SMEM] * scalars + [HBM] * streamed + [VMEM] * held + [ANY] * many,
        out_specs=[VMEM] * len(out),
        out_shape=list(out),
        scratch_shapes=list(scratch),
        compiler_params=pltpu.CompilerParams(vmem_limit_bytes=limit * MIB),
        cost_estimate=cost(flops, moved) if counted else cost(0, 0),
        name=name,
    )(*[place(a, scalars <= i < scalars + streamed) for i, a in enumerate(operands)], *after)


def lane_mask(length, cols):
    return (lax.broadcasted_iota(jnp.int32, (1, cols), 1) < length).astype(F32)


def reorder(bits):
    return [sum(bit for b, bit in enumerate(bits) if t >> b & 1) for t in range(1 << len(bits))]


def put_shards(me, acc, bits, outs):
    for t, j in enumerate(reorder(bits)):
        out = outs[t % len(outs)]
        out[t // len(outs)] = acc[:, me ^ j].astype(out.dtype)


BLOCK = 4
STEP = 1
AHEAD = 7


def query_key_kernel(bits, me, lengths, sheet, wq, wk, qk, held, seen, *rest):
    outs, (wt, acc, number, sems) = rest[:-4], rest[-4:]
    rows, cols, width = sheet.shape
    local = wq.shape[0]
    heads = local // HEAD_DIM
    copies = []

    def copy(source, target):
        copies.append(pltpu.make_async_copy(source, target, sems.at[len(copies)]))

    copy(lengths, number)
    copy(lengths, seen)
    copy(wq, wt.at[:local])
    copy(wk, wt.at[local:])
    for first in range(0, rows, STEP):
        some = pl.ds(first, STEP)
        copy(sheet.at[some], held.at[some])
    for one in copies[:AHEAD]:
        one.start()
    for one in copies[:4]:
        one.wait()
    flat = (BLOCK * HEAD_DIM, cols)
    for first in range(0, rows, BLOCK):
        for r in range(first, first + BLOCK):
            if r % STEP == 0:
                at = 4 + r // STEP
                copies[at].wait()
                for later in copies[at + AHEAD - 4 : at + AHEAD - 3]:
                    later.start()
            value = (mm(wt[...], held[r], NT) * lane_mask(number[0, r], cols)).astype(BF16)
            qk[r] = value.reshape(2 * heads, HEAD_DIM, cols)
        some = pl.ds(first, BLOCK)
        for h in range(heads):
            term = mm(qk[some, h].reshape(flat), qk[some, heads + h].reshape(flat), TN)
            term = term.reshape(acc.shape[1:])
            acc[h] = term if first == 0 else acc[h] + term
    put_shards(me[0], acc, bits, outs)


def query_key(me, lengths, sheet, wq, wk, bits):
    rows, cols, width = sheet.shape
    shards = 1 << len(bits)
    local = wq.shape[0]
    heads = local // HEAD_DIM
    return in_vmem(
        functools.partial(query_key_kernel, bits),
        "query_key",
        [like((rows, 2 * heads, HEAD_DIM, cols)), like(sheet.shape), like(lengths.shape, jnp.int32)]
        + part_shapes(shards, heads, cols),
        me,
        lengths,
        sheet,
        wq,
        wk,
        scalars=1,
        streamed=4,
        scratch=(
            pltpu.VMEM((2 * local, width), BF16),
            pltpu.VMEM((heads, shards, cols // shards, cols), F32),
            pltpu.SMEM(lengths.shape, jnp.int32),
            pltpu.SemaphoreType.DMA((4 + rows // STEP,)),
        ),
        limit=14,
        flops=rows * cols * local * (2 * width + cols) // 2,
    )


def value_kernel(bits, fars, where, sheet, wv, cot, *rest):
    outs, halves, acc = rest[: -1 - len(fars)], rest[-1 - len(fars) : -1], rest[-1]
    rows, cols, width = sheet.shape
    for far, half in zip(fars, halves):
        near = half.shape[1]
        side = lax.shift_right_logical(where[1], 1) ^ (far // 2)
        for s in range(width // near):
            @pl.when(side == s)
            def _():
                half[...] = wv[:, s * near : (s + 1) * near]
    local = wv.shape[0]
    heads = local // HEAD_DIM
    flat = (BLOCK * HEAD_DIM, cols)
    for first in range(0, rows, BLOCK):
        values = []
        for r in range(first, first + BLOCK):
            value = (mm(wv[...], sheet[r], NT) * lane_mask(where[2 + r], cols)).astype(BF16)
            values.append(value.reshape(heads, HEAD_DIM, cols))
        for h in range(heads):
            left = cot[pl.ds(first, BLOCK), h * HEAD_DIM : (h + 1) * HEAD_DIM].reshape(flat)
            right = jnp.concatenate([v[h] for v in values], axis=0)
            term = mm(left, right, TN).reshape(acc.shape[1:])
            acc[h] = term if first == 0 else acc[h] + term
    put_shards(where[0], acc, bits, outs)


def value_dprob(where, sheet, wv, cot, after, bits, fars, devices):
    rows, cols, width = sheet.shape
    shards = 1 << len(bits)
    local = wv.shape[0]
    heads = local // HEAD_DIM
    return in_vmem(
        functools.partial(value_kernel, bits, fars),
        "value_dprob",
        part_shapes(shards, heads, cols) + [like((local, 2 * width // devices))] * len(fars),
        where,
        sheet,
        wv,
        cot,
        scalars=1,
        after=after,
        scratch=(pltpu.VMEM((heads, shards, cols // shards, cols), F32),),
        limit=16,
        flops=4 * rows * cols * local * (width + cols),
    )


def turn_kernel(where, wq, wk, wv, natural, *full):
    near, share, columns = natural.shape
    local = wq.shape[0]
    for index, (weight, held) in enumerate(zip((wq, wk, wv), full)):
        held[...] = weight[...].T.reshape(held.shape)
        mine = where[1] & (held.shape[0] - 1)
        for j in range(near):
            natural[j, :, index * local : (index + 1) * local] = held[mine ^ j]


def turn(where, wq, wk, wv, devices, after):
    local, width = wq.shape
    share = width // devices
    return in_vmem(
        turn_kernel,
        "turn",
        (like((2, share, 3 * local)),),
        where,
        wq,
        wk,
        wv,
        scalars=1,
        after=after,
        scratch=[pltpu.VMEM((w.shape[1] // share, share, local), BF16) for w in (wq, wk, wv)],
    )[0]


def far_query_key_kernel(where, sheet, wq, wk, qk):
    local = wq.shape[0]
    rows, cols, _ = sheet.shape
    both = jnp.concatenate([wq[...], wk[...]], axis=0)
    for r in range(rows):
        value = (mm(both, sheet[r], NT) * lane_mask(where[2 + r], cols)).astype(BF16)
        qk[r] = value.reshape(2 * local // HEAD_DIM, HEAD_DIM, cols)


def far_query_key(where, sheet, wq, wk, after):
    rows, cols, width = sheet.shape
    local = wq.shape[0]
    return in_vmem(
        far_query_key_kernel,
        "far_query_key",
        (like((rows, 2 * local // HEAD_DIM, HEAD_DIM, cols)),),
        where,
        sheet,
        wq,
        wk,
        scalars=1,
        after=after,
        flops=4 * rows * cols * local * width,
    )[0]


def part_shapes(shards, heads, cols):
    if shards == 1:
        return [like((1, heads, cols, cols), F32)]
    half = (shards // 2, heads, cols // shards, cols)
    return [like(half, F32), like(half)]


def hold_kernel(values, out):
    out[...] = values[...]


def hold(values, after):
    return in_vmem(hold_kernel, "hold", (like(values.shape),), values, after=after)[0]


def add_split_kernel(keep, got, give_out, keep_out):
    for j in range(keep.shape[0]):
        total = keep[j].astype(F32) + got[j].astype(F32)
        out = give_out if j % 2 else keep_out
        out[j // 2] = total.astype(out.dtype)


def add_split(keep, got, after=(), flops=0):
    half = (keep.shape[0] // 2,) + keep.shape[1:]
    return in_vmem(add_split_kernel, "add_split", (like(half), like(half, keep.dtype)), keep, got, after=after, flops=flops)


def halve(keep, give, axis, bits, after=(), flops=0):
    after = list(after) + [()] * len(bits)
    for bit, waits in zip(bits[:-1], after):
        give, keep = add_split(keep, flip(give, axis, bit), waits, flops)
    return keep, flip(give, axis, bits[-1])


def softmax_kernel(scale, *refs):
    *terms, probs_out, dscore_out = refs
    half = len(terms) // 2
    total = lambda some: functools.reduce(jnp.add, [t[0].astype(F32) for t in some])
    logits = total(terms[:half]) * scale
    dprob = total(terms[half:])
    shifted = jnp.exp(logits - jnp.max(logits, axis=-1, keepdims=True))
    probs = shifted / jnp.sum(shifted, axis=-1, keepdims=True)
    inner = jnp.sum(probs * dprob, axis=-1, keepdims=True)
    probs_out[0] = probs.astype(BF16)
    dscore_out[0] = (scale * probs * (dprob - inner)).astype(BF16)


def softmax_back(logits, dprob, scale, after=()):
    out = like(logits[0].shape)
    return in_vmem(
        functools.partial(softmax_kernel, scale), "softmax_back", (out, out), *logits, *dprob, limit=16, after=after
    )


def join_kernel(one, other, out):
    out[: one.shape[0]] = one[...]
    out[one.shape[0] :] = other[...]


def join(one, other, after):
    shape = (one.shape[0] + other.shape[0],) + one.shape[1:]
    return in_vmem(join_kernel, "join", (like(shape),), one, other, after=after)[0]


def double(values, axis, bits, after=()):
    order = [0]
    after = list(after) + [()] * len(bits)
    for bit, waits in zip(bits[:-1], after):
        values = join(values, flip(values, axis, bit), waits)
        order = order + [j ^ bit for j in order]
    other = flip(values, axis, bits[-1])
    return (values, other), (order, [j ^ bits[-1] for j in order])


def assemble_kernel(orders, where, *refs):
    *pieces, out = refs
    for piece, (kind, order) in zip(pieces, orders):
        for t, j in enumerate(order):
            out[kind, where[0] ^ j] = piece[t]


def assemble(where, probs, dscore, orders, shards, after):
    orders = [(kind, order) for kind, both in enumerate(orders) for order in both]
    out = like((2, shards) + probs[0].shape[1:])
    return in_vmem(
        functools.partial(assemble_kernel, orders),
        "assemble",
        (out,),
        where,
        *probs,
        *dscore,
        scalars=1,
        after=after,
    )[0]


def gradients(where, first, count, scores, qk, cot, grads):
    cols = qk.shape[-1]
    heads = qk.shape[1] // 2
    rows = pl.ds(first, count)
    flat = (count * HEAD_DIM, cols)
    split = (count, HEAD_DIM, cols)
    masks = jnp.stack([lane_mask(where[2 + first + r], cols) for r in range(count)])
    for h in range(heads):
        p, ds = [scores[kind, :, h].reshape(cols, cols) for kind in range(2)]
        g = cot[rows, h * HEAD_DIM : (h + 1) * HEAD_DIM].reshape(flat)
        dq = mm(qk[rows, heads + h].reshape(flat), ds, NT)
        dk = mm(qk[rows, h].reshape(flat), ds, NN)
        dv = mm(g, p, NN)
        for index, value in enumerate((dq, dk, dv)):
            grads[:, index * heads + h] = (value.reshape(split) * masks).astype(BF16)


def gradients_kernel(where, scores, qk, cot, grads):
    gradients(where, 0, qk.shape[0], scores, qk, cot, grads)


def all_gradients(where, scores, qk, cot, name, after, counted=True):
    rows, two, _, cols = qk.shape
    return in_vmem(
        gradients_kernel,
        name,
        (like((rows, two // 2 * 3, HEAD_DIM, cols)),),
        where,
        scores,
        qk,
        cot,
        scalars=1,
        after=after,
        limit=14,
        counted=counted,
        flops=3 * rows * two * HEAD_DIM * cols * cols,
    )[0]


def own_input_kernel(grads, weights, out):
    near, share, columns = weights.shape
    left = weights[...].reshape(near * share, columns)
    for r in range(grads.shape[0]):
        part = mm(left, grads[r].reshape(columns, grads.shape[-1]), NN).astype(BF16)
        out[:, r] = part.reshape(near, share, grads.shape[-1])


def own_input(grads, weights, after):
    rows, cols = grads.shape[0], grads.shape[-1]
    near, share, columns = weights.shape
    return in_vmem(
        own_input_kernel,
        "own_input",
        (like((near, rows, share, cols)),),
        grads,
        weights,
        after=after,
        flops=2 * rows * cols * near * share * columns,
    )[0]


def far_input_kernel(first, own, *refs):
    *refs, keep, give = refs
    count, share, cols = keep.shape
    for r in range(count):
        total = own[:, first + r].astype(F32)
        for i in range(0, len(refs), 2):
            grads, weights = refs[i : i + 2]
            near, _, columns = weights.shape
            left = weights[...].reshape(near * share, columns)
            part = mm(left, grads[first + r].reshape(columns, cols), NN).astype(BF16)
            total = total + part.reshape(near, share, cols).astype(F32)
        keep[r] = total[0].astype(keep.dtype)
        give[r] = total[1].astype(give.dtype)


def far_input(first, count, own, far, after):
    _, rows, share, cols = own.shape
    columns = far[0][1].shape[-1]
    out = like((count, share, cols))
    return in_vmem(
        functools.partial(far_input_kernel, first),
        "far_input",
        (out, out),
        own,
        *[a for one in far for a in one],
        after=after,
        limit=14,
        flops=4 * len(far) * count * cols * columns * share,
    )


def finish_kernel(*refs):
    *terms, out, total, sems = refs
    copies = []
    first = 0
    for index in range(0, len(terms), 2):
        keep, got = terms[index : index + 2]
        some = pl.ds(first, keep.shape[0])
        total[some] = (keep[...].astype(F32) + got[...].astype(F32)).astype(BF16)
        copies.append(pltpu.make_async_copy(total.at[some], out.at[some], sems.at[index // 2]))
        copies[-1].start()
        first += keep.shape[0]
    for copy in copies:
        copy.wait()


def finish(chunks):
    _, share, cols = chunks[0][0].shape
    rows = sum(keep.shape[0] for keep, _ in chunks)
    terms = [a for chunk in chunks for a in chunk]
    return pl.pallas_call(
        finish_kernel,
        in_specs=[VMEM] * len(terms),
        out_specs=HBM,
        out_shape=like((rows, share, cols)),
        scratch_shapes=[pltpu.VMEM((rows, share, cols), BF16), pltpu.SemaphoreType.DMA((len(chunks),))],
        compiler_params=pltpu.CompilerParams(vmem_limit_bytes=12 * MIB),
        cost_estimate=cost(rows * share * cols, 6 * rows * share * cols),
        name="finish",
    )(*terms)


def weight_product(sheet, grads):
    rows, cols, width = sheet.shape
    columns = grads.shape[1] * HEAD_DIM
    left = [grads[r].reshape(columns, cols) for r in range(rows)]
    return mm(jnp.concatenate(left, axis=1), sheet[...].reshape(rows * cols, width), NN).T


def weight_kernel(bits, where, sheet, grads, *rest):
    outs, full = rest[:-1], rest[-1]
    full[...] = weight_product(sheet, grads).reshape(full.shape)
    for t, j in enumerate(reorder(bits)):
        first = 0
        for keep, give in zip(outs[::2], outs[1::2]):
            out = (keep, give)[t % 2]
            last = first + out.shape[-1]
            out[t // 2] = full[where[0] ^ j, :, first:last].astype(out.dtype)
            first = last


def whole_weight_kernel(_, where, sheet, grads, out):
    out[...] = weight_product(sheet, grads)


def weight_part(where, sheet, grads, cuts, bits, after):
    rows, cols, width = sheet.shape
    shards = 1 << len(bits)
    columns = grads.shape[1] * HEAD_DIM
    if shards == 1:
        kernel, outs, scratch = whole_weight_kernel, [like((width, columns), F32)], ()
    else:
        halves = [(shards // 2, width // shards, cut) for cut in cuts]
        kernel = weight_kernel
        outs = [o for half in halves for o in (like(half, F32), like(half))]
        scratch = (pltpu.VMEM((shards, width // shards, columns), F32),)
    return in_vmem(
        functools.partial(kernel, bits),
        "weight_part",
        outs,
        where,
        sheet,
        grads,
        scalars=1,
        after=after,
        scratch=scratch,
        limit=18,
        flops=2 * rows * cols * width * columns,
    )


def last_kernel(_, keep, got, out):
    total = keep[0] + got[0].astype(F32)
    local = out.shape[-1]
    for index in range(out.shape[0]):
        out[index] = total[:, index * local : (index + 1) * local]


def last_sum(before, keep, got, local):
    shape = (keep.shape[2] // local, keep.shape[1], local)
    return in_vmem(last_kernel, "last_sum", (like(shape, F32),), before, keep, got, streamed=1)[0]


def body(sheet, w_query, w_key, w_value, cotangent, lengths):
    row_dev, cols, width = sheet.shape
    local = w_query.shape[1]
    n_rows = lax.axis_size("rows")
    n_heads = lax.axis_size("heads")
    scale = float(1.0 / (HEAD_DIM * row_dev * n_rows) ** 0.5)
    direct = n_rows <= 8
    shards = n_rows if direct else 1
    row_bits = [1 << b for b in range(n_rows.bit_length() - 1)]
    chunk = row_dev // 2

    me = jnp.stack([lax.axis_index("rows"), lax.axis_index("heads")]).astype(jnp.int32)
    wq, wk, wv = w_query.T, w_key.T, w_value.T
    cot = jnp.swapaxes(cotangent, 1, 2)

    fars = range(2, n_heads, 2)
    far_cot = [flip(cot, "heads", f) for f in fars]
    fq, fk = [[flip(w, "heads", f) for f in fars] for w in (wq, wk)]
    up = row_bits if direct else []
    turn_about = up[1:] + up[:1]
    qk, held, seen, *logits = query_key(me, lengths.reshape(1, row_dev), sheet, wq, wk, turn_about)
    where = jnp.concatenate([me, seen.reshape(row_dev)])
    dprob = value_dprob(where, held, wv, cot, logits[-1:], up, fars, n_heads)
    dprob, halves = dprob[: -len(fars)], dprob[-len(fars) :]
    fv = [flip(half, "heads", f) for half, f in zip(halves, fars)]
    weights = turn(where, wq, wk, wv, n_heads, dprob[-1:])
    if direct:
        logits = halve(*logits, "rows", turn_about)
        dprob = halve(*dprob, "rows", up)
        probs, dscore = softmax_back(logits, dprob, scale, [weights])
        probs, probs_order = double(probs, "rows", up[::-1], [far_cot])
        dscore, dscore_order = double(dscore, "rows", turn_about[::-1])
        scores = assemble(where, probs, dscore, (probs_order, dscore_order), shards, fq)
    else:
        logits, dprob = lax.psum((logits, dprob), "rows")
        scores = jnp.stack(softmax_back(logits, dprob, scale))
    far_scores = [flip(scores, "heads", f) for f in fars]
    grads = all_gradients(where, scores, qk, cot, "own_gradients", ())
    weight_bits = up[:1] + up[1:][::-1]
    parts = weight_part(where, held, grads, (3 * local,), weight_bits, fv)
    ready = [parts[-1]]
    far_qk = [far_query_key(where, held, *w, ready) for w in zip(fq, fk)]
    far_natural = [turn(where, *w, n_heads, ready) for w in zip(fq, fk, fv)]
    own = own_input(grads, weights, ready)
    ready = [own] + far_qk + far_natural
    first_sum = []
    if direct:
        keep, give = parts
        give, keep = add_split(keep, flip(give, "rows", weight_bits[0]), ready)
        first_sum = [keep]
    else:
        weight_grad = lax.psum_scatter(parts[0], "rows", scatter_dimension=0, tiled=True)
        weight_grad = weight_grad.reshape(width // n_rows, 3, local)
    far_grads = [
        all_gradients(where, *args, "far_gradients", first_sum, False)
        for args in zip(far_scores, far_qk, far_cot)
    ]
    chunks = []
    for first in range(0, row_dev, chunk):
        keep_rows, give_rows = far_input(first, chunk, own, list(zip(far_grads, far_natural)), ())
        chunks.append((keep_rows, flip(give_rows, "heads", 1)))
    if direct:
        last = halve(keep, give, "rows", weight_bits[1:], [[chunks[-1][0]]], 1 << 34)
    out = finish(chunks)
    if direct:
        weight_grad = jnp.swapaxes(last_sum(out, *last, local), 0, 1)
    return (jnp.swapaxes(out, 1, 2), weight_grad)


def solution(mesh):
    in_specs = (
        P("rows", None, None),
        P(None, "heads"),
        P(None, "heads"),
        P(None, "heads"),
        P("rows", None, "heads"),
        P("rows"),
    )
    out_specs = (P("rows", None, "heads"), P("rows", None, "heads"))
    return jax.shard_map(body, mesh=mesh, in_specs=in_specs, out_specs=out_specs, check_vma=False)
```
